32 devices in a mesh: tile: 16 (over z, y, x), head: 2 (over core).
Axes of the slice: x: 2, y: 2, z: 4, core: 2. Of those that a mesh axis runs over, the one named last changes fastest.
Arguments:
- queries: bfloat16 [4096, 1024], P('tile', 'head'), may hold values from -6 to 6
- keys: bfloat16 [4096, 1024], P('tile', 'head'), may hold values from -6 to 6
- values: bfloat16 [4096, 1024], P('tile', 'head'), may hold values from -6 to 6
- grad_output: bfloat16 [4096, 1024], P('tile', 'head'), may hold values from -6 to 6
- out_weight: bfloat16 [1024, 1024], P(None, 'head'), may hold values from -0.1875 to 0.1875
- rotations: int32 [16, 4], P('tile'), may hold values from 0 to 3, as said below
Outputs:
- grad_queries: bfloat16 [4096, 1024], P('tile', 'head')
- grad_keys: bfloat16 [4096, 1024], P('tile', 'head')
- grad_values: bfloat16 [4096, 1024], P('tile', 'head')
- grad_out_weight: float32 [1024, 1024], P('tile', 'head')
The draws below stay inside these ranges and needn't reach their ends.
Inputs may be any that keep to these rules, and one draw needn't show every extreme that they name: The tiles form 4 rows of 4 in row-major order, grouped into faces of max(1, 2) whole columns; rotations[t, s] is 0 unless side s of tile t crosses a seam, that is an east or west side between two faces or a north or south side between the last and the first row. Across a seam the two facing sides hold r and (4 - r) mod 4 with r equal to 1 or 3.
All inputs are finite; a program needn't handle non-finite values.
Results may differ from the reference program's by a relative error of at most 0.012.
Values may be sent and summed in bfloat16 or wider, within the bound.
No kernel may reach another device: no remote copies, remote signals or barrier semaphores. Data moves between devices by JAX's collectives and lax.ppermute only.
A program may use at most 64 MiB of HBM per device.

```python
import functools
import math
import jax
import jax.numpy as jnp
from jax import lax

D = 1024
HEAD_DIM = 64
RADIUS = 6
SIDE = 16
TOKENS = 4096
N_TILE = 16


def query_key_pair(key):
    base = jax.random.fold_in(key, 4242)
    first, second = jax.random.split(base, 2)
    shape = (TOKENS, D)
    query_part = jnp.clip(jax.random.normal(first, shape, jnp.float32), -6.0, 6.0)
    key_part = jnp.clip(jax.random.normal(second, shape, jnp.float32), -6.0, 6.0)
    return (query_part, key_part)


def draw_queries(key, part):
    return query_key_pair(key)[0].astype(jnp.bfloat16)


def draw_keys(key, part):
    return query_key_pair(key)[1].astype(jnp.bfloat16)


def draw_rotations(key, part):
    columns = N_TILE // 4
    face_cols = max(N_TILE // 16, 2)
    base = jax.random.fold_in(key, 7717)
    east_key, south_key = jax.random.split(base, 2)
    east_table = jax.random.randint(east_key, (N_TILE,), 0, 2, dtype=jnp.int32) * 2 + 1
    south_table = jax.random.randint(south_key, (N_TILE,), 0, 2, dtype=jnp.int32) * 2 + 1
    tiles = jnp.arange(N_TILE, dtype=jnp.int32)
    column = tiles % columns
    west_tile = (tiles - 1) % N_TILE
    north_tile = (tiles - columns) % N_TILE
    east_seam = (column + 1) % face_cols == 0
    west_seam = (west_tile % columns + 1) % face_cols == 0
    south_seam = tiles >= N_TILE - columns
    north_seam = tiles < columns
    zero = jnp.zeros((N_TILE,), jnp.int32)
    east = jnp.where(east_seam, east_table, zero)
    west = jnp.where(west_seam, (4 - east_table[west_tile]) % 4, zero)
    south = jnp.where(south_seam, south_table, zero)
    north = jnp.where(north_seam, (4 - south_table[north_tile]) % 4, zero)
    return jnp.stack([north, east, south, west], axis=1).astype(jnp.int32)


def raised(array, key, source, target, shards_of, factor):
    owner, partner = [(jnp.arange(array.shape[dim]) // (array.shape[dim] // shards_of)).reshape([-1 if axis == dim else 1 for axis in range(array.ndim)]) for dim in (source, target)]
    chosen = jax.random.permutation(key, shards_of)[partner]
    strong = (owner == chosen) | (owner == (partner + shards_of // 2) % shards_of)
    return jnp.where(strong, factor * array, array)


def block_scale(key, dims, cuts, least, largest):
    level, own = 1.0, jax.random.fold_in(key, 6)
    for axis_at, blocks in cuts:
        heights = jnp.exp(jax.random.uniform(jax.random.fold_in(own, axis_at), (blocks,), jnp.float32, least / len(cuts), largest / len(cuts)))
        level = level * jnp.repeat(heights, dims[axis_at] // blocks).reshape([-1 if axis == axis_at else 1 for axis in range(len(dims))])
    return level


def noise(stream_key, shape, spread, limit, cuts=(), kind=jnp.bfloat16):
    level = block_scale(stream_key, shape, cuts, -0.22, 0.18) if cuts else 1.0
    array = jax.random.normal(stream_key, shape, jnp.float32) * spread * level
    return jnp.minimum(jnp.maximum(array, -limit), limit).astype(kind)


def heavy_noise(rng, shape, width, bound, cuts, heavy, kind=jnp.bfloat16):
    values = width * jax.random.normal(rng, shape, jnp.float32)
    if cuts:
        values = values * block_scale(rng, shape, cuts, -0.22, 0.18)
    return jnp.clip(raised(values, jax.random.fold_in(rng, 3), *heavy), -bound, bound).astype(kind)


def setup_inputs(seed: int = 0) -> dict:
    splits = jax.random.split(jax.random.key(seed), 7)
    queries = draw_queries(jax.random.fold_in(splits[6], 71), 0)
    keys = draw_keys(jax.random.fold_in(splits[6], 71), 0)
    values = noise(splits[2], (TOKENS, D), 1.0, 6.0, ((0, 16), (1, 2)))
    grad_output = heavy_noise(splits[3], (TOKENS, D), 1.0, 6.0, ((0, 16), (1, 2)), (0, 1, 16, 2.0))
    out_weight = noise(splits[4], (D, D), D ** -0.5, 0.1875, ((1, 2),))
    rotations = draw_rotations(jax.random.fold_in(splits[6], 71), 0)
    return {"queries": queries, "keys": keys, "values": values, "grad_output": grad_output, "out_weight": out_weight, "rotations": rotations}


def turned_rim(tile_grid, number):
    return jnp.rot90(tile_grid, number)[tile_grid.shape[0] - RADIUS:]

def rim_strip(tile_grid, turn_count):
    branches = [functools.partial(turned_rim, number=number) for number in range(4)]
    return lax.switch(turn_count, branches, tile_grid)

def placed_back(strip, number, tile_side):
    padded = jnp.pad(strip, ((tile_side - RADIUS, 0), (0, 0), (0, 0)))
    return jnp.rot90(padded, -number)

def place_back(strip, turn_count, tile_side):
    branches = [functools.partial(placed_back, number=number, tile_side=tile_side) for number in range(4)]
    return lax.switch(turn_count, branches, strip)

def extend(tile_grid, strips):
    tile_side = tile_grid.shape[0]
    extended = jnp.pad(tile_grid, ((RADIUS, RADIUS), (RADIUS, RADIUS), (0, 0)))
    for side_index in range(4):
        turned = jnp.rot90(extended, side_index)
        turned = turned.at[:RADIUS, RADIUS:RADIUS + tile_side].set(strips[side_index])
        extended = jnp.rot90(turned, -side_index)
    return extended

def inner_rim(extended, side_index, tile_side):
    return jnp.rot90(extended, side_index)[:RADIUS, RADIUS:RADIUS + tile_side]

def window_backward(query_grid, key_ext, value_ext, dout_grid):
    tile_side = query_grid.shape[0]
    features = query_grid.shape[-1]
    extended = tile_side + 2 * RADIUS
    score_scale = HEAD_DIM ** (-0.5)
    query_rows = query_grid.reshape(tile_side * tile_side, features)
    dout_rows = dout_grid.reshape(tile_side * tile_side, features)
    key_rows = key_ext.reshape(extended * extended, features)
    value_rows = value_ext.reshape(extended * extended, features)
    query_index = jnp.arange(tile_side * tile_side, dtype=jnp.int32)
    query_row = query_index // tile_side + RADIUS
    query_col = query_index % tile_side + RADIUS
    cell_index = jnp.arange(extended * extended, dtype=jnp.int32)
    cell_row = cell_index // extended
    cell_col = cell_index % extended
    outer_row = (cell_row < RADIUS) | (cell_row >= RADIUS + tile_side)
    outer_col = (cell_col < RADIUS) | (cell_col >= RADIUS + tile_side)
    corner = outer_row & outer_col
    allowed = (jnp.abs(cell_row[None, :] - query_row[:, None]) <= RADIUS) & (jnp.abs(cell_col[None, :] - query_col[:, None]) <= RADIUS) & jnp.logical_not(corner)[None, :]
    attention_list = []
    grad_query_list = []
    grad_key_list = []
    grad_value_list = []
    for head_index in range(features // HEAD_DIM):
        head_cols = slice(head_index * HEAD_DIM, (head_index + 1) * HEAD_DIM)
        query_head = query_rows[:, head_cols]
        key_head = key_rows[:, head_cols]
        value_head = value_rows[:, head_cols]
        dout_head = dout_rows[:, head_cols]
        scores = lax.dot_general(query_head, key_head, (((1,), (1,)), ((), ())), preferred_element_type=jnp.float32) * score_scale
        scores = jnp.where(allowed, scores, -1e+30)
        row_max = lax.optimization_barrier(jnp.max(scores, axis=1, keepdims=True))
        raw_weights = jnp.exp(scores - row_max)
        weights = raw_weights / lax.optimization_barrier(jnp.sum(raw_weights, axis=1, keepdims=True))
        weights_bf = weights.astype(jnp.bfloat16)
        attention = jnp.dot(weights_bf, value_head, preferred_element_type=jnp.float32)
        row_delta = lax.optimization_barrier(jnp.sum(dout_head.astype(jnp.float32) * attention, axis=1, keepdims=True))
        grad_weights = lax.dot_general(dout_head, value_head, (((1,), (1,)), ((), ())), preferred_element_type=jnp.float32)
        dscore = (weights * (grad_weights - row_delta)).astype(jnp.bfloat16)
        grad_query = jnp.dot(dscore, key_head, preferred_element_type=jnp.float32) * score_scale
        grad_key = lax.dot_general(dscore, query_head, (((0,), (0,)), ((), ())), preferred_element_type=jnp.float32) * score_scale
        grad_value = lax.dot_general(weights_bf, dout_head, (((0,), (0,)), ((), ())), preferred_element_type=jnp.float32)
        attention_list.append(attention)
        grad_query_list.append(grad_query)
        grad_key_list.append(grad_key)
        grad_value_list.append(grad_value)
    attention_all = jnp.concatenate(attention_list, axis=1)
    grad_query_all = jnp.concatenate(grad_query_list, axis=1)
    grad_key_all = jnp.concatenate(grad_key_list, axis=1).reshape(extended, extended, features)
    grad_value_all = jnp.concatenate(grad_value_list, axis=1).reshape(extended, extended, features)
    return (attention_all, grad_query_all, grad_key_all, grad_value_all)

def reference(queries, keys, values, grad_output, out_weight, rotations):
    tile_count = N_TILE
    features = D
    tile_side = SIDE
    dout = jnp.dot(grad_output, out_weight, preferred_element_type=jnp.float32).astype(jnp.bfloat16)
    query_tiles = queries.reshape(tile_count, tile_side, tile_side, features)
    dout_tiles = dout.reshape(tile_count, tile_side, tile_side, features)
    pair_tiles = jnp.concatenate([keys, values], axis=1).reshape(tile_count, tile_side, tile_side, 2 * features)
    offsets = (-(tile_count // 4), 1, tile_count // 4, -1)
    tile_numbers = jnp.arange(tile_count, dtype=jnp.int32)

    def one_tile(tile_index):
        strips = []
        for side_index in range(4):
            neighbour = (tile_index + offsets[side_index]) % tile_count
            turn_count = ((side_index + rotations[tile_index, side_index]) % 4).astype(jnp.int32)
            strips.append(rim_strip(pair_tiles[neighbour], turn_count))
        extended = extend(pair_tiles[tile_index], strips)
        attention, grad_query, grad_key, grad_value = window_backward(query_tiles[tile_index], extended[..., :features], extended[..., features:], dout_tiles[tile_index])
        grad_pair = jnp.concatenate([grad_key, grad_value], axis=-1)
        centre = grad_pair[RADIUS:RADIUS + tile_side, RADIUS:RADIUS + tile_side]
        backs = jnp.stack([inner_rim(grad_pair, side_index, tile_side) for side_index in range(4)])
        return (attention.astype(jnp.bfloat16), grad_query.astype(jnp.bfloat16), centre, backs)
    attention_bf, grad_query, centres, backs = lax.map(one_tile, tile_numbers)

    def owner(tile_index):
        total = centres[tile_index]
        for side_index in range(4):
            source = (tile_index - offsets[side_index]) % tile_count
            turn_count = ((side_index + rotations[source, side_index]) % 4).astype(jnp.int32)
            total = total + place_back(backs[source, side_index], turn_count, tile_side)
        return total.astype(jnp.bfloat16)
    grad_pair = lax.map(owner, tile_numbers)
    grad_keys = grad_pair[..., :features].reshape(TOKENS, features)
    grad_values = grad_pair[..., features:].reshape(TOKENS, features)
    grad_queries = grad_query.reshape(TOKENS, features)
    attention_rows = attention_bf.reshape(TOKENS, features)
    grad_out_weight = lax.dot_general(grad_output, attention_rows, (((0,), (0,)), ((), ())), preferred_element_type=jnp.float32) * (1.0 / math.sqrt(TOKENS))
    return (grad_queries, grad_keys, grad_values, grad_out_weight)
```

```python
import functools
import math

import jax
import jax.numpy as jnp
from jax import lax
from jax.experimental import pallas as pl
from jax.experimental.pallas import tpu as pltpu
from jax.sharding import PartitionSpec as P

HEAD_DIM = 64
RADIUS = 6
SIDE = 16
CELLS = SIDE * SIDE
STRIP = RADIUS * SIDE
EXT = CELLS + 4 * STRIP
PAIR = 2 * HEAD_DIM
VMEM_LIMIT = 40 * 1024 * 1024
NT = (((1,), (1,)), ((), ()))


def mm(a, b):
    return jnp.dot(a, b, preferred_element_type=jnp.float32)


def mm_nt(a, b):
    return lax.dot_general(a, b, NT, preferred_element_type=jnp.float32)


def strip_token(side_index, rotation, cell):
    turn = lax.rem(side_index + 6 - rotation, 4)
    depth = cell >> 4
    along = cell & (SIDE - 1)
    far = SIDE - 1 - along
    near_rim = RADIUS - 1 - depth
    far_rim = SIDE - RADIUS + depth
    row = jnp.where(turn == 0, far_rim, jnp.where(turn == 1, along, jnp.where(turn == 2, near_rim, far)))
    col = jnp.where(turn == 0, along, jnp.where(turn == 1, near_rim, jnp.where(turn == 2, far, far_rim)))
    return row * SIDE + col


def pick_kernel(rotations_ref, keys_ref, values_ref, north_ref, east_ref, south_ref, west_ref):
    cell = lax.broadcasted_iota(jnp.int32, (STRIP, CELLS), 0)
    token = lax.broadcasted_iota(jnp.int32, (STRIP, CELLS), 1)
    for side_index, out_ref in enumerate((north_ref, east_ref, south_ref, west_ref)):
        wanted = strip_token(side_index, rotations_ref[0, side_index], cell)
        chosen = jnp.where(token == wanted, 1.0, 0.0).astype(jnp.bfloat16)
        out_ref[0] = mm(chosen, keys_ref[...]).astype(jnp.bfloat16)
        out_ref[1] = mm(chosen, values_ref[...]).astype(jnp.bfloat16)


def merge_kernel(rotations_ref, centre_ref, north_ref, east_ref, south_ref, west_ref, keys_ref, values_ref):
    token = lax.broadcasted_iota(jnp.int32, (CELLS, STRIP), 0)
    cell = lax.broadcasted_iota(jnp.int32, (CELLS, STRIP), 1)
    total_keys = centre_ref[0]
    total_values = centre_ref[1]
    for side_index, back_ref in enumerate((north_ref, east_ref, south_ref, west_ref)):
        wanted = strip_token(side_index, rotations_ref[0, side_index], cell)
        chosen = jnp.where(token == wanted, 1.0, 0.0).astype(jnp.bfloat16)
        total_keys += mm(chosen, back_ref[0])
        total_values += mm(chosen, back_ref[1])
    keys_ref[...] = total_keys.astype(jnp.bfloat16)
    values_ref[...] = total_values.astype(jnp.bfloat16)


def window_bias(bias_ref):
    query = lax.broadcasted_iota(jnp.int32, (CELLS, CELLS), 1)
    cell = lax.broadcasted_iota(jnp.int32, (CELLS, CELLS), 0)

    def bias(cell_row, cell_col, query):
        query_row = (query >> 4) + RADIUS
        query_col = (query & (SIDE - 1)) + RADIUS
        near = (jnp.abs(cell_row - query_row) <= RADIUS) & (jnp.abs(cell_col - query_col) <= RADIUS)
        return jnp.where(near, 0.0, -1e30)

    bias_ref[0:CELLS, :] = bias((cell >> 4) + RADIUS, (cell & (SIDE - 1)) + RADIUS, query)
    query = lax.broadcasted_iota(jnp.int32, (STRIP, CELLS), 1)
    cell = lax.broadcasted_iota(jnp.int32, (STRIP, CELLS), 0)
    depth = cell >> 4
    along = cell & (SIDE - 1)
    last = SIDE + 2 * RADIUS - 1
    places = (
        (depth, RADIUS + along),
        (RADIUS + along, last - depth),
        (last - depth, last - RADIUS - along),
        (last - RADIUS - along, depth),
    )
    for side_index, (cell_row, cell_col) in enumerate(places):
        start = CELLS + side_index * STRIP
        bias_ref[start : start + STRIP, :] = bias(cell_row, cell_col, query)


def one_head(block, head):
    lane = lax.broadcasted_iota(jnp.int32, block.shape, 1)
    kept = (lane >= HEAD_DIM) if head else (lane < HEAD_DIM)
    return jnp.where(kept, block, jnp.zeros_like(block))


def joined(own_ref, strip_refs, index):
    return jnp.concatenate([own_ref[...]] + [ref[index] for ref in strip_refs], axis=0)


def forward_kernel(
    pairs, query_ref, key_ref, value_ref, north_ref, east_ref, south_ref, west_ref, turned_ref,
    weights_ref, partial_ref, bias_ref, attention_ref,
):
    step = pl.program_id(0)

    @pl.when(step == 0)
    def _():
        window_bias(bias_ref)

    strips = (north_ref, east_ref, south_ref, west_ref)
    key_ext = joined(key_ref, strips, 0)
    value_turned = joined(value_ref, strips, 1).T
    query = query_ref[...]
    scale = HEAD_DIM ** (-0.5) * math.log2(math.e)
    parts = []
    for head in range(2):
        scores = mm_nt(key_ext, one_head(query, head)) + bias_ref[...]
        top = jnp.max(scores, axis=0, keepdims=True)
        raw = jnp.exp2((scores - top) * scale)
        weights = (raw * (1.0 / jnp.sum(raw, axis=0, keepdims=True))).astype(jnp.bfloat16)
        weights_ref[0, :, head * CELLS : (head + 1) * CELLS] = weights
        parts.append(mm(value_turned[head * HEAD_DIM : (head + 1) * HEAD_DIM], weights))
    attention = jnp.concatenate(parts, axis=0).T
    start = pl.multiple_of(step * PAIR, PAIR)
    attention_ref[:, pl.ds(start, PAIR)] = attention.astype(jnp.bfloat16)

    @pl.when(step == pairs - 1)
    def _():
        partial_ref[...] = mm(turned_ref[...], attention_ref[...]).astype(jnp.bfloat16)


def backward_kernel(
    query_ref, key_ref, value_ref, north_ref, east_ref, south_ref, west_ref, dout_ref, weights_ref,
    grad_query_ref, centre_ref, north_out, east_out, south_out, west_out,
):
    strips = (north_ref, east_ref, south_ref, west_ref)
    key_turned = joined(key_ref, strips, 0).T
    value_ext = joined(value_ref, strips, 1)
    query = query_ref[...]
    dout = dout_ref[...]
    score_scale = HEAD_DIM ** (-0.5)
    grad_key = None
    grad_value = None
    parts = []
    for head in range(2):
        query_head = one_head(query, head)
        dout_head = one_head(dout, head)
        weights_bf = weights_ref[0, :, head * CELLS : (head + 1) * CELLS]
        weights = weights_bf.astype(jnp.float32)
        grad_weights = mm_nt(value_ext, dout_head)
        row_delta = jnp.sum(weights * grad_weights, axis=0, keepdims=True)
        dscore = (weights * (grad_weights - row_delta)).astype(jnp.bfloat16)
        key_term = mm(dscore, query_head)
        value_term = mm(weights_bf, dout_head)
        grad_key = key_term if grad_key is None else grad_key + key_term
        grad_value = value_term if grad_value is None else grad_value + value_term
        parts.append(mm(key_turned[head * HEAD_DIM : (head + 1) * HEAD_DIM], dscore))
    grad_query = jnp.concatenate(parts, axis=0).T * score_scale
    grad_query_ref[...] = grad_query.astype(jnp.bfloat16)
    grad_key = grad_key * score_scale
    centre_ref[0] = grad_key[:CELLS]
    centre_ref[1] = grad_value[:CELLS]
    for side_index, out_ref in enumerate((north_out, east_out, south_out, west_out)):
        start = CELLS + side_index * STRIP
        out_ref[0] = grad_key[start : start + STRIP].astype(jnp.bfloat16)
        out_ref[1] = grad_value[start : start + STRIP].astype(jnp.bfloat16)


def params():
    return pltpu.CompilerParams(vmem_limit_bytes=VMEM_LIMIT)


def from_behind(block, axis, distance):
    devices = range(lax.axis_size(axis))
    route = [((i - distance) % len(devices), i) for i in devices]
    return lax.ppermute(block, axis, route)


def shards(queries, keys, values, grad_output, out_weight, rotations):
    tile_count = lax.axis_size("tile")
    token_count, features = queries.shape
    model = out_weight.shape[0]
    pairs = features // PAIR
    bf16 = jnp.bfloat16
    offsets = (-(tile_count // 4), 1, tile_count // 4, -1)
    smem = pl.BlockSpec(memory_space=pltpu.SMEM)
    vmem = pl.BlockSpec(memory_space=pltpu.VMEM)
    strip_type = jax.ShapeDtypeStruct((2, STRIP, features), bf16)

    picked = pl.pallas_call(
        pick_kernel,
        out_shape=[strip_type] * 4,
        in_specs=[smem, vmem, vmem],
        out_specs=[vmem] * 4,
        compiler_params=params(),
        name="pick_strips",
    )(rotations, keys, values)
    strips = [from_behind(picked[(s + 2) % 4], "tile", -offsets[s]) for s in range(4)]

    cotangent = lax.all_gather(grad_output, "head", axis=1, tiled=True)
    dout = jnp.dot(cotangent, out_weight, preferred_element_type=jnp.float32).astype(bf16)

    rows_spec = pl.BlockSpec((CELLS, PAIR), lambda p: (0, p))
    strip_spec = pl.BlockSpec((2, STRIP, PAIR), lambda p: (0, 0, p))
    weights_spec = pl.BlockSpec((1, EXT, 2 * CELLS), lambda p: (p, 0, 0))
    weights, partial = pl.pallas_call(
        functools.partial(forward_kernel, pairs),
        grid=(pairs,),
        out_shape=[
            jax.ShapeDtypeStruct((pairs, EXT, 2 * CELLS), bf16),
            jax.ShapeDtypeStruct((model, features), bf16),
        ],
        in_specs=[rows_spec] * 3 + [strip_spec] * 4 + [pl.BlockSpec((model, CELLS), lambda p: (0, 0))],
        out_specs=[weights_spec, pl.BlockSpec((model, features), lambda p: (0, 0))],
        scratch_shapes=[pltpu.VMEM((EXT, CELLS), jnp.float32), pltpu.VMEM((CELLS, features), bf16)],
        compiler_params=params(),
        name="attention_forward",
    )(queries, keys, values, *strips, cotangent.T)

    chunk = model // tile_count
    spread = lax.all_to_all(
        partial.reshape(tile_count, chunk, features), "tile", split_axis=0, concat_axis=0
    )

    grad_queries, centre, *backs = pl.pallas_call(
        backward_kernel,
        grid=(pairs,),
        out_shape=[
            jax.ShapeDtypeStruct((CELLS, features), bf16),
            jax.ShapeDtypeStruct((2, CELLS, features), jnp.float32),
        ]
        + [strip_type] * 4,
        in_specs=[rows_spec] * 3 + [strip_spec] * 4 + [rows_spec, weights_spec],
        out_specs=[rows_spec, pl.BlockSpec((2, CELLS, PAIR), lambda p: (0, 0, p))] + [strip_spec] * 4,
        compiler_params=params(),
        name="attention_backward",
    )(queries, keys, values, *strips, dout, weights)

    returned = [from_behind(backs[(s + 2) % 4], "tile", -offsets[s]) for s in range(4)]
    grad_keys, grad_values = pl.pallas_call(
        merge_kernel,
        out_shape=[jax.ShapeDtypeStruct((CELLS, features), bf16)] * 2,
        in_specs=[smem] + [vmem] * 5,
        out_specs=[vmem] * 2,
        compiler_params=params(),
        name="merge_strips",
    )(rotations, centre, *returned)

    grad_out_weight = jnp.sum(spread.astype(jnp.float32), axis=0) * (
        1.0 / math.sqrt(token_count * tile_count)
    )
    return (grad_queries, grad_keys, grad_values, grad_out_weight)


def solution(mesh):
    placed = (
        P("tile", "head"),
        P("tile", "head"),
        P("tile", "head"),
        P("tile", "head"),
        P(None, "head"),
        P("tile", None),
    )
    return jax.shard_map(
        shards,
        mesh=mesh,
        in_specs=placed,
        out_specs=(P("tile", "head"), P("tile", "head"), P("tile", "head"), P("tile", "head")),
        check_vma=False,
    )
```

```python
import functools
import math

import jax
import jax.numpy as jnp
from jax import lax
from jax.experimental import pallas as pl
from jax.experimental.pallas import tpu as pltpu
from jax.sharding import PartitionSpec as P

HEAD_DIM = 64
RADIUS = 6
SIDE = 16
CELLS = SIDE * SIDE
STRIP = RADIUS * SIDE
EXT = CELLS + 4 * STRIP
PAIR = 2 * HEAD_DIM
VMEM_LIMIT = 32 * 1024 * 1024
NT = (((1,), (1,)), ((), ()))


def mm(a, b):
    return jnp.dot(a, b, preferred_element_type=jnp.float32)


def mm_nt(a, b):
    return lax.dot_general(a, b, NT, preferred_element_type=jnp.float32)


def strip_token(side_index, rotation, cell):
    turn = lax.rem(side_index + 6 - rotation, 4)
    depth = cell >> 4
    along = cell & (SIDE - 1)
    far = SIDE - 1 - along
    near_rim = RADIUS - 1 - depth
    far_rim = SIDE - RADIUS + depth
    row = jnp.where(turn == 0, far_rim, jnp.where(turn == 1, along, jnp.where(turn == 2, near_rim, far)))
    col = jnp.where(turn == 0, along, jnp.where(turn == 1, near_rim, jnp.where(turn == 2, far, far_rim)))
    return row * SIDE + col


def pick_kernel(rotations_ref, keys_ref, values_ref, north_ref, east_ref, south_ref, west_ref):
    cell = lax.broadcasted_iota(jnp.int32, (STRIP, CELLS), 0)
    token = lax.broadcasted_iota(jnp.int32, (STRIP, CELLS), 1)
    for side_index, out_ref in enumerate((north_ref, east_ref, south_ref, west_ref)):
        wanted = strip_token(side_index, rotations_ref[0, side_index], cell)
        chosen = jnp.where(token == wanted, 1.0, 0.0).astype(jnp.bfloat16)
        out_ref[0] = mm(chosen, keys_ref[...]).astype(jnp.bfloat16)
        out_ref[1] = mm(chosen, values_ref[...]).astype(jnp.bfloat16)


def finish_kernel(
    scale, rotations_ref, centre_ref, north_ref, east_ref, south_ref, west_ref, terms_ref,
    keys_ref, values_ref, weight_ref,
):
    token = lax.broadcasted_iota(jnp.int32, (CELLS, STRIP), 0)
    cell = lax.broadcasted_iota(jnp.int32, (CELLS, STRIP), 1)
    total_keys = centre_ref[0]
    total_values = centre_ref[1]
    for side_index, back_ref in enumerate((north_ref, east_ref, south_ref, west_ref)):
        wanted = strip_token(side_index, rotations_ref[0, side_index], cell)
        chosen = jnp.where(token == wanted, 1.0, 0.0).astype(jnp.bfloat16)
        total_keys += mm(chosen, back_ref[0])
        total_values += mm(chosen, back_ref[1])
    keys_ref[...] = total_keys.astype(jnp.bfloat16)
    values_ref[...] = total_values.astype(jnp.bfloat16)
    weight_ref[...] = summed(terms_ref) * scale


def summed(terms_ref):
    total = terms_ref[0].astype(jnp.float32)
    for index in range(1, terms_ref.shape[0]):
        total += terms_ref[index].astype(jnp.float32)
    return total


def sum_kernel(terms_ref, total_ref):
    total_ref[...] = summed(terms_ref).astype(jnp.bfloat16)


def cotangent_kernel(*refs):
    blocks, (out_weight_ref, dout_ref, turned_ref) = refs[:-3], refs[-3:]
    heads = len(blocks)
    me = lax.axis_index("head")
    width = blocks[0].shape[1]
    total = None
    for distance, block_ref in enumerate(blocks):
        start = pl.multiple_of(lax.rem(me + distance, heads) * width, width)
        block = block_ref[...]
        term = mm(block, out_weight_ref[pl.ds(start, width), :])
        total = term if total is None else total + term
        turned_ref[pl.ds(start, width), :] = block.T
    dout_ref[...] = total.astype(jnp.bfloat16)


def window_bias(bias_ref):
    query = lax.broadcasted_iota(jnp.int32, (CELLS, CELLS), 1)
    cell = lax.broadcasted_iota(jnp.int32, (CELLS, CELLS), 0)

    def bias(cell_row, cell_col, query):
        query_row = (query >> 4) + RADIUS
        query_col = (query & (SIDE - 1)) + RADIUS
        near = (jnp.abs(cell_row - query_row) <= RADIUS) & (jnp.abs(cell_col - query_col) <= RADIUS)
        return jnp.where(near, 0.0, -1e30)

    bias_ref[0:CELLS, :] = bias((cell >> 4) + RADIUS, (cell & (SIDE - 1)) + RADIUS, query)
    query = lax.broadcasted_iota(jnp.int32, (STRIP, CELLS), 1)
    cell = lax.broadcasted_iota(jnp.int32, (STRIP, CELLS), 0)
    depth = cell >> 4
    along = cell & (SIDE - 1)
    last = SIDE + 2 * RADIUS - 1
    places = (
        (depth, RADIUS + along),
        (RADIUS + along, last - depth),
        (last - depth, last - RADIUS - along),
        (last - RADIUS - along, depth),
    )
    for side_index, (cell_row, cell_col) in enumerate(places):
        start = CELLS + side_index * STRIP
        bias_ref[start : start + STRIP, :] = bias(cell_row, cell_col, query)


def one_head(block, head):
    lane = lax.broadcasted_iota(jnp.int32, block.shape, 1)
    kept = (lane >= HEAD_DIM) if head else (lane < HEAD_DIM)
    return jnp.where(kept, block, jnp.zeros_like(block))


def joined(own_ref, strip_refs, index):
    return jnp.concatenate([own_ref[...]] + [ref[index] for ref in strip_refs], axis=0)


def forward_kernel(
    pairs, query_ref, key_ref, value_ref, north_ref, east_ref, south_ref, west_ref, turned_ref,
    weights_ref, partial_ref, bias_ref, attention_ref,
):
    step = pl.program_id(0)

    @pl.when(step == 0)
    def _():
        window_bias(bias_ref)

    strips = (north_ref, east_ref, south_ref, west_ref)
    key_ext = joined(key_ref, strips, 0)
    value_turned = joined(value_ref, strips, 1).T
    query = query_ref[...]
    scale = HEAD_DIM ** (-0.5) * math.log2(math.e)
    parts = []
    for head in range(2):
        scores = mm_nt(key_ext, one_head(query, head)) + bias_ref[...]
        top = jnp.max(scores, axis=0, keepdims=True)
        raw = jnp.exp2((scores - top) * scale)
        weights = (raw * (1.0 / jnp.sum(raw, axis=0, keepdims=True))).astype(jnp.bfloat16)
        weights_ref[0, :, head * CELLS : (head + 1) * CELLS] = weights
        parts.append(mm(value_turned[head * HEAD_DIM : (head + 1) * HEAD_DIM], weights))
    attention = jnp.concatenate(parts, axis=0).T
    start = pl.multiple_of(step * PAIR, PAIR)
    attention_ref[:, pl.ds(start, PAIR)] = attention.astype(jnp.bfloat16)

    @pl.when(step == pairs - 1)
    def _():
        partial = mm(turned_ref[...], attention_ref[...])
        near, far, chunk = partial_ref.shape[:3]
        for index in range(near * far):
            rows = partial[index * chunk : (index + 1) * chunk]
            partial_ref[index % near, index // near] = rows.astype(jnp.bfloat16)


def backward_kernel(
    query_ref, key_ref, value_ref, north_ref, east_ref, south_ref, west_ref, dout_ref, weights_ref,
    grad_query_ref, centre_ref, north_out, east_out, south_out, west_out,
):
    strips = (north_ref, east_ref, south_ref, west_ref)
    key_turned = joined(key_ref, strips, 0).T
    value_ext = joined(value_ref, strips, 1)
    query = query_ref[...]
    dout = dout_ref[...]
    score_scale = HEAD_DIM ** (-0.5)
    grad_key = None
    grad_value = None
    parts = []
    for head in range(2):
        query_head = one_head(query, head)
        dout_head = one_head(dout, head)
        weights_bf = weights_ref[0, :, head * CELLS : (head + 1) * CELLS]
        weights = weights_bf.astype(jnp.float32)
        grad_weights = mm_nt(value_ext, dout_head)
        row_delta = jnp.sum(weights * grad_weights, axis=0, keepdims=True)
        dscore = (weights * (grad_weights - row_delta)).astype(jnp.bfloat16)
        key_term = mm(dscore, query_head)
        value_term = mm(weights_bf, dout_head)
        grad_key = key_term if grad_key is None else grad_key + key_term
        grad_value = value_term if grad_value is None else grad_value + value_term
        parts.append(mm(key_turned[head * HEAD_DIM : (head + 1) * HEAD_DIM], dscore))
    grad_query = jnp.concatenate(parts, axis=0).T * score_scale
    grad_query_ref[...] = grad_query.astype(jnp.bfloat16)
    grad_key = grad_key * score_scale
    centre_ref[0] = grad_key[:CELLS]
    centre_ref[1] = grad_value[:CELLS]
    for side_index, out_ref in enumerate((north_out, east_out, south_out, west_out)):
        start = CELLS + side_index * STRIP
        out_ref[0] = grad_key[start : start + STRIP].astype(jnp.bfloat16)
        out_ref[1] = grad_value[start : start + STRIP].astype(jnp.bfloat16)


def params():
    return pltpu.CompilerParams(vmem_limit_bytes=VMEM_LIMIT)


def in_hbm(array):
    return pltpu.with_memory_space_constraint(array, pltpu.HBM)


def from_behind(block, axis, distance):
    devices = range(lax.axis_size(axis))
    route = [((i - distance) % len(devices), i) for i in devices]
    return lax.ppermute(block, axis, route)


def shards(queries, keys, values, grad_output, out_weight, rotations):
    tile_count = lax.axis_size("tile")
    token_count, features = queries.shape
    model = out_weight.shape[0]
    pairs = features // PAIR
    bf16 = jnp.bfloat16
    offsets = (-(tile_count // 4), 1, tile_count // 4, -1)
    smem = pl.BlockSpec(memory_space=pltpu.SMEM)
    vmem = pl.BlockSpec(memory_space=pltpu.VMEM)
    strip_type = jax.ShapeDtypeStruct((2, STRIP, features), bf16)

    queries, keys, values, out_weight, rotations = (
        in_hbm(a) for a in (queries, keys, values, out_weight, rotations)
    )

    picked = pl.pallas_call(
        pick_kernel,
        out_shape=[strip_type] * 4,
        in_specs=[smem, vmem, vmem],
        out_specs=[vmem] * 4,
        compiler_params=params(),
        name="pick_strips",
    )(rotations, keys, values)
    grad_output, *picked = lax.optimization_barrier((grad_output, *picked))
    strips = [from_behind(picked[(s + 2) % 4], "tile", -offsets[s]) for s in range(4)]

    heads = lax.axis_size("head")
    cotangents = [grad_output] + [from_behind(grad_output, "head", -k) for k in range(1, heads)]
    dout, turned = pl.pallas_call(
        cotangent_kernel,
        out_shape=[
            jax.ShapeDtypeStruct((CELLS, features), bf16),
            jax.ShapeDtypeStruct((model, CELLS), bf16),
        ],
        in_specs=[vmem] * (heads + 1),
        out_specs=[vmem] * 2,
        compiler_params=params(),
        name="cotangent",
    )(in_hbm(grad_output), *cotangents[1:], out_weight)

    rows_spec = pl.BlockSpec((CELLS, PAIR), lambda p: (0, p))
    strip_spec = pl.BlockSpec((2, STRIP, PAIR), lambda p: (0, 0, p))
    near = 4
    far = tile_count // near
    chunk = model // tile_count
    weights_spec = pl.BlockSpec((1, EXT, 2 * CELLS), lambda p: (p, 0, 0))
    weights, partial = pl.pallas_call(
        functools.partial(forward_kernel, pairs),
        grid=(pairs,),
        out_shape=[
            pltpu.HBM((pairs, EXT, 2 * CELLS), bf16),
            jax.ShapeDtypeStruct((near, far, chunk, features), bf16),
        ],
        in_specs=[rows_spec] * 3 + [strip_spec] * 4 + [pl.BlockSpec((model, CELLS), lambda p: (0, 0))],
        out_specs=[weights_spec, pl.BlockSpec((near, far, chunk, features), lambda p: (0, 0, 0, 0))],
        scratch_shapes=[pltpu.VMEM((EXT, CELLS), jnp.float32), pltpu.VMEM((CELLS, features), bf16)],
        compiler_params=params(),
        name="attention_forward",
    )(queries, keys, values, *strips, turned)

    planes = [[far_index * near + i for i in range(near)] for far_index in range(far)]
    lines = [[far_index * near + i for far_index in range(far)] for i in range(near)]
    spread = lax.all_to_all(partial, "tile", 0, 0, axis_index_groups=planes)
    plane_sum = pl.pallas_call(
        sum_kernel,
        out_shape=jax.ShapeDtypeStruct((far, chunk, features), bf16),
        in_specs=[vmem],
        out_specs=vmem,
        compiler_params=params(),
        name="plane_sum",
    )(spread)
    terms = lax.all_to_all(plane_sum, "tile", 0, 0, axis_index_groups=lines)

    grad_queries, centre, *backs = pl.pallas_call(
        backward_kernel,
        grid=(pairs,),
        out_shape=[
            jax.ShapeDtypeStruct((CELLS, features), bf16),
            jax.ShapeDtypeStruct((2, CELLS, features), jnp.float32),
        ]
        + [strip_type] * 4,
        in_specs=[rows_spec] * 3 + [strip_spec] * 4 + [rows_spec, weights_spec],
        out_specs=[rows_spec, pl.BlockSpec((2, CELLS, PAIR), lambda p: (0, 0, p))] + [strip_spec] * 4,
        compiler_params=params(),
        name="attention_backward",
    )(queries, keys, values, *strips, dout, in_hbm(weights))

    returned = [from_behind(backs[(s + 2) % 4], "tile", -offsets[s]) for s in range(4)]
    grad_keys, grad_values, grad_out_weight = pl.pallas_call(
        functools.partial(finish_kernel, 1.0 / math.sqrt(token_count * tile_count)),
        out_shape=[jax.ShapeDtypeStruct((CELLS, features), bf16)] * 2
        + [jax.ShapeDtypeStruct((chunk, features), jnp.float32)],
        in_specs=[smem] + [vmem] * 6,
        out_specs=[vmem] * 3,
        compiler_params=params(),
        name="finish",
    )(rotations, centre, *returned, terms)
    return (grad_queries, grad_keys, grad_values, grad_out_weight)


def solution(mesh):
    placed = (
        P("tile", "head"),
        P("tile", "head"),
        P("tile", "head"),
        P("tile", "head"),
        P(None, "head"),
        P("tile", None),
    )
    return jax.shard_map(
        shards,
        mesh=mesh,
        in_specs=placed,
        out_specs=(P("tile", "head"), P("tile", "head"), P("tile", "head"), P("tile", "head")),
        check_vma=False,
    )
```

```python
import functools
import math

import jax
import jax.numpy as jnp
from jax import lax
from jax.experimental import pallas as pl
from jax.experimental.pallas import tpu as pltpu
from jax.sharding import PartitionSpec as P

HEAD_DIM = 64
RADIUS = 6
SIDE = 16
CELLS = SIDE * SIDE
STRIP = RADIUS * SIDE
ROWS = CELLS + 2 * STRIP
NEAR = 4
PAIR = 2 * HEAD_DIM
VMEM_LIMIT = 32 * 1024 * 1024
NT = (((1,), (1,)), ((), ()))


def mm(a, b):
    return jnp.dot(a, b, preferred_element_type=jnp.float32)


def mm_nt(a, b):
    return lax.dot_general(a, b, NT, preferred_element_type=jnp.float32)


def strip_token(side_index, rotation, cell):
    turn = lax.rem(side_index + 6 - rotation, 4)
    depth = cell >> 4
    along = cell & (SIDE - 1)
    far = SIDE - 1 - along
    near_rim = RADIUS - 1 - depth
    far_rim = SIDE - RADIUS + depth
    row = jnp.where(turn == 0, far_rim, jnp.where(turn == 1, along, jnp.where(turn == 2, near_rim, far)))
    col = jnp.where(turn == 0, along, jnp.where(turn == 1, near_rim, jnp.where(turn == 2, far, far_rim)))
    return row * SIDE + col


def pick_kernel(rotations_ref, keys_ref, values_ref, north_ref, east_ref, south_ref, west_ref):
    cell = lax.broadcasted_iota(jnp.int32, (STRIP, CELLS), 0)
    token = lax.broadcasted_iota(jnp.int32, (STRIP, CELLS), 1)
    for side_index, out_ref in enumerate((north_ref, east_ref, south_ref, west_ref)):
        wanted = strip_token(side_index, rotations_ref[0, side_index], cell)
        chosen = jnp.where(token == wanted, 1.0, 0.0).astype(jnp.bfloat16)
        out_ref[0] = mm(chosen, keys_ref[...]).astype(jnp.bfloat16)
        out_ref[1] = mm(chosen, values_ref[...]).astype(jnp.bfloat16)


def finish_kernel(
    scale, rotations_ref, centre_ref, north_ref, east_ref, south_ref, west_ref, terms_ref,
    keys_ref, values_ref, weight_ref,
):
    token = lax.broadcasted_iota(jnp.int32, (CELLS, STRIP), 0)
    cell = lax.broadcasted_iota(jnp.int32, (CELLS, STRIP), 1)
    total_keys = centre_ref[0]
    total_values = centre_ref[1]
    for side_index, back_ref in enumerate((north_ref, east_ref, south_ref, west_ref)):
        wanted = strip_token(side_index, rotations_ref[0, side_index], cell)
        chosen = jnp.where(token == wanted, 1.0, 0.0).astype(jnp.bfloat16)
        total_keys += mm(chosen, back_ref[0])
        total_values += mm(chosen, back_ref[1])
    keys_ref[...] = total_keys.astype(jnp.bfloat16)
    values_ref[...] = total_values.astype(jnp.bfloat16)
    weight_ref[...] = summed(terms_ref) * scale


def summed(terms_ref):
    total = terms_ref[0].astype(jnp.float32)
    for index in range(1, terms_ref.shape[0]):
        total += terms_ref[index].astype(jnp.float32)
    return total


def sum_kernel(*refs):
    total_ref = refs[-1]
    total = refs[0][...].astype(jnp.float32)
    for ref in refs[1:-1]:
        total += ref[...].astype(jnp.float32)
    total_ref[...] = total.astype(jnp.bfloat16)


def cotangent_kernel(*refs):
    blocks, (out_weight_ref, dout_ref, turned_ref) = refs[:-3], refs[-3:]
    heads = len(blocks)
    head = lax.axis_index("head")
    place = lax.rem(lax.axis_index("tile"), NEAR)
    near, far, chunk, _ = turned_ref.shape
    width = blocks[0].shape[1]
    total = None
    for distance, block_ref in enumerate(blocks):
        owner = lax.rem(head + distance, heads)
        start = pl.multiple_of(owner * width, width)
        block = block_ref[...]
        term = mm(block, out_weight_ref[pl.ds(start, width), :])
        total = term if total is None else total + term
        turned = block.T
        first = owner * (width // chunk)
        for index in range(width // chunk):
            target = first + index
            rows = turned[index * chunk : (index + 1) * chunk]
            turned_ref[lax.rem(target, near) ^ place, lax.div(target, near)] = rows
    dout_ref[...] = total.astype(jnp.bfloat16)


def window(cell_row, cell_col, query):
    query_row = (query >> 4) + RADIUS
    query_col = (query & (SIDE - 1)) + RADIUS
    near = (jnp.abs(cell_row - query_row) <= RADIUS) & (jnp.abs(cell_col - query_col) <= RADIUS)
    return jnp.where(near, 0.0, -1e30)


def centre_bias(bias_ref):
    query = lax.broadcasted_iota(jnp.int32, (CELLS, CELLS), 1)
    cell = lax.broadcasted_iota(jnp.int32, (CELLS, CELLS), 0)
    bias_ref[...] = window((cell >> 4) + RADIUS, (cell & (SIDE - 1)) + RADIUS, query)


def strip_bias(bias_ref):
    query = lax.broadcasted_iota(jnp.int32, (STRIP, CELLS), 1)
    cell = lax.broadcasted_iota(jnp.int32, (STRIP, CELLS), 0)
    depth = cell >> 4
    along = cell & (SIDE - 1)
    last = SIDE + 2 * RADIUS - 1
    north = (depth, RADIUS + along)
    east = (RADIUS + along, last - depth)
    south = (last - depth, last - RADIUS - along)
    west = (last - RADIUS - along, depth)
    for start, kind, first, second in ((0, 0, north, south), (STRIP, 1, west, east)):
        in_first = first_half(query, kind)
        row = jnp.where(in_first, first[0], second[0])
        col = jnp.where(in_first, first[1], second[1])
        bias_ref[start : start + STRIP, :] = window(row, col, query)


def first_half(query, kind):
    return (query & (SIDE - 1)) < SIDE // 2 if kind else query < CELLS // 2


def one_head(block, head):
    lane = lax.broadcasted_iota(jnp.int32, block.shape, 1)
    kept = (lane >= HEAD_DIM) if head else (lane < HEAD_DIM)
    return jnp.where(kept, block, jnp.zeros_like(block))


def halves(block, kind):
    kept = first_half(lax.broadcasted_iota(jnp.int32, block.shape, 0), kind)
    zero = jnp.zeros_like(block)
    return jnp.concatenate([jnp.where(kept, block, zero), jnp.where(kept, zero, block)], axis=1)


def by_half(stacked, kind):
    rows = stacked.shape[0] // 2
    kept = first_half(lax.broadcasted_iota(jnp.int32, (rows, CELLS), 1), kind)
    return jnp.where(kept, stacked[:rows], stacked[rows:])


def side_refs(strips, kind):
    north, east, south, west = strips
    return (west, east) if kind else (north, south)


def side_cells(strips, part, kind, cols):
    return jnp.concatenate([ref[part, :, cols] for ref in side_refs(strips, kind)], axis=1)


def turned_sides(strips, part, kind, cols):
    return [ref[part, :, cols].T for ref in side_refs(strips, kind)]


def pair_cols(pair):
    return pl.ds(pl.multiple_of(pair * PAIR, PAIR), PAIR)


def head_rows(turned, head):
    return turned[head * HEAD_DIM : (head + 1) * HEAD_DIM]


def over_cells(turned_centre, turned_strips, head, centre, sides):
    total = mm(head_rows(turned_centre, head), centre)
    for kind in range(2):
        stacked = jnp.concatenate([head_rows(t, head) for t in turned_strips[kind]], axis=0)
        total += by_half(mm(stacked, sides[kind]), kind)
    return total


SCORE_SCALE = HEAD_DIM ** (-0.5)
LOG_SCALE = SCORE_SCALE * math.log2(math.e)


def lanes_of(head):
    return slice(head * CELLS, (head + 1) * CELLS)


def centre_kernel(
    query_ref, key_ref, value_ref, dout_ref,
    raw_ref, stats_ref, product_ref, query_out, key_out, value_out, bias_ref,
):
    centre_bias(bias_ref)

    def step(pair, carry):
        cols = pair_cols(pair)
        query, key, value, dout = (ref[:, cols] for ref in (query_ref, key_ref, value_ref, dout_ref))
        for head in range(2):
            scores = mm_nt(key, one_head(query, head)) + bias_ref[...]
            top = jnp.max(scores, axis=0, keepdims=True)
            raw = jnp.exp2((scores - top) * LOG_SCALE)
            raw_ref[pair, :, lanes_of(head)] = raw
            stats_ref[pair, 0:1, lanes_of(head)] = top
            stats_ref[pair, 1:2, lanes_of(head)] = jnp.sum(raw, axis=0, keepdims=True)
            product_ref[pair, :, lanes_of(head)] = mm_nt(value, one_head(dout, head))
        query_out[:, cols] = query
        key_out[:, cols] = key
        value_out[:, cols] = value
        return carry

    lax.fori_loop(0, raw_ref.shape[0], step, 0)


def forward_kernel(
    query_ref, value_ref, north_ref, east_ref, south_ref, west_ref, raw_ref, stats_ref, turned_ref,
    weights_ref, own_ref, *refs,
):
    partial_refs, (bias_ref, attention_ref) = (own_ref,) + refs[:-2], refs[-2:]
    strips = (north_ref, east_ref, south_ref, west_ref)
    strip_bias(bias_ref)

    def step(pair, carry):
        cols = pair_cols(pair)
        query = query_ref[:, cols]
        turned_centre = value_ref[:, cols].T
        turned_strips = [turned_sides(strips, 1, kind, cols) for kind in range(2)]
        sides = [side_cells(strips, 0, kind, cols) for kind in range(2)]
        parts = []
        for head in range(2):
            query_head = one_head(query, head)
            scores = [
                mm_nt(sides[kind], halves(query_head, kind)) + bias_ref[kind * STRIP : (kind + 1) * STRIP]
                for kind in range(2)
            ]
            centre_top = stats_ref[pair, 0:1, lanes_of(head)]
            top = jnp.maximum(jnp.max(jnp.maximum(scores[0], scores[1]), axis=0, keepdims=True), centre_top)
            raw = [jnp.exp2((s - top) * LOG_SCALE) for s in scores]
            lifted = jnp.exp2((centre_top - top) * LOG_SCALE)
            total = jnp.sum(raw[0] + raw[1], axis=0, keepdims=True)
            total += lifted * stats_ref[pair, 1:2, lanes_of(head)]
            inverse = 1.0 / total
            centre = (raw_ref[pair, :, lanes_of(head)] * (lifted * inverse)).astype(jnp.bfloat16)
            outer = [(r * inverse).astype(jnp.bfloat16) for r in raw]
            weights_ref[pair, :CELLS, lanes_of(head)] = centre
            for kind in range(2):
                start = CELLS + kind * STRIP
                weights_ref[pair, start : start + STRIP, lanes_of(head)] = outer[kind]
            parts.append(over_cells(turned_centre, turned_strips, head, centre, outer))
        attention_ref[:, cols] = jnp.concatenate(parts, axis=0).T.astype(jnp.bfloat16)
        return carry

    lax.fori_loop(0, raw_ref.shape[0], step, 0)
    attention = attention_ref[...]
    for index, partial_ref in enumerate(partial_refs):
        turned = turned_ref[index]
        turned = turned.reshape(turned.shape[0] * turned.shape[1], turned.shape[2])
        partial_ref[...] = mm(turned, attention).astype(jnp.bfloat16).reshape(partial_ref.shape)


def strip_grad_kernel(
    query_ref, dout_ref, north_ref, east_ref, south_ref, west_ref, weights_ref, product_ref,
    dscore_ref, north_out, east_out, south_out, west_out,
):
    strips = (north_ref, east_ref, south_ref, west_ref)
    outs = (north_out, east_out, south_out, west_out)

    def step(pair, carry):
        cols = pair_cols(pair)
        query = query_ref[:, cols]
        dout = dout_ref[:, cols]
        query_halves = []
        dout_halves = []
        sides = [side_cells(strips, 1, kind, cols) for kind in range(2)]
        for head in range(2):
            lanes = lanes_of(head)
            query_halves.append([halves(one_head(query, head), kind) for kind in range(2)])
            dout_halves.append([halves(one_head(dout, head), kind) for kind in range(2)])
            products = [product_ref[pair, :, lanes]]
            products += [mm_nt(sides[kind], dout_halves[head][kind]) for kind in range(2)]
            bounds = (0, CELLS, CELLS + STRIP, CELLS + 2 * STRIP)
            weights = [
                weights_ref[pair, start:end, lanes].astype(jnp.float32)
                for start, end in zip(bounds, bounds[1:])
            ]
            delta = sum(jnp.sum(w * g, axis=0, keepdims=True) for w, g in zip(weights, products))
            for start, end, w, g in zip(bounds, bounds[1:], weights, products):
                dscore_ref[pair, start:end, lanes] = (w * (g - delta)).astype(jnp.bfloat16)
        for kind in range(2):
            start = CELLS + kind * STRIP
            grad_key = mm(
                dscore_ref[pair, start : start + STRIP, :],
                jnp.concatenate([query_halves[head][kind] for head in range(2)], axis=0),
            )
            grad_value = mm(
                weights_ref[pair, start : start + STRIP, :],
                jnp.concatenate([dout_halves[head][kind] for head in range(2)], axis=0),
            )
            for index, out_ref in enumerate(side_refs(outs, kind)):
                lanes = slice(index * PAIR, (index + 1) * PAIR)
                out_ref[0, :, cols] = (grad_key[:, lanes] * SCORE_SCALE).astype(jnp.bfloat16)
                out_ref[1, :, cols] = grad_value[:, lanes].astype(jnp.bfloat16)
        return carry

    lax.fori_loop(0, weights_ref.shape[0], step, 0)


def centre_grad_kernel(
    query_ref, key_ref, dout_ref, north_ref, east_ref, south_ref, west_ref, weights_ref, dscore_ref,
    grad_query_ref, centre_ref,
):
    strips = (north_ref, east_ref, south_ref, west_ref)

    def step(pair, carry):
        cols = pair_cols(pair)
        query = query_ref[:, cols]
        dout = dout_ref[:, cols]
        turned_centre = key_ref[:, cols].T
        turned_strips = [turned_sides(strips, 0, kind, cols) for kind in range(2)]
        parts = []
        for head in range(2):
            lanes = lanes_of(head)
            outer = [
                dscore_ref[pair, CELLS + kind * STRIP : CELLS + (kind + 1) * STRIP, lanes] for kind in range(2)
            ]
            parts.append(over_cells(turned_centre, turned_strips, head, dscore_ref[pair, :CELLS, lanes], outer))
        grad_query = jnp.concatenate(parts, axis=0).T * SCORE_SCALE
        grad_query_ref[:, cols] = grad_query.astype(jnp.bfloat16)
        grad_key = mm(
            dscore_ref[pair, :CELLS, :], jnp.concatenate([one_head(query, head) for head in range(2)], axis=0)
        )
        grad_value = mm(
            weights_ref[pair, :CELLS, :], jnp.concatenate([one_head(dout, head) for head in range(2)], axis=0)
        )
        centre_ref[0, :, cols] = grad_key * SCORE_SCALE
        centre_ref[1, :, cols] = grad_value
        return carry

    lax.fori_loop(0, weights_ref.shape[0], step, 0)


def call(kernel, name, out_shape, operands, scratch=(), smem=0, gflop=0.0):
    specs = [pl.BlockSpec(memory_space=pltpu.SMEM)] * smem
    specs += [pl.BlockSpec(memory_space=pltpu.VMEM)] * (len(operands) - smem)
    single = not isinstance(out_shape, list)
    outs = pl.BlockSpec(memory_space=pltpu.VMEM)
    return pl.pallas_call(
        kernel,
        out_shape=out_shape,
        in_specs=specs,
        out_specs=outs if single else [outs] * len(out_shape),
        scratch_shapes=list(scratch),
        compiler_params=pltpu.CompilerParams(vmem_limit_bytes=VMEM_LIMIT),
        cost_estimate=pl.CostEstimate(flops=int(gflop * 1e9), bytes_accessed=1 << 20, transcendentals=0),
        name=name,
    )(*operands)


def in_hbm(array):
    return pltpu.with_memory_space_constraint(array, pltpu.HBM)


def from_behind(block, axis, distance):
    devices = range(lax.axis_size(axis))
    route = [((i - distance) % len(devices), i) for i in devices]
    return lax.ppermute(block, axis, route)


def shards(queries, keys, values, grad_output, out_weight, rotations):
    tile_count = lax.axis_size("tile")
    token_count, features = queries.shape
    model = out_weight.shape[0]
    pairs = features // PAIR
    far = tile_count // NEAR
    chunk = model // tile_count
    heads = lax.axis_size("head")
    offsets = (-(tile_count // 4), 1, tile_count // 4, -1)
    queries, keys, values, out_weight, rotations = (
        in_hbm(a) for a in (queries, keys, values, out_weight, rotations)
    )

    def bf16(*shape):
        return jax.ShapeDtypeStruct(shape, jnp.bfloat16)

    def f32(*shape):
        return jax.ShapeDtypeStruct(shape, jnp.float32)

    strip_types = [bf16(2, STRIP, features)] * 4
    picked = call(pick_kernel, "pick_strips", strip_types, (rotations, keys, values), smem=1, gflop=0.2)
    grad_output, *picked = lax.optimization_barrier((grad_output, *picked))
    strips = [from_behind(picked[(s + 2) % 4], "tile", -offsets[s]) for s in range(4)]

    cotangents = [from_behind(grad_output, "head", -k) for k in range(1, heads)]
    dout, turned = call(
        cotangent_kernel,
        "cotangent",
        [bf16(CELLS, features), bf16(NEAR, far, chunk, CELLS)],
        (in_hbm(grad_output), *cotangents, out_weight),
        gflop=1.0,
    )
    raw, stats, product, queries, keys, values = call(
        centre_kernel,
        "centre",
        [f32(pairs, CELLS, 2 * CELLS), f32(pairs, 2, 2 * CELLS), f32(pairs, CELLS, 2 * CELLS)]
        + [bf16(CELLS, features)] * 3,
        (queries, keys, values, dout),
        scratch=[pltpu.VMEM((CELLS, CELLS), jnp.float32)],
        gflop=3.0,
    )
    weights, *partials = call(
        forward_kernel,
        "forward",
        [bf16(pairs, ROWS, 2 * CELLS)] + [bf16(far, chunk, features)] * NEAR,
        (queries, values, *strips, raw, stats, turned),
        scratch=[pltpu.VMEM((2 * STRIP, CELLS), jnp.float32), pltpu.VMEM((CELLS, features), jnp.bfloat16)],
        gflop=4.0,
    )
    terms = partials[:1]
    for distance in range(1, NEAR):
        route = [(tile, tile ^ distance) for tile in range(tile_count)]
        terms.append(lax.ppermute(partials[distance], "tile", route))

    dscore, *backs = call(
        strip_grad_kernel,
        "strip_grad",
        [bf16(pairs, ROWS, 2 * CELLS)] + strip_types,
        (queries, dout, *strips, weights, product),
        gflop=4.0,
    )
    returned = [from_behind(backs[(s + 2) % 4], "tile", -offsets[s]) for s in range(4)]

    grad_queries, centre = call(
        centre_grad_kernel,
        "centre_grad",
        [bf16(CELLS, features), f32(2, CELLS, features)],
        (queries, keys, dout, *strips, weights, dscore),
        gflop=3.0,
    )
    plane_sum = call(sum_kernel, "plane_sum", bf16(far, chunk, features), terms, gflop=1.0)
    lines = [[far_index * NEAR + i for far_index in range(far)] for i in range(NEAR)]
    spread = lax.all_to_all(plane_sum, "tile", 0, 0, axis_index_groups=lines)

    grad_keys, grad_values, grad_out_weight = call(
        functools.partial(finish_kernel, 1.0 / math.sqrt(token_count * tile_count)),
        "finish",
        [bf16(CELLS, features)] * 2 + [f32(chunk, features)],
        (rotations, centre, *returned, spread),
        smem=1,
        gflop=1.0,
    )
    return (grad_queries, grad_keys, grad_values, grad_out_weight)


def solution(mesh):
    placed = (
        P("tile", "head"),
        P("tile", "head"),
        P("tile", "head"),
        P("tile", "head"),
        P(None, "head"),
        P("tile", None),
    )
    return jax.shard_map(
        shards,
        mesh=mesh,
        in_specs=placed,
        out_specs=(P("tile", "head"), P("tile", "head"), P("tile", "head"), P("tile", "head")),
        check_vma=False,
    )
```

```python
import functools
import math

import jax
import jax.numpy as jnp
from jax import lax
from jax.experimental import pallas as pl
from jax.experimental.pallas import tpu as pltpu
from jax.sharding import PartitionSpec as P

HEAD_DIM = 64
RADIUS = 6
SIDE = 16
CELLS = SIDE * SIDE
STRIP = RADIUS * SIDE
ROWS = CELLS + 2 * STRIP
NEAR = 4
PAIR = 2 * HEAD_DIM
VMEM_LIMIT = 32 * 1024 * 1024
NT = (((1,), (1,)), ((), ()))


def mm(a, b):
    return jnp.dot(a, b, preferred_element_type=jnp.float32)


def mm_nt(a, b):
    return lax.dot_general(a, b, NT, preferred_element_type=jnp.float32)


def strip_token(side_index, rotation, cell):
    turn = lax.rem(side_index + 6 - rotation, 4)
    depth = cell >> 4
    along = cell & (SIDE - 1)
    far = SIDE - 1 - along
    near_rim = RADIUS - 1 - depth
    far_rim = SIDE - RADIUS + depth
    row = jnp.where(turn == 0, far_rim, jnp.where(turn == 1, along, jnp.where(turn == 2, near_rim, far)))
    col = jnp.where(turn == 0, along, jnp.where(turn == 1, near_rim, jnp.where(turn == 2, far, far_rim)))
    return row * SIDE + col


def pick_kernel(rotations_ref, keys_ref, values_ref, north_ref, east_ref, south_ref, west_ref):
    cell = lax.broadcasted_iota(jnp.int32, (STRIP, CELLS), 0)
    token = lax.broadcasted_iota(jnp.int32, (STRIP, CELLS), 1)
    for side_index, out_ref in enumerate((north_ref, east_ref, south_ref, west_ref)):
        wanted = strip_token(side_index, rotations_ref[0, side_index], cell)
        chosen = jnp.where(token == wanted, 1.0, 0.0).astype(jnp.bfloat16)
        out_ref[0] = mm(chosen, keys_ref[...]).astype(jnp.bfloat16)
        out_ref[1] = mm(chosen, values_ref[...]).astype(jnp.bfloat16)


def finish_kernel(
    scale, rotations_ref, centre_ref, north_ref, east_ref, south_ref, west_ref, *refs,
):
    terms, (keys_ref, values_ref, weight_ref) = refs[:-3], refs[-3:]
    token = lax.broadcasted_iota(jnp.int32, (CELLS, STRIP), 0)
    cell = lax.broadcasted_iota(jnp.int32, (CELLS, STRIP), 1)
    total_keys = centre_ref[0]
    total_values = centre_ref[1]
    for side_index, back_ref in enumerate((north_ref, east_ref, south_ref, west_ref)):
        wanted = strip_token(side_index, rotations_ref[0, side_index], cell)
        chosen = jnp.where(token == wanted, 1.0, 0.0).astype(jnp.bfloat16)
        total_keys += mm(chosen, back_ref[0])
        total_values += mm(chosen, back_ref[1])
    keys_ref[...] = total_keys.astype(jnp.bfloat16)
    values_ref[...] = total_values.astype(jnp.bfloat16)
    weight = terms[0][0].astype(jnp.float32)
    for ref in terms[1:]:
        weight += ref[0].astype(jnp.float32)
    weight_ref[...] = weight * scale


def sum_kernel(count, *refs):
    terms, outs = refs[:count], refs[count + 1 :]
    for q in range(terms[0].shape[0]):
        total = terms[0][q].astype(jnp.float32)
        for ref in terms[1:]:
            total += ref[q].astype(jnp.float32)
        outs[q % len(outs)][q // len(outs)] = total.astype(jnp.bfloat16)


def cotangent_kernel(*refs):
    blocks, (out_weight_ref, dout_ref, turned_ref) = refs[:-3], refs[-3:]
    heads = len(blocks)
    head = lax.axis_index("head")
    tile = lax.axis_index("tile")
    near, _, chunk, _ = turned_ref.shape
    width = blocks[0].shape[1]
    total = None
    for distance, block_ref in enumerate(blocks):
        owner = lax.rem(head + distance, heads)
        start = pl.multiple_of(owner * width, width)
        block = block_ref[...]
        term = mm(block, out_weight_ref[pl.ds(start, width), :])
        total = term if total is None else total + term
        turned = block.T
        first = owner * (width // chunk)
        for index in range(width // chunk):
            target = (first + index) ^ tile
            rows = turned[index * chunk : (index + 1) * chunk]
            turned_ref[lax.rem(target, near), lax.div(target, near)] = rows
    dout_ref[...] = total.astype(jnp.bfloat16)


def window(cell_row, cell_col, query):
    query_row = (query >> 4) + RADIUS
    query_col = (query & (SIDE - 1)) + RADIUS
    near = (jnp.abs(cell_row - query_row) <= RADIUS) & (jnp.abs(cell_col - query_col) <= RADIUS)
    return jnp.where(near, 0.0, -1e30)


def centre_bias(bias_ref):
    query = lax.broadcasted_iota(jnp.int32, (CELLS, CELLS), 1)
    cell = lax.broadcasted_iota(jnp.int32, (CELLS, CELLS), 0)
    bias_ref[...] = window((cell >> 4) + RADIUS, (cell & (SIDE - 1)) + RADIUS, query)


def strip_bias(bias_ref):
    query = lax.broadcasted_iota(jnp.int32, (STRIP, CELLS), 1)
    cell = lax.broadcasted_iota(jnp.int32, (STRIP, CELLS), 0)
    depth = cell >> 4
    along = cell & (SIDE - 1)
    last = SIDE + 2 * RADIUS - 1
    north = (depth, RADIUS + along)
    east = (RADIUS + along, last - depth)
    south = (last - depth, last - RADIUS - along)
    west = (last - RADIUS - along, depth)
    for start, kind, first, second in ((0, 0, north, south), (STRIP, 1, west, east)):
        in_first = first_half(query, kind)
        row = jnp.where(in_first, first[0], second[0])
        col = jnp.where(in_first, first[1], second[1])
        bias_ref[start : start + STRIP, :] = window(row, col, query)


def first_half(query, kind):
    return (query & (SIDE - 1)) < SIDE // 2 if kind else query < CELLS // 2


def one_head(block, head):
    lane = lax.broadcasted_iota(jnp.int32, block.shape, 1)
    kept = (lane >= HEAD_DIM) if head else (lane < HEAD_DIM)
    return jnp.where(kept, block, jnp.zeros_like(block))


def halves(block, kind):
    kept = first_half(lax.broadcasted_iota(jnp.int32, block.shape, 0), kind)
    zero = jnp.zeros_like(block)
    return jnp.concatenate([jnp.where(kept, block, zero), jnp.where(kept, zero, block)], axis=1)


def by_half(stacked, kind):
    rows = stacked.shape[0] // 2
    kept = first_half(lax.broadcasted_iota(jnp.int32, (rows, CELLS), 1), kind)
    return jnp.where(kept, stacked[:rows], stacked[rows:])


def side_refs(strips, kind):
    north, east, south, west = strips
    return (west, east) if kind else (north, south)


def side_cells(strips, part, kind, cols):
    return jnp.concatenate([ref[part, :, cols] for ref in side_refs(strips, kind)], axis=1)


def turned_sides(strips, part, kind, cols):
    return [ref[part, :, cols].T for ref in side_refs(strips, kind)]


def pair_cols(pair):
    return pl.ds(pl.multiple_of(pair * PAIR, PAIR), PAIR)


def head_rows(turned, head):
    return turned[head * HEAD_DIM : (head + 1) * HEAD_DIM]


def over_cells(turned_centre, turned_strips, head, centre, sides):
    total = mm(head_rows(turned_centre, head), centre)
    for kind in range(2):
        stacked = jnp.concatenate([head_rows(t, head) for t in turned_strips[kind]], axis=0)
        total += by_half(mm(stacked, sides[kind]), kind)
    return total


SCORE_SCALE = HEAD_DIM ** (-0.5)
LOG_SCALE = SCORE_SCALE * math.log2(math.e)


def lanes_of(head):
    return slice(head * CELLS, (head + 1) * CELLS)


def centre_kernel(
    query_ref, key_ref, value_ref, dout_ref,
    raw_ref, stats_ref, product_ref, query_out, key_out, value_out, bias_ref,
):
    centre_bias(bias_ref)

    def step(pair, carry):
        cols = pair_cols(pair)
        query, key, value, dout = (ref[:, cols] for ref in (query_ref, key_ref, value_ref, dout_ref))
        for head in range(2):
            scores = mm_nt(key, one_head(query, head)) + bias_ref[...]
            top = jnp.max(scores, axis=0, keepdims=True)
            raw = jnp.exp2((scores - top) * LOG_SCALE)
            raw_ref[pair, :, lanes_of(head)] = raw
            stats_ref[pair, 0:1, lanes_of(head)] = top
            stats_ref[pair, 1:2, lanes_of(head)] = jnp.sum(raw, axis=0, keepdims=True)
            product_ref[pair, :, lanes_of(head)] = mm_nt(value, one_head(dout, head))
        query_out[:, cols] = query
        key_out[:, cols] = key
        value_out[:, cols] = value
        return carry

    lax.fori_loop(0, raw_ref.shape[0], step, 0)


def forward_kernel(
    query_ref, value_ref, north_ref, east_ref, south_ref, west_ref, raw_ref, stats_ref, turned_ref,
    weights_ref, own_ref, *refs,
):
    partial_refs, (bias_ref, attention_ref) = (own_ref,) + refs[:-2], refs[-2:]
    strips = (north_ref, east_ref, south_ref, west_ref)
    strip_bias(bias_ref)

    def step(pair, carry):
        cols = pair_cols(pair)
        query = query_ref[:, cols]
        turned_centre = value_ref[:, cols].T
        turned_strips = [turned_sides(strips, 1, kind, cols) for kind in range(2)]
        sides = [side_cells(strips, 0, kind, cols) for kind in range(2)]
        parts = []
        for head in range(2):
            query_head = one_head(query, head)
            scores = [
                mm_nt(sides[kind], halves(query_head, kind)) + bias_ref[kind * STRIP : (kind + 1) * STRIP]
                for kind in range(2)
            ]
            centre_top = stats_ref[pair, 0:1, lanes_of(head)]
            top = jnp.maximum(jnp.max(jnp.maximum(scores[0], scores[1]), axis=0, keepdims=True), centre_top)
            raw = [jnp.exp2((s - top) * LOG_SCALE) for s in scores]
            lifted = jnp.exp2((centre_top - top) * LOG_SCALE)
            total = jnp.sum(raw[0] + raw[1], axis=0, keepdims=True)
            total += lifted * stats_ref[pair, 1:2, lanes_of(head)]
            inverse = 1.0 / total
            centre = (raw_ref[pair, :, lanes_of(head)] * (lifted * inverse)).astype(jnp.bfloat16)
            outer = [(r * inverse).astype(jnp.bfloat16) for r in raw]
            weights_ref[pair, :CELLS, lanes_of(head)] = centre
            for kind in range(2):
                start = CELLS + kind * STRIP
                weights_ref[pair, start : start + STRIP, lanes_of(head)] = outer[kind]
            parts.append(over_cells(turned_centre, turned_strips, head, centre, outer))
        attention_ref[:, cols] = jnp.concatenate(parts, axis=0).T.astype(jnp.bfloat16)
        return carry

    lax.fori_loop(0, raw_ref.shape[0], step, 0)
    attention = attention_ref[...]
    for index, partial_ref in enumerate(partial_refs):
        turned = turned_ref[index]
        turned = turned.reshape(turned.shape[0] * turned.shape[1], turned.shape[2])
        partial_ref[...] = mm(turned, attention).astype(jnp.bfloat16).reshape(partial_ref.shape)


def strip_grad_kernel(
    query_ref, dout_ref, north_ref, east_ref, south_ref, west_ref, weights_ref, product_ref,
    dscore_ref, north_out, east_out, south_out, west_out,
):
    strips = (north_ref, east_ref, south_ref, west_ref)
    outs = (north_out, east_out, south_out, west_out)

    def step(pair, carry):
        cols = pair_cols(pair)
        query = query_ref[:, cols]
        dout = dout_ref[:, cols]
        query_halves = []
        dout_halves = []
        sides = [side_cells(strips, 1, kind, cols) for kind in range(2)]
        for head in range(2):
            lanes = lanes_of(head)
            query_halves.append([halves(one_head(query, head), kind) for kind in range(2)])
            dout_halves.append([halves(one_head(dout, head), kind) for kind in range(2)])
            products = [product_ref[pair, :, lanes]]
            products += [mm_nt(sides[kind], dout_halves[head][kind]) for kind in range(2)]
            bounds = (0, CELLS, CELLS + STRIP, CELLS + 2 * STRIP)
            weights = [
                weights_ref[pair, start:end, lanes].astype(jnp.float32)
                for start, end in zip(bounds, bounds[1:])
            ]
            delta = sum(jnp.sum(w * g, axis=0, keepdims=True) for w, g in zip(weights, products))
            for start, end, w, g in zip(bounds, bounds[1:], weights, products):
                dscore_ref[pair, start:end, lanes] = (w * (g - delta)).astype(jnp.bfloat16)
        for kind in range(2):
            start = CELLS + kind * STRIP
            grad_key = mm(
                dscore_ref[pair, start : start + STRIP, :],
                jnp.concatenate([query_halves[head][kind] for head in range(2)], axis=0),
            )
            grad_value = mm(
                weights_ref[pair, start : start + STRIP, :],
                jnp.concatenate([dout_halves[head][kind] for head in range(2)], axis=0),
            )
            for index, out_ref in enumerate(side_refs(outs, kind)):
                lanes = slice(index * PAIR, (index + 1) * PAIR)
                out_ref[0, :, cols] = (grad_key[:, lanes] * SCORE_SCALE).astype(jnp.bfloat16)
                out_ref[1, :, cols] = grad_value[:, lanes].astype(jnp.bfloat16)
        return carry

    lax.fori_loop(0, weights_ref.shape[0], step, 0)


def centre_grad_kernel(
    query_ref, key_ref, dout_ref, north_ref, east_ref, south_ref, west_ref, weights_ref, dscore_ref,
    grad_query_ref, centre_ref,
):
    strips = (north_ref, east_ref, south_ref, west_ref)

    def step(pair, carry):
        cols = pair_cols(pair)
        query = query_ref[:, cols]
        dout = dout_ref[:, cols]
        turned_centre = key_ref[:, cols].T
        turned_strips = [turned_sides(strips, 0, kind, cols) for kind in range(2)]
        parts = []
        for head in range(2):
            lanes = lanes_of(head)
            outer = [
                dscore_ref[pair, CELLS + kind * STRIP : CELLS + (kind + 1) * STRIP, lanes] for kind in range(2)
            ]
            parts.append(over_cells(turned_centre, turned_strips, head, dscore_ref[pair, :CELLS, lanes], outer))
        grad_query = jnp.concatenate(parts, axis=0).T * SCORE_SCALE
        grad_query_ref[:, cols] = grad_query.astype(jnp.bfloat16)
        grad_key = mm(
            dscore_ref[pair, :CELLS, :], jnp.concatenate([one_head(query, head) for head in range(2)], axis=0)
        )
        grad_value = mm(
            weights_ref[pair, :CELLS, :], jnp.concatenate([one_head(dout, head) for head in range(2)], axis=0)
        )
        centre_ref[0, :, cols] = grad_key * SCORE_SCALE
        centre_ref[1, :, cols] = grad_value
        return carry

    lax.fori_loop(0, weights_ref.shape[0], step, 0)


def call(kernel, name, out_shape, operands, scratch=(), smem=0, unused=0, gflop=0.0):
    specs = [pl.BlockSpec(memory_space=pltpu.SMEM)] * smem
    specs += [pl.BlockSpec(memory_space=pltpu.VMEM)] * (len(operands) - smem - unused)
    specs += [pl.BlockSpec(memory_space=pl.ANY)] * unused
    single = not isinstance(out_shape, list)
    outs = pl.BlockSpec(memory_space=pltpu.VMEM)
    return pl.pallas_call(
        kernel,
        out_shape=out_shape,
        in_specs=specs,
        out_specs=outs if single else [outs] * len(out_shape),
        scratch_shapes=list(scratch),
        compiler_params=pltpu.CompilerParams(vmem_limit_bytes=VMEM_LIMIT),
        cost_estimate=pl.CostEstimate(flops=int(gflop * 1e9), bytes_accessed=1 << 20, transcendentals=0),
        name=name,
    )(*operands)


def in_hbm(array):
    return pltpu.with_memory_space_constraint(array, pltpu.HBM)


def from_behind(block, axis, distance):
    devices = range(lax.axis_size(axis))
    route = [((i - distance) % len(devices), i) for i in devices]
    return lax.ppermute(block, axis, route)


def exchanged(blocks, stride):
    terms = list(blocks[:1])
    for distance in range(1, len(blocks)):
        route = [(tile, tile ^ (distance * stride)) for tile in range(lax.axis_size("tile"))]
        terms.append(lax.ppermute(blocks[distance], "tile", route))
    return terms


def to_sides(blocks, offsets):
    arrived = {s: from_behind(blocks[(s + 2) % 4], "tile", -offsets[s]) for s in (0, 2, 1, 3)}
    return [arrived[s] for s in range(4)]


def shards(queries, keys, values, grad_output, out_weight, rotations):
    tile_count = lax.axis_size("tile")
    token_count, features = queries.shape
    model = out_weight.shape[0]
    pairs = features // PAIR
    far = tile_count // NEAR
    chunk = model // tile_count
    heads = lax.axis_size("head")
    offsets = (-(tile_count // 4), 1, tile_count // 4, -1)
    queries, keys, values, out_weight, rotations = (
        in_hbm(a) for a in (queries, keys, values, out_weight, rotations)
    )

    def bf16(*shape):
        return jax.ShapeDtypeStruct(shape, jnp.bfloat16)

    def f32(*shape):
        return jax.ShapeDtypeStruct(shape, jnp.float32)

    strip_types = [bf16(2, STRIP, features)] * 4
    picked = call(pick_kernel, "pick_strips", strip_types, (rotations, keys, values), smem=1, gflop=0.2)
    grad_output, *picked = lax.optimization_barrier((grad_output, *picked))
    strips = to_sides(picked, offsets)

    cotangents = [from_behind(grad_output, "head", -k) for k in range(1, heads)]
    dout, turned = call(
        cotangent_kernel,
        "cotangent",
        [bf16(CELLS, features), bf16(NEAR, far, chunk, CELLS)],
        (in_hbm(grad_output), *cotangents, out_weight),
        gflop=1.0,
    )
    raw, stats, product, queries, keys, values = call(
        centre_kernel,
        "centre",
        [f32(pairs, CELLS, 2 * CELLS), f32(pairs, 2, 2 * CELLS), f32(pairs, CELLS, 2 * CELLS)]
        + [bf16(CELLS, features)] * 3,
        (queries, keys, values, dout),
        scratch=[pltpu.VMEM((CELLS, CELLS), jnp.float32)],
        gflop=3.0,
    )
    weights, *partials = call(
        forward_kernel,
        "forward",
        [bf16(pairs, ROWS, 2 * CELLS)] + [bf16(far, chunk, features)] * NEAR,
        (queries, values, *strips, raw, stats, turned),
        scratch=[pltpu.VMEM((2 * STRIP, CELLS), jnp.float32), pltpu.VMEM((CELLS, features), jnp.bfloat16)],
        gflop=4.0,
    )
    terms = exchanged(partials, 1)

    dscore, *backs = call(
        strip_grad_kernel,
        "strip_grad",
        [bf16(pairs, ROWS, 2 * CELLS)] + strip_types,
        (queries, dout, *strips, weights, product),
        gflop=4.0,
    )
    returned = to_sides(backs, offsets)

    grad_queries, centre = call(
        centre_grad_kernel,
        "centre_grad",
        [bf16(CELLS, features), f32(2, CELLS, features)],
        (queries, keys, dout, *strips, weights, dscore),
        gflop=3.0,
    )
    stride = NEAR
    while stride < tile_count:
        ways = min(NEAR, tile_count // stride)
        sums = call(
            functools.partial(sum_kernel, len(terms)),
            "plane_sum",
            [bf16(tile_count // stride // ways, chunk, features)] * ways,
            (*terms, centre),
            unused=1,
            gflop=1.0,
        )
        terms = exchanged(sums, stride)
        stride *= ways

    grad_keys, grad_values, grad_out_weight = call(
        functools.partial(finish_kernel, 1.0 / math.sqrt(token_count * tile_count)),
        "finish",
        [bf16(CELLS, features)] * 2 + [f32(chunk, features)],
        (rotations, centre, *returned, *terms),
        smem=1,
        gflop=1.0,
    )
    return (grad_queries, grad_keys, grad_values, grad_out_weight)


def solution(mesh):
    placed = (
        P("tile", "head"),
        P("tile", "head"),
        P("tile", "head"),
        P("tile", "head"),
        P(None, "head"),
        P("tile", None),
    )
    return jax.shard_map(
        shards,
        mesh=mesh,
        in_specs=placed,
        out_specs=(P("tile", "head"), P("tile", "head"), P("tile", "head"), P("tile", "head")),
        check_vma=False,
    )
```

```python
import functools
import math

import jax
import jax.numpy as jnp
from jax import lax
from jax.experimental import pallas as pl
from jax.experimental.pallas import tpu as pltpu
from jax.sharding import PartitionSpec as P

HEAD_DIM = 64
RADIUS = 6
SIDE = 16
CELLS = SIDE * SIDE
STRIP = RADIUS * SIDE
ROWS = CELLS + 2 * STRIP
NEAR = 4
PAIR = 2 * HEAD_DIM
VMEM_LIMIT = 32 * 1024 * 1024
NT = (((1,), (1,)), ((), ()))


def mm(a, b):
    return jnp.dot(a, b, preferred_element_type=jnp.float32)


def mm_nt(a, b):
    return lax.dot_general(a, b, NT, preferred_element_type=jnp.float32)


def strip_token(side_index, rotation, cell):
    turn = lax.rem(side_index + 6 - rotation, 4)
    depth = cell >> 4
    along = cell & (SIDE - 1)
    far = SIDE - 1 - along
    near_rim = RADIUS - 1 - depth
    far_rim = SIDE - RADIUS + depth
    row = jnp.where(turn == 0, far_rim, jnp.where(turn == 1, along, jnp.where(turn == 2, near_rim, far)))
    col = jnp.where(turn == 0, along, jnp.where(turn == 1, near_rim, jnp.where(turn == 2, far, far_rim)))
    return row * SIDE + col


def pick_kernel(rotations_ref, keys_ref, values_ref, north_ref, east_ref, south_ref, west_ref):
    cell = lax.broadcasted_iota(jnp.int32, (STRIP, CELLS), 0)
    token = lax.broadcasted_iota(jnp.int32, (STRIP, CELLS), 1)
    for side_index, out_ref in enumerate((north_ref, east_ref, south_ref, west_ref)):
        wanted = strip_token(side_index, rotations_ref[0, side_index], cell)
        chosen = jnp.where(token == wanted, 1.0, 0.0).astype(jnp.bfloat16)
        out_ref[0] = mm(chosen, keys_ref[...]).astype(jnp.bfloat16)
        out_ref[1] = mm(chosen, values_ref[...]).astype(jnp.bfloat16)


def merge_kernel(
    rotations_ref, centre_ref, north_ref, east_ref, south_ref, west_ref, keys_ref, values_ref
):
    token = lax.broadcasted_iota(jnp.int32, (CELLS, STRIP), 0)
    cell = lax.broadcasted_iota(jnp.int32, (CELLS, STRIP), 1)
    total_keys = centre_ref[0]
    total_values = centre_ref[1]
    for side_index, back_ref in enumerate((north_ref, east_ref, south_ref, west_ref)):
        wanted = strip_token(side_index, rotations_ref[0, side_index], cell)
        chosen = jnp.where(token == wanted, 1.0, 0.0).astype(jnp.bfloat16)
        total_keys += mm(chosen, back_ref[0])
        total_values += mm(chosen, back_ref[1])
    keys_ref[...] = total_keys.astype(jnp.bfloat16)
    values_ref[...] = total_values.astype(jnp.bfloat16)


def weight_kernel(scale, *refs):
    total = refs[0][0].astype(jnp.float32)
    for ref in refs[1:-1]:
        total += ref[0].astype(jnp.float32)
    refs[-1][...] = total * scale


def partial_kernel(attention_ref, arrived_ref, turned_ref, turned_arrived_ref, unused_ref, kept_ref, sent_ref):
    for index, out_ref in enumerate((kept_ref, sent_ref)):
        total = None
        for turned_part, attention_part in ((turned_ref, attention_ref), (turned_arrived_ref, arrived_ref)):
            turned = turned_part[index]
            turned = turned.reshape(turned.shape[0] * turned.shape[1], turned.shape[2])
            term = mm(turned, attention_part[...])
            total = term if total is None else total + term
        out_ref[...] = total.astype(out_ref.dtype).reshape(out_ref.shape)


def sum_kernel(count, *refs):
    terms, outs = refs[:count], refs[count + 1 :]
    for q in range(terms[0].shape[0]):
        total = terms[0][q].astype(jnp.float32)
        for ref in terms[1:]:
            total += ref[q].astype(jnp.float32)
        outs[q % len(outs)][q // len(outs)] = total.astype(jnp.bfloat16)


def cotangent_kernel(*refs):
    blocks, (out_weight_ref, dout_ref, *turned_refs) = refs[:-4], refs[-4:]
    heads = len(blocks)
    head = lax.axis_index("head")
    tile = lax.axis_index("tile")
    chunk = turned_refs[0].shape[2]
    width = blocks[0].shape[1]
    total = None
    for distance, block_ref in enumerate(blocks):
        owner = lax.rem(head + distance, heads)
        start = pl.multiple_of(owner * width, width)
        block = block_ref[...]
        term = mm(block, out_weight_ref[pl.ds(start, width), :])
        total = term if total is None else total + term
        turned = block.T
        first = owner * (width // chunk)
        for index in range(width // chunk):
            target = (first + index) ^ tile
            rows = turned[index * chunk : (index + 1) * chunk]
            for parity, turned_ref in enumerate(turned_refs):

                @pl.when(target & 1 == parity)
                def _():
                    turned_ref[(target & 3) >> 1, target >> 2] = rows
    dout_ref[...] = total.astype(jnp.bfloat16)


def window(cell_row, cell_col, query):
    query_row = (query >> 4) + RADIUS
    query_col = (query & (SIDE - 1)) + RADIUS
    near = (jnp.abs(cell_row - query_row) <= RADIUS) & (jnp.abs(cell_col - query_col) <= RADIUS)
    return jnp.where(near, 0.0, -1e30)


def centre_bias(bias_ref):
    query = lax.broadcasted_iota(jnp.int32, (CELLS, CELLS), 1)
    cell = lax.broadcasted_iota(jnp.int32, (CELLS, CELLS), 0)
    bias_ref[...] = window((cell >> 4) + RADIUS, (cell & (SIDE - 1)) + RADIUS, query)


def strip_bias(bias_ref):
    query = lax.broadcasted_iota(jnp.int32, (STRIP, CELLS), 1)
    cell = lax.broadcasted_iota(jnp.int32, (STRIP, CELLS), 0)
    depth = cell >> 4
    along = cell & (SIDE - 1)
    last = SIDE + 2 * RADIUS - 1
    north = (depth, RADIUS + along)
    east = (RADIUS + along, last - depth)
    south = (last - depth, last - RADIUS - along)
    west = (last - RADIUS - along, depth)
    for start, kind, first, second in ((0, 0, north, south), (STRIP, 1, west, east)):
        in_first = first_half(query, kind)
        row = jnp.where(in_first, first[0], second[0])
        col = jnp.where(in_first, first[1], second[1])
        bias_ref[start : start + STRIP, :] = window(row, col, query)


def first_half(query, kind):
    return (query & (SIDE - 1)) < SIDE // 2 if kind else query < CELLS // 2


def one_head(block, head):
    lane = lax.broadcasted_iota(jnp.int32, block.shape, 1)
    kept = (lane >= HEAD_DIM) if head else (lane < HEAD_DIM)
    return jnp.where(kept, block, jnp.zeros_like(block))


def halves(block, kind):
    kept = first_half(lax.broadcasted_iota(jnp.int32, block.shape, 0), kind)
    zero = jnp.zeros_like(block)
    return jnp.concatenate([jnp.where(kept, block, zero), jnp.where(kept, zero, block)], axis=1)


def by_half(stacked, kind):
    rows = stacked.shape[0] // 2
    kept = first_half(lax.broadcasted_iota(jnp.int32, (rows, CELLS), 1), kind)
    return jnp.where(kept, stacked[:rows], stacked[rows:])


def side_refs(strips, kind):
    north, east, south, west = strips
    return (west, east) if kind else (north, south)


def side_cells(strips, part, kind, cols):
    return jnp.concatenate([ref[part, :, cols] for ref in side_refs(strips, kind)], axis=1)


def turned_sides(strips, part, kind, cols):
    return [ref[part, :, cols].T for ref in side_refs(strips, kind)]


def pair_cols(pair):
    return pl.ds(pl.multiple_of(pair * PAIR, PAIR), PAIR)


def head_rows(turned, head):
    return turned[head * HEAD_DIM : (head + 1) * HEAD_DIM]


def over_cells(turned_centre, turned_strips, head, centre, sides):
    total = mm(head_rows(turned_centre, head), centre)
    for kind in range(2):
        stacked = jnp.concatenate([head_rows(t, head) for t in turned_strips[kind]], axis=0)
        total += by_half(mm(stacked, sides[kind]), kind)
    return total


SCORE_SCALE = HEAD_DIM ** (-0.5)
LOG_SCALE = SCORE_SCALE * math.log2(math.e)


def lanes_of(head):
    return slice(head * CELLS, (head + 1) * CELLS)


def centre_kernel(
    query_ref, key_ref, value_ref, dout_ref,
    raw_ref, stats_ref, product_ref, query_out, key_out, value_out, bias_ref,
):
    centre_bias(bias_ref)

    def step(pair, carry):
        cols = pair_cols(pair)
        query, key, value, dout = (ref[:, cols] for ref in (query_ref, key_ref, value_ref, dout_ref))
        for head in range(2):
            scores = mm_nt(key, one_head(query, head)) + bias_ref[...]
            top = jnp.max(scores, axis=0, keepdims=True)
            raw = jnp.exp2((scores - top) * LOG_SCALE)
            raw_ref[pair, :, lanes_of(head)] = raw
            stats_ref[pair, 0:1, lanes_of(head)] = top
            stats_ref[pair, 1:2, lanes_of(head)] = jnp.sum(raw, axis=0, keepdims=True)
            product_ref[pair, :, lanes_of(head)] = mm_nt(value, one_head(dout, head))
        query_out[:, cols] = query
        key_out[:, cols] = key
        value_out[:, cols] = value
        return carry

    lax.fori_loop(0, raw_ref.shape[0], step, 0)


def forward_kernel(
    query_ref, value_ref, north_ref, east_ref, south_ref, west_ref, raw_ref, stats_ref, unused_ref,
    weights_ref, attention_ref, bias_ref,
):
    strips = (north_ref, east_ref, south_ref, west_ref)
    strip_bias(bias_ref)

    def step(pair, carry):
        cols = pair_cols(pair)
        query = query_ref[:, cols]
        turned_centre = value_ref[:, cols].T
        turned_strips = [turned_sides(strips, 1, kind, cols) for kind in range(2)]
        sides = [side_cells(strips, 0, kind, cols) for kind in range(2)]
        parts = []
        for head in range(2):
            query_head = one_head(query, head)
            scores = [
                mm_nt(sides[kind], halves(query_head, kind)) + bias_ref[kind * STRIP : (kind + 1) * STRIP]
                for kind in range(2)
            ]
            centre_top = stats_ref[pair, 0:1, lanes_of(head)]
            top = jnp.maximum(jnp.max(jnp.maximum(scores[0], scores[1]), axis=0, keepdims=True), centre_top)
            raw = [jnp.exp2((s - top) * LOG_SCALE) for s in scores]
            lifted = jnp.exp2((centre_top - top) * LOG_SCALE)
            total = jnp.sum(raw[0] + raw[1], axis=0, keepdims=True)
            total += lifted * stats_ref[pair, 1:2, lanes_of(head)]
            inverse = 1.0 / total
            centre = (raw_ref[pair, :, lanes_of(head)] * (lifted * inverse)).astype(jnp.bfloat16)
            outer = [(r * inverse).astype(jnp.bfloat16) for r in raw]
            weights_ref[pair, :CELLS, lanes_of(head)] = centre
            for kind in range(2):
                start = CELLS + kind * STRIP
                weights_ref[pair, start : start + STRIP, lanes_of(head)] = outer[kind]
            parts.append(over_cells(turned_centre, turned_strips, head, centre, outer))
        attention_ref[:, cols] = jnp.concatenate(parts, axis=0).T.astype(jnp.bfloat16)
        return carry

    lax.fori_loop(0, raw_ref.shape[0], step, 0)


def strip_grad_kernel(
    query_ref, dout_ref, north_ref, east_ref, south_ref, west_ref, weights_ref, product_ref,
    dscore_ref, north_out, east_out, south_out, west_out,
):
    strips = (north_ref, east_ref, south_ref, west_ref)
    outs = (north_out, east_out, south_out, west_out)

    def step(pair, carry):
        cols = pair_cols(pair)
        query = query_ref[:, cols]
        dout = dout_ref[:, cols]
        query_halves = []
        dout_halves = []
        sides = [side_cells(strips, 1, kind, cols) for kind in range(2)]
        for head in range(2):
            lanes = lanes_of(head)
            query_halves.append([halves(one_head(query, head), kind) for kind in range(2)])
            dout_halves.append([halves(one_head(dout, head), kind) for kind in range(2)])
            products = [product_ref[pair, :, lanes]]
            products += [mm_nt(sides[kind], dout_halves[head][kind]) for kind in range(2)]
            bounds = (0, CELLS, CELLS + STRIP, CELLS + 2 * STRIP)
            weights = [
                weights_ref[pair, start:end, lanes].astype(jnp.float32)
                for start, end in zip(bounds, bounds[1:])
            ]
            delta = sum(jnp.sum(w * g, axis=0, keepdims=True) for w, g in zip(weights, products))
            for start, end, w, g in zip(bounds, bounds[1:], weights, products):
                dscore_ref[pair, start:end, lanes] = (w * (g - delta)).astype(jnp.bfloat16)
        for kind in range(2):
            start = CELLS + kind * STRIP
            grad_key = mm(
                dscore_ref[pair, start : start + STRIP, :],
                jnp.concatenate([query_halves[head][kind] for head in range(2)], axis=0),
            )
            grad_value = mm(
                weights_ref[pair, start : start + STRIP, :],
                jnp.concatenate([dout_halves[head][kind] for head in range(2)], axis=0),
            )
            for index, out_ref in enumerate(side_refs(outs, kind)):
                lanes = slice(index * PAIR, (index + 1) * PAIR)
                out_ref[0, :, cols] = (grad_key[:, lanes] * SCORE_SCALE).astype(jnp.bfloat16)
                out_ref[1, :, cols] = grad_value[:, lanes].astype(jnp.bfloat16)
        return carry

    lax.fori_loop(0, weights_ref.shape[0], step, 0)


def centre_grad_kernel(
    query_ref, key_ref, dout_ref, north_ref, east_ref, south_ref, west_ref, weights_ref, dscore_ref, unused_ref,
    grad_query_ref, centre_ref,
):
    strips = (north_ref, east_ref, south_ref, west_ref)

    def step(pair, carry):
        cols = pair_cols(pair)
        query = query_ref[:, cols]
        dout = dout_ref[:, cols]
        turned_centre = key_ref[:, cols].T
        turned_strips = [turned_sides(strips, 0, kind, cols) for kind in range(2)]
        parts = []
        for head in range(2):
            lanes = lanes_of(head)
            outer = [
                dscore_ref[pair, CELLS + kind * STRIP : CELLS + (kind + 1) * STRIP, lanes] for kind in range(2)
            ]
            parts.append(over_cells(turned_centre, turned_strips, head, dscore_ref[pair, :CELLS, lanes], outer))
        grad_query = jnp.concatenate(parts, axis=0).T * SCORE_SCALE
        grad_query_ref[:, cols] = grad_query.astype(jnp.bfloat16)
        grad_key = mm(
            dscore_ref[pair, :CELLS, :], jnp.concatenate([one_head(query, head) for head in range(2)], axis=0)
        )
        grad_value = mm(
            weights_ref[pair, :CELLS, :], jnp.concatenate([one_head(dout, head) for head in range(2)], axis=0)
        )
        centre_ref[0, :, cols] = grad_key * SCORE_SCALE
        centre_ref[1, :, cols] = grad_value
        return carry

    lax.fori_loop(0, weights_ref.shape[0], step, 0)


def call(kernel, name, out_shape, operands, scratch=(), smem=0, unused=0, gflop=0.0):
    specs = [pl.BlockSpec(memory_space=pltpu.SMEM)] * smem
    specs += [pl.BlockSpec(memory_space=pltpu.VMEM)] * (len(operands) - smem - unused)
    specs += [pl.BlockSpec(memory_space=pl.ANY)] * unused
    single = not isinstance(out_shape, list)
    outs = pl.BlockSpec(memory_space=pltpu.VMEM)
    return pl.pallas_call(
        kernel,
        out_shape=out_shape,
        in_specs=specs,
        out_specs=outs if single else [outs] * len(out_shape),
        scratch_shapes=list(scratch),
        compiler_params=pltpu.CompilerParams(vmem_limit_bytes=VMEM_LIMIT),
        cost_estimate=pl.CostEstimate(flops=int(gflop * 1e9), bytes_accessed=1 << 20, transcendentals=0),
        name=name,
    )(*operands)


def in_hbm(array):
    return pltpu.with_memory_space_constraint(array, pltpu.HBM)


def from_behind(block, axis, distance):
    devices = range(lax.axis_size(axis))
    route = [((i - distance) % len(devices), i) for i in devices]
    return lax.ppermute(block, axis, route)


def exchanged(blocks, stride):
    terms = list(blocks[:1])
    for distance in range(1, len(blocks)):
        route = [(tile, tile ^ (distance * stride)) for tile in range(lax.axis_size("tile"))]
        terms.append(lax.ppermute(blocks[distance], "tile", route))
    return terms


def to_sides(blocks, offsets):
    arrived = {s: from_behind(blocks[(s + 2) % 4], "tile", -offsets[s]) for s in (0, 2, 1, 3)}
    return [arrived[s] for s in range(4)]


def shards(queries, keys, values, grad_output, out_weight, rotations):
    tile_count = lax.axis_size("tile")
    token_count, features = queries.shape
    model = out_weight.shape[0]
    pairs = features // PAIR
    far = tile_count // NEAR
    chunk = model // tile_count
    heads = lax.axis_size("head")
    offsets = (-(tile_count // 4), 1, tile_count // 4, -1)
    queries, keys, values, out_weight, rotations = (
        in_hbm(a) for a in (queries, keys, values, out_weight, rotations)
    )

    def bf16(*shape):
        return jax.ShapeDtypeStruct(shape, jnp.bfloat16)

    def f32(*shape):
        return jax.ShapeDtypeStruct(shape, jnp.float32)

    strip_types = [bf16(2, STRIP, features)] * 4
    picked = call(pick_kernel, "pick_strips", strip_types, (rotations, keys, values), smem=1, gflop=0.2)
    grad_output, *picked = lax.optimization_barrier((grad_output, *picked))
    strips = to_sides(picked, offsets)

    cotangents = [from_behind(grad_output, "head", -k) for k in range(1, heads)]
    dout, turned, turned_sent = call(
        cotangent_kernel,
        "cotangent",
        [bf16(CELLS, features)] + [bf16(2, far, chunk, CELLS)] * 2,
        (in_hbm(grad_output), *cotangents, out_weight),
        gflop=1.0,
    )
    turned_arrived = exchanged((turned, turned_sent), 1)[1]
    raw, stats, product, queries, keys, values = call(
        centre_kernel,
        "centre",
        [f32(pairs, CELLS, 2 * CELLS), f32(pairs, 2, 2 * CELLS), f32(pairs, CELLS, 2 * CELLS)]
        + [bf16(CELLS, features)] * 3,
        (queries, keys, values, dout),
        scratch=[pltpu.VMEM((CELLS, CELLS), jnp.float32)],
        gflop=3.0,
    )
    weights, attention = call(
        forward_kernel,
        "forward",
        [bf16(pairs, ROWS, 2 * CELLS), bf16(CELLS, features)],
        (queries, values, *strips, raw, stats, turned_arrived),
        unused=1,
        scratch=[pltpu.VMEM((2 * STRIP, CELLS), jnp.float32)],
        gflop=4.0,
    )
    attention_arrived = exchanged((attention, attention), 1)[1]

    dscore, *backs = call(
        strip_grad_kernel,
        "strip_grad",
        [bf16(pairs, ROWS, 2 * CELLS)] + strip_types,
        (queries, dout, *strips, weights, product),
        gflop=4.0,
    )
    returned = to_sides(backs, offsets)
    kept, sent = call(
        partial_kernel,
        "partial",
        [f32(far, chunk, features), bf16(far, chunk, features)],
        (attention, attention_arrived, turned, turned_arrived, backs[0]),
        unused=1,
        gflop=1.0,
    )
    terms = exchanged((kept, sent), 2)

    grad_queries, centre = call(
        centre_grad_kernel,
        "centre_grad",
        [bf16(CELLS, features), f32(2, CELLS, features)],
        (queries, keys, dout, *strips, weights, dscore, sent),
        unused=1,
        gflop=3.0,
    )
    stride = NEAR
    while stride < tile_count:
        ways = min(NEAR, tile_count // stride)
        sums = call(
            functools.partial(sum_kernel, len(terms)),
            "plane_sum",
            [bf16(tile_count // stride // ways, chunk, features)] * ways,
            (*terms, centre),
            unused=1,
            gflop=1.0,
        )
        terms = exchanged(sums, stride)
        stride *= ways

    grad_keys, grad_values = call(
        merge_kernel,
        "merge",
        [bf16(CELLS, features)] * 2,
        (rotations, centre, *returned),
        smem=1,
        gflop=1.0,
    )
    grad_out_weight = call(
        functools.partial(weight_kernel, 1.0 / math.sqrt(token_count * tile_count)),
        "weight_sum",
        f32(chunk, features),
        terms,
    )
    return (grad_queries, grad_keys, grad_values, grad_out_weight)


def solution(mesh):
    placed = (
        P("tile", "head"),
        P("tile", "head"),
        P("tile", "head"),
        P("tile", "head"),
        P(None, "head"),
        P("tile", None),
    )
    return jax.shard_map(
        shards,
        mesh=mesh,
        in_specs=placed,
        out_specs=(P("tile", "head"), P("tile", "head"), P("tile", "head"), P("tile", "head")),
        check_vma=False,
    )
```

```python
import functools
import math

import jax
import jax.numpy as jnp
from jax import lax
from jax.experimental import pallas as pl
from jax.experimental.pallas import tpu as pltpu
from jax.sharding import PartitionSpec as P

HEAD_DIM = 64
RADIUS = 6
SIDE = 16
CELLS = SIDE * SIDE
STRIP = RADIUS * SIDE
ROWS = CELLS + 2 * STRIP
NEAR = 4
LANES = 128
PAIR = 2 * HEAD_DIM
VMEM_LIMIT = 32 * 1024 * 1024
NT = (((1,), (1,)), ((), ()))


def mm(a, b):
    return jnp.dot(a, b, preferred_element_type=jnp.float32)


def mm_nt(a, b):
    return lax.dot_general(a, b, NT, preferred_element_type=jnp.float32)


def strip_token(side_index, rotation, cell):
    turn = lax.rem(side_index + 6 - rotation, 4)
    depth = cell >> 4
    along = cell & (SIDE - 1)
    far = SIDE - 1 - along
    near_rim = RADIUS - 1 - depth
    far_rim = SIDE - RADIUS + depth
    row = jnp.where(turn == 0, far_rim, jnp.where(turn == 1, along, jnp.where(turn == 2, near_rim, far)))
    col = jnp.where(turn == 0, along, jnp.where(turn == 1, near_rim, jnp.where(turn == 2, far, far_rim)))
    return row * SIDE + col


def pick_kernel(rotations_ref, keys_ref, values_ref, north_ref, east_ref, south_ref, west_ref):
    cell = lax.broadcasted_iota(jnp.int32, (STRIP, CELLS), 0)
    token = lax.broadcasted_iota(jnp.int32, (STRIP, CELLS), 1)
    for side_index, out_ref in enumerate((north_ref, east_ref, south_ref, west_ref)):
        wanted = strip_token(side_index, rotations_ref[0, side_index], cell)
        chosen = jnp.where(token == wanted, 1.0, 0.0).astype(jnp.bfloat16)
        out_ref[0] = mm(chosen, keys_ref[...]).astype(jnp.bfloat16)
        out_ref[1] = mm(chosen, values_ref[...]).astype(jnp.bfloat16)


def weight_kernel(scale, *refs):
    total = refs[0][0].astype(jnp.float32)
    for ref in refs[1:-1]:
        total += ref[0].astype(jnp.float32)
    refs[-1][...] = total * scale


def partial_kernel(attention_ref, arrived_ref, turned_ref, turned_arrived_ref, unused_ref, kept_ref, sent_ref):
    for index, out_ref in enumerate((kept_ref, sent_ref)):
        total = None
        for turned_part, attention_part in ((turned_ref, attention_ref), (turned_arrived_ref, arrived_ref)):
            turned = turned_part[index]
            turned = turned.reshape(turned.shape[0] * turned.shape[1], turned.shape[2])
            term = mm(turned, attention_part[...])
            total = term if total is None else total + term
        out_ref[...] = total.astype(out_ref.dtype).reshape(out_ref.shape)


def sum_kernel(count, *refs):
    terms, outs = refs[:count], refs[count + 1 :]
    for q in range(terms[0].shape[0]):
        total = terms[0][q].astype(jnp.float32)
        for ref in terms[1:]:
            total += ref[q].astype(jnp.float32)
        outs[q % len(outs)][q // len(outs)] = total.astype(jnp.bfloat16)


def rim_token(side_index, place):
    depth = place >> 4
    along = place & (SIDE - 1)
    last = SIDE - 1
    row, col = ((depth, along), (along, last - depth), (last - depth, last - along), (last - along, depth))[side_index]
    return row * SIDE + col


def cotangent_kernel(heads, *refs):
    blocks, out_weight_ref, outs = refs[:heads], refs[heads], refs[heads + 1 :]
    dout_ref, dout_turned_ref, turned_ref, turned_sent_ref = outs
    head = lax.axis_index("head")
    tile = lax.axis_index("tile")
    chunk = turned_ref.shape[2]
    width = blocks[0].shape[1]
    total = None
    for distance, block_ref in enumerate(blocks):
        owner = lax.rem(head + distance, heads)
        start = pl.multiple_of(owner * width, width)
        block = block_ref[...]
        term = mm(block, out_weight_ref[pl.ds(start, width), :])
        total = term if total is None else total + term
        turned = block.T
        first = owner * (width // chunk)
        for index in range(width // chunk):
            target = (first + index) ^ tile
            rows = turned[index * chunk : (index + 1) * chunk]
            for parity, out_ref in enumerate((turned_ref, turned_sent_ref)):

                @pl.when((target >> 1) & 1 == parity)
                def _():
                    out_ref[target & 1, target >> 2] = rows

    dout = total.astype(jnp.bfloat16)
    dout_ref[...] = dout
    dout_turned_ref[...] = dout.T


def split(exact, count):
    parts = []
    for _ in range(count):
        part = exact.astype(jnp.bfloat16).astype(jnp.float32)
        parts.append(part)
        exact = exact - part
    return parts


PARTS = (3, 2, 2)


def rim_kernel(query_ref, dout_ref, rows_ref, *rim_refs):
    place = lax.broadcasted_iota(jnp.int32, (LANES, CELLS), 0)
    token = lax.broadcasted_iota(jnp.int32, (LANES, CELLS), 1)
    parts = [part for kind, count in enumerate(PARTS) for part in split(rows_ref[kind], count)]
    pairs = rows_ref.shape[1] // 2
    filler = jnp.zeros((16 - 2 * len(parts), CELLS), jnp.float32)
    rows = [
        jnp.concatenate([part[2 * pair : 2 * pair + 2] for part in parts] + [filler], axis=0) for pair in range(pairs)
    ]
    rows = jnp.concatenate(rows, axis=0).astype(jnp.bfloat16)
    for side_index, rim_ref in enumerate(rim_refs):
        chosen = jnp.where((token == rim_token(side_index, place)) & (place < STRIP), 1.0, 0.0).astype(jnp.bfloat16)
        rim_ref[:STRIP] = mm(chosen[:STRIP], query_ref[...]).astype(jnp.bfloat16)
        rim_ref[STRIP : 2 * STRIP] = mm(chosen[:STRIP], dout_ref[...]).astype(jnp.bfloat16)
        spread = mm_nt(rows, chosen).astype(jnp.bfloat16)
        for pair in range(pairs):
            rim_ref[2 * STRIP :, pair * PAIR : (pair + 1) * PAIR] = spread[16 * pair : 16 * pair + 16]


def window(cell_row, cell_col, query):
    query_row = (query >> 4) + RADIUS
    query_col = (query & (SIDE - 1)) + RADIUS
    near = (jnp.abs(cell_row - query_row) <= RADIUS) & (jnp.abs(cell_col - query_col) <= RADIUS)
    return jnp.where(near, 0.0, -1e30)


def centre_bias(bias_ref):
    query = lax.broadcasted_iota(jnp.int32, (CELLS, CELLS), 1)
    cell = lax.broadcasted_iota(jnp.int32, (CELLS, CELLS), 0)
    bias_ref[...] = window((cell >> 4) + RADIUS, (cell & (SIDE - 1)) + RADIUS, query)


def strip_bias(bias_ref):
    query = lax.broadcasted_iota(jnp.int32, (STRIP, CELLS), 1)
    cell = lax.broadcasted_iota(jnp.int32, (STRIP, CELLS), 0)
    depth = cell >> 4
    along = cell & (SIDE - 1)
    last = SIDE + 2 * RADIUS - 1
    north = (depth, RADIUS + along)
    east = (RADIUS + along, last - depth)
    south = (last - depth, last - RADIUS - along)
    west = (last - RADIUS - along, depth)
    for start, kind, first, second in ((0, 0, north, south), (STRIP, 1, west, east)):
        in_first = first_half(query, kind)
        row = jnp.where(in_first, first[0], second[0])
        col = jnp.where(in_first, first[1], second[1])
        bias_ref[start : start + STRIP, :] = window(row, col, query)


def first_half(query, kind):
    return (query & (SIDE - 1)) < SIDE // 2 if kind else query < CELLS // 2


def one_head(block, head):
    lane = lax.broadcasted_iota(jnp.int32, block.shape, 1)
    kept = (lane >= HEAD_DIM) if head else (lane < HEAD_DIM)
    return jnp.where(kept, block, jnp.zeros_like(block))


def halves(block, kind):
    kept = first_half(lax.broadcasted_iota(jnp.int32, block.shape, 0), kind)
    zero = jnp.zeros_like(block)
    return jnp.concatenate([jnp.where(kept, block, zero), jnp.where(kept, zero, block)], axis=1)


def by_half(stacked, kind):
    rows = stacked.shape[0] // 2
    kept = first_half(lax.broadcasted_iota(jnp.int32, (rows, CELLS), 1), kind)
    return jnp.where(kept, stacked[:rows], stacked[rows:])


def side_refs(strips, kind):
    north, east, south, west = strips
    return (west, east) if kind else (north, south)


def side_cells(strips, part, kind, cols):
    return jnp.concatenate([ref[part, :, cols] for ref in side_refs(strips, kind)], axis=1)


def turned_sides(strips, part, kind, cols):
    return [ref[part, :, cols].T for ref in side_refs(strips, kind)]


def pair_cols(pair):
    return pl.ds(pl.multiple_of(pair * PAIR, PAIR), PAIR)


def head_rows(turned, head):
    return turned[head * HEAD_DIM : (head + 1) * HEAD_DIM]


def over_cells(turned_centre, turned_strips, head, centre, sides):
    total = mm(head_rows(turned_centre, head), centre)
    for kind in range(2):
        stacked = jnp.concatenate([head_rows(t, head) for t in turned_strips[kind]], axis=0)
        total += by_half(mm(stacked, sides[kind]), kind)
    return total


SCORE_SCALE = HEAD_DIM ** (-0.5)
LOG_SCALE = SCORE_SCALE * math.log2(math.e)


def lanes_of(head):
    return slice(head * CELLS, (head + 1) * CELLS)


def centre_kernel(
    query_ref, key_ref, value_ref, dout_ref,
    raw_ref, stats_ref, product_ref, query_out, key_out, value_out, bias_ref,
):
    centre_bias(bias_ref)

    def step(pair, carry):
        cols = pair_cols(pair)
        query, key, value, dout = (ref[:, cols] for ref in (query_ref, key_ref, value_ref, dout_ref))
        for head in range(2):
            scores = mm_nt(key, one_head(query, head)) + bias_ref[...]
            top = jnp.max(scores, axis=0, keepdims=True)
            raw = jnp.exp2((scores - top) * LOG_SCALE)
            raw_ref[pair, :, lanes_of(head)] = raw
            stats_ref[pair, 0:1, lanes_of(head)] = top
            stats_ref[pair, 1:2, lanes_of(head)] = jnp.sum(raw, axis=0, keepdims=True)
            product_ref[pair, :, lanes_of(head)] = mm_nt(value, one_head(dout, head))
        query_out[:, cols] = query
        key_out[:, cols] = key
        value_out[:, cols] = value
        return carry

    lax.fori_loop(0, raw_ref.shape[0], step, 0)


def forward_kernel(
    query_ref, value_ref, dout_turned_ref, north_ref, east_ref, south_ref, west_ref, raw_ref, stats_ref, unused_ref,
    weights_ref, attention_ref, rows_ref, bias_ref,
):
    strips = (north_ref, east_ref, south_ref, west_ref)
    strip_bias(bias_ref)

    def step(pair, carry):
        cols = pair_cols(pair)
        query = query_ref[:, cols]
        turned_centre = value_ref[:, cols].T
        turned_strips = [turned_sides(strips, 1, kind, cols) for kind in range(2)]
        sides = [side_cells(strips, 0, kind, cols) for kind in range(2)]
        parts = []
        for head in range(2):
            query_head = one_head(query, head)
            scores = [
                mm_nt(sides[kind], halves(query_head, kind)) + bias_ref[kind * STRIP : (kind + 1) * STRIP]
                for kind in range(2)
            ]
            centre_top = stats_ref[pair, 0:1, lanes_of(head)]
            top = jnp.maximum(jnp.max(jnp.maximum(scores[0], scores[1]), axis=0, keepdims=True), centre_top)
            raw = [jnp.exp2((s - top) * LOG_SCALE) for s in scores]
            lifted = jnp.exp2((centre_top - top) * LOG_SCALE)
            total = jnp.sum(raw[0] + raw[1], axis=0, keepdims=True)
            total += lifted * stats_ref[pair, 1:2, lanes_of(head)]
            inverse = 1.0 / total
            centre = (raw_ref[pair, :, lanes_of(head)] * (lifted * inverse)).astype(jnp.bfloat16)
            outer = [(r * inverse).astype(jnp.bfloat16) for r in raw]
            weights_ref[pair, :CELLS, lanes_of(head)] = centre
            for kind in range(2):
                start = CELLS + kind * STRIP
                weights_ref[pair, start : start + STRIP, lanes_of(head)] = outer[kind]
            part = over_cells(turned_centre, turned_strips, head, centre, outer)
            parts.append(part)
            place = pl.ds(2 * pair + head, 1)
            features = pl.ds(pl.multiple_of((2 * pair + head) * HEAD_DIM, HEAD_DIM), HEAD_DIM)
            product = dout_turned_ref[features, :].astype(jnp.float32) * part
            rows_ref[0, place, :] = top
            rows_ref[1, place, :] = inverse
            rows_ref[2, place, :] = jnp.sum(product, axis=0, keepdims=True)
        attention_ref[:, cols] = jnp.concatenate(parts, axis=0).T.astype(jnp.bfloat16)
        return carry

    lax.fori_loop(0, raw_ref.shape[0], step, 0)


def backward_kernel(
    query_ref, key_ref, dout_ref, north_ref, east_ref, south_ref, west_ref, weights_ref, product_ref, rows_ref,
    unused_ref, grad_query_ref, centre_ref,
):
    strips = (north_ref, east_ref, south_ref, west_ref)

    def step(pair, carry):
        cols = pair_cols(pair)
        query = query_ref[:, cols]
        dout = dout_ref[:, cols]
        turned_centre = key_ref[:, cols].T
        turned_strips = [turned_sides(strips, 0, kind, cols) for kind in range(2)]
        sides = [side_cells(strips, 1, kind, cols) for kind in range(2)]
        bounds = (0, CELLS, CELLS + STRIP, CELLS + 2 * STRIP)
        parts = []
        centre_scores = []
        for head in range(2):
            lanes = lanes_of(head)
            dout_head = one_head(dout, head)
            delta = rows_ref[2, pl.ds(2 * pair + head, 1), :]
            products = [product_ref[pair, :, lanes]]
            products += [mm_nt(sides[kind], halves(dout_head, kind)) for kind in range(2)]
            dscore = [
                (weights_ref[pair, start:end, lanes].astype(jnp.float32) * (g - delta)).astype(jnp.bfloat16)
                for start, end, g in zip(bounds, bounds[1:], products)
            ]
            centre_scores.append(dscore[0])
            parts.append(over_cells(turned_centre, turned_strips, head, dscore[0], dscore[1:]))
        grad_query = jnp.concatenate(parts, axis=0).T * SCORE_SCALE
        grad_query_ref[:, cols] = grad_query.astype(jnp.bfloat16)
        grad_key = mm(jnp.concatenate(centre_scores, axis=1), both_heads(query))
        centre_ref[0, :, cols] = grad_key * SCORE_SCALE
        centre_ref[1, :, cols] = mm(weights_ref[pair, :CELLS, :], both_heads(dout))
        return carry

    lax.fori_loop(0, weights_ref.shape[0], step, 0)


def both_heads(block):
    return jnp.concatenate([one_head(block, head) for head in range(2)], axis=0)


def padded(block):
    return jnp.concatenate([block, jnp.zeros((LANES - block.shape[0], block.shape[1]), block.dtype)], axis=0)


def statistics(rows):
    first = 0
    for count in PARTS:
        heads = []
        for head in range(2):
            parts = [rows[2 * index + head : 2 * index + head + 1] for index in range(first, first + count)]
            heads.append(functools.reduce(jnp.add, parts))
        first += count
        yield jnp.concatenate(heads, axis=1)


def side_kernel(rotations_ref, centre_ref, *refs):
    picked, rims = refs[:4], refs[4:8]
    keys_ref, values_ref, chosen_ref, bias_ref = refs[8:]
    cell = lax.broadcasted_iota(jnp.int32, (STRIP, LANES), 0)
    query = lax.broadcasted_iota(jnp.int32, (STRIP, LANES), 1)
    near = jnp.abs((cell & (SIDE - 1)) - (query & (SIDE - 1))) <= RADIUS
    near = near & ((cell >> 4) >= (query >> 4)) & (query < STRIP)
    bias_ref[...] = jnp.where(near, 0.0, -1e30)
    token = lax.broadcasted_iota(jnp.int32, (CELLS, LANES), 0)
    place = lax.broadcasted_iota(jnp.int32, (CELLS, LANES), 1)
    for side_index in range(4):
        wanted = jnp.where(place < STRIP, strip_token(side_index, rotations_ref[0, side_index], place), -1)
        chosen = jnp.where(token == wanted, 1.0, 0.0).astype(jnp.bfloat16)
        chosen_ref[:, side_index * LANES : (side_index + 1) * LANES] = chosen

    def step(pair, carry):
        cols = pair_cols(pair)
        grad_keys = []
        grad_values = []
        bias = jnp.concatenate([bias_ref[...]] * 2, axis=1)
        for side_index in range(4):
            query = both_heads(padded(rims[side_index][:STRIP, cols]))
            dout = both_heads(padded(rims[side_index][STRIP : 2 * STRIP, cols]))
            rows = rims[side_index][2 * STRIP :, cols].astype(jnp.float32)
            top, inverse, delta = statistics(rows)
            scores = mm_nt(picked[side_index][0, :, cols], query) + bias
            weights = jnp.exp2((scores - top) * LOG_SCALE) * inverse
            product = mm_nt(picked[side_index][1, :, cols], dout)
            dscore = (weights * (product - delta)).astype(jnp.bfloat16)
            grad_keys.append(padded((mm(dscore, query) * SCORE_SCALE).astype(jnp.bfloat16)))
            grad_values.append(padded(mm(weights.astype(jnp.bfloat16), dout).astype(jnp.bfloat16)))
        chosen = chosen_ref[...]
        total = centre_ref[0, :, cols] + mm(chosen, jnp.concatenate(grad_keys, axis=0))
        keys_ref[:, cols] = total.astype(jnp.bfloat16)
        total = centre_ref[1, :, cols] + mm(chosen, jnp.concatenate(grad_values, axis=0))
        values_ref[:, cols] = total.astype(jnp.bfloat16)
        return carry

    lax.fori_loop(0, keys_ref.shape[1] // PAIR, step, 0)


def call(kernel, name, out_shape, operands, scratch=(), smem=0, unused=0, gflop=0.1):
    specs = [pl.BlockSpec(memory_space=pltpu.SMEM)] * smem
    specs += [pl.BlockSpec(memory_space=pltpu.VMEM)] * (len(operands) - smem - unused)
    specs += [pl.BlockSpec(memory_space=pl.ANY)] * unused
    single = not isinstance(out_shape, list)
    outs = pl.BlockSpec(memory_space=pltpu.VMEM)
    return pl.pallas_call(
        kernel,
        out_shape=out_shape,
        in_specs=specs,
        out_specs=outs if single else [outs] * len(out_shape),
        scratch_shapes=list(scratch),
        compiler_params=pltpu.CompilerParams(vmem_limit_bytes=VMEM_LIMIT),
        cost_estimate=pl.CostEstimate(flops=int(gflop * 1e9), bytes_accessed=1 << 20, transcendentals=0),
        name=name,
    )(*operands)


def in_hbm(array):
    return pltpu.with_memory_space_constraint(array, pltpu.HBM)


def from_behind(block, axis, distance):
    devices = range(lax.axis_size(axis))
    route = [((i - distance) % len(devices), i) for i in devices]
    return lax.ppermute(block, axis, route)


def exchanged(blocks, stride):
    terms = list(blocks[:1])
    for distance in range(1, len(blocks)):
        route = [(tile, tile ^ (distance * stride)) for tile in range(lax.axis_size("tile"))]
        terms.append(lax.ppermute(blocks[distance], "tile", route))
    return terms


def to_sides(blocks, offsets):
    arrived = {s: from_behind(blocks[(s + 2) % 4], "tile", -offsets[s]) for s in (0, 2, 1, 3)}
    return [arrived[s] for s in range(4)]


def shards(queries, keys, values, grad_output, out_weight, rotations):
    tile_count = lax.axis_size("tile")
    token_count, features = queries.shape
    model = out_weight.shape[0]
    pairs = features // PAIR
    far = tile_count // NEAR
    chunk = model // tile_count
    heads = lax.axis_size("head")
    offsets = (-(tile_count // 4), 1, tile_count // 4, -1)
    queries, keys, values, out_weight, rotations = (
        in_hbm(a) for a in (queries, keys, values, out_weight, rotations)
    )

    def bf16(*shape):
        return jax.ShapeDtypeStruct(shape, jnp.bfloat16)

    def f32(*shape):
        return jax.ShapeDtypeStruct(shape, jnp.float32)

    strip_types = [bf16(2, STRIP, features)] * 4
    picked = call(pick_kernel, "pick_strips", strip_types, (rotations, keys, values), smem=1)
    grad_output, *picked = lax.optimization_barrier((grad_output, *picked))
    strips = to_sides(picked, offsets)

    cotangents = [from_behind(grad_output, "head", -k) for k in range(1, heads)]
    dout, dout_turned, turned, turned_sent = call(
        functools.partial(cotangent_kernel, heads),
        "cotangent",
        [bf16(CELLS, features), bf16(features, CELLS)] + [bf16(2, far, chunk, CELLS)] * 2,
        (in_hbm(grad_output), *cotangents, out_weight),
        gflop=1.0,
    )
    turned_arrived = exchanged((turned, turned_sent), 2)[1]
    raw, stats, product, queries, keys, values = call(
        centre_kernel,
        "centre",
        [f32(pairs, CELLS, 2 * CELLS), f32(pairs, 2, 2 * CELLS), f32(pairs, CELLS, 2 * CELLS)]
        + [bf16(CELLS, features)] * 3,
        (queries, keys, values, dout),
        scratch=[pltpu.VMEM((CELLS, CELLS), jnp.float32)],
        gflop=3.0,
    )
    weights, attention, rows = call(
        forward_kernel,
        "forward",
        [bf16(pairs, ROWS, 2 * CELLS), bf16(CELLS, features), f32(3, 2 * pairs, CELLS)],
        (queries, values, dout_turned, *strips, raw, stats, turned_arrived),
        scratch=[pltpu.VMEM((2 * STRIP, CELLS), jnp.float32)],
        unused=1,
        gflop=4.0,
    )
    attention_arrived = exchanged((attention, attention), 2)[1]
    rims = call(
        rim_kernel,
        "rims",
        [bf16(2 * STRIP + 16, features)] * 4,
        (queries, dout, rows),
    )
    rims_arrived = to_sides(rims, offsets)
    kept, sent = call(
        partial_kernel,
        "partial",
        [f32(far, chunk, features), bf16(far, chunk, features)],
        (attention, attention_arrived, turned, turned_arrived, rims[0]),
        unused=1,
    )
    terms = exchanged((kept, sent), 1)

    grad_queries, centre = call(
        backward_kernel,
        "backward",
        [bf16(CELLS, features), f32(2, CELLS, features)],
        (queries, keys, dout, *strips, weights, product, rows, sent),
        unused=1,
        gflop=3.0,
    )
    stride = NEAR
    while stride < tile_count:
        ways = min(NEAR, tile_count // stride)
        sums = call(
            functools.partial(sum_kernel, len(terms)),
            "plane_sum",
            [bf16(tile_count // stride // ways, chunk, features)] * ways,
            (*terms, centre),
            unused=1,
        )
        terms = exchanged(sums, stride)
        stride *= ways

    grad_keys, grad_values = call(
        side_kernel,
        "sides",
        [bf16(CELLS, features)] * 2,
        (rotations, centre, *picked, *rims_arrived),
        scratch=[
            pltpu.VMEM((CELLS, 4 * LANES), jnp.bfloat16),
            pltpu.VMEM((STRIP, LANES), jnp.float32),
        ],
        smem=1,
        gflop=3.0,
    )
    grad_out_weight = call(
        functools.partial(weight_kernel, 1.0 / math.sqrt(token_count * tile_count)),
        "weight_sum",
        f32(chunk, features),
        terms,
    )
    return (grad_queries, grad_keys, grad_values, grad_out_weight)


def solution(mesh):
    placed = (
        P("tile", "head"),
        P("tile", "head"),
        P("tile", "head"),
        P("tile", "head"),
        P(None, "head"),
        P("tile", None),
    )
    return jax.shard_map(
        shards,
        mesh=mesh,
        in_specs=placed,
        out_specs=(P("tile", "head"), P("tile", "head"), P("tile", "head"), P("tile", "head")),
        check_vma=False,
    )
```

```python
import functools
import math

import jax
import jax.numpy as jnp
from jax import lax
from jax.experimental import pallas as pl
from jax.experimental.pallas import tpu as pltpu
from jax.sharding import PartitionSpec as P

HEAD_DIM = 64
RADIUS = 6
SIDE = 16
CELLS = SIDE * SIDE
STRIP = RADIUS * SIDE
ROWS = CELLS + 2 * STRIP
NEAR = 4
LANES = 128
PAIR = 2 * HEAD_DIM
VMEM_LIMIT = 32 * 1024 * 1024
NT = (((1,), (1,)), ((), ()))


def mm(a, b):
    return jnp.dot(a, b, preferred_element_type=jnp.float32)


def mm_nt(a, b):
    return lax.dot_general(a, b, NT, preferred_element_type=jnp.float32)


def strip_token(side_index, rotation, cell):
    turn = lax.rem(side_index + 6 - rotation, 4)
    depth = cell >> 4
    along = cell & (SIDE - 1)
    far = SIDE - 1 - along
    near_rim = RADIUS - 1 - depth
    far_rim = SIDE - RADIUS + depth
    row = jnp.where(turn == 0, far_rim, jnp.where(turn == 1, along, jnp.where(turn == 2, near_rim, far)))
    col = jnp.where(turn == 0, along, jnp.where(turn == 1, near_rim, jnp.where(turn == 2, far, far_rim)))
    return row * SIDE + col


def pick_kernel(rotations_ref, keys_ref, values_ref, north_ref, east_ref, south_ref, west_ref):
    cell = lax.broadcasted_iota(jnp.int32, (STRIP, CELLS), 0)
    token = lax.broadcasted_iota(jnp.int32, (STRIP, CELLS), 1)
    for side_index, out_ref in enumerate((north_ref, east_ref, south_ref, west_ref)):
        wanted = strip_token(side_index, rotations_ref[0, side_index], cell)
        chosen = jnp.where(token == wanted, 1.0, 0.0).astype(jnp.bfloat16)
        out_ref[0] = mm(chosen, keys_ref[...]).astype(jnp.bfloat16)
        out_ref[1] = mm(chosen, values_ref[...]).astype(jnp.bfloat16)


def weight_kernel(scale, *refs):
    total = refs[0][0].astype(jnp.float32)
    for ref in refs[1:-1]:
        total += ref[0].astype(jnp.float32)
    refs[-1][...] = total * scale


def partial_kernel(attention_ref, arrived_ref, turned_ref, turned_arrived_ref, unused_ref, kept_ref, sent_ref):
    for index, out_ref in enumerate((kept_ref, sent_ref)):
        total = None
        for turned_part, attention_part in ((turned_ref, attention_ref), (turned_arrived_ref, arrived_ref)):
            turned = turned_part[index]
            turned = turned.reshape(turned.shape[0] * turned.shape[1], turned.shape[2])
            term = mm(turned, attention_part[...])
            total = term if total is None else total + term
        out_ref[...] = total.astype(out_ref.dtype).reshape(out_ref.shape)


def sum_kernel(count, *refs):
    terms, outs = refs[:count], refs[count + 1 :]
    for q in range(terms[0].shape[0]):
        total = terms[0][q].astype(jnp.float32)
        for ref in terms[1:]:
            total += ref[q].astype(jnp.float32)
        outs[q % len(outs)][q // len(outs)] = total.astype(jnp.bfloat16)


def rim_token(side_index, place):
    depth = place >> 4
    along = place & (SIDE - 1)
    last = SIDE - 1
    row, col = ((depth, along), (along, last - depth), (last - depth, last - along), (last - along, depth))[side_index]
    return row * SIDE + col


def cotangent_kernel(heads, *refs):
    blocks, out_weight_ref, outs = refs[:heads], refs[heads], refs[heads + 1 :]
    dout_ref, dout_turned_ref, turned_ref, turned_sent_ref = outs
    head = lax.axis_index("head")
    tile = lax.axis_index("tile")
    chunk = turned_ref.shape[2]
    width = blocks[0].shape[1]
    total = None
    for distance, block_ref in enumerate(blocks):
        owner = lax.rem(head + distance, heads)
        start = pl.multiple_of(owner * width, width)
        block = block_ref[...]
        term = mm(block, out_weight_ref[pl.ds(start, width), :])
        total = term if total is None else total + term
        turned = block.T
        first = owner * (width // chunk)
        for index in range(width // chunk):
            target = (first + index) ^ tile
            rows = turned[index * chunk : (index + 1) * chunk]
            for parity, out_ref in enumerate((turned_ref, turned_sent_ref)):

                @pl.when(target & 1 == parity)
                def _():
                    out_ref[(target & 3) >> 1, target >> 2] = rows

    dout = total.astype(jnp.bfloat16)
    dout_ref[...] = dout
    dout_turned_ref[...] = dout.T


def split(exact, count):
    parts = []
    for _ in range(count):
        part = exact.astype(jnp.bfloat16).astype(jnp.float32)
        parts.append(part)
        exact = exact - part
    return parts


PARTS = (3, 2, 2)


def rim_kernel(query_ref, dout_ref, rows_ref, unused_ref, *rim_refs):
    place = lax.broadcasted_iota(jnp.int32, (LANES, CELLS), 0)
    token = lax.broadcasted_iota(jnp.int32, (LANES, CELLS), 1)
    parts = [part for kind, count in enumerate(PARTS) for part in split(rows_ref[kind], count)]
    pairs = rows_ref.shape[1] // 2
    filler = jnp.zeros((16 - 2 * len(parts), CELLS), jnp.float32)
    rows = [
        jnp.concatenate([part[2 * pair : 2 * pair + 2] for part in parts] + [filler], axis=0) for pair in range(pairs)
    ]
    rows = jnp.concatenate(rows, axis=0).astype(jnp.bfloat16)
    for side_index, rim_ref in enumerate(rim_refs):
        chosen = jnp.where((token == rim_token(side_index, place)) & (place < STRIP), 1.0, 0.0).astype(jnp.bfloat16)
        rim_ref[:STRIP] = mm(chosen[:STRIP], query_ref[...]).astype(jnp.bfloat16)
        rim_ref[STRIP : 2 * STRIP] = mm(chosen[:STRIP], dout_ref[...]).astype(jnp.bfloat16)
        spread = mm_nt(rows, chosen).astype(jnp.bfloat16)
        for pair in range(pairs):
            rim_ref[2 * STRIP :, pair * PAIR : (pair + 1) * PAIR] = spread[16 * pair : 16 * pair + 16]


def window(cell_row, cell_col, query):
    query_row = (query >> 4) + RADIUS
    query_col = (query & (SIDE - 1)) + RADIUS
    near = (jnp.abs(cell_row - query_row) <= RADIUS) & (jnp.abs(cell_col - query_col) <= RADIUS)
    return jnp.where(near, 0.0, -1e30)


def centre_bias(bias_ref):
    query = lax.broadcasted_iota(jnp.int32, (CELLS, CELLS), 1)
    cell = lax.broadcasted_iota(jnp.int32, (CELLS, CELLS), 0)
    bias_ref[...] = window((cell >> 4) + RADIUS, (cell & (SIDE - 1)) + RADIUS, query)


def strip_bias(bias_ref):
    query = lax.broadcasted_iota(jnp.int32, (STRIP, CELLS), 1)
    cell = lax.broadcasted_iota(jnp.int32, (STRIP, CELLS), 0)
    depth = cell >> 4
    along = cell & (SIDE - 1)
    last = SIDE + 2 * RADIUS - 1
    north = (depth, RADIUS + along)
    east = (RADIUS + along, last - depth)
    south = (last - depth, last - RADIUS - along)
    west = (last - RADIUS - along, depth)
    for start, kind, first, second in ((0, 0, north, south), (STRIP, 1, west, east)):
        in_first = first_half(query, kind)
        row = jnp.where(in_first, first[0], second[0])
        col = jnp.where(in_first, first[1], second[1])
        bias_ref[start : start + STRIP, :] = window(row, col, query)


def first_half(query, kind):
    return (query & (SIDE - 1)) < SIDE // 2 if kind else query < CELLS // 2


def one_head(block, head):
    lane = lax.broadcasted_iota(jnp.int32, block.shape, 1)
    kept = (lane >= HEAD_DIM) if head else (lane < HEAD_DIM)
    return jnp.where(kept, block, jnp.zeros_like(block))


def halves(block, kind):
    kept = first_half(lax.broadcasted_iota(jnp.int32, block.shape, 0), kind)
    zero = jnp.zeros_like(block)
    return jnp.concatenate([jnp.where(kept, block, zero), jnp.where(kept, zero, block)], axis=1)


def by_half(stacked, kind):
    rows = stacked.shape[0] // 2
    kept = first_half(lax.broadcasted_iota(jnp.int32, (rows, CELLS), 1), kind)
    return jnp.where(kept, stacked[:rows], stacked[rows:])


def side_refs(strips, kind):
    north, east, south, west = strips
    return (west, east) if kind else (north, south)


def side_cells(strips, part, kind, cols):
    return jnp.concatenate([ref[part, :, cols] for ref in side_refs(strips, kind)], axis=1)


def turned_sides(strips, part, kind, cols):
    return [ref[part, :, cols].T for ref in side_refs(strips, kind)]


def pair_cols(pair):
    return pl.ds(pl.multiple_of(pair * PAIR, PAIR), PAIR)


def head_rows(turned, head):
    return turned[head * HEAD_DIM : (head + 1) * HEAD_DIM]


def over_cells(turned_centre, turned_strips, head, centre, sides):
    total = mm(head_rows(turned_centre, head), centre)
    for kind in range(2):
        stacked = jnp.concatenate([head_rows(t, head) for t in turned_strips[kind]], axis=0)
        total += by_half(mm(stacked, sides[kind]), kind)
    return total


SCORE_SCALE = HEAD_DIM ** (-0.5)
LOG_SCALE = SCORE_SCALE * math.log2(math.e)


def lanes_of(head):
    return slice(head * CELLS, (head + 1) * CELLS)


def centre_kernel(
    query_ref, key_ref, value_ref, dout_ref,
    raw_ref, stats_ref, product_ref, query_out, key_out, value_out, bias_ref,
):
    centre_bias(bias_ref)

    def step(pair, carry):
        cols = pair_cols(pair)
        query, key, value, dout = (ref[:, cols] for ref in (query_ref, key_ref, value_ref, dout_ref))
        for head in range(2):
            scores = mm_nt(key, one_head(query, head)) + bias_ref[...]
            top = jnp.max(scores, axis=0, keepdims=True)
            raw = jnp.exp2((scores - top) * LOG_SCALE)
            raw_ref[pair, :, lanes_of(head)] = raw
            stats_ref[pair, 0:1, lanes_of(head)] = top
            stats_ref[pair, 1:2, lanes_of(head)] = jnp.sum(raw, axis=0, keepdims=True)
            product_ref[pair, :, lanes_of(head)] = mm_nt(value, one_head(dout, head))
        query_out[:, cols] = query
        key_out[:, cols] = key
        value_out[:, cols] = value
        return carry

    lax.fori_loop(0, raw_ref.shape[0], step, 0)


def forward_kernel(
    north_ref, south_ref, east_ref, west_ref, query_ref, value_ref, dout_turned_ref, raw_ref, stats_ref,
    weights_ref, attention_ref, rows_ref, bias_ref,
):
    strips = (north_ref, east_ref, south_ref, west_ref)
    strip_bias(bias_ref)

    def step(pair, carry):
        cols = pair_cols(pair)
        query = query_ref[:, cols]
        turned_centre = value_ref[:, cols].T
        turned_strips = [turned_sides(strips, 1, kind, cols) for kind in range(2)]
        sides = [side_cells(strips, 0, kind, cols) for kind in range(2)]
        parts = []
        for head in range(2):
            query_head = one_head(query, head)
            scores = [
                mm_nt(sides[kind], halves(query_head, kind)) + bias_ref[kind * STRIP : (kind + 1) * STRIP]
                for kind in range(2)
            ]
            centre_top = stats_ref[pair, 0:1, lanes_of(head)]
            top = jnp.maximum(jnp.max(jnp.maximum(scores[0], scores[1]), axis=0, keepdims=True), centre_top)
            raw = [jnp.exp2((s - top) * LOG_SCALE) for s in scores]
            lifted = jnp.exp2((centre_top - top) * LOG_SCALE)
            total = jnp.sum(raw[0] + raw[1], axis=0, keepdims=True)
            total += lifted * stats_ref[pair, 1:2, lanes_of(head)]
            inverse = 1.0 / total
            centre = (raw_ref[pair, :, lanes_of(head)] * (lifted * inverse)).astype(jnp.bfloat16)
            outer = [(r * inverse).astype(jnp.bfloat16) for r in raw]
            weights_ref[pair, :CELLS, lanes_of(head)] = centre
            for kind in range(2):
                start = CELLS + kind * STRIP
                weights_ref[pair, start : start + STRIP, lanes_of(head)] = outer[kind]
            part = over_cells(turned_centre, turned_strips, head, centre, outer)
            parts.append(part)
            place = pl.ds(2 * pair + head, 1)
            features = pl.ds(pl.multiple_of((2 * pair + head) * HEAD_DIM, HEAD_DIM), HEAD_DIM)
            product = dout_turned_ref[features, :].astype(jnp.float32) * part
            rows_ref[0, place, :] = top
            rows_ref[1, place, :] = inverse
            rows_ref[2, place, :] = jnp.sum(product, axis=0, keepdims=True)
        attention_ref[:, cols] = jnp.concatenate(parts, axis=0).T.astype(jnp.bfloat16)
        return carry

    lax.fori_loop(0, raw_ref.shape[0], step, 0)


def backward_kernel(
    query_ref, key_ref, dout_ref, north_ref, south_ref, east_ref, west_ref, weights_ref, product_ref, rows_ref,
    unused_ref, grad_query_ref, centre_ref,
):
    strips = (north_ref, east_ref, south_ref, west_ref)

    def step(pair, carry):
        cols = pair_cols(pair)
        query = query_ref[:, cols]
        dout = dout_ref[:, cols]
        turned_centre = key_ref[:, cols].T
        turned_strips = [turned_sides(strips, 0, kind, cols) for kind in range(2)]
        sides = [side_cells(strips, 1, kind, cols) for kind in range(2)]
        bounds = (0, CELLS, CELLS + STRIP, CELLS + 2 * STRIP)
        parts = []
        centre_scores = []
        for head in range(2):
            lanes = lanes_of(head)
            dout_head = one_head(dout, head)
            delta = rows_ref[2, pl.ds(2 * pair + head, 1), :]
            products = [product_ref[pair, :, lanes]]
            products += [mm_nt(sides[kind], halves(dout_head, kind)) for kind in range(2)]
            dscore = [
                (weights_ref[pair, start:end, lanes].astype(jnp.float32) * (g - delta)).astype(jnp.bfloat16)
                for start, end, g in zip(bounds, bounds[1:], products)
            ]
            centre_scores.append(dscore[0])
            parts.append(over_cells(turned_centre, turned_strips, head, dscore[0], dscore[1:]))
        grad_query = jnp.concatenate(parts, axis=0).T * SCORE_SCALE
        grad_query_ref[:, cols] = grad_query.astype(jnp.bfloat16)
        grad_key = mm(jnp.concatenate(centre_scores, axis=1), both_heads(query))
        centre_ref[0, :, cols] = grad_key * SCORE_SCALE
        centre_ref[1, :, cols] = mm(weights_ref[pair, :CELLS, :], both_heads(dout))
        return carry

    lax.fori_loop(0, weights_ref.shape[0], step, 0)


def both_heads(block):
    return jnp.concatenate([one_head(block, head) for head in range(2)], axis=0)


def padded(block):
    return jnp.concatenate([block, jnp.zeros((LANES - block.shape[0], block.shape[1]), block.dtype)], axis=0)


def statistics(rows):
    first = 0
    for count in PARTS:
        heads = []
        for head in range(2):
            parts = [rows[2 * index + head : 2 * index + head + 1] for index in range(first, first + count)]
            heads.append(functools.reduce(jnp.add, parts))
        first += count
        yield jnp.concatenate(heads, axis=1)


def side_kernel(rotations_ref, centre_ref, *refs):
    picked, rims = refs[:4], in_order(refs[4:8])
    keys_ref, values_ref, chosen_ref, bias_ref = refs[8:]
    cell = lax.broadcasted_iota(jnp.int32, (STRIP, LANES), 0)
    query = lax.broadcasted_iota(jnp.int32, (STRIP, LANES), 1)
    near = jnp.abs((cell & (SIDE - 1)) - (query & (SIDE - 1))) <= RADIUS
    near = near & ((cell >> 4) >= (query >> 4)) & (query < STRIP)
    bias_ref[...] = jnp.where(near, 0.0, -1e30)
    token = lax.broadcasted_iota(jnp.int32, (CELLS, LANES), 0)
    place = lax.broadcasted_iota(jnp.int32, (CELLS, LANES), 1)
    for side_index in range(4):
        wanted = jnp.where(place < STRIP, strip_token(side_index, rotations_ref[0, side_index], place), -1)
        chosen = jnp.where(token == wanted, 1.0, 0.0).astype(jnp.bfloat16)
        chosen_ref[:, side_index * LANES : (side_index + 1) * LANES] = chosen

    def step(pair, carry):
        cols = pair_cols(pair)
        grad_keys = []
        grad_values = []
        bias = jnp.concatenate([bias_ref[...]] * 2, axis=1)
        for side_index in range(4):
            query = both_heads(padded(rims[side_index][:STRIP, cols]))
            dout = both_heads(padded(rims[side_index][STRIP : 2 * STRIP, cols]))
            rows = rims[side_index][2 * STRIP :, cols].astype(jnp.float32)
            top, inverse, delta = statistics(rows)
            scores = mm_nt(picked[side_index][0, :, cols], query) + bias
            weights = jnp.exp2((scores - top) * LOG_SCALE) * inverse
            product = mm_nt(picked[side_index][1, :, cols], dout)
            dscore = (weights * (product - delta)).astype(jnp.bfloat16)
            grad_keys.append(padded((mm(dscore, query) * SCORE_SCALE).astype(jnp.bfloat16)))
            grad_values.append(padded(mm(weights.astype(jnp.bfloat16), dout).astype(jnp.bfloat16)))
        chosen = chosen_ref[...]
        total = centre_ref[0, :, cols] + mm(chosen, jnp.concatenate(grad_keys, axis=0))
        keys_ref[:, cols] = total.astype(jnp.bfloat16)
        total = centre_ref[1, :, cols] + mm(chosen, jnp.concatenate(grad_values, axis=0))
        values_ref[:, cols] = total.astype(jnp.bfloat16)
        return carry

    lax.fori_loop(0, keys_ref.shape[1] // PAIR, step, 0, unroll=True)


def call(kernel, name, out_shape, operands, scratch=(), smem=0, unused=0, gflop=0.1):
    specs = [pl.BlockSpec(memory_space=pltpu.SMEM)] * smem
    specs += [pl.BlockSpec(memory_space=pltpu.VMEM)] * (len(operands) - smem - unused)
    specs += [pl.BlockSpec(memory_space=pl.ANY)] * unused
    single = not isinstance(out_shape, list)
    outs = pl.BlockSpec(memory_space=pltpu.VMEM)
    return pl.pallas_call(
        kernel,
        out_shape=out_shape,
        in_specs=specs,
        out_specs=outs if single else [outs] * len(out_shape),
        scratch_shapes=list(scratch),
        compiler_params=pltpu.CompilerParams(vmem_limit_bytes=VMEM_LIMIT),
        cost_estimate=pl.CostEstimate(flops=int(gflop * 1e9), bytes_accessed=1 << 20, transcendentals=0),
        name=name,
    )(*operands)


def in_hbm(array):
    return pltpu.with_memory_space_constraint(array, pltpu.HBM)


def from_behind(block, axis, distance):
    devices = range(lax.axis_size(axis))
    route = [((i - distance) % len(devices), i) for i in devices]
    return lax.ppermute(block, axis, route)


def exchanged(blocks, stride):
    terms = list(blocks[:1])
    for distance in range(1, len(blocks)):
        route = [(tile, tile ^ (distance * stride)) for tile in range(lax.axis_size("tile"))]
        terms.append(lax.ppermute(blocks[distance], "tile", route))
    return terms


def in_order(sides):
    first, second, third, fourth = sides
    return (first, third, second, fourth)


def to_sides(blocks, offsets):
    arrived = {s: from_behind(blocks[(s + 2) % 4], "tile", -offsets[s]) for s in (0, 2, 1, 3)}
    return [arrived[s] for s in range(4)]


def shards(queries, keys, values, grad_output, out_weight, rotations):
    tile_count = lax.axis_size("tile")
    token_count, features = queries.shape
    model = out_weight.shape[0]
    pairs = features // PAIR
    far = tile_count // NEAR
    chunk = model // tile_count
    heads = lax.axis_size("head")
    offsets = (-(tile_count // 4), 1, tile_count // 4, -1)
    queries, keys, values, out_weight, rotations = (
        in_hbm(a) for a in (queries, keys, values, out_weight, rotations)
    )

    def bf16(*shape):
        return jax.ShapeDtypeStruct(shape, jnp.bfloat16)

    def f32(*shape):
        return jax.ShapeDtypeStruct(shape, jnp.float32)

    strip_types = [bf16(2, STRIP, features)] * 4
    picked = call(pick_kernel, "pick_strips", strip_types, (rotations, keys, values), smem=1)
    grad_output, *picked = lax.optimization_barrier((grad_output, *picked))
    strips = to_sides(picked, offsets)

    cotangents = [from_behind(grad_output, "head", -k) for k in range(1, heads)]
    dout, dout_turned, turned, turned_sent = call(
        functools.partial(cotangent_kernel, heads),
        "cotangent",
        [bf16(CELLS, features), bf16(features, CELLS)] + [bf16(2, far, chunk, CELLS)] * 2,
        (in_hbm(grad_output), *cotangents, out_weight),
        gflop=1.0,
    )
    turned_arrived = exchanged((turned, turned_sent), 1)[1]
    raw, stats, product, queries, keys, values = call(
        centre_kernel,
        "centre",
        [f32(pairs, CELLS, 2 * CELLS), f32(pairs, 2, 2 * CELLS), f32(pairs, CELLS, 2 * CELLS)]
        + [bf16(CELLS, features)] * 3,
        (queries, keys, values, dout),
        scratch=[pltpu.VMEM((CELLS, CELLS), jnp.float32)],
        gflop=3.0,
    )
    weights, attention, rows = call(
        forward_kernel,
        "forward",
        [bf16(pairs, ROWS, 2 * CELLS), bf16(CELLS, features), f32(3, 2 * pairs, CELLS)],
        (*in_order(strips), queries, values, dout_turned, raw, stats),
        scratch=[pltpu.VMEM((2 * STRIP, CELLS), jnp.float32)],
        gflop=4.0,
    )
    attention_arrived = exchanged((attention, attention), 1)[1]
    rims = call(
        rim_kernel,
        "rims",
        [bf16(2 * STRIP + 16, features)] * 4,
        (queries, dout, rows, turned_arrived),
        unused=1,
    )
    rims_arrived = to_sides(rims, offsets)
    kept, sent = call(
        partial_kernel,
        "partial",
        [f32(far, chunk, features), bf16(far, chunk, features)],
        (attention, attention_arrived, turned, turned_arrived, rims[0]),
        unused=1,
    )
    terms = exchanged((kept, sent), 2)

    grad_queries, centre = call(
        backward_kernel,
        "backward",
        [bf16(CELLS, features), f32(2, CELLS, features)],
        (queries, keys, dout, *in_order(strips), weights, product, rows, sent),
        unused=1,
        gflop=3.0,
    )
    stride = NEAR
    while stride < tile_count:
        ways = min(NEAR, tile_count // stride)
        sums = call(
            functools.partial(sum_kernel, len(terms)),
            "plane_sum",
            [bf16(tile_count // stride // ways, chunk, features)] * ways,
            (*terms, centre),
            unused=1,
        )
        terms = exchanged(sums, stride)
        stride *= ways

    grad_keys, grad_values = call(
        side_kernel,
        "sides",
        [bf16(CELLS, features)] * 2,
        (rotations, centre, *picked, *in_order(rims_arrived)),
        scratch=[
            pltpu.VMEM((CELLS, 4 * LANES), jnp.bfloat16),
            pltpu.VMEM((STRIP, LANES), jnp.float32),
        ],
        smem=1,
        gflop=3.0,
    )
    grad_out_weight = call(
        functools.partial(weight_kernel, 1.0 / math.sqrt(token_count * tile_count)),
        "weight_sum",
        f32(chunk, features),
        terms,
    )
    return (grad_queries, grad_keys, grad_values, grad_out_weight)


def solution(mesh):
    placed = (
        P("tile", "head"),
        P("tile", "head"),
        P("tile", "head"),
        P("tile", "head"),
        P(None, "head"),
        P("tile", None),
    )
    return jax.shard_map(
        shards,
        mesh=mesh,
        in_specs=placed,
        out_specs=(P("tile", "head"), P("tile", "head"), P("tile", "head"), P("tile", "head")),
        check_vma=False,
    )
```

```python
import functools
import math

import jax
import jax.numpy as jnp
from jax import lax
from jax.experimental import pallas as pl
from jax.experimental.pallas import tpu as pltpu
from jax.sharding import PartitionSpec as P

HEAD_DIM = 64
RADIUS = 6
SIDE = 16
CELLS = SIDE * SIDE
STRIP = RADIUS * SIDE
ROWS = CELLS + 2 * STRIP
NEAR = 4
LANES = 128
PAIR = 2 * HEAD_DIM
VMEM_LIMIT = 32 * 1024 * 1024
NT = (((1,), (1,)), ((), ()))


def mm(a, b):
    return jnp.dot(a, b, preferred_element_type=jnp.float32)


def mm_nt(a, b):
    return lax.dot_general(a, b, NT, preferred_element_type=jnp.float32)


def strip_token(side_index, rotation, cell):
    turn = lax.rem(side_index + 6 - rotation, 4)
    depth = cell >> 4
    along = cell & (SIDE - 1)
    far = SIDE - 1 - along
    near_rim = RADIUS - 1 - depth
    far_rim = SIDE - RADIUS + depth
    row = jnp.where(turn == 0, far_rim, jnp.where(turn == 1, along, jnp.where(turn == 2, near_rim, far)))
    col = jnp.where(turn == 0, along, jnp.where(turn == 1, near_rim, jnp.where(turn == 2, far, far_rim)))
    return row * SIDE + col


def pick_kernel(rotations_ref, keys_ref, values_ref, north_ref, east_ref, south_ref, west_ref):
    cell = lax.broadcasted_iota(jnp.int32, (STRIP, CELLS), 0)
    token = lax.broadcasted_iota(jnp.int32, (STRIP, CELLS), 1)
    for side_index, out_ref in enumerate((north_ref, east_ref, south_ref, west_ref)):
        wanted = strip_token(side_index, rotations_ref[0, side_index], cell)
        chosen = jnp.where(token == wanted, 1.0, 0.0).astype(jnp.bfloat16)
        out_ref[0] = mm(chosen, keys_ref[...]).astype(jnp.bfloat16)
        out_ref[1] = mm(chosen, values_ref[...]).astype(jnp.bfloat16)


def weight_kernel(scale, *refs):
    total = refs[0][0].astype(jnp.float32)
    for ref in refs[1:-1]:
        total += ref[0].astype(jnp.float32)
    refs[-1][...] = total * scale


def partial_kernel(attention_ref, arrived_ref, turned_ref, turned_arrived_ref, unused_ref, kept_ref, sent_ref):
    for index, out_ref in enumerate((kept_ref, sent_ref)):
        total = None
        for turned_part, attention_part in ((turned_ref, attention_ref), (turned_arrived_ref, arrived_ref)):
            turned = turned_part[index]
            turned = turned.reshape(turned.shape[0] * turned.shape[1], turned.shape[2])
            term = mm(turned, attention_part[...])
            total = term if total is None else total + term
        out_ref[...] = total.astype(out_ref.dtype).reshape(out_ref.shape)


def sum_kernel(count, *refs):
    terms, outs = refs[:count], refs[count + 1 :]
    for q in range(terms[0].shape[0]):
        total = terms[0][q].astype(jnp.float32)
        for ref in terms[1:]:
            total += ref[q].astype(jnp.float32)
        outs[q % len(outs)][q // len(outs)] = total.astype(jnp.bfloat16)


def rim_token(side_index, place):
    depth = place >> 4
    along = place & (SIDE - 1)
    last = SIDE - 1
    row, col = ((depth, along), (along, last - depth), (last - depth, last - along), (last - along, depth))[side_index]
    return row * SIDE + col


def cotangent_kernel(heads, *refs):
    blocks, out_weight_ref, outs = refs[:heads], refs[heads], refs[heads + 1 :]
    dout_ref, dout_turned_ref, turned_ref, turned_sent_ref = outs
    head = lax.axis_index("head")
    tile = lax.axis_index("tile")
    chunk = turned_ref.shape[2]
    width = blocks[0].shape[1]
    total = None
    for distance, block_ref in enumerate(blocks):
        owner = lax.rem(head + distance, heads)
        start = pl.multiple_of(owner * width, width)
        block = block_ref[...]
        term = mm(block, out_weight_ref[pl.ds(start, width), :])
        total = term if total is None else total + term
        turned = block.T
        first = owner * (width // chunk)
        for index in range(width // chunk):
            target = (first + index) ^ tile
            rows = turned[index * chunk : (index + 1) * chunk]
            for parity, out_ref in enumerate((turned_ref, turned_sent_ref)):

                @pl.when(target & 1 == parity)
                def _():
                    out_ref[(target & 3) >> 1, target >> 2] = rows

    dout = total.astype(jnp.bfloat16)
    dout_ref[...] = dout
    dout_turned_ref[...] = dout.T


def split(exact, count):
    parts = []
    for _ in range(count):
        part = exact.astype(jnp.bfloat16).astype(jnp.float32)
        parts.append(part)
        exact = exact - part
    return parts


PARTS = (3, 2, 2)


def rim_kernel(query_ref, dout_ref, rows_ref, unused_ref, *rim_refs):
    place = lax.broadcasted_iota(jnp.int32, (LANES, CELLS), 0)
    token = lax.broadcasted_iota(jnp.int32, (LANES, CELLS), 1)
    parts = [part for kind, count in enumerate(PARTS) for part in split(rows_ref[kind], count)]
    pairs = rows_ref.shape[1] // 2
    filler = jnp.zeros((16 - 2 * len(parts), CELLS), jnp.float32)
    rows = [
        jnp.concatenate([part[2 * pair : 2 * pair + 2] for part in parts] + [filler], axis=0) for pair in range(pairs)
    ]
    rows = jnp.concatenate(rows, axis=0).astype(jnp.bfloat16)
    for side_index, rim_ref in enumerate(rim_refs):
        chosen = jnp.where((token == rim_token(side_index, place)) & (place < STRIP), 1.0, 0.0).astype(jnp.bfloat16)
        rim_ref[:STRIP] = mm(chosen[:STRIP], query_ref[...]).astype(jnp.bfloat16)
        rim_ref[STRIP : 2 * STRIP] = mm(chosen[:STRIP], dout_ref[...]).astype(jnp.bfloat16)
        spread = mm_nt(rows, chosen).astype(jnp.bfloat16)
        for pair in range(pairs):
            rim_ref[2 * STRIP :, pair * PAIR : (pair + 1) * PAIR] = spread[16 * pair : 16 * pair + 16]


def window(cell_row, cell_col, query):
    query_row = (query >> 4) + RADIUS
    query_col = (query & (SIDE - 1)) + RADIUS
    near = (jnp.abs(cell_row - query_row) <= RADIUS) & (jnp.abs(cell_col - query_col) <= RADIUS)
    return jnp.where(near, 0.0, -1e30)


def centre_bias(bias_ref):
    query = lax.broadcasted_iota(jnp.int32, (CELLS, CELLS), 1)
    cell = lax.broadcasted_iota(jnp.int32, (CELLS, CELLS), 0)
    bias_ref[...] = window((cell >> 4) + RADIUS, (cell & (SIDE - 1)) + RADIUS, query)


def strip_bias(bias_ref):
    query = lax.broadcasted_iota(jnp.int32, (STRIP, CELLS), 1)
    cell = lax.broadcasted_iota(jnp.int32, (STRIP, CELLS), 0)
    depth = cell >> 4
    along = cell & (SIDE - 1)
    last = SIDE + 2 * RADIUS - 1
    north = (depth, RADIUS + along)
    east = (RADIUS + along, last - depth)
    south = (last - depth, last - RADIUS - along)
    west = (last - RADIUS - along, depth)
    for start, kind, first, second in ((0, 0, north, south), (STRIP, 1, west, east)):
        in_first = first_half(query, kind)
        row = jnp.where(in_first, first[0], second[0])
        col = jnp.where(in_first, first[1], second[1])
        bias_ref[start : start + STRIP, :] = window(row, col, query)


def first_half(query, kind):
    return (query & (SIDE - 1)) < SIDE // 2 if kind else query < CELLS // 2


def one_head(block, head):
    lane = lax.broadcasted_iota(jnp.int32, block.shape, 1)
    kept = (lane >= HEAD_DIM) if head else (lane < HEAD_DIM)
    return jnp.where(kept, block, jnp.zeros_like(block))


def by_half(stacked, kind):
    rows = stacked.shape[0] // 2
    kept = first_half(lax.broadcasted_iota(jnp.int32, (rows, CELLS), 1), kind)
    return jnp.where(kept, stacked[:rows], stacked[rows:])


def side_refs(strips, kind):
    north, east, south, west = strips
    return (west, east) if kind else (north, south)


def side_cells(strips, part, cols):
    return jnp.concatenate([ref[part, :, cols] for kind in range(2) for ref in side_refs(strips, kind)], axis=0)


def side_products(cells, rows_head):
    products = mm_nt(cells, rows_head)
    return [by_half(products[2 * kind * STRIP : 2 * (kind + 1) * STRIP], kind) for kind in range(2)]


def turned_sides(strips, part, kind, cols):
    return [ref[part, :, cols].T for ref in side_refs(strips, kind)]


def pair_cols(pair):
    return pl.ds(pl.multiple_of(pair * PAIR, PAIR), PAIR)


def head_rows(turned, head):
    return turned[head * HEAD_DIM : (head + 1) * HEAD_DIM]


def over_cells(turned_centre, turned_strips, head, centre, sides):
    total = mm(head_rows(turned_centre, head), centre)
    for kind in range(2):
        stacked = jnp.concatenate([head_rows(t, head) for t in turned_strips[kind]], axis=0)
        total += by_half(mm(stacked, sides[kind]), kind)
    return total


SCORE_SCALE = HEAD_DIM ** (-0.5)
LOG_SCALE = SCORE_SCALE * math.log2(math.e)


def lanes_of(head):
    return slice(head * CELLS, (head + 1) * CELLS)


def centre_kernel(
    query_ref, key_ref, value_ref, dout_ref,
    raw_ref, stats_ref, product_ref, query_out, key_out, value_out, bias_ref,
):
    centre_bias(bias_ref)

    def step(pair, carry):
        cols = pair_cols(pair)
        query, key, value, dout = (ref[:, cols] for ref in (query_ref, key_ref, value_ref, dout_ref))
        for head in range(2):
            scores = mm_nt(key, one_head(query, head)) + bias_ref[...]
            top = jnp.max(scores, axis=0, keepdims=True)
            raw = jnp.exp2((scores - top) * LOG_SCALE)
            raw_ref[pair, :, lanes_of(head)] = raw
            stats_ref[pair, 0:1, lanes_of(head)] = top
            stats_ref[pair, 1:2, lanes_of(head)] = jnp.sum(raw, axis=0, keepdims=True)
            product_ref[pair, :, lanes_of(head)] = mm_nt(value, one_head(dout, head))
        query_out[:, cols] = query
        key_out[:, cols] = key
        value_out[:, cols] = value
        return carry

    lax.fori_loop(0, raw_ref.shape[0], step, 0)


def forward_kernel(
    north_ref, south_ref, east_ref, west_ref, query_ref, value_ref, dout_turned_ref, raw_ref, stats_ref,
    weights_ref, attention_ref, rows_ref, bias_ref,
):
    strips = (north_ref, east_ref, south_ref, west_ref)
    strip_bias(bias_ref)

    def step(pair, carry):
        cols = pair_cols(pair)
        query = query_ref[:, cols]
        turned_centre = value_ref[:, cols].T
        turned_strips = [turned_sides(strips, 1, kind, cols) for kind in range(2)]
        sides = side_cells(strips, 0, cols)
        parts = []
        for head in range(2):
            query_head = one_head(query, head)
            scores = [
                product + bias_ref[kind * STRIP : (kind + 1) * STRIP]
                for kind, product in enumerate(side_products(sides, query_head))
            ]
            centre_top = stats_ref[pair, 0:1, lanes_of(head)]
            top = jnp.maximum(jnp.max(jnp.maximum(scores[0], scores[1]), axis=0, keepdims=True), centre_top)
            raw = [jnp.exp2((s - top) * LOG_SCALE) for s in scores]
            lifted = jnp.exp2((centre_top - top) * LOG_SCALE)
            total = jnp.sum(raw[0] + raw[1], axis=0, keepdims=True)
            total += lifted * stats_ref[pair, 1:2, lanes_of(head)]
            inverse = 1.0 / total
            centre = (raw_ref[pair, :, lanes_of(head)] * (lifted * inverse)).astype(jnp.bfloat16)
            outer = [(r * inverse).astype(jnp.bfloat16) for r in raw]
            weights_ref[pair, :CELLS, lanes_of(head)] = centre
            for kind in range(2):
                start = CELLS + kind * STRIP
                weights_ref[pair, start : start + STRIP, lanes_of(head)] = outer[kind]
            part = over_cells(turned_centre, turned_strips, head, centre, outer)
            parts.append(part)
            place = pl.ds(2 * pair + head, 1)
            features = pl.ds(pl.multiple_of((2 * pair + head) * HEAD_DIM, HEAD_DIM), HEAD_DIM)
            product = dout_turned_ref[features, :].astype(jnp.float32) * part
            rows_ref[0, place, :] = top
            rows_ref[1, place, :] = inverse
            rows_ref[2, place, :] = jnp.sum(product, axis=0, keepdims=True)
        attention_ref[:, cols] = jnp.concatenate(parts, axis=0).T.astype(jnp.bfloat16)
        return carry

    lax.fori_loop(0, raw_ref.shape[0], step, 0)


def backward_kernel(
    query_ref, key_ref, dout_ref, north_ref, south_ref, east_ref, west_ref, weights_ref, product_ref, rows_ref,
    unused_ref, grad_query_ref, centre_ref,
):
    strips = (north_ref, east_ref, south_ref, west_ref)

    def step(pair, carry):
        cols = pair_cols(pair)
        query = query_ref[:, cols]
        dout = dout_ref[:, cols]
        turned_centre = key_ref[:, cols].T
        turned_strips = [turned_sides(strips, 0, kind, cols) for kind in range(2)]
        sides = side_cells(strips, 1, cols)
        bounds = (0, CELLS, CELLS + STRIP, CELLS + 2 * STRIP)
        parts = []
        centre_scores = []
        for head in range(2):
            lanes = lanes_of(head)
            dout_head = one_head(dout, head)
            delta = rows_ref[2, pl.ds(2 * pair + head, 1), :]
            products = [product_ref[pair, :, lanes]] + side_products(sides, dout_head)
            dscore = [
                (weights_ref[pair, start:end, lanes].astype(jnp.float32) * (g - delta)).astype(jnp.bfloat16)
                for start, end, g in zip(bounds, bounds[1:], products)
            ]
            centre_scores.append(dscore[0])
            parts.append(over_cells(turned_centre, turned_strips, head, dscore[0], dscore[1:]))
        grad_query = jnp.concatenate(parts, axis=0).T * SCORE_SCALE
        grad_query_ref[:, cols] = grad_query.astype(jnp.bfloat16)
        grad_key, grad_value = joint_mm(
            jnp.concatenate(centre_scores, axis=1), weights_ref[pair, :CELLS, :], both_heads(query), both_heads(dout)
        )
        centre_ref[0, :, cols] = grad_key * SCORE_SCALE
        centre_ref[1, :, cols] = grad_value
        return carry

    lax.fori_loop(0, weights_ref.shape[0], step, 0)


def joint_mm(first, second, first_rows, second_rows):
    rows = first.shape[0]
    product = mm(jnp.concatenate([first, second], axis=0), jnp.concatenate([first_rows, second_rows], axis=1))
    return product[:rows, :PAIR], product[rows:, PAIR:]


def both_heads(block):
    return jnp.concatenate([one_head(block, head) for head in range(2)], axis=0)


def padded(block):
    return jnp.concatenate([block, jnp.zeros((LANES - block.shape[0], block.shape[1]), block.dtype)], axis=0)


def statistics(rows):
    first = 0
    for count in PARTS:
        heads = []
        for head in range(2):
            parts = [rows[2 * index + head : 2 * index + head + 1] for index in range(first, first + count)]
            heads.append(functools.reduce(jnp.add, parts))
        first += count
        yield jnp.concatenate(heads, axis=1)


def side_kernel(side_indices, rotations_ref, centre_ref, *refs):
    picked, rims = refs[:2], refs[2:4]
    keys_ref, values_ref, chosen_ref, bias_ref = refs[4:]
    cell = lax.broadcasted_iota(jnp.int32, (STRIP, LANES), 0)
    query = lax.broadcasted_iota(jnp.int32, (STRIP, LANES), 1)
    near = jnp.abs((cell & (SIDE - 1)) - (query & (SIDE - 1))) <= RADIUS
    near = near & ((cell >> 4) >= (query >> 4)) & (query < STRIP)
    bias_ref[...] = jnp.where(near, 0.0, -1e30)
    token = lax.broadcasted_iota(jnp.int32, (CELLS, LANES), 0)
    place = lax.broadcasted_iota(jnp.int32, (CELLS, LANES), 1)
    for index, side_index in enumerate(side_indices):
        wanted = jnp.where(place < STRIP, strip_token(side_index, rotations_ref[0, side_index], place), -1)
        chosen = jnp.where(token == wanted, 1.0, 0.0).astype(jnp.bfloat16)
        chosen_ref[:, index * LANES : (index + 1) * LANES] = chosen

    def step(pair, carry):
        cols = pair_cols(pair)
        grads = []
        bias = jnp.concatenate([bias_ref[...]] * 2, axis=1)
        for picked_ref, rim_ref in zip(picked, rims):
            query = both_heads(padded(rim_ref[:STRIP, cols]))
            dout = both_heads(padded(rim_ref[STRIP : 2 * STRIP, cols]))
            top, inverse, delta = statistics(rim_ref[2 * STRIP :, cols].astype(jnp.float32))
            scores = mm_nt(picked_ref[0, :, cols], query) + bias
            weights = jnp.exp2((scores - top) * LOG_SCALE) * inverse
            product = mm_nt(picked_ref[1, :, cols], dout)
            dscore = (weights * (product - delta)).astype(jnp.bfloat16)
            grad_key, grad_value = joint_mm(dscore, weights.astype(jnp.bfloat16), query, dout)
            grad = jnp.concatenate([grad_key * SCORE_SCALE, grad_value], axis=1)
            grads.append(padded(grad.astype(jnp.bfloat16)))
        total = mm(chosen_ref[...], jnp.concatenate(grads, axis=0))
        keys_ref[:, cols] = (centre_ref[0, :, cols] + total[:, :PAIR]).astype(keys_ref.dtype)
        values_ref[:, cols] = (centre_ref[1, :, cols] + total[:, PAIR:]).astype(values_ref.dtype)
        return carry

    lax.fori_loop(0, keys_ref.shape[-1] // PAIR, step, 0, unroll=2)


def side_pair_kernel(rotations_ref, centre_ref, *refs):
    total_ref = refs[4]
    side_kernel((0, 2), rotations_ref, centre_ref, *refs[:4], total_ref.at[0], total_ref.at[1], *refs[5:])


def call(kernel, name, out_shape, operands, scratch=(), smem=0, unused=0, gflop=0.1):
    specs = [pl.BlockSpec(memory_space=pltpu.SMEM)] * smem
    specs += [pl.BlockSpec(memory_space=pltpu.VMEM)] * (len(operands) - smem - unused)
    specs += [pl.BlockSpec(memory_space=pl.ANY)] * unused
    single = not isinstance(out_shape, list)
    outs = pl.BlockSpec(memory_space=pltpu.VMEM)
    return pl.pallas_call(
        kernel,
        out_shape=out_shape,
        in_specs=specs,
        out_specs=outs if single else [outs] * len(out_shape),
        scratch_shapes=list(scratch),
        compiler_params=pltpu.CompilerParams(vmem_limit_bytes=VMEM_LIMIT),
        cost_estimate=pl.CostEstimate(flops=int(gflop * 1e9), bytes_accessed=1 << 20, transcendentals=0),
        name=name,
    )(*operands)


def in_hbm(array):
    return pltpu.with_memory_space_constraint(array, pltpu.HBM)


def from_behind(block, axis, distance):
    devices = range(lax.axis_size(axis))
    route = [((i - distance) % len(devices), i) for i in devices]
    return lax.ppermute(block, axis, route)


def exchanged(blocks, stride):
    terms = list(blocks[:1])
    for distance in range(1, len(blocks)):
        route = [(tile, tile ^ (distance * stride)) for tile in range(lax.axis_size("tile"))]
        terms.append(lax.ppermute(blocks[distance], "tile", route))
    return terms


def in_order(sides):
    first, second, third, fourth = sides
    return (first, third, second, fourth)


def to_sides(blocks, offsets, sides):
    return {s: from_behind(blocks[(s + 2) % 4], "tile", -offsets[s]) for s in sides}


def shards(queries, keys, values, grad_output, out_weight, rotations):
    tile_count = lax.axis_size("tile")
    token_count, features = queries.shape
    model = out_weight.shape[0]
    pairs = features // PAIR
    far = tile_count // NEAR
    chunk = model // tile_count
    heads = lax.axis_size("head")
    offsets = (-(tile_count // 4), 1, tile_count // 4, -1)
    queries, keys, values, out_weight, rotations = (
        in_hbm(a) for a in (queries, keys, values, out_weight, rotations)
    )

    def bf16(*shape):
        return jax.ShapeDtypeStruct(shape, jnp.bfloat16)

    def f32(*shape):
        return jax.ShapeDtypeStruct(shape, jnp.float32)

    strip_types = [bf16(2, STRIP, features)] * 4
    picked = call(pick_kernel, "pick_strips", strip_types, (rotations, keys, values), smem=1)
    grad_output, *picked = lax.optimization_barrier((grad_output, *picked))
    strips = to_sides(picked, offsets, (0, 2, 1, 3))
    strips = [strips[s] for s in range(4)]

    cotangents = [from_behind(grad_output, "head", -k) for k in range(1, heads)]
    dout, dout_turned, turned, turned_sent = call(
        functools.partial(cotangent_kernel, heads),
        "cotangent",
        [bf16(CELLS, features), bf16(features, CELLS)] + [bf16(2, far, chunk, CELLS)] * 2,
        (in_hbm(grad_output), *cotangents, out_weight),
        gflop=1.0,
    )
    raw, stats, product, queries, keys, values = call(
        centre_kernel,
        "centre",
        [f32(pairs, CELLS, 2 * CELLS), f32(pairs, 2, 2 * CELLS), f32(pairs, CELLS, 2 * CELLS)]
        + [bf16(CELLS, features)] * 3,
        (queries, keys, values, dout),
        scratch=[pltpu.VMEM((CELLS, CELLS), jnp.float32)],
        gflop=3.0,
    )
    *strips, stats, turned_sent = lax.optimization_barrier((*in_order(strips), stats, turned_sent))
    strips = in_order(strips)
    turned_arrived = exchanged((turned, turned_sent), 1)[1]
    weights, attention, rows = call(
        forward_kernel,
        "forward",
        [bf16(pairs, ROWS, 2 * CELLS), bf16(CELLS, features), f32(3, 2 * pairs, CELLS)],
        (*in_order(strips), queries, values, dout_turned, raw, stats),
        scratch=[pltpu.VMEM((2 * STRIP, CELLS), jnp.float32)],
        gflop=4.0,
    )
    attention_arrived = exchanged((attention, attention), 1)[1]
    rims = call(
        rim_kernel,
        "rims",
        [bf16(2 * STRIP + 16, features)] * 4,
        (queries, dout, rows, turned_arrived),
        unused=1,
    )
    rims_arrived = to_sides(rims, offsets, (0, 2))
    kept, sent = call(
        partial_kernel,
        "partial",
        [f32(far, chunk, features), bf16(far, chunk, features)],
        (attention, attention_arrived, turned, turned_arrived, rims[0]),
        unused=1,
    )
    terms = exchanged((kept, sent), 2)
    late_rims = lax.optimization_barrier((*rims, sent))[:4]
    rims_arrived |= to_sides(late_rims, offsets, (1, 3))

    grad_queries, centre = call(
        backward_kernel,
        "backward",
        [bf16(CELLS, features), f32(2, CELLS, features)],
        (queries, keys, dout, *in_order(strips), weights, product, rows, sent),
        unused=1,
        gflop=3.0,
    )
    side_scratch = [pltpu.VMEM((CELLS, 2 * LANES), jnp.bfloat16), pltpu.VMEM((STRIP, LANES), jnp.float32)]
    centre = call(
        side_pair_kernel,
        "sides_north_south",
        f32(2, CELLS, features),
        (rotations, centre, picked[0], picked[2], rims_arrived[0], rims_arrived[2]),
        scratch=side_scratch,
        smem=1,
        gflop=3.0,
    )
    stride = NEAR
    while stride < tile_count:
        ways = min(NEAR, tile_count // stride)
        sums = call(
            functools.partial(sum_kernel, len(terms)),
            "plane_sum",
            [bf16(tile_count // stride // ways, chunk, features)] * ways,
            (*terms, centre),
            unused=1,
        )
        terms = exchanged(sums, stride)
        stride *= ways

    grad_keys, grad_values = call(
        functools.partial(side_kernel, (1, 3)),
        "sides_east_west",
        [bf16(CELLS, features)] * 2,
        (rotations, centre, picked[1], picked[3], rims_arrived[1], rims_arrived[3]),
        scratch=side_scratch,
        smem=1,
        gflop=3.0,
    )
    grad_out_weight = call(
        functools.partial(weight_kernel, 1.0 / math.sqrt(token_count * tile_count)),
        "weight_sum",
        f32(chunk, features),
        terms,
    )
    return (grad_queries, grad_keys, grad_values, grad_out_weight)


def solution(mesh):
    placed = (
        P("tile", "head"),
        P("tile", "head"),
        P("tile", "head"),
        P("tile", "head"),
        P(None, "head"),
        P("tile", None),
    )
    return jax.shard_map(
        shards,
        mesh=mesh,
        in_specs=placed,
        out_specs=(P("tile", "head"), P("tile", "head"), P("tile", "head"), P("tile", "head")),
        check_vma=False,
    )
```

```python
import functools
import math

import jax
import jax.numpy as jnp
from jax import lax
from jax.experimental import pallas as pl
from jax.experimental.pallas import tpu as pltpu
from jax.sharding import PartitionSpec as P

HEAD_DIM = 64
RADIUS = 6
SIDE = 16
CELLS = SIDE * SIDE
STRIP = RADIUS * SIDE
ROWS = CELLS + 2 * STRIP
NEAR = 4
LANES = 128
PAIR = 2 * HEAD_DIM
VMEM_LIMIT = 32 * 1024 * 1024
NT = (((1,), (1,)), ((), ()))


def mm(a, b):
    return jnp.dot(a, b, preferred_element_type=jnp.float32)


def mm_nt(a, b):
    return lax.dot_general(a, b, NT, preferred_element_type=jnp.float32)


def strip_token(side_index, rotation, cell):
    turn = lax.rem(side_index + 6 - rotation, 4)
    depth = cell >> 4
    along = cell & (SIDE - 1)
    far = SIDE - 1 - along
    near_rim = RADIUS - 1 - depth
    far_rim = SIDE - RADIUS + depth
    row = jnp.where(turn == 0, far_rim, jnp.where(turn == 1, along, jnp.where(turn == 2, near_rim, far)))
    col = jnp.where(turn == 0, along, jnp.where(turn == 1, near_rim, jnp.where(turn == 2, far, far_rim)))
    return row * SIDE + col


def pick_kernel(rotations_ref, keys_ref, values_ref, north_ref, east_ref, south_ref, west_ref):
    cell = lax.broadcasted_iota(jnp.int32, (STRIP, CELLS), 0)
    token = lax.broadcasted_iota(jnp.int32, (STRIP, CELLS), 1)
    for side_index, out_ref in enumerate((north_ref, east_ref, south_ref, west_ref)):
        wanted = strip_token(side_index, rotations_ref[0, side_index], cell)
        chosen = jnp.where(token == wanted, 1.0, 0.0).astype(jnp.bfloat16)
        out_ref[0] = mm(chosen, keys_ref[...]).astype(jnp.bfloat16)
        out_ref[1] = mm(chosen, values_ref[...]).astype(jnp.bfloat16)


def weight_kernel(scale, *refs):
    total = refs[0][0].astype(jnp.float32)
    for ref in refs[1:-1]:
        total += ref[0].astype(jnp.float32)
    refs[-1][...] = total * scale


def partial_kernel(attention_ref, arrived_ref, turned_ref, turned_arrived_ref, unused_ref, kept_ref, sent_ref):
    for index, out_ref in enumerate((kept_ref, sent_ref)):
        total = None
        for turned_part, attention_part in ((turned_ref, attention_ref), (turned_arrived_ref, arrived_ref)):
            turned = turned_part[index]
            turned = turned.reshape(turned.shape[0] * turned.shape[1], turned.shape[2])
            term = mm(turned, attention_part[...])
            total = term if total is None else total + term
        out_ref[...] = total.astype(out_ref.dtype).reshape(out_ref.shape)


def sum_kernel(count, *refs):
    terms, outs = refs[:count], refs[count + 1 :]
    for q in range(terms[0].shape[0]):
        total = terms[0][q].astype(jnp.float32)
        for ref in terms[1:]:
            total += ref[q].astype(jnp.float32)
        outs[q % len(outs)][q // len(outs)] = total.astype(jnp.bfloat16)


def rim_token(side_index, place):
    depth = place >> 4
    along = place & (SIDE - 1)
    last = SIDE - 1
    row, col = ((depth, along), (along, last - depth), (last - depth, last - along), (last - along, depth))[side_index]
    return row * SIDE + col


def cotangent_kernel(heads, *refs):
    blocks, out_weight_ref, outs = refs[:heads], refs[heads], refs[heads + 1 :]
    dout_ref, dout_turned_ref, turned_ref, turned_sent_ref = outs
    head = lax.axis_index("head")
    tile = lax.axis_index("tile")
    chunk = turned_ref.shape[2]
    width = blocks[0].shape[1]
    total = None
    for distance, block_ref in enumerate(blocks):
        owner = lax.rem(head + distance, heads)
        start = pl.multiple_of(owner * width, width)
        block = block_ref[...]
        term = mm(block, out_weight_ref[pl.ds(start, width), :])
        total = term if total is None else total + term
        turned = block.T
        first = owner * (width // chunk)
        for index in range(width // chunk):
            target = (first + index) ^ tile
            rows = turned[index * chunk : (index + 1) * chunk]
            for parity, out_ref in enumerate((turned_ref, turned_sent_ref)):

                @pl.when(target & 1 == parity)
                def _():
                    out_ref[(target & 3) >> 1, target >> 2] = rows

    dout = total.astype(jnp.bfloat16)
    dout_ref[...] = dout
    dout_turned_ref[...] = dout.T


def split(exact, count):
    parts = []
    for _ in range(count):
        part = exact.astype(jnp.bfloat16).astype(jnp.float32)
        parts.append(part)
        exact = exact - part
    return parts


PARTS = (3, 2, 2)


def rim_kernel(query_ref, dout_ref, rows_ref, unused_ref, *rim_refs):
    place = lax.broadcasted_iota(jnp.int32, (LANES, CELLS), 0)
    token = lax.broadcasted_iota(jnp.int32, (LANES, CELLS), 1)
    parts = [part for kind, count in enumerate(PARTS) for part in split(rows_ref[kind], count)]
    pairs = rows_ref.shape[1] // 2
    filler = jnp.zeros((16 - 2 * len(parts), CELLS), jnp.float32)
    rows = [
        jnp.concatenate([part[2 * pair : 2 * pair + 2] for part in parts] + [filler], axis=0) for pair in range(pairs)
    ]
    rows = jnp.concatenate(rows, axis=0).astype(jnp.bfloat16)
    for side_index, rim_ref in enumerate(rim_refs):
        chosen = jnp.where((token == rim_token(side_index, place)) & (place < STRIP), 1.0, 0.0).astype(jnp.bfloat16)
        rim_ref[:STRIP] = mm(chosen[:STRIP], query_ref[...]).astype(jnp.bfloat16)
        rim_ref[STRIP : 2 * STRIP] = mm(chosen[:STRIP], dout_ref[...]).astype(jnp.bfloat16)
        spread = mm_nt(rows, chosen).astype(jnp.bfloat16)
        for pair in range(pairs):
            rim_ref[2 * STRIP :, pair * PAIR : (pair + 1) * PAIR] = spread[16 * pair : 16 * pair + 16]


def window(cell_row, cell_col, query):
    query_row = (query >> 4) + RADIUS
    query_col = (query & (SIDE - 1)) + RADIUS
    near = (jnp.abs(cell_row - query_row) <= RADIUS) & (jnp.abs(cell_col - query_col) <= RADIUS)
    return jnp.where(near, 0.0, -1e30)


def centre_bias(bias_ref):
    query = lax.broadcasted_iota(jnp.int32, (CELLS, CELLS), 1)
    cell = lax.broadcasted_iota(jnp.int32, (CELLS, CELLS), 0)
    bias_ref[...] = window((cell >> 4) + RADIUS, (cell & (SIDE - 1)) + RADIUS, query)


def strip_bias(bias_ref):
    query = lax.broadcasted_iota(jnp.int32, (STRIP, CELLS), 1)
    cell = lax.broadcasted_iota(jnp.int32, (STRIP, CELLS), 0)
    depth = cell >> 4
    along = cell & (SIDE - 1)
    last = SIDE + 2 * RADIUS - 1
    north = (depth, RADIUS + along)
    east = (RADIUS + along, last - depth)
    south = (last - depth, last - RADIUS - along)
    west = (last - RADIUS - along, depth)
    for start, kind, first, second in ((0, 0, north, south), (STRIP, 1, west, east)):
        in_first = first_half(query, kind)
        row = jnp.where(in_first, first[0], second[0])
        col = jnp.where(in_first, first[1], second[1])
        bias_ref[start : start + STRIP, :] = window(row, col, query)


def first_half(query, kind):
    return (query & (SIDE - 1)) < SIDE // 2 if kind else query < CELLS // 2


def one_head(block, head):
    lane = lax.broadcasted_iota(jnp.int32, block.shape, 1)
    kept = (lane >= HEAD_DIM) if head else (lane < HEAD_DIM)
    return jnp.where(kept, block, jnp.zeros_like(block))


def halves(block, kind):
    kept = first_half(lax.broadcasted_iota(jnp.int32, block.shape, 0), kind)
    zero = jnp.zeros_like(block)
    return jnp.concatenate([jnp.where(kept, block, zero), jnp.where(kept, zero, block)], axis=1)


def by_half(stacked, kind):
    rows = stacked.shape[0] // 2
    kept = first_half(lax.broadcasted_iota(jnp.int32, (rows, CELLS), 1), kind)
    return jnp.where(kept, stacked[:rows], stacked[rows:])


def side_refs(strips, kind):
    north, east, south, west = strips
    return (west, east) if kind else (north, south)


def side_cells(strips, part, kind, cols):
    return jnp.concatenate([ref[part, :, cols] for ref in side_refs(strips, kind)], axis=1)


def side_products(cells, rows_head):
    return [mm_nt(cells[kind], halves(rows_head, kind)) for kind in range(2)]


def turned_sides(strips, part, kind, cols):
    return [ref[part, :, cols].T for ref in side_refs(strips, kind)]


def pair_cols(pair):
    return pl.ds(pl.multiple_of(pair * PAIR, PAIR), PAIR)


def head_rows(turned, head):
    return turned[head * HEAD_DIM : (head + 1) * HEAD_DIM]


def over_cells(turned_centre, turned_strips, head, centre, sides):
    total = mm(head_rows(turned_centre, head), centre)
    for kind in range(2):
        stacked = jnp.concatenate([head_rows(t, head) for t in turned_strips[kind]], axis=0)
        total += by_half(mm(stacked, sides[kind]), kind)
    return total


SCORE_SCALE = HEAD_DIM ** (-0.5)
LOG_SCALE = SCORE_SCALE * math.log2(math.e)


def lanes_of(head):
    return slice(head * CELLS, (head + 1) * CELLS)


def centre_kernel(
    query_ref, key_ref, value_ref, dout_ref,
    raw_ref, stats_ref, product_ref, query_out, key_out, value_out, bias_ref,
):
    centre_bias(bias_ref)

    def step(pair, carry):
        cols = pair_cols(pair)
        query, key, value, dout = (ref[:, cols] for ref in (query_ref, key_ref, value_ref, dout_ref))
        for head in range(2):
            scores = mm_nt(key, one_head(query, head)) + bias_ref[...]
            top = jnp.max(scores, axis=0, keepdims=True)
            raw = jnp.exp2((scores - top) * LOG_SCALE)
            raw_ref[pair, :, lanes_of(head)] = raw
            stats_ref[pair, 0:1, lanes_of(head)] = top
            stats_ref[pair, 1:2, lanes_of(head)] = jnp.sum(raw, axis=0, keepdims=True)
            product_ref[pair, :, lanes_of(head)] = mm_nt(value, one_head(dout, head))
        query_out[:, cols] = query
        key_out[:, cols] = key
        value_out[:, cols] = value
        return carry

    lax.fori_loop(0, raw_ref.shape[0], step, 0)


def forward_kernel(
    east_ref, west_ref, north_ref, south_ref, query_ref, value_ref, dout_turned_ref, raw_ref, stats_ref,
    weights_ref, attention_ref, rows_ref, bias_ref,
):
    strips = (north_ref, east_ref, south_ref, west_ref)
    strip_bias(bias_ref)

    def step(pair, carry):
        cols = pair_cols(pair)
        query = query_ref[:, cols]
        turned_centre = value_ref[:, cols].T
        turned_strips = [turned_sides(strips, 1, kind, cols) for kind in range(2)]
        sides = [side_cells(strips, 0, kind, cols) for kind in range(2)]
        parts = []
        for head in range(2):
            query_head = one_head(query, head)
            scores = [
                product + bias_ref[kind * STRIP : (kind + 1) * STRIP]
                for kind, product in enumerate(side_products(sides, query_head))
            ]
            centre_top = stats_ref[pair, 0:1, lanes_of(head)]
            top = jnp.maximum(jnp.max(jnp.maximum(scores[0], scores[1]), axis=0, keepdims=True), centre_top)
            raw = [jnp.exp2((s - top) * LOG_SCALE) for s in scores]
            lifted = jnp.exp2((centre_top - top) * LOG_SCALE)
            total = jnp.sum(raw[0] + raw[1], axis=0, keepdims=True)
            total += lifted * stats_ref[pair, 1:2, lanes_of(head)]
            inverse = 1.0 / total
            centre = (raw_ref[pair, :, lanes_of(head)] * (lifted * inverse)).astype(jnp.bfloat16)
            outer = [(r * inverse).astype(jnp.bfloat16) for r in raw]
            weights_ref[pair, :CELLS, lanes_of(head)] = centre
            for kind in range(2):
                start = CELLS + kind * STRIP
                weights_ref[pair, start : start + STRIP, lanes_of(head)] = outer[kind]
            part = over_cells(turned_centre, turned_strips, head, centre, outer)
            parts.append(part)
            place = pl.ds(2 * pair + head, 1)
            features = pl.ds(pl.multiple_of((2 * pair + head) * HEAD_DIM, HEAD_DIM), HEAD_DIM)
            product = dout_turned_ref[features, :].astype(jnp.float32) * part
            rows_ref[0, place, :] = top
            rows_ref[1, place, :] = inverse
            rows_ref[2, place, :] = jnp.sum(product, axis=0, keepdims=True)
        attention_ref[:, cols] = jnp.concatenate(parts, axis=0).T.astype(jnp.bfloat16)
        return carry

    lax.fori_loop(0, raw_ref.shape[0], step, 0)


def backward_kernel(
    query_ref, key_ref, dout_ref, east_ref, west_ref, north_ref, south_ref, weights_ref, product_ref, rows_ref,
    unused_ref, grad_query_ref, centre_ref,
):
    strips = (north_ref, east_ref, south_ref, west_ref)

    def step(pair, carry):
        cols = pair_cols(pair)
        query = query_ref[:, cols]
        dout = dout_ref[:, cols]
        turned_centre = key_ref[:, cols].T
        turned_strips = [turned_sides(strips, 0, kind, cols) for kind in range(2)]
        sides = [side_cells(strips, 1, kind, cols) for kind in range(2)]
        bounds = (0, CELLS, CELLS + STRIP, CELLS + 2 * STRIP)
        parts = []
        centre_scores = []
        for head in range(2):
            lanes = lanes_of(head)
            dout_head = one_head(dout, head)
            delta = rows_ref[2, pl.ds(2 * pair + head, 1), :]
            products = [product_ref[pair, :, lanes]] + side_products(sides, dout_head)
            dscore = [
                (weights_ref[pair, start:end, lanes].astype(jnp.float32) * (g - delta)).astype(jnp.bfloat16)
                for start, end, g in zip(bounds, bounds[1:], products)
            ]
            centre_scores.append(dscore[0])
            parts.append(over_cells(turned_centre, turned_strips, head, dscore[0], dscore[1:]))
        grad_query = jnp.concatenate(parts, axis=0).T * SCORE_SCALE
        grad_query_ref[:, cols] = grad_query.astype(jnp.bfloat16)
        grad_key, grad_value = joint_mm(
            jnp.concatenate(centre_scores, axis=1), weights_ref[pair, :CELLS, :], both_heads(query), both_heads(dout)
        )
        centre_ref[0, :, cols] = grad_key * SCORE_SCALE
        centre_ref[1, :, cols] = grad_value
        return carry

    lax.fori_loop(0, weights_ref.shape[0], step, 0)


def joint_mm(first, second, first_rows, second_rows):
    rows = first.shape[0]
    product = mm(jnp.concatenate([first, second], axis=0), jnp.concatenate([first_rows, second_rows], axis=1))
    return product[:rows, :PAIR], product[rows:, PAIR:]


def both_heads(block):
    return jnp.concatenate([one_head(block, head) for head in range(2)], axis=0)


def padded(block):
    return jnp.concatenate([block, jnp.zeros((LANES - block.shape[0], block.shape[1]), block.dtype)], axis=0)


def statistics(rows):
    first = 0
    for count in PARTS:
        heads = []
        for head in range(2):
            parts = [rows[2 * index + head : 2 * index + head + 1] for index in range(first, first + count)]
            heads.append(functools.reduce(jnp.add, parts))
        first += count
        yield jnp.concatenate(heads, axis=1)


def side_kernel(side_indices, rotations_ref, centre_ref, *refs):
    picked, rims = refs[:2], refs[2:4]
    keys_ref, values_ref, chosen_ref, bias_ref = refs[4:]
    cell = lax.broadcasted_iota(jnp.int32, (STRIP, LANES), 0)
    query = lax.broadcasted_iota(jnp.int32, (STRIP, LANES), 1)
    near = jnp.abs((cell & (SIDE - 1)) - (query & (SIDE - 1))) <= RADIUS
    near = near & ((cell >> 4) >= (query >> 4)) & (query < STRIP)
    bias_ref[...] = jnp.where(near, 0.0, -1e30)
    token = lax.broadcasted_iota(jnp.int32, (CELLS, LANES), 0)
    place = lax.broadcasted_iota(jnp.int32, (CELLS, LANES), 1)
    for index, side_index in enumerate(side_indices):
        wanted = jnp.where(place < STRIP, strip_token(side_index, rotations_ref[0, side_index], place), -1)
        chosen = jnp.where(token == wanted, 1.0, 0.0).astype(jnp.bfloat16)
        chosen_ref[:, index * LANES : (index + 1) * LANES] = chosen

    def step(pair, carry):
        cols = pair_cols(pair)
        grads = []
        bias = jnp.concatenate([bias_ref[...]] * 2, axis=1)
        for picked_ref, rim_ref in zip(picked, rims):
            query = both_heads(padded(rim_ref[:STRIP, cols]))
            dout = both_heads(padded(rim_ref[STRIP : 2 * STRIP, cols]))
            top, inverse, delta = statistics(rim_ref[2 * STRIP :, cols].astype(jnp.float32))
            scores = mm_nt(picked_ref[0, :, cols], query) + bias
            weights = jnp.exp2((scores - top) * LOG_SCALE) * inverse
            product = mm_nt(picked_ref[1, :, cols], dout)
            dscore = (weights * (product - delta)).astype(jnp.bfloat16)
            grad_key, grad_value = joint_mm(dscore, weights.astype(jnp.bfloat16), query, dout)
            grad = jnp.concatenate([grad_key * SCORE_SCALE, grad_value], axis=1)
            grads.append(padded(grad.astype(jnp.bfloat16)))
        total = mm(chosen_ref[...], jnp.concatenate(grads, axis=0))
        keys_ref[:, cols] = (centre_ref[0, :, cols] + total[:, :PAIR]).astype(keys_ref.dtype)
        values_ref[:, cols] = (centre_ref[1, :, cols] + total[:, PAIR:]).astype(values_ref.dtype)
        return carry

    lax.fori_loop(0, keys_ref.shape[-1] // PAIR, step, 0, unroll=2)


def side_pair_kernel(rotations_ref, centre_ref, *refs):
    total_ref = refs[4]
    side_kernel((0, 2), rotations_ref, centre_ref, *refs[:4], total_ref.at[0], total_ref.at[1], *refs[5:])


def call(kernel, name, out_shape, operands, scratch=(), smem=0, unused=0, gflop=0.1):
    specs = [pl.BlockSpec(memory_space=pltpu.SMEM)] * smem
    specs += [pl.BlockSpec(memory_space=pltpu.VMEM)] * (len(operands) - smem - unused)
    specs += [pl.BlockSpec(memory_space=pl.ANY)] * unused
    single = not isinstance(out_shape, list)
    outs = pl.BlockSpec(memory_space=pltpu.VMEM)
    return pl.pallas_call(
        kernel,
        out_shape=out_shape,
        in_specs=specs,
        out_specs=outs if single else [outs] * len(out_shape),
        scratch_shapes=list(scratch),
        compiler_params=pltpu.CompilerParams(vmem_limit_bytes=VMEM_LIMIT),
        cost_estimate=pl.CostEstimate(flops=int(gflop * 1e9), bytes_accessed=1 << 20, transcendentals=0),
        name=name,
    )(*operands)


def in_hbm(array):
    return pltpu.with_memory_space_constraint(array, pltpu.HBM)


def from_behind(block, axis, distance):
    devices = range(lax.axis_size(axis))
    route = [((i - distance) % len(devices), i) for i in devices]
    return lax.ppermute(block, axis, route)


def exchanged(blocks, stride):
    terms = list(blocks[:1])
    for distance in range(1, len(blocks)):
        route = [(tile, tile ^ (distance * stride)) for tile in range(lax.axis_size("tile"))]
        terms.append(lax.ppermute(blocks[distance], "tile", route))
    return terms


def in_order(sides):
    north, east, south, west = sides
    return (east, west, north, south)


def to_sides(blocks, offsets, sides):
    return {s: from_behind(blocks[(s + 2) % 4], "tile", -offsets[s]) for s in sides}


def shards(queries, keys, values, grad_output, out_weight, rotations):
    tile_count = lax.axis_size("tile")
    token_count, features = queries.shape
    model = out_weight.shape[0]
    pairs = features // PAIR
    far = tile_count // NEAR
    chunk = model // tile_count
    heads = lax.axis_size("head")
    offsets = (-(tile_count // 4), 1, tile_count // 4, -1)
    queries, keys, values, out_weight, rotations = (
        in_hbm(a) for a in (queries, keys, values, out_weight, rotations)
    )

    def bf16(*shape):
        return jax.ShapeDtypeStruct(shape, jnp.bfloat16)

    def f32(*shape):
        return jax.ShapeDtypeStruct(shape, jnp.float32)

    strip_types = [bf16(2, STRIP, features)] * 4
    picked = call(pick_kernel, "pick_strips", strip_types, (rotations, keys, values), smem=1)
    grad_output, *picked = lax.optimization_barrier((grad_output, *picked))
    strips = to_sides(picked, offsets, (1, 3, 0, 2))
    strips = [strips[s] for s in range(4)]

    cotangents = [from_behind(grad_output, "head", -k) for k in range(1, heads)]
    dout, dout_turned, turned, turned_sent = call(
        functools.partial(cotangent_kernel, heads),
        "cotangent",
        [bf16(CELLS, features), bf16(features, CELLS)] + [bf16(2, far, chunk, CELLS)] * 2,
        (in_hbm(grad_output), *cotangents, out_weight),
        gflop=1.0,
    )
    raw, stats, product, queries, keys, values = call(
        centre_kernel,
        "centre",
        [f32(pairs, CELLS, 2 * CELLS), f32(pairs, 2, 2 * CELLS), f32(pairs, CELLS, 2 * CELLS)]
        + [bf16(CELLS, features)] * 3,
        (queries, keys, values, dout),
        scratch=[pltpu.VMEM((CELLS, CELLS), jnp.float32)],
        gflop=3.0,
    )
    turned_arrived = exchanged((turned, turned_sent), 1)[1]
    weights, attention, rows = call(
        forward_kernel,
        "forward",
        [bf16(pairs, ROWS, 2 * CELLS), bf16(CELLS, features), f32(3, 2 * pairs, CELLS)],
        (*in_order(strips), queries, values, dout_turned, raw, stats),
        scratch=[pltpu.VMEM((2 * STRIP, CELLS), jnp.float32)],
        gflop=4.0,
    )
    attention_arrived = exchanged((attention, attention), 1)[1]
    rims = call(
        rim_kernel,
        "rims",
        [bf16(2 * STRIP + 16, features)] * 4,
        (queries, dout, rows, turned_arrived),
        unused=1,
    )
    rims_arrived = to_sides(rims, offsets, (0, 2))
    grad_queries, centre = call(
        backward_kernel,
        "backward",
        [bf16(CELLS, features), f32(2, CELLS, features)],
        (queries, keys, dout, *in_order(strips), weights, product, rows, rims[0]),
        unused=1,
        gflop=3.0,
    )
    kept, sent = call(
        partial_kernel,
        "partial",
        [f32(far, chunk, features), bf16(far, chunk, features)],
        (attention, attention_arrived, turned, turned_arrived, centre),
        unused=1,
    )
    terms = exchanged((kept, sent), 2)
    late_rims = lax.optimization_barrier((*rims, sent))[:4]
    rims_arrived |= to_sides(late_rims, offsets, (1, 3))

    side_scratch = [pltpu.VMEM((CELLS, 2 * LANES), jnp.bfloat16), pltpu.VMEM((STRIP, LANES), jnp.float32)]
    centre = call(
        side_pair_kernel,
        "sides_north_south",
        f32(2, CELLS, features),
        (rotations, centre, picked[0], picked[2], rims_arrived[0], rims_arrived[2]),
        scratch=side_scratch,
        smem=1,
        gflop=3.0,
    )
    stride = NEAR
    while stride < tile_count:
        ways = min(NEAR, tile_count // stride)
        sums = call(
            functools.partial(sum_kernel, len(terms)),
            "plane_sum",
            [bf16(tile_count // stride // ways, chunk, features)] * ways,
            (*terms, centre),
            unused=1,
        )
        terms = exchanged(sums, stride)
        stride *= ways

    grad_keys, grad_values = call(
        functools.partial(side_kernel, (1, 3)),
        "sides_east_west",
        [bf16(CELLS, features)] * 2,
        (rotations, centre, picked[1], picked[3], rims_arrived[1], rims_arrived[3]),
        scratch=side_scratch,
        smem=1,
        gflop=3.0,
    )
    grad_out_weight = call(
        functools.partial(weight_kernel, 1.0 / math.sqrt(token_count * tile_count)),
        "weight_sum",
        f32(chunk, features),
        terms,
    )
    return (grad_queries, grad_keys, grad_values, grad_out_weight)


def solution(mesh):
    placed = (
        P("tile", "head"),
        P("tile", "head"),
        P("tile", "head"),
        P("tile", "head"),
        P(None, "head"),
        P("tile", None),
    )
    return jax.shard_map(
        shards,
        mesh=mesh,
        in_specs=placed,
        out_specs=(P("tile", "head"), P("tile", "head"), P("tile", "head"), P("tile", "head")),
        check_vma=False,
    )
```

```python
import functools
import math

import jax
import jax.numpy as jnp
from jax import lax
from jax.experimental import pallas as pl
from jax.experimental.pallas import tpu as pltpu
from jax.sharding import PartitionSpec as P

HEAD_DIM = 64
RADIUS = 6
SIDE = 16
CELLS = SIDE * SIDE
STRIP = RADIUS * SIDE
ROWS = CELLS + 2 * STRIP
NEAR = 4
LANES = 128
PAIR = 2 * HEAD_DIM
VMEM_LIMIT = 32 * 1024 * 1024
NT = (((1,), (1,)), ((), ()))


def mm(a, b):
    return jnp.dot(a, b, preferred_element_type=jnp.float32)


def mm_nt(a, b):
    return lax.dot_general(a, b, NT, preferred_element_type=jnp.float32)


def strip_token(side_index, rotation, cell):
    turn = lax.rem(side_index + 6 - rotation, 4)
    depth = cell >> 4
    along = cell & (SIDE - 1)
    far = SIDE - 1 - along
    near_rim = RADIUS - 1 - depth
    far_rim = SIDE - RADIUS + depth
    row = jnp.where(turn == 0, far_rim, jnp.where(turn == 1, along, jnp.where(turn == 2, near_rim, far)))
    col = jnp.where(turn == 0, along, jnp.where(turn == 1, near_rim, jnp.where(turn == 2, far, far_rim)))
    return row * SIDE + col


def slot_side(slot, columns):
    tile = lax.axis_index("tile")
    if slot < 2:
        return jnp.where((tile + slot) & 1 == 0, 1, 3)
    return jnp.where((lax.div(tile, columns) + slot) & 1 == 0, 2, 0)


def partner(tile, tile_count, slot):
    columns = tile_count // 4
    if slot < 2:
        return (tile + (1 if (tile + slot) % 2 == 0 else -1)) % tile_count
    return (tile + (columns if (tile // columns + slot) % 2 == 0 else -columns)) % tile_count


def pick_kernel(columns, rotations_ref, keys_ref, values_ref, *out_refs):
    cell = lax.broadcasted_iota(jnp.int32, (STRIP, CELLS), 0)
    token = lax.broadcasted_iota(jnp.int32, (STRIP, CELLS), 1)
    for slot, out_ref in enumerate(out_refs):
        side = slot_side(slot, columns)
        wanted = strip_token(side, rotations_ref[0, side], cell)
        chosen = jnp.where(token == wanted, 1.0, 0.0).astype(jnp.bfloat16)
        out_ref[0] = mm(chosen, keys_ref[...]).astype(jnp.bfloat16)
        out_ref[1] = mm(chosen, values_ref[...]).astype(jnp.bfloat16)


def weight_kernel(scale, *refs):
    total = refs[0][0].astype(jnp.float32)
    for ref in refs[1:-1]:
        total += ref[0].astype(jnp.float32)
    refs[-1][...] = total * scale


def partial_kernel(attention_ref, arrived_ref, turned_ref, turned_arrived_ref, unused_ref, kept_ref, sent_ref):
    for index, out_ref in enumerate((kept_ref, sent_ref)):
        total = None
        for turned_part, attention_part in ((turned_ref, attention_ref), (turned_arrived_ref, arrived_ref)):
            turned = turned_part[index]
            turned = turned.reshape(turned.shape[0] * turned.shape[1], turned.shape[2])
            term = mm(turned, attention_part[...])
            total = term if total is None else total + term
        out_ref[...] = total.astype(out_ref.dtype).reshape(out_ref.shape)


def sum_kernel(count, *refs):
    terms, outs = refs[:count], refs[count + 1 :]
    for q in range(terms[0].shape[0]):
        total = terms[0][q].astype(jnp.float32)
        for ref in terms[1:]:
            total += ref[q].astype(jnp.float32)
        outs[q % len(outs)][q // len(outs)] = total.astype(jnp.bfloat16)


def rim_token(side_index, place):
    depth = place >> 4
    along = place & (SIDE - 1)
    last = SIDE - 1
    north, east, south = side_index == 0, side_index == 1, side_index == 2
    row = jnp.where(north, depth, jnp.where(east, along, jnp.where(south, last - depth, last - along)))
    col = jnp.where(north, along, jnp.where(east, last - depth, jnp.where(south, last - along, depth)))
    return row * SIDE + col


def cotangent_kernel(heads, *refs):
    blocks, out_weight_ref, outs = refs[:heads], refs[heads], refs[heads + 1 :]
    dout_ref, dout_turned_ref, turned_ref, turned_sent_ref = outs
    head = lax.axis_index("head")
    tile = lax.axis_index("tile")
    chunk = turned_ref.shape[2]
    width = blocks[0].shape[1]
    total = None
    for distance, block_ref in enumerate(blocks):
        owner = lax.rem(head + distance, heads)
        start = pl.multiple_of(owner * width, width)
        block = block_ref[...]
        term = mm(block, out_weight_ref[pl.ds(start, width), :])
        total = term if total is None else total + term
        turned = block.T
        first = owner * (width // chunk)
        for index in range(width // chunk):
            target = (first + index) ^ tile
            rows = turned[index * chunk : (index + 1) * chunk]
            for parity, out_ref in enumerate((turned_ref, turned_sent_ref)):

                @pl.when(target & 1 == parity)
                def _():
                    out_ref[(target & 3) >> 1, target >> 2] = rows

    dout = total.astype(jnp.bfloat16)
    dout_ref[...] = dout
    dout_turned_ref[...] = dout.T


def split(exact, count):
    parts = []
    for _ in range(count):
        part = exact.astype(jnp.bfloat16).astype(jnp.float32)
        parts.append(part)
        exact = exact - part
    return parts


PARTS = (3, 2, 2)


def rim_kernel(columns, query_ref, dout_ref, rows_ref, unused_ref, *rim_refs):
    place = lax.broadcasted_iota(jnp.int32, (LANES, CELLS), 0)
    token = lax.broadcasted_iota(jnp.int32, (LANES, CELLS), 1)
    parts = [part for kind, count in enumerate(PARTS) for part in split(rows_ref[kind], count)]
    pairs = rows_ref.shape[1] // 2
    filler = jnp.zeros((16 - 2 * len(parts), CELLS), jnp.float32)
    rows = [
        jnp.concatenate([part[2 * pair : 2 * pair + 2] for part in parts] + [filler], axis=0) for pair in range(pairs)
    ]
    rows = jnp.concatenate(rows, axis=0).astype(jnp.bfloat16)
    for slot, rim_ref in enumerate(rim_refs):
        wanted = rim_token(slot_side(slot, columns), place)
        chosen = jnp.where((token == wanted) & (place < STRIP), 1.0, 0.0).astype(jnp.bfloat16)
        rim_ref[:STRIP] = mm(chosen[:STRIP], query_ref[...]).astype(jnp.bfloat16)
        rim_ref[STRIP : 2 * STRIP] = mm(chosen[:STRIP], dout_ref[...]).astype(jnp.bfloat16)
        spread = mm_nt(rows, chosen).astype(jnp.bfloat16)
        for pair in range(pairs):
            rim_ref[2 * STRIP :, pair * PAIR : (pair + 1) * PAIR] = spread[16 * pair : 16 * pair + 16]


def window(cell_row, cell_col, query):
    query_row = (query >> 4) + RADIUS
    query_col = (query & (SIDE - 1)) + RADIUS
    near = (jnp.abs(cell_row - query_row) <= RADIUS) & (jnp.abs(cell_col - query_col) <= RADIUS)
    return jnp.where(near, 0.0, -1e30)


def centre_bias(bias_ref):
    query = lax.broadcasted_iota(jnp.int32, (CELLS, CELLS), 1)
    cell = lax.broadcasted_iota(jnp.int32, (CELLS, CELLS), 0)
    bias_ref[...] = window((cell >> 4) + RADIUS, (cell & (SIDE - 1)) + RADIUS, query)


def strip_bias(bias_ref):
    query = lax.broadcasted_iota(jnp.int32, (STRIP, CELLS), 1)
    cell = lax.broadcasted_iota(jnp.int32, (STRIP, CELLS), 0)
    depth = cell >> 4
    along = cell & (SIDE - 1)
    last = SIDE + 2 * RADIUS - 1
    north = (depth, RADIUS + along)
    east = (RADIUS + along, last - depth)
    south = (last - depth, last - RADIUS - along)
    west = (last - RADIUS - along, depth)
    for start, kind, first, second in ((0, 0, north, south), (STRIP, 1, west, east)):
        in_first = first_half(query, kind)
        row = jnp.where(in_first, first[0], second[0])
        col = jnp.where(in_first, first[1], second[1])
        bias_ref[start : start + STRIP, :] = window(row, col, query)


def first_half(query, kind):
    return (query & (SIDE - 1)) < SIDE // 2 if kind else query < CELLS // 2


def one_head(block, head):
    lane = lax.broadcasted_iota(jnp.int32, block.shape, 1)
    kept = (lane >= HEAD_DIM) if head else (lane < HEAD_DIM)
    return jnp.where(kept, block, jnp.zeros_like(block))


def halves(block, kind):
    kept = first_half(lax.broadcasted_iota(jnp.int32, block.shape, 0), kind)
    zero = jnp.zeros_like(block)
    return jnp.concatenate([jnp.where(kept, block, zero), jnp.where(kept, zero, block)], axis=1)


def by_half(stacked, kind):
    rows = stacked.shape[0] // 2
    kept = first_half(lax.broadcasted_iota(jnp.int32, (rows, CELLS), 1), kind)
    return jnp.where(kept, stacked[:rows], stacked[rows:])


def side_blocks(strips, part, kind, cols):
    tile = lax.axis_index("tile")
    if kind:
        second, first = strips[:2]
        straight = tile & 1 == 0
    else:
        second, first = strips[2:]
        straight = lax.div(tile, lax.axis_size("tile") // 4) & 1 == 0
    first, second = first[part, :, cols], second[part, :, cols]
    return jnp.where(straight, first, second), jnp.where(straight, second, first)


def side_cells(strips, part, kind, cols):
    return jnp.concatenate(side_blocks(strips, part, kind, cols), axis=1)


def side_products(cells, rows_head):
    return [mm_nt(cells[kind], halves(rows_head, kind)) for kind in range(2)]


def turned_sides(strips, part, kind, cols):
    return [block.T for block in side_blocks(strips, part, kind, cols)]


def pair_cols(pair):
    return pl.ds(pl.multiple_of(pair * PAIR, PAIR), PAIR)


def head_rows(turned, head):
    return turned[head * HEAD_DIM : (head + 1) * HEAD_DIM]


def over_cells(turned_centre, turned_strips, head, centre, sides):
    total = mm(head_rows(turned_centre, head), centre)
    for kind in range(2):
        stacked = jnp.concatenate([head_rows(t, head) for t in turned_strips[kind]], axis=0)
        total += by_half(mm(stacked, sides[kind]), kind)
    return total


SCORE_SCALE = HEAD_DIM ** (-0.5)
LOG_SCALE = SCORE_SCALE * math.log2(math.e)


def lanes_of(head):
    return slice(head * CELLS, (head + 1) * CELLS)


def centre_kernel(
    query_ref, key_ref, value_ref, dout_ref,
    raw_ref, stats_ref, product_ref, query_out, key_out, value_out, bias_ref,
):
    centre_bias(bias_ref)

    def step(pair, carry):
        cols = pair_cols(pair)
        query, key, value, dout = (ref[:, cols] for ref in (query_ref, key_ref, value_ref, dout_ref))
        for head in range(2):
            scores = mm_nt(key, one_head(query, head)) + bias_ref[...]
            top = jnp.max(scores, axis=0, keepdims=True)
            raw = jnp.exp2((scores - top) * LOG_SCALE)
            raw_ref[pair, :, lanes_of(head)] = raw
            stats_ref[pair, 0:1, lanes_of(head)] = top
            stats_ref[pair, 1:2, lanes_of(head)] = jnp.sum(raw, axis=0, keepdims=True)
            product_ref[pair, :, lanes_of(head)] = mm_nt(value, one_head(dout, head))
        query_out[:, cols] = query
        key_out[:, cols] = key
        value_out[:, cols] = value
        return carry

    lax.fori_loop(0, raw_ref.shape[0], step, 0)


def forward_kernel(
    *refs,
):
    strips = refs[3::-1]
    query_ref, value_ref, dout_turned_ref, raw_ref, stats_ref, weights_ref, attention_ref, rows_ref, bias_ref = refs[4:]
    strip_bias(bias_ref)

    def step(pair, carry):
        cols = pair_cols(pair)
        query = query_ref[:, cols]
        turned_centre = value_ref[:, cols].T
        turned_strips = [turned_sides(strips, 1, kind, cols) for kind in range(2)]
        sides = [side_cells(strips, 0, kind, cols) for kind in range(2)]
        parts = []
        for head in range(2):
            query_head = one_head(query, head)
            scores = [
                product + bias_ref[kind * STRIP : (kind + 1) * STRIP]
                for kind, product in enumerate(side_products(sides, query_head))
            ]
            centre_top = stats_ref[pair, 0:1, lanes_of(head)]
            top = jnp.maximum(jnp.max(jnp.maximum(scores[0], scores[1]), axis=0, keepdims=True), centre_top)
            raw = [jnp.exp2((s - top) * LOG_SCALE) for s in scores]
            lifted = jnp.exp2((centre_top - top) * LOG_SCALE)
            total = jnp.sum(raw[0] + raw[1], axis=0, keepdims=True)
            total += lifted * stats_ref[pair, 1:2, lanes_of(head)]
            inverse = 1.0 / total
            centre = (raw_ref[pair, :, lanes_of(head)] * (lifted * inverse)).astype(jnp.bfloat16)
            outer = [(r * inverse).astype(jnp.bfloat16) for r in raw]
            weights_ref[pair, :CELLS, lanes_of(head)] = centre
            for kind in range(2):
                start = CELLS + kind * STRIP
                weights_ref[pair, start : start + STRIP, lanes_of(head)] = outer[kind]
            part = over_cells(turned_centre, turned_strips, head, centre, outer)
            parts.append(part)
            place = pl.ds(2 * pair + head, 1)
            features = pl.ds(pl.multiple_of((2 * pair + head) * HEAD_DIM, HEAD_DIM), HEAD_DIM)
            product = dout_turned_ref[features, :].astype(jnp.float32) * part
            rows_ref[0, place, :] = top
            rows_ref[1, place, :] = inverse
            rows_ref[2, place, :] = jnp.sum(product, axis=0, keepdims=True)
        attention_ref[:, cols] = jnp.concatenate(parts, axis=0).T.astype(jnp.bfloat16)
        return carry

    lax.fori_loop(0, raw_ref.shape[0], step, 0)


def backward_kernel(
    *refs,
):
    strips = refs[3::-1]
    query_ref, key_ref, dout_ref, weights_ref, product_ref, rows_ref, unused_ref, grad_query_ref, centre_ref = refs[4:]

    def step(pair, carry):
        cols = pair_cols(pair)
        query = query_ref[:, cols]
        dout = dout_ref[:, cols]
        turned_centre = key_ref[:, cols].T
        turned_strips = [turned_sides(strips, 0, kind, cols) for kind in range(2)]
        sides = [side_cells(strips, 1, kind, cols) for kind in range(2)]
        bounds = (0, CELLS, CELLS + STRIP, CELLS + 2 * STRIP)
        parts = []
        centre_scores = []
        for head in range(2):
            lanes = lanes_of(head)
            dout_head = one_head(dout, head)
            delta = rows_ref[2, pl.ds(2 * pair + head, 1), :]
            products = [product_ref[pair, :, lanes]] + side_products(sides, dout_head)
            dscore = [
                (weights_ref[pair, start:end, lanes].astype(jnp.float32) * (g - delta)).astype(jnp.bfloat16)
                for start, end, g in zip(bounds, bounds[1:], products)
            ]
            centre_scores.append(dscore[0])
            parts.append(over_cells(turned_centre, turned_strips, head, dscore[0], dscore[1:]))
        grad_query = jnp.concatenate(parts, axis=0).T * SCORE_SCALE
        grad_query_ref[:, cols] = grad_query.astype(jnp.bfloat16)
        grad_key, grad_value = joint_mm(
            jnp.concatenate(centre_scores, axis=1), weights_ref[pair, :CELLS, :], both_heads(query), both_heads(dout)
        )
        centre_ref[0, :, cols] = grad_key * SCORE_SCALE
        centre_ref[1, :, cols] = grad_value
        return carry

    lax.fori_loop(0, weights_ref.shape[0], step, 0)


def joint_mm(first, second, first_rows, second_rows):
    rows = first.shape[0]
    product = mm(jnp.concatenate([first, second], axis=0), jnp.concatenate([first_rows, second_rows], axis=1))
    return product[:rows, :PAIR], product[rows:, PAIR:]


def both_heads(block):
    return jnp.concatenate([one_head(block, head) for head in range(2)], axis=0)


def padded(block):
    return jnp.concatenate([block, jnp.zeros((LANES - block.shape[0], block.shape[1]), block.dtype)], axis=0)


def statistics(rows):
    first = 0
    for count in PARTS:
        heads = []
        for head in range(2):
            parts = [rows[2 * index + head : 2 * index + head + 1] for index in range(first, first + count)]
            heads.append(functools.reduce(jnp.add, parts))
        first += count
        yield jnp.concatenate(heads, axis=1)


def side_kernel(slots, columns, rotations_ref, centre_ref, *refs):
    picked, rims = refs[:2], refs[2:4]
    keys_ref, values_ref, chosen_ref, bias_ref = refs[4:]
    cell = lax.broadcasted_iota(jnp.int32, (STRIP, LANES), 0)
    query = lax.broadcasted_iota(jnp.int32, (STRIP, LANES), 1)
    near = jnp.abs((cell & (SIDE - 1)) - (query & (SIDE - 1))) <= RADIUS
    near = near & ((cell >> 4) >= (query >> 4)) & (query < STRIP)
    bias_ref[...] = jnp.where(near, 0.0, -1e30)
    token = lax.broadcasted_iota(jnp.int32, (CELLS, LANES), 0)
    place = lax.broadcasted_iota(jnp.int32, (CELLS, LANES), 1)
    for index, slot in enumerate(slots):
        side = slot_side(slot, columns)
        wanted = jnp.where(place < STRIP, strip_token(side, rotations_ref[0, side], place), -1)
        chosen = jnp.where(token == wanted, 1.0, 0.0).astype(jnp.bfloat16)
        chosen_ref[:, index * LANES : (index + 1) * LANES] = chosen

    def step(pair, carry):
        cols = pair_cols(pair)
        grads = []
        bias = jnp.concatenate([bias_ref[...]] * 2, axis=1)
        for picked_ref, rim_ref in zip(picked, rims):
            query = both_heads(padded(rim_ref[:STRIP, cols]))
            dout = both_heads(padded(rim_ref[STRIP : 2 * STRIP, cols]))
            top, inverse, delta = statistics(rim_ref[2 * STRIP :, cols].astype(jnp.float32))
            scores = mm_nt(picked_ref[0, :, cols], query) + bias
            weights = jnp.exp2((scores - top) * LOG_SCALE) * inverse
            product = mm_nt(picked_ref[1, :, cols], dout)
            dscore = (weights * (product - delta)).astype(jnp.bfloat16)
            grad_key, grad_value = joint_mm(dscore, weights.astype(jnp.bfloat16), query, dout)
            grad = jnp.concatenate([grad_key * SCORE_SCALE, grad_value], axis=1)
            grads.append(padded(grad.astype(jnp.bfloat16)))
        total = mm(chosen_ref[...], jnp.concatenate(grads, axis=0))
        keys_ref[:, cols] = (centre_ref[0, :, cols] + total[:, :PAIR]).astype(keys_ref.dtype)
        values_ref[:, cols] = (centre_ref[1, :, cols] + total[:, PAIR:]).astype(values_ref.dtype)
        return carry

    lax.fori_loop(0, keys_ref.shape[-1] // PAIR, step, 0, unroll=2)


def side_pair_kernel(columns, rotations_ref, centre_ref, *refs):
    total_ref = refs[4]
    side_kernel((3, 2), columns, rotations_ref, centre_ref, *refs[:4], total_ref.at[0], total_ref.at[1], *refs[5:])


def call(kernel, name, out_shape, operands, scratch=(), smem=0, unused=0, gflop=0.1):
    specs = [pl.BlockSpec(memory_space=pltpu.SMEM)] * smem
    specs += [pl.BlockSpec(memory_space=pltpu.VMEM)] * (len(operands) - smem - unused)
    specs += [pl.BlockSpec(memory_space=pl.ANY)] * unused
    single = not isinstance(out_shape, list)
    outs = pl.BlockSpec(memory_space=pltpu.VMEM)
    return pl.pallas_call(
        kernel,
        out_shape=out_shape,
        in_specs=specs,
        out_specs=outs if single else [outs] * len(out_shape),
        scratch_shapes=list(scratch),
        compiler_params=pltpu.CompilerParams(vmem_limit_bytes=VMEM_LIMIT),
        cost_estimate=pl.CostEstimate(flops=int(gflop * 1e9), bytes_accessed=1 << 20, transcendentals=0),
        name=name,
    )(*operands)


def in_hbm(array):
    return pltpu.with_memory_space_constraint(array, pltpu.HBM)


def exchanged(blocks, stride):
    terms = list(blocks[:1])
    for distance in range(1, len(blocks)):
        route = [(tile, tile ^ (distance * stride)) for tile in range(lax.axis_size("tile"))]
        terms.append(lax.ppermute(blocks[distance], "tile", route))
    return terms


def with_partners(blocks, slots):
    tile_count = lax.axis_size("tile")
    routes = {s: [(tile, partner(tile, tile_count, s)) for tile in range(tile_count)] for s in slots}
    return {s: lax.ppermute(blocks[s], "tile", routes[s]) for s in slots}


def shards(queries, keys, values, grad_output, out_weight, rotations):
    tile_count = lax.axis_size("tile")
    token_count, features = queries.shape
    model = out_weight.shape[0]
    pairs = features // PAIR
    far = tile_count // NEAR
    chunk = model // tile_count
    heads = lax.axis_size("head")
    columns = tile_count // 4
    queries, keys, values, out_weight, rotations = (
        in_hbm(a) for a in (queries, keys, values, out_weight, rotations)
    )

    def bf16(*shape):
        return jax.ShapeDtypeStruct(shape, jnp.bfloat16)

    def f32(*shape):
        return jax.ShapeDtypeStruct(shape, jnp.float32)

    strip_types = [bf16(2, STRIP, features)] * 4
    picked = call(
        functools.partial(pick_kernel, columns), "pick_strips", strip_types, (rotations, keys, values), smem=1
    )
    grad_output, *picked = lax.optimization_barrier((grad_output, *picked))
    strips = with_partners(picked, (3, 2, 1, 0))
    strips = [strips[s] for s in range(4)]

    cotangents = [
        lax.ppermute(grad_output, "head", [((h + k) % heads, h) for h in range(heads)]) for k in range(1, heads)
    ]
    dout, dout_turned, turned, turned_sent = call(
        functools.partial(cotangent_kernel, heads),
        "cotangent",
        [bf16(CELLS, features), bf16(features, CELLS)] + [bf16(2, far, chunk, CELLS)] * 2,
        (in_hbm(grad_output), *cotangents, out_weight),
        gflop=1.0,
    )
    raw, stats, product, queries, keys, values = call(
        centre_kernel,
        "centre",
        [f32(pairs, CELLS, 2 * CELLS), f32(pairs, 2, 2 * CELLS), f32(pairs, CELLS, 2 * CELLS)]
        + [bf16(CELLS, features)] * 3,
        (queries, keys, values, dout),
        scratch=[pltpu.VMEM((CELLS, CELLS), jnp.float32)],
        gflop=3.0,
    )
    turned_arrived = exchanged((turned, turned_sent), 1)[1]
    weights, attention, rows = call(
        forward_kernel,
        "forward",
        [bf16(pairs, ROWS, 2 * CELLS), bf16(CELLS, features), f32(3, 2 * pairs, CELLS)],
        (*strips[::-1], queries, values, dout_turned, raw, stats),
        scratch=[pltpu.VMEM((2 * STRIP, CELLS), jnp.float32)],
        gflop=4.0,
    )
    attention_arrived = exchanged((attention, attention), 1)[1]
    rims = call(
        functools.partial(rim_kernel, columns),
        "rims",
        [bf16(2 * STRIP + 16, features)] * 4,
        (queries, dout, rows, turned_arrived),
        unused=1,
    )
    rims_arrived = with_partners(rims, (3, 2))
    kept, sent = call(
        partial_kernel,
        "partial",
        [f32(far, chunk, features), bf16(far, chunk, features)],
        (attention, attention_arrived, turned, turned_arrived, rims[0]),
        unused=1,
    )
    terms = exchanged((kept, sent), 2)
    late_rims = lax.optimization_barrier((*rims, sent))[:4]
    rims_arrived |= with_partners(late_rims, (1, 0))

    grad_queries, centre = call(
        backward_kernel,
        "backward",
        [bf16(CELLS, features), f32(2, CELLS, features)],
        (*strips[::-1], queries, keys, dout, weights, product, rows, sent),
        unused=1,
        gflop=3.0,
    )
    side_scratch = [pltpu.VMEM((CELLS, 2 * LANES), jnp.bfloat16), pltpu.VMEM((STRIP, LANES), jnp.float32)]
    centre = call(
        functools.partial(side_pair_kernel, columns),
        "sides_columns",
        f32(2, CELLS, features),
        (rotations, centre, picked[3], picked[2], rims_arrived[3], rims_arrived[2]),
        scratch=side_scratch,
        smem=1,
        gflop=3.0,
    )
    stride = NEAR
    while stride < tile_count:
        ways = min(NEAR, tile_count // stride)
        sums = call(
            functools.partial(sum_kernel, len(terms)),
            "plane_sum",
            [bf16(tile_count // stride // ways, chunk, features)] * ways,
            (*terms, centre),
            unused=1,
        )
        terms = exchanged(sums, stride)
        stride *= ways

    grad_keys, grad_values = call(
        functools.partial(side_kernel, (1, 0), columns),
        "sides_rows",
        [bf16(CELLS, features)] * 2,
        (rotations, centre, picked[1], picked[0], rims_arrived[1], rims_arrived[0]),
        scratch=side_scratch,
        smem=1,
        gflop=3.0,
    )
    grad_out_weight = call(
        functools.partial(weight_kernel, 1.0 / math.sqrt(token_count * tile_count)),
        "weight_sum",
        f32(chunk, features),
        terms,
    )
    return (grad_queries, grad_keys, grad_values, grad_out_weight)


def solution(mesh):
    placed = (
        P("tile", "head"),
        P("tile", "head"),
        P("tile", "head"),
        P("tile", "head"),
        P(None, "head"),
        P("tile", None),
    )
    return jax.shard_map(
        shards,
        mesh=mesh,
        in_specs=placed,
        out_specs=(P("tile", "head"), P("tile", "head"), P("tile", "head"), P("tile", "head")),
        check_vma=False,
    )
```

```python
import functools
import math

import jax
import jax.numpy as jnp
from jax import lax
from jax.experimental import pallas as pl
from jax.experimental.pallas import tpu as pltpu
from jax.sharding import PartitionSpec as P

HEAD_DIM = 64
RADIUS = 6
SIDE = 16
CELLS = SIDE * SIDE
STRIP = RADIUS * SIDE
NEAR = 4
LANES = 128
PAIR = 2 * HEAD_DIM
VMEM_LIMIT = 32 * 1024 * 1024
NT = (((1,), (1,)), ((), ()))


def mm(a, b):
    return jnp.dot(a, b, preferred_element_type=jnp.float32)


def mm_nt(a, b):
    return lax.dot_general(a, b, NT, preferred_element_type=jnp.float32)


def strip_token(side_index, rotation, cell):
    turn = lax.rem(side_index + 6 - rotation, 4)
    depth = cell >> 4
    along = cell & (SIDE - 1)
    far = SIDE - 1 - along
    near_rim = RADIUS - 1 - depth
    far_rim = SIDE - RADIUS + depth
    row = jnp.where(turn == 0, far_rim, jnp.where(turn == 1, along, jnp.where(turn == 2, near_rim, far)))
    col = jnp.where(turn == 0, along, jnp.where(turn == 1, near_rim, jnp.where(turn == 2, far, far_rim)))
    return row * SIDE + col


def slot_side(slot, columns):
    tile = lax.axis_index("tile")
    if slot < 2:
        return jnp.where((tile + slot) & 1 == 0, 1, 3)
    return jnp.where((lax.div(tile, columns) + slot) & 1 == 0, 2, 0)


def partner(tile, tile_count, slot):
    columns = tile_count // 4
    if slot < 2:
        return (tile + (1 if (tile + slot) % 2 == 0 else -1)) % tile_count
    return (tile + (columns if (tile // columns + slot) % 2 == 0 else -columns)) % tile_count


def pick_kernel(columns, rotations_ref, keys_ref, values_ref, *out_refs):
    cell = lax.broadcasted_iota(jnp.int32, (STRIP, CELLS), 0)
    token = lax.broadcasted_iota(jnp.int32, (STRIP, CELLS), 1)
    for slot, out_ref in enumerate(out_refs):
        side = slot_side(slot, columns)
        wanted = strip_token(side, rotations_ref[0, side], cell)
        chosen = jnp.where(token == wanted, 1.0, 0.0).astype(jnp.bfloat16)
        out_ref[0] = mm(chosen, keys_ref[...]).astype(jnp.bfloat16)
        out_ref[1] = mm(chosen, values_ref[...]).astype(jnp.bfloat16)


def weight_kernel(scale, *refs):
    total = refs[0][0].astype(jnp.float32)
    for ref in refs[1:-1]:
        total += ref[0].astype(jnp.float32)
    refs[-1][...] = total * scale


def partial_kernel(attention_ref, arrived_ref, turned_ref, turned_arrived_ref, unused_ref, kept_ref, sent_ref):
    for index, out_ref in enumerate((kept_ref, sent_ref)):
        total = None
        for turned_part, attention_part in ((turned_ref, attention_ref), (turned_arrived_ref, arrived_ref)):
            turned = turned_part[index]
            turned = turned.reshape(turned.shape[0] * turned.shape[1], turned.shape[2])
            term = mm(turned, attention_part[...])
            total = term if total is None else total + term
        out_ref[...] = total.astype(out_ref.dtype).reshape(out_ref.shape)


def sum_kernel(count, *refs):
    terms, outs = refs[:count], refs[count + 1 :]
    for q in range(terms[0].shape[0]):
        total = terms[0][q].astype(jnp.float32)
        for ref in terms[1:]:
            total += ref[q].astype(jnp.float32)
        outs[q % len(outs)][q // len(outs)] = total.astype(jnp.bfloat16)


def rim_token(side_index, place):
    depth = place >> 4
    along = place & (SIDE - 1)
    last = SIDE - 1
    north, east, south = side_index == 0, side_index == 1, side_index == 2
    row = jnp.where(north, depth, jnp.where(east, along, jnp.where(south, last - depth, last - along)))
    col = jnp.where(north, along, jnp.where(east, last - depth, jnp.where(south, last - along, depth)))
    return row * SIDE + col


def cotangent_kernel(heads, *refs):
    blocks, out_weight_ref, outs = refs[:heads], refs[heads], refs[heads + 1 :]
    dout_ref, dout_turned_ref, turned_ref, turned_sent_ref = outs
    head = lax.axis_index("head")
    tile = lax.axis_index("tile")
    chunk = turned_ref.shape[2]
    width = blocks[0].shape[1]
    total = None
    for distance, block_ref in enumerate(blocks):
        owner = lax.rem(head + distance, heads)
        start = pl.multiple_of(owner * width, width)
        block = block_ref[...]
        term = mm(block, out_weight_ref[pl.ds(start, width), :])
        total = term if total is None else total + term
        turned = block.T
        first = owner * (width // chunk)
        for index in range(width // chunk):
            target = (first + index) ^ tile
            rows = turned[index * chunk : (index + 1) * chunk]
            for parity, out_ref in enumerate((turned_ref, turned_sent_ref)):

                @pl.when((target >> 1) & 1 == parity)
                def _():
                    out_ref[target & 1, target >> 2] = rows

    dout = total.astype(jnp.bfloat16)
    dout_ref[...] = dout
    dout_turned_ref[...] = dout.T


def split(exact, count):
    parts = []
    for _ in range(count):
        part = exact.astype(jnp.bfloat16).astype(jnp.float32)
        parts.append(part)
        exact = exact - part
    return parts


PARTS = (3, 2, 2)


def rim_kernel(columns, query_ref, dout_ref, rows_ref, unused_ref, *rim_refs):
    place = lax.broadcasted_iota(jnp.int32, (LANES, CELLS), 0)
    token = lax.broadcasted_iota(jnp.int32, (LANES, CELLS), 1)
    parts = [part for kind, count in enumerate(PARTS) for part in split(rows_ref[kind], count)]
    pairs = rows_ref.shape[1] // 2
    filler = jnp.zeros((16 - 2 * len(parts), CELLS), jnp.float32)
    rows = [
        jnp.concatenate([part[2 * pair : 2 * pair + 2] for part in parts] + [filler], axis=0) for pair in range(pairs)
    ]
    rows = jnp.concatenate(rows, axis=0).astype(jnp.bfloat16)
    for slot, rim_ref in enumerate(rim_refs):
        wanted = rim_token(slot_side(slot, columns), place)
        chosen = jnp.where((token == wanted) & (place < STRIP), 1.0, 0.0).astype(jnp.bfloat16)
        rim_ref[:STRIP] = mm(chosen[:STRIP], query_ref[...]).astype(jnp.bfloat16)
        rim_ref[STRIP : 2 * STRIP] = mm(chosen[:STRIP], dout_ref[...]).astype(jnp.bfloat16)
        spread = mm_nt(rows, chosen).astype(jnp.bfloat16)
        for pair in range(pairs):
            rim_ref[2 * STRIP :, pair * PAIR : (pair + 1) * PAIR] = spread[16 * pair : 16 * pair + 16]


def window(cell_row, cell_col, query):
    query_row = (query >> 4) + RADIUS
    query_col = (query & (SIDE - 1)) + RADIUS
    near = (jnp.abs(cell_row - query_row) <= RADIUS) & (jnp.abs(cell_col - query_col) <= RADIUS)
    return jnp.where(near, 0.0, -1e30)


def centre_bias(bias_ref):
    query = lax.broadcasted_iota(jnp.int32, (CELLS, CELLS), 1)
    cell = lax.broadcasted_iota(jnp.int32, (CELLS, CELLS), 0)
    bias_ref[...] = window((cell >> 4) + RADIUS, (cell & (SIDE - 1)) + RADIUS, query)


def strip_bias(kind, bias_ref):
    query = lax.broadcasted_iota(jnp.int32, (STRIP, CELLS), 1)
    cell = lax.broadcasted_iota(jnp.int32, (STRIP, CELLS), 0)
    depth = cell >> 4
    along = cell & (SIDE - 1)
    last = SIDE + 2 * RADIUS - 1
    if kind:
        first, second = (last - RADIUS - along, depth), (RADIUS + along, last - depth)
    else:
        first, second = (depth, RADIUS + along), (last - depth, last - RADIUS - along)
    in_first = first_half(query, kind)
    row = jnp.where(in_first, first[0], second[0])
    col = jnp.where(in_first, first[1], second[1])
    bias_ref[...] = window(row, col, query)


def first_half(query, kind):
    return (query & (SIDE - 1)) < SIDE // 2 if kind else query < CELLS // 2


def one_head(block, head):
    lane = lax.broadcasted_iota(jnp.int32, block.shape, 1)
    kept = (lane >= HEAD_DIM) if head else (lane < HEAD_DIM)
    return jnp.where(kept, block, jnp.zeros_like(block))


def halves(block, kind):
    kept = first_half(lax.broadcasted_iota(jnp.int32, block.shape, 0), kind)
    zero = jnp.zeros_like(block)
    return jnp.concatenate([jnp.where(kept, block, zero), jnp.where(kept, zero, block)], axis=1)


def by_half(stacked, kind):
    rows = stacked.shape[0] // 2
    kept = first_half(lax.broadcasted_iota(jnp.int32, (rows, CELLS), 1), kind)
    return jnp.where(kept, stacked[:rows], stacked[rows:])


def side_blocks(strips, part, kind, cols):
    tile = lax.axis_index("tile")
    second, first = strips
    straight = (tile if kind else lax.div(tile, lax.axis_size("tile") // 4)) & 1 == 0
    first, second = first[part, :, cols], second[part, :, cols]
    return jnp.where(straight, first, second), jnp.where(straight, second, first)


def side_cells(strips, part, kind, cols):
    return jnp.concatenate(side_blocks(strips, part, kind, cols), axis=1)


def halves(block, kind):
    kept = first_half(lax.broadcasted_iota(jnp.int32, block.shape, 0), kind)
    zero = jnp.zeros_like(block)
    return jnp.concatenate([jnp.where(kept, block, zero), jnp.where(kept, zero, block)], axis=1)


def by_half(stacked, kind):
    rows = stacked.shape[0] // 2
    kept = first_half(lax.broadcasted_iota(jnp.int32, (rows, CELLS), 1), kind)
    return jnp.where(kept, stacked[:rows], stacked[rows:])


def side_blocks(strips, part, kind, cols):
    tile = lax.axis_index("tile")
    second, first = strips
    straight = (tile if kind else lax.div(tile, lax.axis_size("tile") // 4)) & 1 == 0
    first, second = first[part, :, cols], second[part, :, cols]
    return jnp.where(straight, first, second), jnp.where(straight, second, first)


def side_cells(strips, part, kind, cols):
    return jnp.concatenate(side_blocks(strips, part, kind, cols), axis=1)


def side_products(cells, rows_head):
    return [mm_nt(cells[kind], halves(rows_head, kind)) for kind in range(2)]


def turned_sides(strips, part, kind, cols):
    return [block.T for block in side_blocks(strips, part, kind, cols)]


def pair_cols(pair):
    return pl.ds(pl.multiple_of(pair * PAIR, PAIR), PAIR)


def head_rows(turned, head):
    return turned[head * HEAD_DIM : (head + 1) * HEAD_DIM]


def over_side(turned, head, kind, sides):
    return by_half(mm(jnp.concatenate([head_rows(t, head) for t in turned], axis=0), sides), kind)


SCORE_SCALE = HEAD_DIM ** (-0.5)
LOG_SCALE = SCORE_SCALE * math.log2(math.e)


def lanes_of(head):
    return slice(head * CELLS, (head + 1) * CELLS)


def centre_kernel(
    query_ref, key_ref, value_ref, dout_ref,
    raw_ref, stats_ref, sums_ref, product_ref, query_out, key_out, bias_ref,
):
    centre_bias(bias_ref)

    def step(pair, carry):
        cols = pair_cols(pair)
        query, key, value, dout = (ref[:, cols] for ref in (query_ref, key_ref, value_ref, dout_ref))
        turned = value.T
        for head in range(2):
            lanes = lanes_of(head)
            scores = mm_nt(key, one_head(query, head)) + bias_ref[...]
            top = jnp.max(scores, axis=0, keepdims=True)
            raw = jnp.exp2((scores - top) * LOG_SCALE)
            raw_ref[pair, :, lanes] = raw
            stats_ref[pair, 0:1, lanes] = top
            stats_ref[pair, 1:2, lanes] = jnp.sum(raw, axis=0, keepdims=True)
            sums_ref[pair, :, lanes] = mm(head_rows(turned, head), raw.astype(jnp.bfloat16))
            product_ref[pair, :, lanes] = mm_nt(value, one_head(dout, head))
        query_out[:, cols] = query
        key_out[:, cols] = key
        return carry

    lax.fori_loop(0, raw_ref.shape[0], step, 0)


def column_kernel(
    first_ref, second_ref, query_ref, dout_ref, raw_ref, stats_ref, sums_ref, product_ref, bias_ref
):
    strips = (first_ref, second_ref)
    strip_bias(0, bias_ref)

    def step(pair, carry):
        cols = pair_cols(pair)
        keys = side_cells(strips, 0, 0, cols)
        values = side_cells(strips, 1, 0, cols)
        turned = turned_sides(strips, 1, 0, cols)
        for head in range(2):
            lanes = lanes_of(head)
            scores = mm_nt(keys, halves(one_head(query_ref[:, cols], head), 0)) + bias_ref[...]
            top = jnp.max(scores, axis=0, keepdims=True)
            raw = jnp.exp2((scores - top) * LOG_SCALE)
            raw_ref[pair, :, lanes] = raw
            stats_ref[pair, 0:1, lanes] = top
            stats_ref[pair, 1:2, lanes] = jnp.sum(raw, axis=0, keepdims=True)
            sums_ref[pair, :, lanes] = over_side(turned, head, 0, raw.astype(jnp.bfloat16))
            product_ref[pair, :, lanes] = mm_nt(values, halves(one_head(dout_ref[:, cols], head), 0))
        return carry

    lax.fori_loop(0, raw_ref.shape[0], step, 0)


def row_kernel(
    first_ref, second_ref, query_ref, dout_turned_ref, centre_stats_ref, centre_sums_ref, stats_ref, sums_ref,
    raw_ref, attention_ref, rows_ref, factors_ref, bias_ref,
):
    strips = (first_ref, second_ref)
    strip_bias(1, bias_ref)

    def step(pair, carry):
        cols = pair_cols(pair)
        keys = side_cells(strips, 0, 1, cols)
        turned = turned_sides(strips, 1, 1, cols)
        parts = []
        for head in range(2):
            lanes = lanes_of(head)
            scores = mm_nt(keys, halves(one_head(query_ref[:, cols], head), 1)) + bias_ref[...]
            tops = [ref[pair, 0:1, lanes] for ref in (centre_stats_ref, stats_ref)]
            top = jnp.maximum(jnp.max(scores, axis=0, keepdims=True), jnp.maximum(*tops))
            raw = jnp.exp2((scores - top) * LOG_SCALE)
            raw_ref[pair, :, lanes] = raw
            lifted = [jnp.exp2((t - top) * LOG_SCALE) for t in tops]
            total = jnp.sum(raw, axis=0, keepdims=True)
            total += lifted[0] * centre_stats_ref[pair, 1:2, lanes] + lifted[1] * stats_ref[pair, 1:2, lanes]
            inverse = 1.0 / total
            factors = [l * inverse for l in lifted]
            part = over_side(turned, head, 1, raw.astype(jnp.bfloat16)) * inverse
            part += factors[0] * centre_sums_ref[pair, :, lanes] + factors[1] * sums_ref[pair, :, lanes]
            parts.append(part)
            place = pl.ds(2 * pair + head, 1)
            features = pl.ds(pl.multiple_of((2 * pair + head) * HEAD_DIM, HEAD_DIM), HEAD_DIM)
            product = dout_turned_ref[features, :].astype(jnp.float32) * part
            rows_ref[0, place, :] = top
            rows_ref[1, place, :] = inverse
            rows_ref[2, place, :] = jnp.sum(product, axis=0, keepdims=True)
            factors_ref[0, place, :] = factors[0]
            factors_ref[1, place, :] = factors[1]
        attention_ref[:, cols] = jnp.concatenate(parts, axis=0).T.astype(jnp.bfloat16)
        return carry

    lax.fori_loop(0, raw_ref.shape[0], step, 0)


def backward_kernel(
    fourth_ref, third_ref, second_ref, first_ref, query_ref, key_ref, dout_ref, centre_raw_ref, column_raw_ref,
    row_raw_ref, centre_product_ref, column_product_ref, rows_ref, factors_ref, unused_ref,
    grad_query_ref, centre_ref,
):
    columns, rows = (third_ref, fourth_ref), (first_ref, second_ref)

    def step(pair, carry):
        cols = pair_cols(pair)
        query = query_ref[:, cols]
        dout = dout_ref[:, cols]
        turned_centre = key_ref[:, cols].T
        turned_columns = turned_sides(columns, 0, 0, cols)
        turned_rows = turned_sides(rows, 0, 1, cols)
        row_values = side_cells(rows, 1, 1, cols)
        parts = []
        centre_scores = []
        centre_weights = []
        for head in range(2):
            lanes = lanes_of(head)
            place = pl.ds(2 * pair + head, 1)
            delta = rows_ref[2, place, :]
            row_product = mm_nt(row_values, halves(one_head(dout, head), 1))

            def dscore(weights, product):
                return (weights * (product - delta)).astype(jnp.bfloat16)

            weights = centre_raw_ref[pair, :, lanes] * factors_ref[0, place, :]
            centre_weights.append(weights.astype(jnp.bfloat16))
            centre_scores.append(dscore(weights, centre_product_ref[pair, :, lanes]))
            column_weights = column_raw_ref[pair, :, lanes] * factors_ref[1, place, :]
            column_score = dscore(column_weights, column_product_ref[pair, :, lanes])
            row_score = dscore(row_raw_ref[pair, :, lanes] * rows_ref[1, place, :], row_product)
            part = mm(head_rows(turned_centre, head), centre_scores[-1])
            part += over_side(turned_columns, head, 0, column_score) + over_side(turned_rows, head, 1, row_score)
            parts.append(part)
        grad_query = jnp.concatenate(parts, axis=0).T * SCORE_SCALE
        grad_query_ref[:, cols] = grad_query.astype(jnp.bfloat16)
        grad_key, grad_value = joint_mm(
            jnp.concatenate(centre_scores, axis=1),
            jnp.concatenate(centre_weights, axis=1),
            both_heads(query),
            both_heads(dout),
        )
        centre_ref[0, :, cols] = grad_key * SCORE_SCALE
        centre_ref[1, :, cols] = grad_value
        return carry

    lax.fori_loop(0, centre_raw_ref.shape[0], step, 0)


def joint_mm(first, second, first_rows, second_rows):
    rows = first.shape[0]
    product = mm(jnp.concatenate([first, second], axis=0), jnp.concatenate([first_rows, second_rows], axis=1))
    return product[:rows, :PAIR], product[rows:, PAIR:]


def both_heads(block):
    return jnp.concatenate([one_head(block, head) for head in range(2)], axis=0)


def padded(block):
    return jnp.concatenate([block, jnp.zeros((LANES - block.shape[0], block.shape[1]), block.dtype)], axis=0)


def statistics(rows):
    first = 0
    for count in PARTS:
        heads = []
        for head in range(2):
            parts = [rows[2 * index + head : 2 * index + head + 1] for index in range(first, first + count)]
            heads.append(functools.reduce(jnp.add, parts))
        first += count
        yield jnp.concatenate(heads, axis=1)


def side_kernel(columns, rotations_ref, centre_ref, *refs):
    picked, rims = refs[:4], refs[4:8]
    keys_ref, values_ref, chosen_ref, bias_ref, keys_done, values_done, sems = refs[8:]
    cell = lax.broadcasted_iota(jnp.int32, (STRIP, LANES), 0)
    query = lax.broadcasted_iota(jnp.int32, (STRIP, LANES), 1)
    near = jnp.abs((cell & (SIDE - 1)) - (query & (SIDE - 1))) <= RADIUS
    near = near & ((cell >> 4) >= (query >> 4)) & (query < STRIP)
    bias_ref[...] = jnp.where(near, 0.0, -1e30)
    token = lax.broadcasted_iota(jnp.int32, (CELLS, LANES), 0)
    place = lax.broadcasted_iota(jnp.int32, (CELLS, LANES), 1)
    for slot in range(4):
        side = slot_side(slot, columns)
        wanted = jnp.where(place < STRIP, strip_token(side, rotations_ref[0, side], place), -1)
        chosen = jnp.where(token == wanted, 1.0, 0.0).astype(jnp.bfloat16)
        chosen_ref[:, slot * LANES : (slot + 1) * LANES] = chosen

    copies = []
    for pair in range(keys_ref.shape[1] // PAIR):
        cols = slice(pair * PAIR, (pair + 1) * PAIR)
        grads = []
        bias = jnp.concatenate([bias_ref[...]] * 2, axis=1)
        for picked_ref, rim_ref in zip(picked, rims):
            query = both_heads(padded(rim_ref[:STRIP, cols]))
            dout = both_heads(padded(rim_ref[STRIP : 2 * STRIP, cols]))
            top, inverse, delta = statistics(rim_ref[2 * STRIP :, cols].astype(jnp.float32))
            scores = mm_nt(picked_ref[0, :, cols], query) + bias
            weights = jnp.exp2((scores - top) * LOG_SCALE) * inverse
            product = mm_nt(picked_ref[1, :, cols], dout)
            dscore = (weights * (product - delta)).astype(jnp.bfloat16)
            grad = jnp.concatenate([mm(dscore, query) * SCORE_SCALE, mm(weights.astype(jnp.bfloat16), dout)], axis=1)
            grads.append(padded(grad.astype(jnp.bfloat16)))
        total = mm(chosen_ref[...], jnp.concatenate(grads, axis=0))
        keys_done[:, cols] = (centre_ref[0, :, cols] + total[:, :PAIR]).astype(jnp.bfloat16)
        values_done[:, cols] = (centre_ref[1, :, cols] + total[:, PAIR:]).astype(jnp.bfloat16)
        for index, (done, out_ref) in enumerate(((keys_done, keys_ref), (values_done, values_ref))):
            copy = pltpu.make_async_copy(done.at[:, cols], out_ref.at[:, cols], sems.at[2 * pair + index])
            copy.start()
            copies.append(copy)
    for copy in copies:
        copy.wait()


def call(kernel, name, out_shape, operands, scratch=(), smem=0, unused=0, gflop=0.1, out_space=pltpu.VMEM):
    specs = [pl.BlockSpec(memory_space=pltpu.SMEM)] * smem
    specs += [pl.BlockSpec(memory_space=pltpu.VMEM)] * (len(operands) - smem - unused)
    specs += [pl.BlockSpec(memory_space=pl.ANY)] * unused
    single = not isinstance(out_shape, list)
    outs = pl.BlockSpec(memory_space=out_space)
    return pl.pallas_call(
        kernel,
        out_shape=out_shape,
        in_specs=specs,
        out_specs=outs if single else [outs] * len(out_shape),
        scratch_shapes=list(scratch),
        compiler_params=pltpu.CompilerParams(vmem_limit_bytes=VMEM_LIMIT),
        cost_estimate=pl.CostEstimate(flops=int(gflop * 1e9), bytes_accessed=1 << 20, transcendentals=0),
        name=name,
    )(*operands)


def in_hbm(array):
    return pltpu.with_memory_space_constraint(array, pltpu.HBM)


def exchanged(blocks, stride):
    terms = list(blocks[:1])
    for distance in range(1, len(blocks)):
        route = [(tile, tile ^ (distance * stride)) for tile in range(lax.axis_size("tile"))]
        terms.append(lax.ppermute(blocks[distance], "tile", route))
    return terms


def with_partners(blocks, slots):
    tile_count = lax.axis_size("tile")
    routes = {s: [(tile, partner(tile, tile_count, s)) for tile in range(tile_count)] for s in slots}
    return {s: lax.ppermute(blocks[s], "tile", routes[s]) for s in slots}


def shards(queries, keys, values, grad_output, out_weight, rotations):
    tile_count = lax.axis_size("tile")
    token_count, features = queries.shape
    model = out_weight.shape[0]
    pairs = features // PAIR
    far = tile_count // NEAR
    chunk = model // tile_count
    heads = lax.axis_size("head")
    columns = tile_count // 4
    queries, keys, values, out_weight, rotations = (
        in_hbm(a) for a in (queries, keys, values, out_weight, rotations)
    )

    def bf16(*shape):
        return jax.ShapeDtypeStruct(shape, jnp.bfloat16)

    def f32(*shape):
        return jax.ShapeDtypeStruct(shape, jnp.float32)

    strip_types = [bf16(2, STRIP, features)] * 4
    picked = call(
        functools.partial(pick_kernel, columns), "pick_strips", strip_types, (rotations, keys, values), smem=1
    )
    grad_output, *picked = lax.optimization_barrier((grad_output, *picked))
    strips = with_partners(picked, (3, 2, 1, 0))
    strips = [strips[s] for s in range(4)]

    cotangents = [
        lax.ppermute(grad_output, "head", [((h + k) % heads, h) for h in range(heads)]) for k in range(1, heads)
    ]
    dout, dout_turned, turned, turned_sent = call(
        functools.partial(cotangent_kernel, heads),
        "cotangent",
        [bf16(CELLS, features), bf16(features, CELLS)] + [bf16(2, far, chunk, CELLS)] * 2,
        (in_hbm(grad_output), *cotangents, out_weight),
        gflop=1.0,
    )
    turned_arrived = exchanged((turned, turned_sent), 2)[1]
    part_types = [f32(pairs, 2, 2 * CELLS), f32(pairs, HEAD_DIM, 2 * CELLS)]
    raw_centre, stats_centre, sums_centre, product_centre, queries, keys = call(
        centre_kernel,
        "centre",
        [f32(pairs, CELLS, 2 * CELLS)] + part_types + [f32(pairs, CELLS, 2 * CELLS)] + [bf16(CELLS, features)] * 2,
        (queries, keys, values, dout),
        scratch=[pltpu.VMEM((CELLS, CELLS), jnp.float32)],
        gflop=3.0,
    )
    strip_scratch = [pltpu.VMEM((STRIP, CELLS), jnp.float32)]
    raw_columns, stats_columns, sums_columns, product_columns = call(
        column_kernel,
        "columns",
        [f32(pairs, STRIP, 2 * CELLS)] + part_types + [f32(pairs, STRIP, 2 * CELLS)],
        (strips[2], strips[3], queries, dout),
        scratch=strip_scratch,
        gflop=2.0,
    )
    raw_rows, attention, rows, factors = call(
        row_kernel,
        "rows",
        [f32(pairs, STRIP, 2 * CELLS), bf16(CELLS, features)] + [f32(k, 2 * pairs, CELLS) for k in (3, 2)],
        (strips[0], strips[1], queries, dout_turned, stats_centre, sums_centre, stats_columns, sums_columns),
        scratch=strip_scratch,
    )
    attention_arrived = exchanged((attention, attention), 2)[1]
    rims = call(
        functools.partial(rim_kernel, columns),
        "rims",
        [bf16(2 * STRIP + 16, features)] * 4,
        (queries, dout, rows, turned_arrived),
        unused=1,
    )
    rims_arrived = with_partners(rims, (3, 2, 1, 0))
    kept, sent = call(
        partial_kernel,
        "partial",
        [f32(far, chunk, features), bf16(far, chunk, features)],
        (attention, attention_arrived, turned, turned_arrived, rims[0]),
        unused=1,
    )
    terms = exchanged((kept, sent), 1)
    grad_queries, centre = call(
        backward_kernel,
        "backward",
        [bf16(CELLS, features), f32(2, CELLS, features)],
        (
            *strips[::-1], queries, keys, dout, raw_centre, raw_columns, raw_rows, product_centre, product_columns,
            rows, factors, sent,
        ),
        unused=1,
        gflop=3.0,
    )
    stride = NEAR
    while stride < tile_count:
        ways = min(NEAR, tile_count // stride)
        sums = call(
            functools.partial(sum_kernel, len(terms)),
            "plane_sum",
            [bf16(tile_count // stride // ways, chunk, features)] * ways,
            (*terms, centre),
            unused=1,
        )
        terms = exchanged(sums, stride)
        stride *= ways

    grad_keys, grad_values = call(
        functools.partial(side_kernel, columns),
        "sides",
        [bf16(CELLS, features)] * 2,
        (rotations, centre, *picked, *(rims_arrived[s] for s in range(4))),
        scratch=[pltpu.VMEM((CELLS, 4 * LANES), jnp.bfloat16), pltpu.VMEM((STRIP, LANES), jnp.float32)]
        + [pltpu.VMEM((CELLS, features), jnp.bfloat16)] * 2
        + [pltpu.SemaphoreType.DMA((2 * pairs,))],
        smem=1,
        gflop=3.0,
        out_space=pl.ANY,
    )
    grad_out_weight = call(
        functools.partial(weight_kernel, 1.0 / math.sqrt(token_count * tile_count)),
        "weight_sum",
        f32(chunk, features),
        terms,
    )
    return (grad_queries, grad_keys, grad_values, grad_out_weight)


def solution(mesh):
    placed = (
        P("tile", "head"),
        P("tile", "head"),
        P("tile", "head"),
        P("tile", "head"),
        P(None, "head"),
        P("tile", None),
    )
    return jax.shard_map(
        shards,
        mesh=mesh,
        in_specs=placed,
        out_specs=(P("tile", "head"), P("tile", "head"), P("tile", "head"), P("tile", "head")),
        check_vma=False,
    )
```

```python
import functools
import math

import jax
import jax.numpy as jnp
from jax import lax
from jax.experimental import pallas as pl
from jax.experimental.pallas import tpu as pltpu
from jax.sharding import PartitionSpec as P

HEAD_DIM = 64
RADIUS = 6
SIDE = 16
CELLS = SIDE * SIDE
STRIP = RADIUS * SIDE
NEAR = 4
LANES = 128
PAIR = 2 * HEAD_DIM
VMEM_LIMIT = 32 * 1024 * 1024
NT = (((1,), (1,)), ((), ()))


def mm(a, b):
    return jnp.dot(a, b, preferred_element_type=jnp.float32)


def mm_nt(a, b):
    return lax.dot_general(a, b, NT, preferred_element_type=jnp.float32)


def strip_token(side_index, rotation, cell):
    turn = lax.rem(side_index + 6 - rotation, 4)
    depth = cell >> 4
    along = cell & (SIDE - 1)
    far = SIDE - 1 - along
    near_rim = RADIUS - 1 - depth
    far_rim = SIDE - RADIUS + depth
    row = jnp.where(turn == 0, far_rim, jnp.where(turn == 1, along, jnp.where(turn == 2, near_rim, far)))
    col = jnp.where(turn == 0, along, jnp.where(turn == 1, near_rim, jnp.where(turn == 2, far, far_rim)))
    return row * SIDE + col


def slot_side(slot, columns):
    tile = lax.axis_index("tile")
    if slot < 2:
        return jnp.where((tile + slot) & 1 == 0, 1, 3)
    return jnp.where((lax.div(tile, columns) + slot) & 1 == 0, 2, 0)


def partner(tile, tile_count, slot):
    columns = tile_count // 4
    if slot < 2:
        return (tile + (1 if (tile + slot) % 2 == 0 else -1)) % tile_count
    return (tile + (columns if (tile // columns + slot) % 2 == 0 else -columns)) % tile_count


def pick_kernel(columns, rotations_ref, keys_ref, values_ref, *out_refs):
    cell = lax.broadcasted_iota(jnp.int32, (STRIP, CELLS), 0)
    token = lax.broadcasted_iota(jnp.int32, (STRIP, CELLS), 1)
    for slot, out_ref in enumerate(out_refs):
        side = slot_side(slot, columns)
        wanted = strip_token(side, rotations_ref[0, side], cell)
        chosen = jnp.where(token == wanted, 1.0, 0.0).astype(jnp.bfloat16)
        out_ref[0] = mm(chosen, keys_ref[...]).astype(jnp.bfloat16)
        out_ref[1] = mm(chosen, values_ref[...]).astype(jnp.bfloat16)


def weight_kernel(scale, *refs):
    total = refs[0][0].astype(jnp.float32)
    for ref in refs[1:-1]:
        total += ref[0].astype(jnp.float32)
    refs[-1][...] = total * scale


def partial_kernel(gathered_ref, arrived_ref, turned_ref, early_ref, unused_ref, kept_ref, sent_ref):
    rows = turned_ref.shape[1] * turned_ref.shape[2]
    for index, out_ref in enumerate((kept_ref, sent_ref)):
        total = mm(turned_ref[index].reshape(rows, CELLS), gathered_ref[:CELLS])
        total += mm(early_ref[index * rows : (index + 1) * rows], arrived_ref[:CELLS])
        out_ref[...] = total.astype(out_ref.dtype).reshape(out_ref.shape)


def sum_kernel(count, *refs):
    terms, outs = refs[:count], refs[count + 1 :]
    for q in range(terms[0].shape[0]):
        total = terms[0][q].astype(jnp.float32)
        for ref in terms[1:]:
            total += ref[q].astype(jnp.float32)
        outs[q % len(outs)][q // len(outs)] = total.astype(jnp.bfloat16)


def rim_token(side_index, place):
    depth = place >> 4
    along = place & (SIDE - 1)
    last = SIDE - 1
    north, east, south = side_index == 0, side_index == 1, side_index == 2
    row = jnp.where(north, depth, jnp.where(east, along, jnp.where(south, last - depth, last - along)))
    col = jnp.where(north, along, jnp.where(east, last - depth, jnp.where(south, last - along, depth)))
    return row * SIDE + col


def split(exact, count):
    parts = []
    for _ in range(count):
        part = exact.astype(jnp.bfloat16).astype(jnp.float32)
        parts.append(part)
        exact = exact - part
    return parts


PARTS = (3, 2, 2)


def packed_statistics(rows_ref):
    parts = [part for kind, count in enumerate(PARTS) for part in split(rows_ref[kind], count)]
    filler = jnp.zeros((16 - 2 * len(parts), CELLS), jnp.float32)
    rows = [
        jnp.concatenate([part[2 * pair : 2 * pair + 2] for part in parts] + [filler], axis=0)
        for pair in range(rows_ref.shape[1] // 2)
    ]
    return jnp.concatenate(rows, axis=0).astype(jnp.bfloat16)


def put_statistics(packed, chosen, out_ref):
    spread = mm_nt(packed, chosen).astype(jnp.bfloat16)
    for pair in range(packed.shape[0] // 16):
        out_ref[:, pair * PAIR : (pair + 1) * PAIR] = spread[16 * pair : 16 * pair + 16]


def rim_choice(slot, columns):
    place = lax.broadcasted_iota(jnp.int32, (LANES, CELLS), 0)
    token = lax.broadcasted_iota(jnp.int32, (LANES, CELLS), 1)
    wanted = rim_token(slot_side(slot, columns), place)
    return jnp.where((token == wanted) & (place < STRIP), 1.0, 0.0).astype(jnp.bfloat16)


def rim_rows(features):
    return [(block, 2 * STRIP * block) for block in range(features // CELLS)]


def cotangent_kernel(heads, columns, *refs):
    blocks, (out_weight_ref, query_ref), outs = refs[:heads], refs[heads : heads + 2], refs[heads + 2 :]
    dout_ref, dout_turned_ref, turned_ref, early_ref, turned_sent_ref = outs
    head = lax.axis_index("head")
    tile = lax.axis_index("tile")
    _, far, chunk, _ = turned_ref.shape
    width = blocks[0].shape[1]
    total = None
    for distance, block_ref in enumerate(blocks):
        owner = lax.rem(head + distance, heads)
        start = pl.multiple_of(owner * width, width)
        block = block_ref[...]
        term = mm(block, out_weight_ref[pl.ds(start, width), :])
        total = term if total is None else total + term
        turned = block.T
        first = owner * (width // chunk)
        for index in range(width // chunk):
            target = (first + index) ^ tile
            rows = turned[index * chunk : (index + 1) * chunk]
            for parity, out_ref in enumerate((turned_ref, turned_sent_ref)):

                @pl.when(target & 1 == parity)
                def _():
                    out_ref[(target & 3) >> 1, target >> 2] = rows

    dout = total.astype(jnp.bfloat16)
    dout_ref[...] = dout
    dout_turned_ref[...] = dout.T
    for index in range(2 * far):
        early_ref[index * chunk : (index + 1) * chunk] = turned_sent_ref[index // far, index % far]
    chosen = rim_choice(0, columns)[:STRIP]
    for block, start in rim_rows(width):
        lanes = slice(block * CELLS, (block + 1) * CELLS)
        start += 2 * far * chunk
        early_ref[start : start + STRIP] = mm(chosen, query_ref[:, lanes]).astype(jnp.bfloat16)
        early_ref[start + STRIP : start + 2 * STRIP] = mm(chosen, dout[:, lanes]).astype(jnp.bfloat16)


def rim_kernel(columns, query_ref, dout_ref, rows_ref, *rim_refs):
    packed = packed_statistics(rows_ref)
    for slot, rim_ref in enumerate(rim_refs, 1):
        chosen = rim_choice(slot, columns)
        rim_ref[:STRIP] = mm(chosen[:STRIP], query_ref[...]).astype(jnp.bfloat16)
        rim_ref[STRIP : 2 * STRIP] = mm(chosen[:STRIP], dout_ref[...]).astype(jnp.bfloat16)
        put_statistics(packed, chosen, rim_ref.at[2 * STRIP :])


def window(cell_row, cell_col, query):
    query_row = (query >> 4) + RADIUS
    query_col = (query & (SIDE - 1)) + RADIUS
    near = (jnp.abs(cell_row - query_row) <= RADIUS) & (jnp.abs(cell_col - query_col) <= RADIUS)
    return jnp.where(near, 0.0, -1e30)


def centre_bias(bias_ref):
    query = lax.broadcasted_iota(jnp.int32, (CELLS, CELLS), 1)
    cell = lax.broadcasted_iota(jnp.int32, (CELLS, CELLS), 0)
    bias_ref[...] = window((cell >> 4) + RADIUS, (cell & (SIDE - 1)) + RADIUS, query)


def strip_bias(kind, bias_ref):
    query = lax.broadcasted_iota(jnp.int32, (STRIP, CELLS), 1)
    cell = lax.broadcasted_iota(jnp.int32, (STRIP, CELLS), 0)
    depth = cell >> 4
    along = cell & (SIDE - 1)
    last = SIDE + 2 * RADIUS - 1
    if kind:
        first, second = (last - RADIUS - along, depth), (RADIUS + along, last - depth)
    else:
        first, second = (depth, RADIUS + along), (last - depth, last - RADIUS - along)
    in_first = first_half(query, kind)
    row = jnp.where(in_first, first[0], second[0])
    col = jnp.where(in_first, first[1], second[1])
    bias_ref[...] = window(row, col, query)


def first_half(query, kind):
    return (query & (SIDE - 1)) < SIDE // 2 if kind else query < CELLS // 2


def one_head(block, head):
    lane = lax.broadcasted_iota(jnp.int32, block.shape, 1)
    kept = (lane >= HEAD_DIM) if head else (lane < HEAD_DIM)
    return jnp.where(kept, block, jnp.zeros_like(block))


def halves(block, kind):
    kept = first_half(lax.broadcasted_iota(jnp.int32, block.shape, 0), kind)
    zero = jnp.zeros_like(block)
    return jnp.concatenate([jnp.where(kept, block, zero), jnp.where(kept, zero, block)], axis=1)


def by_half(stacked, kind):
    rows = stacked.shape[0] // 2
    kept = first_half(lax.broadcasted_iota(jnp.int32, (rows, CELLS), 1), kind)
    return jnp.where(kept, stacked[:rows], stacked[rows:])


def side_blocks(strips, part, kind, cols):
    tile = lax.axis_index("tile")
    second, first = strips
    straight = (tile if kind else lax.div(tile, lax.axis_size("tile") // 4)) & 1 == 0
    first, second = first[part, :, cols], second[part, :, cols]
    return jnp.where(straight, first, second), jnp.where(straight, second, first)


def side_cells(strips, part, kind, cols):
    return jnp.concatenate(side_blocks(strips, part, kind, cols), axis=1)


def halves(block, kind):
    kept = first_half(lax.broadcasted_iota(jnp.int32, block.shape, 0), kind)
    zero = jnp.zeros_like(block)
    return jnp.concatenate([jnp.where(kept, block, zero), jnp.where(kept, zero, block)], axis=1)


def by_half(stacked, kind):
    rows = stacked.shape[0] // 2
    kept = first_half(lax.broadcasted_iota(jnp.int32, (rows, CELLS), 1), kind)
    return jnp.where(kept, stacked[:rows], stacked[rows:])


def side_blocks(strips, part, kind, cols):
    tile = lax.axis_index("tile")
    second, first = strips
    straight = (tile if kind else lax.div(tile, lax.axis_size("tile") // 4)) & 1 == 0
    first, second = first[part, :, cols], second[part, :, cols]
    return jnp.where(straight, first, second), jnp.where(straight, second, first)


def side_cells(strips, part, kind, cols):
    return jnp.concatenate(side_blocks(strips, part, kind, cols), axis=1)


def side_products(cells, rows_head):
    return [mm_nt(cells[kind], halves(rows_head, kind)) for kind in range(2)]


def turned_sides(strips, part, kind, cols):
    return [block.T for block in side_blocks(strips, part, kind, cols)]


def pair_cols(pair):
    return pl.ds(pl.multiple_of(pair * PAIR, PAIR), PAIR)


def head_rows(turned, head):
    return turned[head * HEAD_DIM : (head + 1) * HEAD_DIM]


def over_side(turned, head, kind, sides):
    return by_half(mm(jnp.concatenate([head_rows(t, head) for t in turned], axis=0), sides), kind)


SCORE_SCALE = HEAD_DIM ** (-0.5)
LOG_SCALE = SCORE_SCALE * math.log2(math.e)


def lanes_of(head):
    return slice(head * CELLS, (head + 1) * CELLS)


def centre_kernel(
    query_ref, key_ref, value_ref, dout_ref,
    raw_ref, stats_ref, sums_ref, product_ref, query_out, key_out, bias_ref,
):
    centre_bias(bias_ref)

    def step(pair, carry):
        cols = pair_cols(pair)
        query, key, value, dout = (ref[:, cols] for ref in (query_ref, key_ref, value_ref, dout_ref))
        turned = value.T
        for head in range(2):
            lanes = lanes_of(head)
            scores = mm_nt(key, one_head(query, head)) + bias_ref[...]
            top = jnp.max(scores, axis=0, keepdims=True)
            raw = jnp.exp2((scores - top) * LOG_SCALE)
            raw_ref[pair, :, lanes] = raw
            stats_ref[pair, 0:1, lanes] = top
            stats_ref[pair, 1:2, lanes] = jnp.sum(raw, axis=0, keepdims=True)
            sums_ref[pair, :, lanes] = mm(head_rows(turned, head), raw.astype(jnp.bfloat16))
            product_ref[pair, :, lanes] = mm_nt(value, one_head(dout, head))
        query_out[:, cols] = query
        key_out[:, cols] = key
        return carry

    lax.fori_loop(0, raw_ref.shape[0], step, 0)


def column_kernel(
    first_ref, second_ref, query_ref, dout_ref, raw_ref, stats_ref, sums_ref, product_ref, bias_ref
):
    strips = (first_ref, second_ref)
    strip_bias(0, bias_ref)

    def step(pair, carry):
        cols = pair_cols(pair)
        keys = side_cells(strips, 0, 0, cols)
        values = side_cells(strips, 1, 0, cols)
        turned = turned_sides(strips, 1, 0, cols)
        for head in range(2):
            lanes = lanes_of(head)
            scores = mm_nt(keys, halves(one_head(query_ref[:, cols], head), 0)) + bias_ref[...]
            top = jnp.max(scores, axis=0, keepdims=True)
            raw = jnp.exp2((scores - top) * LOG_SCALE)
            raw_ref[pair, :, lanes] = raw
            stats_ref[pair, 0:1, lanes] = top
            stats_ref[pair, 1:2, lanes] = jnp.sum(raw, axis=0, keepdims=True)
            sums_ref[pair, :, lanes] = over_side(turned, head, 0, raw.astype(jnp.bfloat16))
            product_ref[pair, :, lanes] = mm_nt(values, halves(one_head(dout_ref[:, cols], head), 0))
        return carry

    lax.fori_loop(0, raw_ref.shape[0], step, 0)


def row_kernel(
    columns, first_ref, second_ref, query_ref, dout_turned_ref, centre_stats_ref, centre_sums_ref, stats_ref, sums_ref,
    raw_ref, gathered_ref, rows_ref, factors_ref, bias_ref,
):
    strips = (first_ref, second_ref)
    strip_bias(1, bias_ref)

    def step(pair, carry):
        cols = pair_cols(pair)
        keys = side_cells(strips, 0, 1, cols)
        turned = turned_sides(strips, 1, 1, cols)
        parts = []
        for head in range(2):
            lanes = lanes_of(head)
            scores = mm_nt(keys, halves(one_head(query_ref[:, cols], head), 1)) + bias_ref[...]
            tops = [ref[pair, 0:1, lanes] for ref in (centre_stats_ref, stats_ref)]
            top = jnp.maximum(jnp.max(scores, axis=0, keepdims=True), jnp.maximum(*tops))
            raw = jnp.exp2((scores - top) * LOG_SCALE)
            raw_ref[pair, :, lanes] = raw
            lifted = [jnp.exp2((t - top) * LOG_SCALE) for t in tops]
            total = jnp.sum(raw, axis=0, keepdims=True)
            total += lifted[0] * centre_stats_ref[pair, 1:2, lanes] + lifted[1] * stats_ref[pair, 1:2, lanes]
            inverse = 1.0 / total
            factors = [l * inverse for l in lifted]
            part = over_side(turned, head, 1, raw.astype(jnp.bfloat16)) * inverse
            part += factors[0] * centre_sums_ref[pair, :, lanes] + factors[1] * sums_ref[pair, :, lanes]
            parts.append(part)
            place = pl.ds(2 * pair + head, 1)
            features = pl.ds(pl.multiple_of((2 * pair + head) * HEAD_DIM, HEAD_DIM), HEAD_DIM)
            product = dout_turned_ref[features, :].astype(jnp.float32) * part
            rows_ref[0, place, :] = top
            rows_ref[1, place, :] = inverse
            rows_ref[2, place, :] = jnp.sum(product, axis=0, keepdims=True)
            factors_ref[0, place, :] = factors[0]
            factors_ref[1, place, :] = factors[1]
        gathered_ref[:CELLS, cols] = jnp.concatenate(parts, axis=0).T.astype(jnp.bfloat16)
        return carry

    lax.fori_loop(0, raw_ref.shape[0], step, 0, unroll=True)
    put_statistics(packed_statistics(rows_ref), rim_choice(0, columns), gathered_ref.at[CELLS:])


def backward_kernel(
    fourth_ref, third_ref, second_ref, first_ref, query_ref, key_ref, dout_ref, centre_raw_ref, column_raw_ref,
    row_raw_ref, centre_product_ref, column_product_ref, rows_ref, factors_ref, unused_ref,
    grad_query_ref, centre_ref,
):
    columns, rows = (third_ref, fourth_ref), (first_ref, second_ref)

    def step(pair, carry):
        cols = pair_cols(pair)
        query = query_ref[:, cols]
        dout = dout_ref[:, cols]
        turned_centre = key_ref[:, cols].T
        turned_columns = turned_sides(columns, 0, 0, cols)
        turned_rows = turned_sides(rows, 0, 1, cols)
        row_values = side_cells(rows, 1, 1, cols)
        parts = []
        centre_scores = []
        centre_weights = []
        for head in range(2):
            lanes = lanes_of(head)
            place = pl.ds(2 * pair + head, 1)
            delta = rows_ref[2, place, :]
            row_product = mm_nt(row_values, halves(one_head(dout, head), 1))

            def dscore(weights, product):
                return (weights * (product - delta)).astype(jnp.bfloat16)

            weights = centre_raw_ref[pair, :, lanes] * factors_ref[0, place, :]
            centre_weights.append(weights.astype(jnp.bfloat16))
            centre_scores.append(dscore(weights, centre_product_ref[pair, :, lanes]))
            column_weights = column_raw_ref[pair, :, lanes] * factors_ref[1, place, :]
            column_score = dscore(column_weights, column_product_ref[pair, :, lanes])
            row_score = dscore(row_raw_ref[pair, :, lanes] * rows_ref[1, place, :], row_product)
            part = mm(head_rows(turned_centre, head), centre_scores[-1])
            part += over_side(turned_columns, head, 0, column_score) + over_side(turned_rows, head, 1, row_score)
            parts.append(part)
        grad_query = jnp.concatenate(parts, axis=0).T * SCORE_SCALE
        grad_query_ref[:, cols] = grad_query.astype(jnp.bfloat16)
        grad_key, grad_value = joint_mm(
            jnp.concatenate(centre_scores, axis=1),
            jnp.concatenate(centre_weights, axis=1),
            both_heads(query),
            both_heads(dout),
        )
        centre_ref[0, :, cols] = grad_key * SCORE_SCALE
        centre_ref[1, :, cols] = grad_value
        return carry

    lax.fori_loop(0, centre_raw_ref.shape[0], step, 0)


def joint_mm(first, second, first_rows, second_rows):
    rows = first.shape[0]
    product = mm(jnp.concatenate([first, second], axis=0), jnp.concatenate([first_rows, second_rows], axis=1))
    return product[:rows, :PAIR], product[rows:, PAIR:]


def both_heads(block):
    return jnp.concatenate([one_head(block, head) for head in range(2)], axis=0)


def padded(block):
    return jnp.concatenate([block, jnp.zeros((LANES - block.shape[0], block.shape[1]), block.dtype)], axis=0)


def statistics(rows):
    first = 0
    for count in PARTS:
        heads = []
        for head in range(2):
            parts = [rows[2 * index + head : 2 * index + head + 1] for index in range(first, first + count)]
            heads.append(functools.reduce(jnp.add, parts))
        first += count
        yield jnp.concatenate(heads, axis=1)


def side_kernel(columns, rotations_ref, centre_ref, *refs):
    picked, early_ref, gathered_ref, rims = refs[:4], refs[4], refs[5], refs[6:9]
    keys_ref, values_ref, chosen_ref, bias_ref, keys_done, values_done, sems = refs[9:]
    cell = lax.broadcasted_iota(jnp.int32, (STRIP, LANES), 0)
    query = lax.broadcasted_iota(jnp.int32, (STRIP, LANES), 1)
    near = jnp.abs((cell & (SIDE - 1)) - (query & (SIDE - 1))) <= RADIUS
    near = near & ((cell >> 4) >= (query >> 4)) & (query < STRIP)
    bias_ref[...] = jnp.where(near, 0.0, -1e30)
    token = lax.broadcasted_iota(jnp.int32, (CELLS, LANES), 0)
    place = lax.broadcasted_iota(jnp.int32, (CELLS, LANES), 1)
    for slot in range(4):
        side = slot_side(slot, columns)
        wanted = jnp.where(place < STRIP, strip_token(side, rotations_ref[0, side], place), -1)
        chosen = jnp.where(token == wanted, 1.0, 0.0).astype(jnp.bfloat16)
        chosen_ref[:, slot * LANES : (slot + 1) * LANES] = chosen

    copies = []
    for pair in range(keys_ref.shape[1] // PAIR):
        cols = slice(pair * PAIR, (pair + 1) * PAIR)
        grads = []
        bias = jnp.concatenate([bias_ref[...]] * 2, axis=1)
        start = early_ref.shape[0] - 2 * STRIP * (keys_ref.shape[1] // CELLS - pair * PAIR // CELLS)
        lanes = slice(pair * PAIR % CELLS, pair * PAIR % CELLS + PAIR)
        early = (
            early_ref[start : start + STRIP, lanes],
            early_ref[start + STRIP : start + 2 * STRIP, lanes],
            gathered_ref[CELLS:, cols],
        )
        late = [(ref[:STRIP, cols], ref[STRIP : 2 * STRIP, cols], ref[2 * STRIP :, cols]) for ref in rims]
        for picked_ref, (query, dout, rows) in zip(picked, [early] + late):
            query = both_heads(padded(query))
            dout = both_heads(padded(dout))
            top, inverse, delta = statistics(rows.astype(jnp.float32))
            scores = mm_nt(picked_ref[0, :, cols], query) + bias
            weights = jnp.exp2((scores - top) * LOG_SCALE) * inverse
            product = mm_nt(picked_ref[1, :, cols], dout)
            dscore = (weights * (product - delta)).astype(jnp.bfloat16)
            grad = jnp.concatenate([mm(dscore, query) * SCORE_SCALE, mm(weights.astype(jnp.bfloat16), dout)], axis=1)
            grads.append(padded(grad.astype(jnp.bfloat16)))
        total = mm(chosen_ref[...], jnp.concatenate(grads, axis=0))
        keys_done[:, cols] = (centre_ref[0, :, cols] + total[:, :PAIR]).astype(jnp.bfloat16)
        values_done[:, cols] = (centre_ref[1, :, cols] + total[:, PAIR:]).astype(jnp.bfloat16)
        for index, (done, out_ref) in enumerate(((keys_done, keys_ref), (values_done, values_ref))):
            copy = pltpu.make_async_copy(done.at[:, cols], out_ref.at[:, cols], sems.at[2 * pair + index])
            copy.start()
            copies.append(copy)
    for copy in copies:
        copy.wait()


def call(kernel, name, out_shape, operands, scratch=(), smem=0, unused=0, gflop=0.1, out_space=pltpu.VMEM):
    specs = [pl.BlockSpec(memory_space=pltpu.SMEM)] * smem
    specs += [pl.BlockSpec(memory_space=pltpu.VMEM)] * (len(operands) - smem - unused)
    specs += [pl.BlockSpec(memory_space=pl.ANY)] * unused
    single = not isinstance(out_shape, list)
    outs = pl.BlockSpec(memory_space=out_space)
    return pl.pallas_call(
        kernel,
        out_shape=out_shape,
        in_specs=specs,
        out_specs=outs if single else [outs] * len(out_shape),
        scratch_shapes=list(scratch),
        compiler_params=pltpu.CompilerParams(vmem_limit_bytes=VMEM_LIMIT),
        cost_estimate=pl.CostEstimate(flops=int(gflop * 1e9), bytes_accessed=1 << 20, transcendentals=0),
        name=name,
    )(*operands)


def in_hbm(array):
    return pltpu.with_memory_space_constraint(array, pltpu.HBM)


def exchanged(blocks, stride):
    terms = list(blocks[:1])
    for distance in range(1, len(blocks)):
        route = [(tile, tile ^ (distance * stride)) for tile in range(lax.axis_size("tile"))]
        terms.append(lax.ppermute(blocks[distance], "tile", route))
    return terms


def with_partners(blocks, slots):
    tile_count = lax.axis_size("tile")
    routes = {s: [(tile, partner(tile, tile_count, s)) for tile in range(tile_count)] for s in slots}
    return {s: lax.ppermute(blocks[s], "tile", routes[s]) for s in slots}


def shards(queries, keys, values, grad_output, out_weight, rotations):
    tile_count = lax.axis_size("tile")
    token_count, features = queries.shape
    model = out_weight.shape[0]
    pairs = features // PAIR
    far = tile_count // NEAR
    chunk = model // tile_count
    heads = lax.axis_size("head")
    columns = tile_count // 4
    queries, keys, values, out_weight, rotations = (
        in_hbm(a) for a in (queries, keys, values, out_weight, rotations)
    )

    def bf16(*shape):
        return jax.ShapeDtypeStruct(shape, jnp.bfloat16)

    def f32(*shape):
        return jax.ShapeDtypeStruct(shape, jnp.float32)

    strip_types = [bf16(2, STRIP, features)] * 4
    picked = call(
        functools.partial(pick_kernel, columns), "pick_strips", strip_types, (rotations, keys, values), smem=1
    )
    grad_output, *picked = lax.optimization_barrier((grad_output, *picked))
    strips = with_partners(picked, (3, 2, 1, 0))
    strips = [strips[s] for s in range(4)]

    cotangents = [
        lax.ppermute(grad_output, "head", [((h + k) % heads, h) for h in range(heads)]) for k in range(1, heads)
    ]
    early_rows = model // 2 + 2 * STRIP * (features // CELLS)
    dout, dout_turned, turned, early = call(
        functools.partial(cotangent_kernel, heads, columns),
        "cotangent",
        [bf16(CELLS, features), bf16(features, CELLS), bf16(2, far, chunk, CELLS), bf16(early_rows, CELLS)],
        (in_hbm(grad_output), *cotangents, out_weight, queries),
        scratch=[pltpu.VMEM((2, far, chunk, CELLS), jnp.bfloat16)],
        gflop=1.0,
    )
    early_arrived = with_partners({0: early}, (0,))[0]
    part_types = [f32(pairs, 2, 2 * CELLS), f32(pairs, HEAD_DIM, 2 * CELLS)]
    raw_centre, stats_centre, sums_centre, product_centre, queries, keys = call(
        centre_kernel,
        "centre",
        [f32(pairs, CELLS, 2 * CELLS)] + part_types + [f32(pairs, CELLS, 2 * CELLS)] + [bf16(CELLS, features)] * 2,
        (queries, keys, values, dout),
        scratch=[pltpu.VMEM((CELLS, CELLS), jnp.float32)],
        gflop=3.0,
    )
    strip_scratch = [pltpu.VMEM((STRIP, CELLS), jnp.float32)]
    raw_columns, stats_columns, sums_columns, product_columns = call(
        column_kernel,
        "columns",
        [f32(pairs, STRIP, 2 * CELLS)] + part_types + [f32(pairs, STRIP, 2 * CELLS)],
        (strips[2], strips[3], queries, dout),
        scratch=strip_scratch,
    )
    raw_rows, gathered, rows, factors = call(
        functools.partial(row_kernel, columns),
        "rows",
        [f32(pairs, STRIP, 2 * CELLS), bf16(CELLS + 16, features)] + [f32(k, 2 * pairs, CELLS) for k in (3, 2)],
        (strips[0], strips[1], queries, dout_turned, stats_centre, sums_centre, stats_columns, sums_columns),
        scratch=strip_scratch,
    )
    gathered_arrived = with_partners({0: gathered}, (0,))[0]
    rims = call(
        functools.partial(rim_kernel, columns),
        "rims",
        [bf16(2 * STRIP + 16, features)] * 3,
        (queries, dout, rows),
    )
    rims = dict(enumerate(rims, 1))
    rims_arrived = with_partners(rims, (3, 2))
    kept, sent = call(
        partial_kernel,
        "partial",
        [f32(far, chunk, features), bf16(far, chunk, features)],
        (gathered, gathered_arrived, turned, early_arrived, rims[3]),
        unused=1,
    )
    terms = exchanged((kept, sent), 2)
    grad_queries, centre = call(
        backward_kernel,
        "backward",
        [bf16(CELLS, features), f32(2, CELLS, features)],
        (
            *strips[::-1], queries, keys, dout, raw_centre, raw_columns, raw_rows, product_centre, product_columns,
            rows, factors, sent,
        ),
        unused=1,
        gflop=3.0,
    )
    rims[1], centre = lax.optimization_barrier((rims[1], centre))
    rims_arrived |= with_partners(rims, (1,))
    stride = NEAR
    while stride < tile_count:
        ways = min(NEAR, tile_count // stride)
        sums = call(
            functools.partial(sum_kernel, len(terms)),
            "plane_sum",
            [bf16(tile_count // stride // ways, chunk, features)] * ways,
            (*terms, centre),
            unused=1,
        )
        terms = exchanged(sums, stride)
        stride *= ways

    grad_keys, grad_values = call(
        functools.partial(side_kernel, columns),
        "sides",
        [bf16(CELLS, features)] * 2,
        (rotations, centre, *picked, early_arrived, gathered_arrived, *(rims_arrived[s] for s in (1, 2, 3))),
        scratch=[pltpu.VMEM((CELLS, 4 * LANES), jnp.bfloat16), pltpu.VMEM((STRIP, LANES), jnp.float32)]
        + [pltpu.VMEM((CELLS, features), jnp.bfloat16)] * 2
        + [pltpu.SemaphoreType.DMA((2 * pairs,))],
        smem=1,
        gflop=3.0,
        out_space=pl.ANY,
    )
    grad_out_weight = call(
        functools.partial(weight_kernel, 1.0 / math.sqrt(token_count * tile_count)),
        "weight_sum",
        f32(chunk, features),
        terms,
    )
    return (grad_queries, grad_keys, grad_values, grad_out_weight)


def solution(mesh):
    placed = (
        P("tile", "head"),
        P("tile", "head"),
        P("tile", "head"),
        P("tile", "head"),
        P(None, "head"),
        P("tile", None),
    )
    return jax.shard_map(
        shards,
        mesh=mesh,
        in_specs=placed,
        out_specs=(P("tile", "head"), P("tile", "head"), P("tile", "head"), P("tile", "head")),
        check_vma=False,
    )
```

```python
import functools
import math

import jax
import jax.numpy as jnp
from jax import lax
from jax.experimental import pallas as pl
from jax.experimental.pallas import tpu as pltpu
from jax.sharding import PartitionSpec as P

HEAD_DIM = 64
RADIUS = 6
SIDE = 16
CELLS = SIDE * SIDE
STRIP = RADIUS * SIDE
NEAR = 4
LANES = 128
PAIR = 2 * HEAD_DIM
VMEM_LIMIT = 32 * 1024 * 1024
NT = (((1,), (1,)), ((), ()))


def mm(a, b):
    return jnp.dot(a, b, preferred_element_type=jnp.float32)


def mm_nt(a, b):
    return lax.dot_general(a, b, NT, preferred_element_type=jnp.float32)


def strip_token(side_index, rotation, cell):
    turn = lax.rem(side_index + 6 - rotation, 4)
    depth = cell >> 4
    along = cell & (SIDE - 1)
    far = SIDE - 1 - along
    near_rim = RADIUS - 1 - depth
    far_rim = SIDE - RADIUS + depth
    row = jnp.where(turn == 0, far_rim, jnp.where(turn == 1, along, jnp.where(turn == 2, near_rim, far)))
    col = jnp.where(turn == 0, along, jnp.where(turn == 1, near_rim, jnp.where(turn == 2, far, far_rim)))
    return row * SIDE + col


def slot_side(slot, columns):
    tile = lax.axis_index("tile")
    if slot < 2:
        return jnp.where((tile + slot) & 1 == 0, 1, 3)
    return jnp.where((lax.div(tile, columns) + slot) & 1 == 0, 2, 0)


def partner(tile, tile_count, slot):
    columns = tile_count // 4
    if slot < 2:
        return (tile + (1 if (tile + slot) % 2 == 0 else -1)) % tile_count
    return (tile + (columns if (tile // columns + slot) % 2 == 0 else -columns)) % tile_count


def pick_kernel(columns, rotations_ref, keys_ref, values_ref, *out_refs):
    cell = lax.broadcasted_iota(jnp.int32, (STRIP, CELLS), 0)
    token = lax.broadcasted_iota(jnp.int32, (STRIP, CELLS), 1)
    for slot, out_ref in enumerate(out_refs):
        side = slot_side(slot, columns)
        wanted = strip_token(side, rotations_ref[0, side], cell)
        chosen = jnp.where(token == wanted, 1.0, 0.0).astype(jnp.bfloat16)
        out_ref[0] = mm(chosen, keys_ref[...]).astype(jnp.bfloat16)
        out_ref[1] = mm(chosen, values_ref[...]).astype(jnp.bfloat16)


def weight_kernel(scale, *refs):
    total = refs[0][0].astype(jnp.float32)
    for ref in refs[1:-1]:
        total += ref[0].astype(jnp.float32)
    refs[-1][...] = total * scale


def partial_kernel(attention_ref, arrived_ref, turned_ref, turned_arrived_ref, unused_ref, kept_ref, sent_ref):
    for index, out_ref in enumerate((kept_ref, sent_ref)):
        total = None
        for turned_part, attention_part in ((turned_ref, attention_ref), (turned_arrived_ref, arrived_ref)):
            turned = turned_part[index]
            turned = turned.reshape(turned.shape[0] * turned.shape[1], turned.shape[2])
            term = mm(turned, attention_part[...])
            total = term if total is None else total + term
        out_ref[...] = total.astype(out_ref.dtype).reshape(out_ref.shape)


def sum_kernel(count, *refs):
    terms, outs = refs[:count], refs[count + 1 :]
    for q in range(terms[0].shape[0]):
        total = terms[0][q].astype(jnp.float32)
        for ref in terms[1:]:
            total += ref[q].astype(jnp.float32)
        outs[q % len(outs)][q // len(outs)] = total.astype(jnp.bfloat16)


def rim_token(side_index, place):
    depth = place >> 4
    along = place & (SIDE - 1)
    last = SIDE - 1
    north, east, south = side_index == 0, side_index == 1, side_index == 2
    row = jnp.where(north, depth, jnp.where(east, along, jnp.where(south, last - depth, last - along)))
    col = jnp.where(north, along, jnp.where(east, last - depth, jnp.where(south, last - along, depth)))
    return row * SIDE + col


def cotangent_kernel(heads, *refs):
    blocks, out_weight_ref, outs = refs[:heads], refs[heads], refs[heads + 1 :]
    dout_ref, dout_turned_ref, turned_ref, turned_sent_ref = outs
    head = lax.axis_index("head")
    axis = head & 1
    tile = lax.axis_index("tile")
    chunk = turned_ref.shape[2]
    width = blocks[0].shape[1]
    total = None
    for distance, block_ref in enumerate(blocks):
        owner = lax.rem(head + distance, heads)
        start = pl.multiple_of(owner * width, width)
        block = block_ref[...]
        term = mm(block, out_weight_ref[pl.ds(start, width), :])
        total = term if total is None else total + term
        turned = block.T
        first = owner * (width // chunk)
        for index in range(width // chunk):
            target = (first + index) ^ tile
            rows = turned[index * chunk : (index + 1) * chunk]
            for parity, out_ref in enumerate((turned_ref, turned_sent_ref)):

                @pl.when((target >> axis) & 1 == parity)
                def _():
                    out_ref[(target >> (1 - axis)) & 1, target >> 2] = rows

    dout = total.astype(jnp.bfloat16)
    dout_ref[...] = dout
    dout_turned_ref[...] = dout.T


def split(exact, count):
    parts = []
    for _ in range(count):
        part = exact.astype(jnp.bfloat16).astype(jnp.float32)
        parts.append(part)
        exact = exact - part
    return parts


PARTS = (3, 2, 2)


def rim_kernel(columns, query_ref, dout_ref, rows_ref, unused_ref, *rim_refs):
    place = lax.broadcasted_iota(jnp.int32, (LANES, CELLS), 0)
    token = lax.broadcasted_iota(jnp.int32, (LANES, CELLS), 1)
    parts = [part for kind, count in enumerate(PARTS) for part in split(rows_ref[kind], count)]
    pairs = rows_ref.shape[1] // 2
    filler = jnp.zeros((16 - 2 * len(parts), CELLS), jnp.float32)
    rows = [
        jnp.concatenate([part[2 * pair : 2 * pair + 2] for part in parts] + [filler], axis=0) for pair in range(pairs)
    ]
    rows = jnp.concatenate(rows, axis=0).astype(jnp.bfloat16)
    for slot, rim_ref in enumerate(rim_refs):
        wanted = rim_token(slot_side(slot, columns), place)
        chosen = jnp.where((token == wanted) & (place < STRIP), 1.0, 0.0).astype(jnp.bfloat16)
        rim_ref[:STRIP] = mm(chosen[:STRIP], query_ref[...]).astype(jnp.bfloat16)
        rim_ref[STRIP : 2 * STRIP] = mm(chosen[:STRIP], dout_ref[...]).astype(jnp.bfloat16)
        spread = mm_nt(rows, chosen).astype(jnp.bfloat16)
        for pair in range(pairs):
            rim_ref[2 * STRIP :, pair * PAIR : (pair + 1) * PAIR] = spread[16 * pair : 16 * pair + 16]


def window(cell_row, cell_col, query):
    query_row = (query >> 4) + RADIUS
    query_col = (query & (SIDE - 1)) + RADIUS
    near = (jnp.abs(cell_row - query_row) <= RADIUS) & (jnp.abs(cell_col - query_col) <= RADIUS)
    return jnp.where(near, 0.0, -1e30)


def centre_bias(bias_ref):
    query = lax.broadcasted_iota(jnp.int32, (CELLS, CELLS), 1)
    cell = lax.broadcasted_iota(jnp.int32, (CELLS, CELLS), 0)
    bias_ref[...] = window((cell >> 4) + RADIUS, (cell & (SIDE - 1)) + RADIUS, query)


def strip_bias(kind, bias_ref):
    query = lax.broadcasted_iota(jnp.int32, (STRIP, CELLS), 1)
    cell = lax.broadcasted_iota(jnp.int32, (STRIP, CELLS), 0)
    depth = cell >> 4
    along = cell & (SIDE - 1)
    last = SIDE + 2 * RADIUS - 1
    if kind:
        first, second = (last - RADIUS - along, depth), (RADIUS + along, last - depth)
    else:
        first, second = (depth, RADIUS + along), (last - depth, last - RADIUS - along)
    in_first = first_half(query, kind)
    row = jnp.where(in_first, first[0], second[0])
    col = jnp.where(in_first, first[1], second[1])
    bias_ref[...] = window(row, col, query)


def first_half(query, kind):
    return (query & (SIDE - 1)) < SIDE // 2 if kind else query < CELLS // 2


def one_head(block, head):
    lane = lax.broadcasted_iota(jnp.int32, block.shape, 1)
    kept = (lane >= HEAD_DIM) if head else (lane < HEAD_DIM)
    return jnp.where(kept, block, jnp.zeros_like(block))


def halves(block, kind):
    kept = first_half(lax.broadcasted_iota(jnp.int32, block.shape, 0), kind)
    zero = jnp.zeros_like(block)
    return jnp.concatenate([jnp.where(kept, block, zero), jnp.where(kept, zero, block)], axis=1)


def by_half(stacked, kind):
    rows = stacked.shape[0] // 2
    kept = first_half(lax.broadcasted_iota(jnp.int32, (rows, CELLS), 1), kind)
    return jnp.where(kept, stacked[:rows], stacked[rows:])


def side_blocks(strips, part, kind, cols):
    tile = lax.axis_index("tile")
    second, first = strips
    straight = (tile if kind else lax.div(tile, lax.axis_size("tile") // 4)) & 1 == 0
    first, second = first[part, :, cols], second[part, :, cols]
    return jnp.where(straight, first, second), jnp.where(straight, second, first)


def side_cells(strips, part, kind, cols):
    return jnp.concatenate(side_blocks(strips, part, kind, cols), axis=1)


def halves(block, kind):
    kept = first_half(lax.broadcasted_iota(jnp.int32, block.shape, 0), kind)
    zero = jnp.zeros_like(block)
    return jnp.concatenate([jnp.where(kept, block, zero), jnp.where(kept, zero, block)], axis=1)


def by_half(stacked, kind):
    rows = stacked.shape[0] // 2
    kept = first_half(lax.broadcasted_iota(jnp.int32, (rows, CELLS), 1), kind)
    return jnp.where(kept, stacked[:rows], stacked[rows:])


def side_blocks(strips, part, kind, cols):
    tile = lax.axis_index("tile")
    second, first = strips
    straight = (tile if kind else lax.div(tile, lax.axis_size("tile") // 4)) & 1 == 0
    first, second = first[part, :, cols], second[part, :, cols]
    return jnp.where(straight, first, second), jnp.where(straight, second, first)


def side_cells(strips, part, kind, cols):
    return jnp.concatenate(side_blocks(strips, part, kind, cols), axis=1)


def side_products(cells, rows_head):
    return [mm_nt(cells[kind], halves(rows_head, kind)) for kind in range(2)]


def turned_sides(strips, part, kind, cols):
    return [block.T for block in side_blocks(strips, part, kind, cols)]


def pair_cols(pair):
    return pl.ds(pl.multiple_of(pair * PAIR, PAIR), PAIR)


def head_rows(turned, head):
    return turned[head * HEAD_DIM : (head + 1) * HEAD_DIM]


def over_side(turned, head, kind, sides):
    return by_half(mm(jnp.concatenate([head_rows(t, head) for t in turned], axis=0), sides), kind)


SCORE_SCALE = HEAD_DIM ** (-0.5)
LOG_SCALE = SCORE_SCALE * math.log2(math.e)


def lanes_of(head):
    return slice(head * CELLS, (head + 1) * CELLS)


def centre_kernel(
    query_ref, key_ref, value_ref, dout_ref,
    raw_ref, stats_ref, sums_ref, product_ref, query_out, key_out, bias_ref,
):
    centre_bias(bias_ref)

    def step(pair, carry):
        cols = pair_cols(pair)
        query, key, value, dout = (ref[:, cols] for ref in (query_ref, key_ref, value_ref, dout_ref))
        turned = value.T
        for head in range(2):
            lanes = lanes_of(head)
            scores = mm_nt(key, one_head(query, head)) + bias_ref[...]
            top = jnp.max(scores, axis=0, keepdims=True)
            raw = jnp.exp2((scores - top) * LOG_SCALE)
            raw_ref[pair, :, lanes] = raw
            stats_ref[pair, 0:1, lanes] = top
            stats_ref[pair, 1:2, lanes] = jnp.sum(raw, axis=0, keepdims=True)
            sums_ref[pair, :, lanes] = mm(head_rows(turned, head), raw.astype(jnp.bfloat16))
            product_ref[pair, :, lanes] = mm_nt(value, one_head(dout, head))
        query_out[:, cols] = query
        key_out[:, cols] = key
        return carry

    lax.fori_loop(0, raw_ref.shape[0], step, 0)


def column_kernel(
    first_ref, second_ref, query_ref, dout_ref, raw_ref, stats_ref, sums_ref, product_ref, bias_ref
):
    strips = (first_ref, second_ref)
    strip_bias(0, bias_ref)

    def step(pair, carry):
        cols = pair_cols(pair)
        keys = side_cells(strips, 0, 0, cols)
        values = side_cells(strips, 1, 0, cols)
        turned = turned_sides(strips, 1, 0, cols)
        for head in range(2):
            lanes = lanes_of(head)
            scores = mm_nt(keys, halves(one_head(query_ref[:, cols], head), 0)) + bias_ref[...]
            top = jnp.max(scores, axis=0, keepdims=True)
            raw = jnp.exp2((scores - top) * LOG_SCALE)
            raw_ref[pair, :, lanes] = raw
            stats_ref[pair, 0:1, lanes] = top
            stats_ref[pair, 1:2, lanes] = jnp.sum(raw, axis=0, keepdims=True)
            sums_ref[pair, :, lanes] = over_side(turned, head, 0, raw.astype(jnp.bfloat16))
            product_ref[pair, :, lanes] = mm_nt(values, halves(one_head(dout_ref[:, cols], head), 0))
        return carry

    lax.fori_loop(0, raw_ref.shape[0], step, 0)


def row_kernel(
    first_ref, second_ref, query_ref, dout_turned_ref, centre_stats_ref, centre_sums_ref, stats_ref, sums_ref,
    raw_ref, attention_ref, rows_ref, factors_ref, bias_ref,
):
    strips = (first_ref, second_ref)
    strip_bias(1, bias_ref)

    def step(pair, carry):
        cols = pair_cols(pair)
        keys = side_cells(strips, 0, 1, cols)
        turned = turned_sides(strips, 1, 1, cols)
        parts = []
        for head in range(2):
            lanes = lanes_of(head)
            scores = mm_nt(keys, halves(one_head(query_ref[:, cols], head), 1)) + bias_ref[...]
            tops = [ref[pair, 0:1, lanes] for ref in (centre_stats_ref, stats_ref)]
            top = jnp.maximum(jnp.max(scores, axis=0, keepdims=True), jnp.maximum(*tops))
            raw = jnp.exp2((scores - top) * LOG_SCALE)
            raw_ref[pair, :, lanes] = raw
            lifted = [jnp.exp2((t - top) * LOG_SCALE) for t in tops]
            total = jnp.sum(raw, axis=0, keepdims=True)
            total += lifted[0] * centre_stats_ref[pair, 1:2, lanes] + lifted[1] * stats_ref[pair, 1:2, lanes]
            inverse = 1.0 / total
            factors = [l * inverse for l in lifted]
            part = over_side(turned, head, 1, raw.astype(jnp.bfloat16)) * inverse
            part += factors[0] * centre_sums_ref[pair, :, lanes] + factors[1] * sums_ref[pair, :, lanes]
            parts.append(part)
            place = pl.ds(2 * pair + head, 1)
            features = pl.ds(pl.multiple_of((2 * pair + head) * HEAD_DIM, HEAD_DIM), HEAD_DIM)
            product = dout_turned_ref[features, :].astype(jnp.float32) * part
            rows_ref[0, place, :] = top
            rows_ref[1, place, :] = inverse
            rows_ref[2, place, :] = jnp.sum(product, axis=0, keepdims=True)
            factors_ref[0, place, :] = factors[0]
            factors_ref[1, place, :] = factors[1]
        attention_ref[:, cols] = jnp.concatenate(parts, axis=0).T.astype(jnp.bfloat16)
        return carry

    lax.fori_loop(0, raw_ref.shape[0], step, 0, unroll=True)


def backward_kernel(
    fourth_ref, third_ref, second_ref, first_ref, query_ref, key_ref, dout_ref, centre_raw_ref, column_raw_ref,
    row_raw_ref, centre_product_ref, column_product_ref, rows_ref, factors_ref, unused_ref,
    grad_query_ref, centre_ref,
):
    columns, rows = (third_ref, fourth_ref), (first_ref, second_ref)

    def step(pair, carry):
        cols = pair_cols(pair)
        query = query_ref[:, cols]
        dout = dout_ref[:, cols]
        turned_centre = key_ref[:, cols].T
        turned_columns = turned_sides(columns, 0, 0, cols)
        turned_rows = turned_sides(rows, 0, 1, cols)
        row_values = side_cells(rows, 1, 1, cols)
        parts = []
        centre_scores = []
        centre_weights = []
        for head in range(2):
            lanes = lanes_of(head)
            place = pl.ds(2 * pair + head, 1)
            delta = rows_ref[2, place, :]
            row_product = mm_nt(row_values, halves(one_head(dout, head), 1))

            def dscore(weights, product):
                return (weights * (product - delta)).astype(jnp.bfloat16)

            weights = centre_raw_ref[pair, :, lanes] * factors_ref[0, place, :]
            centre_weights.append(weights.astype(jnp.bfloat16))
            centre_scores.append(dscore(weights, centre_product_ref[pair, :, lanes]))
            column_weights = column_raw_ref[pair, :, lanes] * factors_ref[1, place, :]
            column_score = dscore(column_weights, column_product_ref[pair, :, lanes])
            row_score = dscore(row_raw_ref[pair, :, lanes] * rows_ref[1, place, :], row_product)
            part = mm(head_rows(turned_centre, head), centre_scores[-1])
            part += over_side(turned_columns, head, 0, column_score) + over_side(turned_rows, head, 1, row_score)
            parts.append(part)
        grad_query = jnp.concatenate(parts, axis=0).T * SCORE_SCALE
        grad_query_ref[:, cols] = grad_query.astype(jnp.bfloat16)
        grad_key, grad_value = joint_mm(
            jnp.concatenate(centre_scores, axis=1),
            jnp.concatenate(centre_weights, axis=1),
            both_heads(query),
            both_heads(dout),
        )
        centre_ref[0, :, cols] = grad_key * SCORE_SCALE
        centre_ref[1, :, cols] = grad_value
        return carry

    lax.fori_loop(0, centre_raw_ref.shape[0], step, 0)


def joint_mm(first, second, first_rows, second_rows):
    rows = first.shape[0]
    product = mm(jnp.concatenate([first, second], axis=0), jnp.concatenate([first_rows, second_rows], axis=1))
    return product[:rows, :PAIR], product[rows:, PAIR:]


def both_heads(block):
    return jnp.concatenate([one_head(block, head) for head in range(2)], axis=0)


def padded(block):
    return jnp.concatenate([block, jnp.zeros((LANES - block.shape[0], block.shape[1]), block.dtype)], axis=0)


def statistics(rows):
    first = 0
    for count in PARTS:
        heads = []
        for head in range(2):
            parts = [rows[2 * index + head : 2 * index + head + 1] for index in range(first, first + count)]
            heads.append(functools.reduce(jnp.add, parts))
        first += count
        yield jnp.concatenate(heads, axis=1)


def side_kernel(columns, rotations_ref, centre_ref, *refs):
    picked, rims = refs[:4], refs[4:8]
    keys_ref, values_ref, chosen_ref, bias_ref, keys_done, values_done, sems = refs[8:]
    cell = lax.broadcasted_iota(jnp.int32, (STRIP, LANES), 0)
    query = lax.broadcasted_iota(jnp.int32, (STRIP, LANES), 1)
    near = jnp.abs((cell & (SIDE - 1)) - (query & (SIDE - 1))) <= RADIUS
    near = near & ((cell >> 4) >= (query >> 4)) & (query < STRIP)
    bias_ref[...] = jnp.where(near, 0.0, -1e30)
    token = lax.broadcasted_iota(jnp.int32, (CELLS, LANES), 0)
    place = lax.broadcasted_iota(jnp.int32, (CELLS, LANES), 1)
    for slot in range(4):
        side = slot_side(slot, columns)
        wanted = jnp.where(place < STRIP, strip_token(side, rotations_ref[0, side], place), -1)
        chosen = jnp.where(token == wanted, 1.0, 0.0).astype(jnp.bfloat16)
        chosen_ref[:, slot * LANES : (slot + 1) * LANES] = chosen

    copies = []
    for pair in range(keys_ref.shape[1] // PAIR):
        cols = slice(pair * PAIR, (pair + 1) * PAIR)
        grads = []
        bias = jnp.concatenate([bias_ref[...]] * 2, axis=1)
        for picked_ref, rim_ref in zip(picked, rims):
            query = both_heads(padded(rim_ref[:STRIP, cols]))
            dout = both_heads(padded(rim_ref[STRIP : 2 * STRIP, cols]))
            top, inverse, delta = statistics(rim_ref[2 * STRIP :, cols].astype(jnp.float32))
            scores = mm_nt(picked_ref[0, :, cols], query) + bias
            weights = jnp.exp2((scores - top) * LOG_SCALE) * inverse
            product = mm_nt(picked_ref[1, :, cols], dout)
            dscore = (weights * (product - delta)).astype(jnp.bfloat16)
            grad = jnp.concatenate([mm(dscore, query) * SCORE_SCALE, mm(weights.astype(jnp.bfloat16), dout)], axis=1)
            grads.append(padded(grad.astype(jnp.bfloat16)))
        total = mm(chosen_ref[...], jnp.concatenate(grads, axis=0))
        keys_done[:, cols] = (centre_ref[0, :, cols] + total[:, :PAIR]).astype(jnp.bfloat16)
        values_done[:, cols] = (centre_ref[1, :, cols] + total[:, PAIR:]).astype(jnp.bfloat16)
        for index, (done, out_ref) in enumerate(((keys_done, keys_ref), (values_done, values_ref))):
            copy = pltpu.make_async_copy(done.at[:, cols], out_ref.at[:, cols], sems.at[2 * pair + index])
            copy.start()
            copies.append(copy)
    for copy in copies:
        copy.wait()


def call(kernel, name, out_shape, operands, scratch=(), smem=0, unused=0, gflop=0.1, out_space=pltpu.VMEM):
    specs = [pl.BlockSpec(memory_space=pltpu.SMEM)] * smem
    specs += [pl.BlockSpec(memory_space=pltpu.VMEM)] * (len(operands) - smem - unused)
    specs += [pl.BlockSpec(memory_space=pl.ANY)] * unused
    single = not isinstance(out_shape, list)
    outs = pl.BlockSpec(memory_space=out_space)
    return pl.pallas_call(
        kernel,
        out_shape=out_shape,
        in_specs=specs,
        out_specs=outs if single else [outs] * len(out_shape),
        scratch_shapes=list(scratch),
        compiler_params=pltpu.CompilerParams(vmem_limit_bytes=VMEM_LIMIT),
        cost_estimate=pl.CostEstimate(flops=int(gflop * 1e9), bytes_accessed=1 << 20, transcendentals=0),
        name=name,
    )(*operands)


def in_hbm(array):
    return pltpu.with_memory_space_constraint(array, pltpu.HBM)


def across(block, distances):
    heads = lax.axis_size("head")
    devices = [(tile, head) for tile in range(lax.axis_size("tile")) for head in range(heads)]
    route = [(tile * heads + head, (tile ^ distances[head % 2]) * heads + head) for tile, head in devices]
    return lax.ppermute(block, ("tile", "head"), route)


def exchanged(blocks, stride):
    terms = list(blocks[:1])
    for distance in range(1, len(blocks)):
        route = [(tile, tile ^ (distance * stride)) for tile in range(lax.axis_size("tile"))]
        terms.append(lax.ppermute(blocks[distance], "tile", route))
    return terms


def with_partners(blocks, slots):
    tile_count = lax.axis_size("tile")
    routes = {s: [(tile, partner(tile, tile_count, s)) for tile in range(tile_count)] for s in slots}
    return {s: lax.ppermute(blocks[s], "tile", routes[s]) for s in slots}


def shards(queries, keys, values, grad_output, out_weight, rotations):
    tile_count = lax.axis_size("tile")
    token_count, features = queries.shape
    model = out_weight.shape[0]
    pairs = features // PAIR
    far = tile_count // NEAR
    chunk = model // tile_count
    heads = lax.axis_size("head")
    columns = tile_count // 4
    queries, keys, values, out_weight, rotations = (
        in_hbm(a) for a in (queries, keys, values, out_weight, rotations)
    )

    def bf16(*shape):
        return jax.ShapeDtypeStruct(shape, jnp.bfloat16)

    def f32(*shape):
        return jax.ShapeDtypeStruct(shape, jnp.float32)

    strip_types = [bf16(2, STRIP, features)] * 4
    picked = call(
        functools.partial(pick_kernel, columns), "pick_strips", strip_types, (rotations, keys, values), smem=1
    )
    grad_output, *picked = lax.optimization_barrier((grad_output, *picked))
    strips = with_partners(picked, (3, 2, 1, 0))
    strips = [strips[s] for s in range(4)]

    cotangents = [
        lax.ppermute(grad_output, "head", [((h + k) % heads, h) for h in range(heads)]) for k in range(1, heads)
    ]
    dout, dout_turned, turned, turned_sent = call(
        functools.partial(cotangent_kernel, heads),
        "cotangent",
        [bf16(CELLS, features), bf16(features, CELLS)] + [bf16(2, far, chunk, CELLS)] * 2,
        (in_hbm(grad_output), *cotangents, out_weight),
        gflop=1.0,
    )
    turned_arrived = across(turned_sent, (1, 2))
    part_types = [f32(pairs, 2, 2 * CELLS), f32(pairs, HEAD_DIM, 2 * CELLS)]
    raw_centre, stats_centre, sums_centre, product_centre, queries, keys = call(
        centre_kernel,
        "centre",
        [f32(pairs, CELLS, 2 * CELLS)] + part_types + [f32(pairs, CELLS, 2 * CELLS)] + [bf16(CELLS, features)] * 2,
        (queries, keys, values, dout),
        scratch=[pltpu.VMEM((CELLS, CELLS), jnp.float32)],
        gflop=3.0,
    )
    strip_scratch = [pltpu.VMEM((STRIP, CELLS), jnp.float32)]
    raw_columns, stats_columns, sums_columns, product_columns = call(
        column_kernel,
        "columns",
        [f32(pairs, STRIP, 2 * CELLS)] + part_types + [f32(pairs, STRIP, 2 * CELLS)],
        (strips[2], strips[3], queries, dout),
        scratch=strip_scratch,
        gflop=2.0,
    )
    raw_rows, attention, rows, factors = call(
        row_kernel,
        "rows",
        [f32(pairs, STRIP, 2 * CELLS), bf16(CELLS, features)] + [f32(k, 2 * pairs, CELLS) for k in (3, 2)],
        (strips[0], strips[1], queries, dout_turned, stats_centre, sums_centre, stats_columns, sums_columns),
        scratch=strip_scratch,
    )
    attention_arrived = across(attention, (1, 2))
    rims = call(
        functools.partial(rim_kernel, columns),
        "rims",
        [bf16(2 * STRIP + 16, features)] * 4,
        (queries, dout, rows, turned_arrived),
        unused=1,
    )
    rims_arrived = with_partners(rims, (3, 2, 1, 0))
    kept, sent = call(
        partial_kernel,
        "partial",
        [f32(far, chunk, features), bf16(far, chunk, features)],
        (attention, attention_arrived, turned, turned_arrived, rims[0]),
        unused=1,
    )
    terms = [kept, across(sent, (2, 1))]
    grad_queries, centre = call(
        backward_kernel,
        "backward",
        [bf16(CELLS, features), f32(2, CELLS, features)],
        (
            *strips[::-1], queries, keys, dout, raw_centre, raw_columns, raw_rows, product_centre, product_columns,
            rows, factors, sent,
        ),
        unused=1,
        gflop=3.0,
    )
    stride = NEAR
    while stride < tile_count:
        ways = min(NEAR, tile_count // stride)
        sums = call(
            functools.partial(sum_kernel, len(terms)),
            "plane_sum",
            [bf16(tile_count // stride // ways, chunk, features)] * ways,
            (*terms, centre),
            unused=1,
        )
        terms = exchanged(sums, stride)
        stride *= ways

    grad_keys, grad_values = call(
        functools.partial(side_kernel, columns),
        "sides",
        [bf16(CELLS, features)] * 2,
        (rotations, centre, *picked, *(rims_arrived[s] for s in range(4))),
        scratch=[pltpu.VMEM((CELLS, 4 * LANES), jnp.bfloat16), pltpu.VMEM((STRIP, LANES), jnp.float32)]
        + [pltpu.VMEM((CELLS, features), jnp.bfloat16)] * 2
        + [pltpu.SemaphoreType.DMA((2 * pairs,))],
        smem=1,
        gflop=3.0,
        out_space=pl.ANY,
    )
    grad_out_weight = call(
        functools.partial(weight_kernel, 1.0 / math.sqrt(token_count * tile_count)),
        "weight_sum",
        f32(chunk, features),
        terms,
    )
    return (grad_queries, grad_keys, grad_values, grad_out_weight)


def solution(mesh):
    placed = (
        P("tile", "head"),
        P("tile", "head"),
        P("tile", "head"),
        P("tile", "head"),
        P(None, "head"),
        P("tile", None),
    )
    return jax.shard_map(
        shards,
        mesh=mesh,
        in_specs=placed,
        out_specs=(P("tile", "head"), P("tile", "head"), P("tile", "head"), P("tile", "head")),
        check_vma=False,
    )
```

```python
import functools
import math

import jax
import jax.numpy as jnp
from jax import lax
from jax.experimental import pallas as pl
from jax.experimental.pallas import tpu as pltpu
from jax.sharding import PartitionSpec as P

HEAD_DIM = 64
RADIUS = 6
SIDE = 16
CELLS = SIDE * SIDE
STRIP = RADIUS * SIDE
NEAR = 4
LANES = 128
PAIR = 2 * HEAD_DIM
VMEM_LIMIT = 32 * 1024 * 1024
NT = (((1,), (1,)), ((), ()))


def mm(a, b):
    return jnp.dot(a, b, preferred_element_type=jnp.float32)


def mm_nt(a, b):
    return lax.dot_general(a, b, NT, preferred_element_type=jnp.float32)


def strip_token(side_index, rotation, cell):
    turn = lax.rem(side_index + 6 - rotation, 4)
    depth = cell >> 4
    along = cell & (SIDE - 1)
    far = SIDE - 1 - along
    near_rim = RADIUS - 1 - depth
    far_rim = SIDE - RADIUS + depth
    row = jnp.where(turn == 0, far_rim, jnp.where(turn == 1, along, jnp.where(turn == 2, near_rim, far)))
    col = jnp.where(turn == 0, along, jnp.where(turn == 1, near_rim, jnp.where(turn == 2, far, far_rim)))
    return row * SIDE + col


def slot_side(slot, columns):
    tile = lax.axis_index("tile")
    if slot < 2:
        return jnp.where((tile + slot) & 1 == 0, 1, 3)
    return jnp.where((lax.div(tile, columns) + slot) & 1 == 0, 2, 0)


def partner(tile, tile_count, slot):
    columns = tile_count // 4
    if slot < 2:
        return (tile + (1 if (tile + slot) % 2 == 0 else -1)) % tile_count
    return (tile + (columns if (tile // columns + slot) % 2 == 0 else -columns)) % tile_count


def pick_kernel(columns, rotations_ref, keys_ref, values_ref, *out_refs):
    cell = lax.broadcasted_iota(jnp.int32, (STRIP, CELLS), 0)
    token = lax.broadcasted_iota(jnp.int32, (STRIP, CELLS), 1)
    for slot, out_ref in enumerate(out_refs):
        side = slot_side(slot, columns)
        wanted = strip_token(side, rotations_ref[0, side], cell)
        chosen = jnp.where(token == wanted, 1.0, 0.0).astype(jnp.bfloat16)
        out_ref[0] = mm(chosen, keys_ref[...]).astype(jnp.bfloat16)
        out_ref[1] = mm(chosen, values_ref[...]).astype(jnp.bfloat16)


def weight_kernel(scale, *refs):
    total = refs[0][0].astype(jnp.float32)
    for ref in refs[1:-1]:
        total += ref[0].astype(jnp.float32)
    refs[-1][...] = total * scale


def partial_kernel(attention_ref, arrived_ref, turned_ref, turned_arrived_ref, unused_ref, kept_ref, sent_ref):
    for index, out_ref in enumerate((kept_ref, sent_ref)):
        total = None
        for turned_part, attention_part in ((turned_ref, attention_ref), (turned_arrived_ref, arrived_ref)):
            turned = turned_part[index]
            turned = turned.reshape(turned.shape[0] * turned.shape[1], turned.shape[2])
            term = mm(turned, attention_part[...])
            total = term if total is None else total + term
        out_ref[...] = total.astype(out_ref.dtype).reshape(out_ref.shape)


def sum_kernel(count, *refs):
    terms, outs = refs[:count], refs[count + 1 :]
    for q in range(terms[0].shape[0]):
        total = terms[0][q].astype(jnp.float32)
        for ref in terms[1:]:
            total += ref[q].astype(jnp.float32)
        outs[q % len(outs)][q // len(outs)] = total.astype(jnp.bfloat16)


def rim_token(side_index, place):
    depth = place >> 4
    along = place & (SIDE - 1)
    last = SIDE - 1
    north, east, south = side_index == 0, side_index == 1, side_index == 2
    row = jnp.where(north, depth, jnp.where(east, along, jnp.where(south, last - depth, last - along)))
    col = jnp.where(north, along, jnp.where(east, last - depth, jnp.where(south, last - along, depth)))
    return row * SIDE + col


def cotangent_kernel(heads, *refs):
    blocks, out_weight_ref, outs = refs[:heads], refs[heads], refs[heads + 1 :]
    dout_ref, dout_turned_ref, turned_ref, turned_sent_ref = outs
    head = lax.axis_index("head")
    axis = head & 1
    tile = lax.axis_index("tile")
    chunk = turned_ref.shape[2]
    width = blocks[0].shape[1]
    total = None
    for distance, block_ref in enumerate(blocks):
        owner = lax.rem(head + distance, heads)
        start = pl.multiple_of(owner * width, width)
        block = block_ref[...]
        term = mm(block, out_weight_ref[pl.ds(start, width), :])
        total = term if total is None else total + term
        turned = block.T
        first = owner * (width // chunk)
        for index in range(width // chunk):
            target = (first + index) ^ tile
            rows = turned[index * chunk : (index + 1) * chunk]
            for parity, out_ref in enumerate((turned_ref, turned_sent_ref)):

                @pl.when((target >> axis) & 1 == parity)
                def _():
                    out_ref[(target >> (1 - axis)) & 1, target >> 2] = rows

    dout = total.astype(jnp.bfloat16)
    dout_ref[...] = dout
    dout_turned_ref[...] = dout.T


def split(exact, count):
    parts = []
    for _ in range(count):
        part = exact.astype(jnp.bfloat16).astype(jnp.float32)
        parts.append(part)
        exact = exact - part
    return parts


PARTS = (3, 2, 2)


def rim_kernel(columns, query_ref, dout_ref, rows_ref, unused_ref, *rim_refs):
    place = lax.broadcasted_iota(jnp.int32, (LANES, CELLS), 0)
    token = lax.broadcasted_iota(jnp.int32, (LANES, CELLS), 1)
    parts = [part for kind, count in enumerate(PARTS) for part in split(rows_ref[kind], count)]
    pairs = rows_ref.shape[1] // 2
    filler = jnp.zeros((16 - 2 * len(parts), CELLS), jnp.float32)
    rows = [
        jnp.concatenate([part[2 * pair : 2 * pair + 2] for part in parts] + [filler], axis=0) for pair in range(pairs)
    ]
    rows = jnp.concatenate(rows, axis=0).astype(jnp.bfloat16)
    for slot, rim_ref in enumerate(rim_refs):
        wanted = rim_token(slot_side(slot, columns), place)
        chosen = jnp.where((token == wanted) & (place < STRIP), 1.0, 0.0).astype(jnp.bfloat16)
        rim_ref[:STRIP] = mm(chosen[:STRIP], query_ref[...]).astype(jnp.bfloat16)
        rim_ref[STRIP : 2 * STRIP] = mm(chosen[:STRIP], dout_ref[...]).astype(jnp.bfloat16)
        spread = mm_nt(rows, chosen).astype(jnp.bfloat16)
        for pair in range(pairs):
            rim_ref[2 * STRIP :, pair * PAIR : (pair + 1) * PAIR] = spread[16 * pair : 16 * pair + 16]


def window(cell_row, cell_col, query):
    query_row = (query >> 4) + RADIUS
    query_col = (query & (SIDE - 1)) + RADIUS
    near = (jnp.abs(cell_row - query_row) <= RADIUS) & (jnp.abs(cell_col - query_col) <= RADIUS)
    return jnp.where(near, 0.0, -1e30)


def centre_bias(bias_ref):
    query = lax.broadcasted_iota(jnp.int32, (CELLS, CELLS), 1)
    cell = lax.broadcasted_iota(jnp.int32, (CELLS, CELLS), 0)
    bias_ref[...] = window((cell >> 4) + RADIUS, (cell & (SIDE - 1)) + RADIUS, query)


def strip_bias(kind, bias_ref):
    query = lax.broadcasted_iota(jnp.int32, (STRIP, CELLS), 1)
    cell = lax.broadcasted_iota(jnp.int32, (STRIP, CELLS), 0)
    depth = cell >> 4
    along = cell & (SIDE - 1)
    last = SIDE + 2 * RADIUS - 1
    if kind:
        first, second = (last - RADIUS - along, depth), (RADIUS + along, last - depth)
    else:
        first, second = (depth, RADIUS + along), (last - depth, last - RADIUS - along)
    in_first = first_half(query, kind)
    row = jnp.where(in_first, first[0], second[0])
    col = jnp.where(in_first, first[1], second[1])
    bias_ref[...] = window(row, col, query)


def first_half(query, kind):
    return (query & (SIDE - 1)) < SIDE // 2 if kind else query < CELLS // 2


def one_head(block, head):
    lane = lax.broadcasted_iota(jnp.int32, block.shape, 1)
    kept = (lane >= HEAD_DIM) if head else (lane < HEAD_DIM)
    return jnp.where(kept, block, jnp.zeros_like(block))


def halves(block, kind):
    kept = first_half(lax.broadcasted_iota(jnp.int32, block.shape, 0), kind)
    zero = jnp.zeros_like(block)
    return jnp.concatenate([jnp.where(kept, block, zero), jnp.where(kept, zero, block)], axis=1)


def by_half(stacked, kind):
    rows = stacked.shape[0] // 2
    kept = first_half(lax.broadcasted_iota(jnp.int32, (rows, CELLS), 1), kind)
    return jnp.where(kept, stacked[:rows], stacked[rows:])


def side_blocks(strips, part, kind, cols):
    tile = lax.axis_index("tile")
    second, first = strips
    straight = (tile if kind else lax.div(tile, lax.axis_size("tile") // 4)) & 1 == 0
    first, second = first[part, :, cols], second[part, :, cols]
    return jnp.where(straight, first, second), jnp.where(straight, second, first)


def side_cells(strips, part, kind, cols):
    return jnp.concatenate(side_blocks(strips, part, kind, cols), axis=1)


def halves(block, kind):
    kept = first_half(lax.broadcasted_iota(jnp.int32, block.shape, 0), kind)
    zero = jnp.zeros_like(block)
    return jnp.concatenate([jnp.where(kept, block, zero), jnp.where(kept, zero, block)], axis=1)


def by_half(stacked, kind):
    rows = stacked.shape[0] // 2
    kept = first_half(lax.broadcasted_iota(jnp.int32, (rows, CELLS), 1), kind)
    return jnp.where(kept, stacked[:rows], stacked[rows:])


def side_blocks(strips, part, kind, cols):
    tile = lax.axis_index("tile")
    second, first = strips
    straight = (tile if kind else lax.div(tile, lax.axis_size("tile") // 4)) & 1 == 0
    first, second = first[part, :, cols], second[part, :, cols]
    return jnp.where(straight, first, second), jnp.where(straight, second, first)


def side_cells(strips, part, kind, cols):
    return jnp.concatenate(side_blocks(strips, part, kind, cols), axis=1)


def side_products(cells, rows_head):
    return [mm_nt(cells[kind], halves(rows_head, kind)) for kind in range(2)]


def turned_sides(strips, part, kind, cols):
    return [block.T for block in side_blocks(strips, part, kind, cols)]


def pair_cols(pair):
    return pl.ds(pl.multiple_of(pair * PAIR, PAIR), PAIR)


def head_rows(turned, head):
    return turned[head * HEAD_DIM : (head + 1) * HEAD_DIM]


def over_side(turned, head, kind, sides):
    return by_half(mm(jnp.concatenate([head_rows(t, head) for t in turned], axis=0), sides), kind)


SCORE_SCALE = HEAD_DIM ** (-0.5)
LOG_SCALE = SCORE_SCALE * math.log2(math.e)


def lanes_of(head):
    return slice(head * CELLS, (head + 1) * CELLS)


def centre_kernel(
    query_ref, key_ref, value_ref, dout_ref,
    raw_ref, stats_ref, sums_ref, product_ref, query_out, key_out, bias_ref,
):
    centre_bias(bias_ref)

    def step(pair, carry):
        cols = pair_cols(pair)
        query, key, value, dout = (ref[:, cols] for ref in (query_ref, key_ref, value_ref, dout_ref))
        turned = value.T
        for head in range(2):
            lanes = lanes_of(head)
            scores = mm_nt(key, one_head(query, head)) + bias_ref[...]
            top = jnp.max(scores, axis=0, keepdims=True)
            raw = jnp.exp2((scores - top) * LOG_SCALE)
            raw_ref[pair, :, lanes] = raw
            stats_ref[pair, 0:1, lanes] = top
            stats_ref[pair, 1:2, lanes] = jnp.sum(raw, axis=0, keepdims=True)
            sums_ref[pair, :, lanes] = mm(head_rows(turned, head), raw.astype(jnp.bfloat16))
            product_ref[pair, :, lanes] = mm_nt(value, one_head(dout, head))
        query_out[:, cols] = query
        key_out[:, cols] = key
        return carry

    lax.fori_loop(0, raw_ref.shape[0], step, 0)


def column_kernel(
    first_ref, second_ref, query_ref, dout_ref, raw_ref, stats_ref, sums_ref, product_ref, bias_ref
):
    strips = (first_ref, second_ref)
    strip_bias(0, bias_ref)

    def step(pair, carry):
        cols = pair_cols(pair)
        keys = side_cells(strips, 0, 0, cols)
        values = side_cells(strips, 1, 0, cols)
        turned = turned_sides(strips, 1, 0, cols)
        for head in range(2):
            lanes = lanes_of(head)
            scores = mm_nt(keys, halves(one_head(query_ref[:, cols], head), 0)) + bias_ref[...]
            top = jnp.max(scores, axis=0, keepdims=True)
            raw = jnp.exp2((scores - top) * LOG_SCALE)
            raw_ref[pair, :, lanes] = raw
            stats_ref[pair, 0:1, lanes] = top
            stats_ref[pair, 1:2, lanes] = jnp.sum(raw, axis=0, keepdims=True)
            sums_ref[pair, :, lanes] = over_side(turned, head, 0, raw.astype(jnp.bfloat16))
            product_ref[pair, :, lanes] = mm_nt(values, halves(one_head(dout_ref[:, cols], head), 0))
        return carry

    lax.fori_loop(0, raw_ref.shape[0], step, 0)


def row_kernel(
    first_ref, second_ref, query_ref, dout_turned_ref, centre_stats_ref, centre_sums_ref, stats_ref, sums_ref,
    raw_ref, attention_ref, rows_ref, factors_ref, bias_ref,
):
    strips = (first_ref, second_ref)
    strip_bias(1, bias_ref)

    def step(pair, carry):
        cols = pair_cols(pair)
        keys = side_cells(strips, 0, 1, cols)
        turned = turned_sides(strips, 1, 1, cols)
        parts = []
        for head in range(2):
            lanes = lanes_of(head)
            scores = mm_nt(keys, halves(one_head(query_ref[:, cols], head), 1)) + bias_ref[...]
            tops = [ref[pair, 0:1, lanes] for ref in (centre_stats_ref, stats_ref)]
            top = jnp.maximum(jnp.max(scores, axis=0, keepdims=True), jnp.maximum(*tops))
            raw = jnp.exp2((scores - top) * LOG_SCALE)
            raw_ref[pair, :, lanes] = raw
            lifted = [jnp.exp2((t - top) * LOG_SCALE) for t in tops]
            total = jnp.sum(raw, axis=0, keepdims=True)
            total += lifted[0] * centre_stats_ref[pair, 1:2, lanes] + lifted[1] * stats_ref[pair, 1:2, lanes]
            inverse = 1.0 / total
            factors = [l * inverse for l in lifted]
            part = over_side(turned, head, 1, raw.astype(jnp.bfloat16)) * inverse
            part += factors[0] * centre_sums_ref[pair, :, lanes] + factors[1] * sums_ref[pair, :, lanes]
            parts.append(part)
            place = pl.ds(2 * pair + head, 1)
            features = pl.ds(pl.multiple_of((2 * pair + head) * HEAD_DIM, HEAD_DIM), HEAD_DIM)
            product = dout_turned_ref[features, :].astype(jnp.float32) * part
            rows_ref[0, place, :] = top
            rows_ref[1, place, :] = inverse
            rows_ref[2, place, :] = jnp.sum(product, axis=0, keepdims=True)
            factors_ref[0, place, :] = factors[0]
            factors_ref[1, place, :] = factors[1]
        attention_ref[:, cols] = jnp.concatenate(parts, axis=0).T.astype(jnp.bfloat16)
        return carry

    lax.fori_loop(0, raw_ref.shape[0], step, 0, unroll=True)


def backward_kernel(
    fourth_ref, third_ref, second_ref, first_ref, query_ref, key_ref, dout_ref, centre_raw_ref, column_raw_ref,
    row_raw_ref, centre_product_ref, column_product_ref, rows_ref, factors_ref, unused_ref,
    grad_query_ref, centre_ref,
):
    columns, rows = (third_ref, fourth_ref), (first_ref, second_ref)

    def step(pair, carry):
        cols = pair_cols(pair)
        query = query_ref[:, cols]
        dout = dout_ref[:, cols]
        turned_centre = key_ref[:, cols].T
        turned_columns = turned_sides(columns, 0, 0, cols)
        turned_rows = turned_sides(rows, 0, 1, cols)
        row_values = side_cells(rows, 1, 1, cols)
        parts = []
        centre_scores = []
        centre_weights = []
        for head in range(2):
            lanes = lanes_of(head)
            place = pl.ds(2 * pair + head, 1)
            delta = rows_ref[2, place, :]
            row_product = mm_nt(row_values, halves(one_head(dout, head), 1))

            def dscore(weights, product):
                return (weights * (product - delta)).astype(jnp.bfloat16)

            weights = centre_raw_ref[pair, :, lanes] * factors_ref[0, place, :]
            centre_weights.append(weights.astype(jnp.bfloat16))
            centre_scores.append(dscore(weights, centre_product_ref[pair, :, lanes]))
            column_weights = column_raw_ref[pair, :, lanes] * factors_ref[1, place, :]
            column_score = dscore(column_weights, column_product_ref[pair, :, lanes])
            row_score = dscore(row_raw_ref[pair, :, lanes] * rows_ref[1, place, :], row_product)
            part = mm(head_rows(turned_centre, head), centre_scores[-1])
            part += over_side(turned_columns, head, 0, column_score) + over_side(turned_rows, head, 1, row_score)
            parts.append(part)
        grad_query = jnp.concatenate(parts, axis=0).T * SCORE_SCALE
        grad_query_ref[:, cols] = grad_query.astype(jnp.bfloat16)
        grad_key, grad_value = joint_mm(
            jnp.concatenate(centre_scores, axis=1),
            jnp.concatenate(centre_weights, axis=1),
            both_heads(query),
            both_heads(dout),
        )
        centre_ref[0, :, cols] = grad_key * SCORE_SCALE
        centre_ref[1, :, cols] = grad_value
        return carry

    lax.fori_loop(0, centre_raw_ref.shape[0], step, 0)


def joint_mm(first, second, first_rows, second_rows):
    rows = first.shape[0]
    product = mm(jnp.concatenate([first, second], axis=0), jnp.concatenate([first_rows, second_rows], axis=1))
    return product[:rows, :PAIR], product[rows:, PAIR:]


def both_heads(block):
    return jnp.concatenate([one_head(block, head) for head in range(2)], axis=0)


def padded(block):
    return jnp.concatenate([block, jnp.zeros((LANES - block.shape[0], block.shape[1]), block.dtype)], axis=0)


def statistics(rows):
    first = 0
    for count in PARTS:
        heads = []
        for head in range(2):
            parts = [rows[2 * index + head : 2 * index + head + 1] for index in range(first, first + count)]
            heads.append(functools.reduce(jnp.add, parts))
        first += count
        yield jnp.concatenate(heads, axis=1)


def side_kernel(slots, columns, rotations_ref, centre_ref, *refs):
    count = len(slots)
    picked, rims, refs = refs[:count], refs[count : 2 * count], refs[2 * count :]
    total_ref, refs = (refs[0], refs[1:]) if len(refs) == 3 else (None, refs)
    chosen_ref, bias_ref = refs[:2] if total_ref is not None else refs[2:4]
    cell = lax.broadcasted_iota(jnp.int32, (STRIP, LANES), 0)
    query = lax.broadcasted_iota(jnp.int32, (STRIP, LANES), 1)
    near = jnp.abs((cell & (SIDE - 1)) - (query & (SIDE - 1))) <= RADIUS
    near = near & ((cell >> 4) >= (query >> 4)) & (query < STRIP)
    bias_ref[...] = jnp.where(near, 0.0, -1e30)
    token = lax.broadcasted_iota(jnp.int32, (CELLS, LANES), 0)
    place = lax.broadcasted_iota(jnp.int32, (CELLS, LANES), 1)
    for index, slot in enumerate(slots):
        side = slot_side(slot, columns)
        wanted = jnp.where(place < STRIP, strip_token(side, rotations_ref[0, side], place), -1)
        chosen = jnp.where(token == wanted, 1.0, 0.0).astype(jnp.bfloat16)
        chosen_ref[:, index * LANES : (index + 1) * LANES] = chosen

    copies = []
    for pair in range(centre_ref.shape[2] // PAIR):
        cols = slice(pair * PAIR, (pair + 1) * PAIR)
        grads = []
        bias = jnp.concatenate([bias_ref[...]] * 2, axis=1)
        for picked_ref, rim_ref in zip(picked, rims):
            query = both_heads(padded(rim_ref[:STRIP, cols]))
            dout = both_heads(padded(rim_ref[STRIP : 2 * STRIP, cols]))
            top, inverse, delta = statistics(rim_ref[2 * STRIP :, cols].astype(jnp.float32))
            scores = mm_nt(picked_ref[0, :, cols], query) + bias
            weights = jnp.exp2((scores - top) * LOG_SCALE) * inverse
            product = mm_nt(picked_ref[1, :, cols], dout)
            dscore = (weights * (product - delta)).astype(jnp.bfloat16)
            grad = jnp.concatenate([mm(dscore, query) * SCORE_SCALE, mm(weights.astype(jnp.bfloat16), dout)], axis=1)
            grads.append(padded(grad.astype(jnp.bfloat16)))
        total = mm(chosen_ref[...], jnp.concatenate(grads, axis=0))
        total_keys = centre_ref[0, :, cols] + total[:, :PAIR]
        total_values = centre_ref[1, :, cols] + total[:, PAIR:]
        if total_ref is not None:
            total_ref[0, :, cols] = total_keys
            total_ref[1, :, cols] = total_values
            continue
        keys_ref, values_ref, _, _, keys_done, values_done, sems = refs
        keys_done[:, cols] = total_keys.astype(jnp.bfloat16)
        values_done[:, cols] = total_values.astype(jnp.bfloat16)
        for index, (done, out_ref) in enumerate(((keys_done, keys_ref), (values_done, values_ref))):
            copy = pltpu.make_async_copy(done.at[:, cols], out_ref.at[:, cols], sems.at[2 * pair + index])
            copy.start()
            copies.append(copy)
    for copy in copies:
        copy.wait()


def call(kernel, name, out_shape, operands, scratch=(), smem=0, unused=0, gflop=0.1, out_space=pltpu.VMEM):
    specs = [pl.BlockSpec(memory_space=pltpu.SMEM)] * smem
    specs += [pl.BlockSpec(memory_space=pltpu.VMEM)] * (len(operands) - smem - unused)
    specs += [pl.BlockSpec(memory_space=pl.ANY)] * unused
    single = not isinstance(out_shape, list)
    outs = pl.BlockSpec(memory_space=out_space)
    return pl.pallas_call(
        kernel,
        out_shape=out_shape,
        in_specs=specs,
        out_specs=outs if single else [outs] * len(out_shape),
        scratch_shapes=list(scratch),
        compiler_params=pltpu.CompilerParams(vmem_limit_bytes=VMEM_LIMIT),
        cost_estimate=pl.CostEstimate(flops=int(gflop * 1e9), bytes_accessed=1 << 20, transcendentals=0),
        name=name,
    )(*operands)


def in_hbm(array):
    return pltpu.with_memory_space_constraint(array, pltpu.HBM)


def across(block, distances):
    heads = lax.axis_size("head")
    devices = [(tile, head) for tile in range(lax.axis_size("tile")) for head in range(heads)]
    route = [(tile * heads + head, (tile ^ distances[head % 2]) * heads + head) for tile, head in devices]
    return lax.ppermute(block, ("tile", "head"), route)


def exchanged(blocks, stride):
    terms = list(blocks[:1])
    for distance in range(1, len(blocks)):
        route = [(tile, tile ^ (distance * stride)) for tile in range(lax.axis_size("tile"))]
        terms.append(lax.ppermute(blocks[distance], "tile", route))
    return terms


def with_partners(blocks, slots):
    tile_count = lax.axis_size("tile")
    routes = {s: [(tile, partner(tile, tile_count, s)) for tile in range(tile_count)] for s in slots}
    return {s: lax.ppermute(blocks[s], "tile", routes[s]) for s in slots}


def shards(queries, keys, values, grad_output, out_weight, rotations):
    tile_count = lax.axis_size("tile")
    token_count, features = queries.shape
    model = out_weight.shape[0]
    pairs = features // PAIR
    far = tile_count // NEAR
    chunk = model // tile_count
    heads = lax.axis_size("head")
    columns = tile_count // 4
    queries, keys, values, out_weight, rotations = (
        in_hbm(a) for a in (queries, keys, values, out_weight, rotations)
    )

    def bf16(*shape):
        return jax.ShapeDtypeStruct(shape, jnp.bfloat16)

    def f32(*shape):
        return jax.ShapeDtypeStruct(shape, jnp.float32)

    strip_types = [bf16(2, STRIP, features)] * 4
    picked = call(
        functools.partial(pick_kernel, columns), "pick_strips", strip_types, (rotations, keys, values), smem=1
    )
    grad_output, *picked = lax.optimization_barrier((grad_output, *picked))
    strips = with_partners(picked, (3, 2, 1, 0))
    strips = [strips[s] for s in range(4)]

    cotangents = [
        lax.ppermute(grad_output, "head", [((h + k) % heads, h) for h in range(heads)]) for k in range(1, heads)
    ]
    dout, dout_turned, turned, turned_sent = call(
        functools.partial(cotangent_kernel, heads),
        "cotangent",
        [bf16(CELLS, features), bf16(features, CELLS)] + [bf16(2, far, chunk, CELLS)] * 2,
        (in_hbm(grad_output), *cotangents, out_weight),
        gflop=1.0,
    )
    turned_arrived = across(turned_sent, (1, 2))
    part_types = [f32(pairs, 2, 2 * CELLS), f32(pairs, HEAD_DIM, 2 * CELLS)]
    raw_centre, stats_centre, sums_centre, product_centre, queries, keys = call(
        centre_kernel,
        "centre",
        [f32(pairs, CELLS, 2 * CELLS)] + part_types + [f32(pairs, CELLS, 2 * CELLS)] + [bf16(CELLS, features)] * 2,
        (queries, keys, values, dout),
        scratch=[pltpu.VMEM((CELLS, CELLS), jnp.float32)],
        gflop=3.0,
    )
    strip_scratch = [pltpu.VMEM((STRIP, CELLS), jnp.float32)]
    raw_columns, stats_columns, sums_columns, product_columns = call(
        column_kernel,
        "columns",
        [f32(pairs, STRIP, 2 * CELLS)] + part_types + [f32(pairs, STRIP, 2 * CELLS)],
        (strips[2], strips[3], queries, dout),
        scratch=strip_scratch,
        gflop=2.0,
    )
    raw_rows, attention, rows, factors = call(
        row_kernel,
        "rows",
        [f32(pairs, STRIP, 2 * CELLS), bf16(CELLS, features)] + [f32(k, 2 * pairs, CELLS) for k in (3, 2)],
        (strips[0], strips[1], queries, dout_turned, stats_centre, sums_centre, stats_columns, sums_columns),
        scratch=strip_scratch,
    )
    attention_arrived = across(attention, (1, 2))
    rims = call(
        functools.partial(rim_kernel, columns),
        "rims",
        [bf16(2 * STRIP + 16, features)] * 4,
        (queries, dout, rows, turned_arrived),
        unused=1,
    )
    rims_arrived = with_partners(rims, (3, 2, 1, 0))
    kept, sent = call(
        partial_kernel,
        "partial",
        [f32(far, chunk, features), bf16(far, chunk, features)],
        (attention, attention_arrived, turned, turned_arrived, rims[0]),
        unused=1,
    )
    terms = [kept, across(sent, (2, 1))]
    grad_queries, centre = call(
        backward_kernel,
        "backward",
        [bf16(CELLS, features), f32(2, CELLS, features)],
        (
            *strips[::-1], queries, keys, dout, raw_centre, raw_columns, raw_rows, product_centre, product_columns,
            rows, factors, sent,
        ),
        unused=1,
        gflop=3.0,
    )
    side_scratch = [pltpu.VMEM((CELLS, 2 * LANES), jnp.bfloat16), pltpu.VMEM((STRIP, LANES), jnp.float32)]
    centre = call(
        functools.partial(side_kernel, (3, 2), columns),
        "sides_columns",
        f32(2, CELLS, features),
        (rotations, centre, picked[3], picked[2], rims_arrived[3], rims_arrived[2]),
        scratch=side_scratch,
        smem=1,
        gflop=3.0,
    )
    stride = NEAR
    while stride < tile_count:
        ways = min(NEAR, tile_count // stride)
        sums = call(
            functools.partial(sum_kernel, len(terms)),
            "plane_sum",
            [bf16(tile_count // stride // ways, chunk, features)] * ways,
            (*terms, centre),
            unused=1,
        )
        terms = exchanged(sums, stride)
        stride *= ways

    grad_keys, grad_values = call(
        functools.partial(side_kernel, (1, 0), columns),
        "sides_rows",
        [bf16(CELLS, features)] * 2,
        (rotations, centre, picked[1], picked[0], rims_arrived[1], rims_arrived[0]),
        scratch=side_scratch
        + [pltpu.VMEM((CELLS, features), jnp.bfloat16)] * 2
        + [pltpu.SemaphoreType.DMA((2 * pairs,))],
        smem=1,
        gflop=3.0,
        out_space=pl.ANY,
    )
    grad_out_weight = call(
        functools.partial(weight_kernel, 1.0 / math.sqrt(token_count * tile_count)),
        "weight_sum",
        f32(chunk, features),
        terms,
    )
    return (grad_queries, grad_keys, grad_values, grad_out_weight)


def solution(mesh):
    placed = (
        P("tile", "head"),
        P("tile", "head"),
        P("tile", "head"),
        P("tile", "head"),
        P(None, "head"),
        P("tile", None),
    )
    return jax.shard_map(
        shards,
        mesh=mesh,
        in_specs=placed,
        out_specs=(P("tile", "head"), P("tile", "head"), P("tile", "head"), P("tile", "head")),
        check_vma=False,
    )
```

```python
import functools
import math

import jax
import jax.numpy as jnp
from jax import lax
from jax.experimental import pallas as pl
from jax.experimental.pallas import tpu as pltpu
from jax.sharding import PartitionSpec as P

HEAD_DIM = 64
RADIUS = 6
SIDE = 16
CELLS = SIDE * SIDE
STRIP = RADIUS * SIDE
NEAR = 4
LANES = 128
PAIR = 2 * HEAD_DIM
VMEM_LIMIT = 32 * 1024 * 1024
NT = (((1,), (1,)), ((), ()))


def mm(a, b):
    return jnp.dot(a, b, preferred_element_type=jnp.float32)


def mm_nt(a, b):
    return lax.dot_general(a, b, NT, preferred_element_type=jnp.float32)


def strip_token(side_index, rotation, cell):
    turn = lax.rem(side_index + 6 - rotation, 4)
    depth = cell >> 4
    along = cell & (SIDE - 1)
    far = SIDE - 1 - along
    near_rim = RADIUS - 1 - depth
    far_rim = SIDE - RADIUS + depth
    row = jnp.where(turn == 0, far_rim, jnp.where(turn == 1, along, jnp.where(turn == 2, near_rim, far)))
    col = jnp.where(turn == 0, along, jnp.where(turn == 1, near_rim, jnp.where(turn == 2, far, far_rim)))
    return row * SIDE + col


def slot_side(slot, columns):
    tile = lax.axis_index("tile")
    if slot < 2:
        return jnp.where((tile + slot) & 1 == 0, 1, 3)
    return jnp.where((lax.div(tile, columns) + slot) & 1 == 0, 2, 0)


def partner(tile, tile_count, slot):
    columns = tile_count // 4
    if slot < 2:
        return (tile + (1 if (tile + slot) % 2 == 0 else -1)) % tile_count
    return (tile + (columns if (tile // columns + slot) % 2 == 0 else -columns)) % tile_count


def pick_kernel(columns, rotations_ref, keys_ref, values_ref, *out_refs):
    cell = lax.broadcasted_iota(jnp.int32, (STRIP, CELLS), 0)
    token = lax.broadcasted_iota(jnp.int32, (STRIP, CELLS), 1)
    for slot, out_ref in enumerate(out_refs):
        side = slot_side(slot, columns)
        wanted = strip_token(side, rotations_ref[0, side], cell)
        chosen = jnp.where(token == wanted, 1.0, 0.0).astype(jnp.bfloat16)
        out_ref[0] = mm(chosen, keys_ref[...]).astype(jnp.bfloat16)
        out_ref[1] = mm(chosen, values_ref[...]).astype(jnp.bfloat16)


def weight_kernel(scale, *refs):
    total = refs[0][0].astype(jnp.float32)
    for ref in refs[1:-1]:
        total += ref[0].astype(jnp.float32)
    refs[-1][...] = total * scale


def partial_kernel(attention_ref, arrived_ref, turned_ref, turned_arrived_ref, unused_ref, kept_ref, sent_ref):
    for index, out_ref in enumerate((kept_ref, sent_ref)):
        total = None
        for turned_part, attention_part in ((turned_ref, attention_ref), (turned_arrived_ref, arrived_ref)):
            turned = turned_part[index]
            turned = turned.reshape(turned.shape[0] * turned.shape[1], turned.shape[2])
            term = mm(turned, attention_part[...])
            total = term if total is None else total + term
        out_ref[...] = total.astype(out_ref.dtype).reshape(out_ref.shape)


def sum_kernel(count, *refs):
    terms, outs = refs[:count], refs[count + 3 :]
    for q in range(terms[0].shape[0]):
        total = terms[0][q].astype(jnp.float32)
        for ref in terms[1:]:
            total += ref[q].astype(jnp.float32)
        outs[q % len(outs)][q // len(outs)] = total.astype(jnp.bfloat16)


def rim_token(side_index, place):
    depth = place >> 4
    along = place & (SIDE - 1)
    last = SIDE - 1
    north, east, south = side_index == 0, side_index == 1, side_index == 2
    row = jnp.where(north, depth, jnp.where(east, along, jnp.where(south, last - depth, last - along)))
    col = jnp.where(north, along, jnp.where(east, last - depth, jnp.where(south, last - along, depth)))
    return row * SIDE + col


def cotangent_kernel(heads, *refs):
    blocks, out_weight_ref, outs = refs[:heads], refs[heads], refs[heads + 1 :]
    dout_ref, dout_turned_ref, turned_ref, turned_sent_ref = outs
    head = lax.axis_index("head")
    axis = head & 1
    tile = lax.axis_index("tile")
    chunk = turned_ref.shape[2]
    width = blocks[0].shape[1]
    total = None
    for distance, block_ref in enumerate(blocks):
        owner = lax.rem(head + distance, heads)
        start = pl.multiple_of(owner * width, width)
        block = block_ref[...]
        term = mm(block, out_weight_ref[pl.ds(start, width), :])
        total = term if total is None else total + term
        turned = block.T
        first = owner * (width // chunk)
        for index in range(width // chunk):
            target = (first + index) ^ tile
            rows = turned[index * chunk : (index + 1) * chunk]
            for parity, out_ref in enumerate((turned_ref, turned_sent_ref)):

                @pl.when((target >> axis) & 1 == parity)
                def _():
                    out_ref[(target >> (1 - axis)) & 1, target >> 2] = rows

    dout = total.astype(jnp.bfloat16)
    dout_ref[...] = dout
    dout_turned_ref[...] = dout.T


def split(exact, count):
    parts = []
    for _ in range(count):
        part = exact.astype(jnp.bfloat16).astype(jnp.float32)
        parts.append(part)
        exact = exact - part
    return parts


PARTS = (3, 2, 2)
SIDE_ORDER = (3, 2, 1, 0)


def rim_kernel(columns, query_ref, dout_ref, rows_ref, unused_ref, *rim_refs):
    place = lax.broadcasted_iota(jnp.int32, (LANES, CELLS), 0)
    token = lax.broadcasted_iota(jnp.int32, (LANES, CELLS), 1)
    parts = [part for kind, count in enumerate(PARTS) for part in split(rows_ref[kind], count)]
    pairs = rows_ref.shape[1] // 2
    filler = jnp.zeros((16 - 2 * len(parts), CELLS), jnp.float32)
    rows = [
        jnp.concatenate([part[2 * pair : 2 * pair + 2] for part in parts] + [filler], axis=0) for pair in range(pairs)
    ]
    rows = jnp.concatenate(rows, axis=0).astype(jnp.bfloat16)
    for slot, rim_ref in enumerate(rim_refs):
        wanted = rim_token(slot_side(slot, columns), place)
        chosen = jnp.where((token == wanted) & (place < STRIP), 1.0, 0.0).astype(jnp.bfloat16)
        rim_ref[:STRIP] = mm(chosen[:STRIP], query_ref[...]).astype(jnp.bfloat16)
        rim_ref[STRIP : 2 * STRIP] = mm(chosen[:STRIP], dout_ref[...]).astype(jnp.bfloat16)
        spread = mm_nt(rows, chosen).astype(jnp.bfloat16)
        for pair in range(pairs):
            rim_ref[2 * STRIP :, pair * PAIR : (pair + 1) * PAIR] = spread[16 * pair : 16 * pair + 16]


def window(cell_row, cell_col, query):
    query_row = (query >> 4) + RADIUS
    query_col = (query & (SIDE - 1)) + RADIUS
    near = (jnp.abs(cell_row - query_row) <= RADIUS) & (jnp.abs(cell_col - query_col) <= RADIUS)
    return jnp.where(near, 0.0, -1e30)


def centre_bias(bias_ref):
    query = lax.broadcasted_iota(jnp.int32, (CELLS, CELLS), 1)
    cell = lax.broadcasted_iota(jnp.int32, (CELLS, CELLS), 0)
    bias_ref[...] = window((cell >> 4) + RADIUS, (cell & (SIDE - 1)) + RADIUS, query)


def strip_bias(kind, bias_ref):
    query = lax.broadcasted_iota(jnp.int32, (STRIP, CELLS), 1)
    cell = lax.broadcasted_iota(jnp.int32, (STRIP, CELLS), 0)
    depth = cell >> 4
    along = cell & (SIDE - 1)
    last = SIDE + 2 * RADIUS - 1
    if kind:
        first, second = (last - RADIUS - along, depth), (RADIUS + along, last - depth)
    else:
        first, second = (depth, RADIUS + along), (last - depth, last - RADIUS - along)
    in_first = first_half(query, kind)
    row = jnp.where(in_first, first[0], second[0])
    col = jnp.where(in_first, first[1], second[1])
    bias_ref[...] = window(row, col, query)


def first_half(query, kind):
    return (query & (SIDE - 1)) < SIDE // 2 if kind else query < CELLS // 2


def one_head(block, head):
    lane = lax.broadcasted_iota(jnp.int32, block.shape, 1)
    kept = (lane >= HEAD_DIM) if head else (lane < HEAD_DIM)
    return jnp.where(kept, block, jnp.zeros_like(block))


def halves(block, kind):
    kept = first_half(lax.broadcasted_iota(jnp.int32, block.shape, 0), kind)
    zero = jnp.zeros_like(block)
    return jnp.concatenate([jnp.where(kept, block, zero), jnp.where(kept, zero, block)], axis=1)


def by_half(stacked, kind):
    rows = stacked.shape[0] // 2
    kept = first_half(lax.broadcasted_iota(jnp.int32, (rows, CELLS), 1), kind)
    return jnp.where(kept, stacked[:rows], stacked[rows:])


def side_blocks(strips, part, kind, cols):
    tile = lax.axis_index("tile")
    second, first = strips
    straight = (tile if kind else lax.div(tile, lax.axis_size("tile") // 4)) & 1 == 0
    first, second = first[part, :, cols], second[part, :, cols]
    return jnp.where(straight, first, second), jnp.where(straight, second, first)


def side_cells(strips, part, kind, cols):
    return jnp.concatenate(side_blocks(strips, part, kind, cols), axis=1)


def halves(block, kind):
    kept = first_half(lax.broadcasted_iota(jnp.int32, block.shape, 0), kind)
    zero = jnp.zeros_like(block)
    return jnp.concatenate([jnp.where(kept, block, zero), jnp.where(kept, zero, block)], axis=1)


def by_half(stacked, kind):
    rows = stacked.shape[0] // 2
    kept = first_half(lax.broadcasted_iota(jnp.int32, (rows, CELLS), 1), kind)
    return jnp.where(kept, stacked[:rows], stacked[rows:])


def side_blocks(strips, part, kind, cols):
    tile = lax.axis_index("tile")
    second, first = strips
    straight = (tile if kind else lax.div(tile, lax.axis_size("tile") // 4)) & 1 == 0
    first, second = first[part, :, cols], second[part, :, cols]
    return jnp.where(straight, first, second), jnp.where(straight, second, first)


def side_cells(strips, part, kind, cols):
    return jnp.concatenate(side_blocks(strips, part, kind, cols), axis=1)


def side_products(cells, rows_head):
    return [mm_nt(cells[kind], halves(rows_head, kind)) for kind in range(2)]


def turned_sides(strips, part, kind, cols):
    return [block.T for block in side_blocks(strips, part, kind, cols)]


def pair_cols(pair):
    return pl.ds(pl.multiple_of(pair * PAIR, PAIR), PAIR)


def head_rows(turned, head):
    return turned[head * HEAD_DIM : (head + 1) * HEAD_DIM]


def over_side(turned, head, kind, sides):
    return by_half(mm(jnp.concatenate([head_rows(t, head) for t in turned], axis=0), sides), kind)


SCORE_SCALE = HEAD_DIM ** (-0.5)
LOG_SCALE = SCORE_SCALE * math.log2(math.e)


def lanes_of(head):
    return slice(head * CELLS, (head + 1) * CELLS)


def centre_kernel(
    query_ref, key_ref, value_ref, dout_ref,
    raw_ref, stats_ref, sums_ref, product_ref, query_out, key_out, bias_ref,
):
    centre_bias(bias_ref)

    def step(pair, carry):
        cols = pair_cols(pair)
        query, key, value, dout = (ref[:, cols] for ref in (query_ref, key_ref, value_ref, dout_ref))
        turned = value.T
        for head in range(2):
            lanes = lanes_of(head)
            scores = mm_nt(key, one_head(query, head)) + bias_ref[...]
            top = jnp.max(scores, axis=0, keepdims=True)
            raw = jnp.exp2((scores - top) * LOG_SCALE)
            raw_ref[pair, :, lanes] = raw
            stats_ref[pair, 0:1, lanes] = top
            stats_ref[pair, 1:2, lanes] = jnp.sum(raw, axis=0, keepdims=True)
            sums_ref[pair, :, lanes] = mm(head_rows(turned, head), raw.astype(jnp.bfloat16))
            product_ref[pair, :, lanes] = mm_nt(value, one_head(dout, head))
        query_out[:, cols] = query
        key_out[:, cols] = key
        return carry

    lax.fori_loop(0, raw_ref.shape[0], step, 0)


def column_kernel(
    first_ref, second_ref, query_ref, dout_ref, raw_ref, stats_ref, sums_ref, product_ref, bias_ref
):
    strips = (first_ref, second_ref)
    strip_bias(0, bias_ref)

    def step(pair, carry):
        cols = pair_cols(pair)
        keys = side_cells(strips, 0, 0, cols)
        values = side_cells(strips, 1, 0, cols)
        turned = turned_sides(strips, 1, 0, cols)
        for head in range(2):
            lanes = lanes_of(head)
            scores = mm_nt(keys, halves(one_head(query_ref[:, cols], head), 0)) + bias_ref[...]
            top = jnp.max(scores, axis=0, keepdims=True)
            raw = jnp.exp2((scores - top) * LOG_SCALE)
            raw_ref[pair, :, lanes] = raw
            stats_ref[pair, 0:1, lanes] = top
            stats_ref[pair, 1:2, lanes] = jnp.sum(raw, axis=0, keepdims=True)
            sums_ref[pair, :, lanes] = over_side(turned, head, 0, raw.astype(jnp.bfloat16))
            product_ref[pair, :, lanes] = mm_nt(values, halves(one_head(dout_ref[:, cols], head), 0))
        return carry

    lax.fori_loop(0, raw_ref.shape[0], step, 0)


def row_kernel(
    first_ref, second_ref, query_ref, dout_turned_ref, centre_stats_ref, centre_sums_ref, stats_ref, sums_ref,
    raw_ref, attention_ref, rows_ref, factors_ref, bias_ref,
):
    strips = (first_ref, second_ref)
    strip_bias(1, bias_ref)

    def step(pair, carry):
        cols = pair_cols(pair)
        keys = side_cells(strips, 0, 1, cols)
        turned = turned_sides(strips, 1, 1, cols)
        parts = []
        for head in range(2):
            lanes = lanes_of(head)
            scores = mm_nt(keys, halves(one_head(query_ref[:, cols], head), 1)) + bias_ref[...]
            tops = [ref[pair, 0:1, lanes] for ref in (centre_stats_ref, stats_ref)]
            top = jnp.maximum(jnp.max(scores, axis=0, keepdims=True), jnp.maximum(*tops))
            raw = jnp.exp2((scores - top) * LOG_SCALE)
            raw_ref[pair, :, lanes] = raw
            lifted = [jnp.exp2((t - top) * LOG_SCALE) for t in tops]
            total = jnp.sum(raw, axis=0, keepdims=True)
            total += lifted[0] * centre_stats_ref[pair, 1:2, lanes] + lifted[1] * stats_ref[pair, 1:2, lanes]
            inverse = 1.0 / total
            factors = [l * inverse for l in lifted]
            part = over_side(turned, head, 1, raw.astype(jnp.bfloat16)) * inverse
            part += factors[0] * centre_sums_ref[pair, :, lanes] + factors[1] * sums_ref[pair, :, lanes]
            parts.append(part)
            place = pl.ds(2 * pair + head, 1)
            features = pl.ds(pl.multiple_of((2 * pair + head) * HEAD_DIM, HEAD_DIM), HEAD_DIM)
            product = dout_turned_ref[features, :].astype(jnp.float32) * part
            rows_ref[0, place, :] = top
            rows_ref[1, place, :] = inverse
            rows_ref[2, place, :] = jnp.sum(product, axis=0, keepdims=True)
            factors_ref[0, place, :] = factors[0]
            factors_ref[1, place, :] = factors[1]
        attention_ref[:, cols] = jnp.concatenate(parts, axis=0).T.astype(jnp.bfloat16)
        return carry

    lax.fori_loop(0, raw_ref.shape[0], step, 0, unroll=True)


def backward_kernel(
    fourth_ref, third_ref, second_ref, first_ref, query_ref, key_ref, dout_ref, centre_raw_ref, column_raw_ref,
    row_raw_ref, centre_product_ref, column_product_ref, rows_ref, factors_ref, unused_ref,
    grad_query_ref, centre_ref,
):
    columns, rows = (third_ref, fourth_ref), (first_ref, second_ref)

    def step(pair, carry):
        cols = pair_cols(pair)
        query = query_ref[:, cols]
        dout = dout_ref[:, cols]
        turned_centre = key_ref[:, cols].T
        turned_columns = turned_sides(columns, 0, 0, cols)
        turned_rows = turned_sides(rows, 0, 1, cols)
        row_values = side_cells(rows, 1, 1, cols)
        parts = []
        centre_scores = []
        centre_weights = []
        for head in range(2):
            lanes = lanes_of(head)
            place = pl.ds(2 * pair + head, 1)
            delta = rows_ref[2, place, :]
            row_product = mm_nt(row_values, halves(one_head(dout, head), 1))

            def dscore(weights, product):
                return (weights * (product - delta)).astype(jnp.bfloat16)

            weights = centre_raw_ref[pair, :, lanes] * factors_ref[0, place, :]
            centre_weights.append(weights.astype(jnp.bfloat16))
            centre_scores.append(dscore(weights, centre_product_ref[pair, :, lanes]))
            column_weights = column_raw_ref[pair, :, lanes] * factors_ref[1, place, :]
            column_score = dscore(column_weights, column_product_ref[pair, :, lanes])
            row_score = dscore(row_raw_ref[pair, :, lanes] * rows_ref[1, place, :], row_product)
            part = mm(head_rows(turned_centre, head), centre_scores[-1])
            part += over_side(turned_columns, head, 0, column_score) + over_side(turned_rows, head, 1, row_score)
            parts.append(part)
        grad_query = jnp.concatenate(parts, axis=0).T * SCORE_SCALE
        grad_query_ref[:, cols] = grad_query.astype(jnp.bfloat16)
        grad_key, grad_value = joint_mm(
            jnp.concatenate(centre_scores, axis=1),
            jnp.concatenate(centre_weights, axis=1),
            both_heads(query),
            both_heads(dout),
        )
        centre_ref[0, :, cols] = grad_key * SCORE_SCALE
        centre_ref[1, :, cols] = grad_value
        return carry

    lax.fori_loop(0, centre_raw_ref.shape[0], step, 0)


def joint_mm(first, second, first_rows, second_rows):
    rows = first.shape[0]
    product = mm(jnp.concatenate([first, second], axis=0), jnp.concatenate([first_rows, second_rows], axis=1))
    return product[:rows, :PAIR], product[rows:, PAIR:]


def both_heads(block):
    return jnp.concatenate([one_head(block, head) for head in range(2)], axis=0)


def padded(block):
    return jnp.concatenate([block, jnp.zeros((LANES - block.shape[0], block.shape[1]), block.dtype)], axis=0)


def statistics(rows):
    first = 0
    for count in PARTS:
        heads = []
        for head in range(2):
            parts = [rows[2 * index + head : 2 * index + head + 1] for index in range(first, first + count)]
            heads.append(functools.reduce(jnp.add, parts))
        first += count
        yield jnp.concatenate(heads, axis=1)


def side_kernel(columns, rotations_ref, centre_ref, *refs):
    picked, rims = refs[:4], refs[4:8]
    keys_ref, values_ref, chosen_ref, bias_ref, keys_done, values_done, sems = refs[8:]
    cell = lax.broadcasted_iota(jnp.int32, (STRIP, LANES), 0)
    query = lax.broadcasted_iota(jnp.int32, (STRIP, LANES), 1)
    near = jnp.abs((cell & (SIDE - 1)) - (query & (SIDE - 1))) <= RADIUS
    near = near & ((cell >> 4) >= (query >> 4)) & (query < STRIP)
    bias_ref[...] = jnp.where(near, 0.0, -1e30)
    token = lax.broadcasted_iota(jnp.int32, (CELLS, LANES), 0)
    place = lax.broadcasted_iota(jnp.int32, (CELLS, LANES), 1)
    for index, slot in enumerate(SIDE_ORDER):
        side = slot_side(slot, columns)
        wanted = jnp.where(place < STRIP, strip_token(side, rotations_ref[0, side], place), -1)
        chosen = jnp.where(token == wanted, 1.0, 0.0).astype(jnp.bfloat16)
        chosen_ref[:, index * LANES : (index + 1) * LANES] = chosen

    copies = []
    for pair in range(keys_ref.shape[1] // PAIR):
        cols = slice(pair * PAIR, (pair + 1) * PAIR)
        grads = []
        bias = jnp.concatenate([bias_ref[...]] * 2, axis=1)
        for picked_ref, rim_ref in zip(picked, rims):
            query = both_heads(padded(rim_ref[:STRIP, cols]))
            dout = both_heads(padded(rim_ref[STRIP : 2 * STRIP, cols]))
            top, inverse, delta = statistics(rim_ref[2 * STRIP :, cols].astype(jnp.float32))
            scores = mm_nt(picked_ref[0, :, cols], query) + bias
            weights = jnp.exp2((scores - top) * LOG_SCALE) * inverse
            product = mm_nt(picked_ref[1, :, cols], dout)
            dscore = (weights * (product - delta)).astype(jnp.bfloat16)
            grad = jnp.concatenate([mm(dscore, query) * SCORE_SCALE, mm(weights.astype(jnp.bfloat16), dout)], axis=1)
            grads.append(padded(grad.astype(jnp.bfloat16)))
        total = mm(chosen_ref[...], jnp.concatenate(grads, axis=0))
        keys_done[:, cols] = (centre_ref[0, :, cols] + total[:, :PAIR]).astype(jnp.bfloat16)
        values_done[:, cols] = (centre_ref[1, :, cols] + total[:, PAIR:]).astype(jnp.bfloat16)
        for index, (done, out_ref) in enumerate(((keys_done, keys_ref), (values_done, values_ref))):
            copy = pltpu.make_async_copy(done.at[:, cols], out_ref.at[:, cols], sems.at[2 * pair + index])
            copy.start()
            copies.append(copy)
    for copy in copies:
        copy.wait()


def call(kernel, name, out_shape, operands, scratch=(), smem=0, unused=0, gflop=0.1, out_space=pltpu.VMEM):
    specs = [pl.BlockSpec(memory_space=pltpu.SMEM)] * smem
    specs += [pl.BlockSpec(memory_space=pltpu.VMEM)] * (len(operands) - smem - unused)
    specs += [pl.BlockSpec(memory_space=pl.ANY)] * unused
    single = not isinstance(out_shape, list)
    outs = pl.BlockSpec(memory_space=out_space)
    return pl.pallas_call(
        kernel,
        out_shape=out_shape,
        in_specs=specs,
        out_specs=outs if single else [outs] * len(out_shape),
        scratch_shapes=list(scratch),
        compiler_params=pltpu.CompilerParams(vmem_limit_bytes=VMEM_LIMIT),
        cost_estimate=pl.CostEstimate(flops=int(gflop * 1e9), bytes_accessed=1 << 20, transcendentals=0),
        name=name,
    )(*operands)


def in_hbm(array):
    return pltpu.with_memory_space_constraint(array, pltpu.HBM)


def across(block, distances):
    heads = lax.axis_size("head")
    devices = [(tile, head) for tile in range(lax.axis_size("tile")) for head in range(heads)]
    route = [(tile * heads + head, (tile ^ distances[head % 2]) * heads + head) for tile, head in devices]
    return lax.ppermute(block, ("tile", "head"), route)


def exchanged(blocks, stride):
    terms = list(blocks[:1])
    for distance in range(1, len(blocks)):
        route = [(tile, tile ^ (distance * stride)) for tile in range(lax.axis_size("tile"))]
        terms.append(lax.ppermute(blocks[distance], "tile", route))
    return terms


def with_partners(blocks, slots):
    tile_count = lax.axis_size("tile")
    routes = {s: [(tile, partner(tile, tile_count, s)) for tile in range(tile_count)] for s in slots}
    return {s: lax.ppermute(blocks[s], "tile", routes[s]) for s in slots}


def shards(queries, keys, values, grad_output, out_weight, rotations):
    tile_count = lax.axis_size("tile")
    token_count, features = queries.shape
    model = out_weight.shape[0]
    pairs = features // PAIR
    far = tile_count // NEAR
    chunk = model // tile_count
    heads = lax.axis_size("head")
    columns = tile_count // 4
    queries, keys, values, out_weight, rotations = (
        in_hbm(a) for a in (queries, keys, values, out_weight, rotations)
    )

    def bf16(*shape):
        return jax.ShapeDtypeStruct(shape, jnp.bfloat16)

    def f32(*shape):
        return jax.ShapeDtypeStruct(shape, jnp.float32)

    strip_types = [bf16(2, STRIP, features)] * 4
    picked = call(
        functools.partial(pick_kernel, columns), "pick_strips", strip_types, (rotations, keys, values), smem=1
    )
    grad_output, *picked = lax.optimization_barrier((grad_output, *picked))
    strips = with_partners(picked, (3, 2, 1, 0))
    strips = [strips[s] for s in range(4)]

    cotangents = [
        lax.ppermute(grad_output, "head", [((h + k) % heads, h) for h in range(heads)]) for k in range(1, heads)
    ]
    dout, dout_turned, turned, turned_sent = call(
        functools.partial(cotangent_kernel, heads),
        "cotangent",
        [bf16(CELLS, features), bf16(features, CELLS)] + [bf16(2, far, chunk, CELLS)] * 2,
        (in_hbm(grad_output), *cotangents, out_weight),
        gflop=1.0,
    )
    turned_arrived = across(turned_sent, (1, 2))
    part_types = [f32(pairs, 2, 2 * CELLS), f32(pairs, HEAD_DIM, 2 * CELLS)]
    raw_centre, stats_centre, sums_centre, product_centre, queries, keys = call(
        centre_kernel,
        "centre",
        [f32(pairs, CELLS, 2 * CELLS)] + part_types + [f32(pairs, CELLS, 2 * CELLS)] + [bf16(CELLS, features)] * 2,
        (queries, keys, values, dout),
        scratch=[pltpu.VMEM((CELLS, CELLS), jnp.float32)],
        gflop=3.0,
    )
    strip_scratch = [pltpu.VMEM((STRIP, CELLS), jnp.float32)]
    raw_columns, stats_columns, sums_columns, product_columns = call(
        column_kernel,
        "columns",
        [f32(pairs, STRIP, 2 * CELLS)] + part_types + [f32(pairs, STRIP, 2 * CELLS)],
        (strips[2], strips[3], queries, dout),
        scratch=strip_scratch,
        gflop=2.0,
    )
    raw_rows, attention, rows, factors = call(
        row_kernel,
        "rows",
        [f32(pairs, STRIP, 2 * CELLS), bf16(CELLS, features)] + [f32(k, 2 * pairs, CELLS) for k in (3, 2)],
        (strips[0], strips[1], queries, dout_turned, stats_centre, sums_centre, stats_columns, sums_columns),
        scratch=strip_scratch,
    )
    attention_arrived = across(attention, (1, 2))
    rims = call(
        functools.partial(rim_kernel, columns),
        "rims",
        [bf16(2 * STRIP + 16, features)] * 4,
        (queries, dout, rows, turned_arrived),
        unused=1,
    )
    rims_arrived = with_partners(rims, (3, 2))
    kept, sent = call(
        partial_kernel,
        "partial",
        [f32(far, chunk, features), bf16(far, chunk, features)],
        (attention, attention_arrived, turned, turned_arrived, rims[0]),
        unused=1,
    )
    terms = [kept, across(sent, (2, 1))]
    rims = lax.optimization_barrier((*rims, sent))[:4]
    rims_arrived |= with_partners(rims, (1, 0))
    grad_queries, centre = call(
        backward_kernel,
        "backward",
        [bf16(CELLS, features), f32(2, CELLS, features)],
        (
            *strips[::-1], queries, keys, dout, raw_centre, raw_columns, raw_rows, product_centre, product_columns,
            rows, factors, sent,
        ),
        unused=1,
        gflop=3.0,
    )
    stride = NEAR
    while stride < tile_count:
        ways = min(NEAR, tile_count // stride)
        sums = call(
            functools.partial(sum_kernel, len(terms)),
            "plane_sum",
            [bf16(tile_count // stride // ways, chunk, features)] * ways,
            (*terms, centre, rims_arrived[3], rims_arrived[2]),
            unused=3,
        )
        terms = exchanged(sums, stride)
        stride *= ways

    grad_keys, grad_values = call(
        functools.partial(side_kernel, columns),
        "sides",
        [bf16(CELLS, features)] * 2,
        (rotations, centre, *(picked[s] for s in SIDE_ORDER), *(rims_arrived[s] for s in SIDE_ORDER)),
        scratch=[pltpu.VMEM((CELLS, 4 * LANES), jnp.bfloat16), pltpu.VMEM((STRIP, LANES), jnp.float32)]
        + [pltpu.VMEM((CELLS, features), jnp.bfloat16)] * 2
        + [pltpu.SemaphoreType.DMA((2 * pairs,))],
        smem=1,
        gflop=3.0,
        out_space=pl.ANY,
    )
    grad_out_weight = call(
        functools.partial(weight_kernel, 1.0 / math.sqrt(token_count * tile_count)),
        "weight_sum",
        f32(chunk, features),
        terms,
    )
    return (grad_queries, grad_keys, grad_values, grad_out_weight)


def solution(mesh):
    placed = (
        P("tile", "head"),
        P("tile", "head"),
        P("tile", "head"),
        P("tile", "head"),
        P(None, "head"),
        P("tile", None),
    )
    return jax.shard_map(
        shards,
        mesh=mesh,
        in_specs=placed,
        out_specs=(P("tile", "head"), P("tile", "head"), P("tile", "head"), P("tile", "head")),
        check_vma=False,
    )
```

```python
import functools
import math

import jax
import jax.numpy as jnp
from jax import lax
from jax.experimental import pallas as pl
from jax.experimental.pallas import tpu as pltpu
from jax.sharding import PartitionSpec as P

HEAD_DIM = 64
RADIUS = 6
SIDE = 16
CELLS = SIDE * SIDE
STRIP = RADIUS * SIDE
NEAR = 4
LANES = 128
PAIR = 2 * HEAD_DIM
VMEM_LIMIT = 32 * 1024 * 1024
NT = (((1,), (1,)), ((), ()))


def mm(a, b):
    return jnp.dot(a, b, preferred_element_type=jnp.float32)


def mm_nt(a, b):
    return lax.dot_general(a, b, NT, preferred_element_type=jnp.float32)


def strip_token(side_index, rotation, cell):
    turn = lax.rem(side_index + 6 - rotation, 4)
    depth = cell >> 4
    along = cell & (SIDE - 1)
    far = SIDE - 1 - along
    near_rim = RADIUS - 1 - depth
    far_rim = SIDE - RADIUS + depth
    row = jnp.where(turn == 0, far_rim, jnp.where(turn == 1, along, jnp.where(turn == 2, near_rim, far)))
    col = jnp.where(turn == 0, along, jnp.where(turn == 1, near_rim, jnp.where(turn == 2, far, far_rim)))
    return row * SIDE + col


def slot_side(slot, columns):
    tile = lax.axis_index("tile")
    if slot < 2:
        return jnp.where((tile + slot) & 1 == 0, 1, 3)
    return jnp.where((lax.div(tile, columns) + slot) & 1 == 0, 2, 0)


def partner(tile, tile_count, slot):
    columns = tile_count // 4
    if slot < 2:
        return (tile + (1 if (tile + slot) % 2 == 0 else -1)) % tile_count
    return (tile + (columns if (tile // columns + slot) % 2 == 0 else -columns)) % tile_count


def pick_kernel(columns, rotations_ref, keys_ref, values_ref, *out_refs):
    cell = lax.broadcasted_iota(jnp.int32, (STRIP, CELLS), 0)
    token = lax.broadcasted_iota(jnp.int32, (STRIP, CELLS), 1)
    for slot, out_ref in enumerate(out_refs):
        side = slot_side(slot, columns)
        wanted = strip_token(side, rotations_ref[0, side], cell)
        chosen = jnp.where(token == wanted, 1.0, 0.0).astype(jnp.bfloat16)
        out_ref[0] = mm(chosen, keys_ref[...]).astype(jnp.bfloat16)
        out_ref[1] = mm(chosen, values_ref[...]).astype(jnp.bfloat16)


def weight_kernel(scale, *refs):
    total = refs[0][0].astype(jnp.float32)
    for ref in refs[1:-1]:
        total += ref[0].astype(jnp.float32)
    refs[-1][...] = total * scale


def partial_kernel(attention_ref, arrived_ref, turned_ref, turned_arrived_ref, unused_ref, kept_ref, sent_ref):
    for index, out_ref in enumerate((kept_ref, sent_ref)):
        total = None
        for turned_part, attention_part in ((turned_ref, attention_ref), (turned_arrived_ref, arrived_ref)):
            turned = turned_part[index]
            turned = turned.reshape(turned.shape[0] * turned.shape[1], turned.shape[2])
            term = mm(turned, attention_part[...])
            total = term if total is None else total + term
        out_ref[...] = total.astype(out_ref.dtype).reshape(out_ref.shape)


def mark_kernel(*refs):
    refs[-1][...] = jnp.zeros(refs[-1].shape, refs[-1].dtype)


def sum_kernel(count, *refs):
    terms, outs = refs[:count], refs[count + 1 :]
    for q in range(terms[0].shape[0]):
        total = terms[0][q].astype(jnp.float32)
        for ref in terms[1:]:
            total += ref[q].astype(jnp.float32)
        outs[q % len(outs)][q // len(outs)] = total.astype(jnp.bfloat16)


def rim_token(side_index, place):
    depth = place >> 4
    along = place & (SIDE - 1)
    last = SIDE - 1
    north, east, south = side_index == 0, side_index == 1, side_index == 2
    row = jnp.where(north, depth, jnp.where(east, along, jnp.where(south, last - depth, last - along)))
    col = jnp.where(north, along, jnp.where(east, last - depth, jnp.where(south, last - along, depth)))
    return row * SIDE + col


def cotangent_kernel(heads, *refs):
    blocks, out_weight_ref, outs = refs[:heads], refs[heads], refs[heads + 1 :]
    dout_ref, dout_turned_ref, turned_ref, turned_sent_ref = outs
    head = lax.axis_index("head")
    axis = head & 1
    tile = lax.axis_index("tile")
    chunk = turned_ref.shape[2]
    width = blocks[0].shape[1]
    total = None
    for distance, block_ref in enumerate(blocks):
        owner = lax.rem(head + distance, heads)
        start = pl.multiple_of(owner * width, width)
        block = block_ref[...]
        term = mm(block, out_weight_ref[pl.ds(start, width), :])
        total = term if total is None else total + term
        turned = block.T
        first = owner * (width // chunk)
        for index in range(width // chunk):
            target = (first + index) ^ tile
            rows = turned[index * chunk : (index + 1) * chunk]
            for parity, out_ref in enumerate((turned_ref, turned_sent_ref)):

                @pl.when((target >> axis) & 1 == parity)
                def _():
                    out_ref[(target >> (1 - axis)) & 1, target >> 2] = rows

    dout = total.astype(jnp.bfloat16)
    dout_ref[...] = dout
    dout_turned_ref[...] = dout.T


def split(exact, count):
    parts = []
    for _ in range(count):
        part = exact.astype(jnp.bfloat16).astype(jnp.float32)
        parts.append(part)
        exact = exact - part
    return parts


PARTS = (3, 2, 2)
SIDE_ORDER = (3, 2, 1, 0)


def rim_kernel(columns, query_ref, dout_ref, rows_ref, unused_ref, *rim_refs):
    place = lax.broadcasted_iota(jnp.int32, (LANES, CELLS), 0)
    token = lax.broadcasted_iota(jnp.int32, (LANES, CELLS), 1)
    parts = [part for kind, count in enumerate(PARTS) for part in split(rows_ref[kind], count)]
    pairs = rows_ref.shape[1] // 2
    filler = jnp.zeros((16 - 2 * len(parts), CELLS), jnp.float32)
    rows = [
        jnp.concatenate([part[2 * pair : 2 * pair + 2] for part in parts] + [filler], axis=0) for pair in range(pairs)
    ]
    rows = jnp.concatenate(rows, axis=0).astype(jnp.bfloat16)
    for slot, rim_ref in enumerate(rim_refs, 2):
        wanted = rim_token(slot_side(slot, columns), place)
        chosen = jnp.where((token == wanted) & (place < STRIP), 1.0, 0.0).astype(jnp.bfloat16)
        rim_ref[:STRIP] = mm(chosen[:STRIP], query_ref[...]).astype(jnp.bfloat16)
        rim_ref[STRIP : 2 * STRIP] = mm(chosen[:STRIP], dout_ref[...]).astype(jnp.bfloat16)
        spread = mm_nt(rows, chosen).astype(jnp.bfloat16)
        for pair in range(pairs):
            rim_ref[2 * STRIP :, pair * PAIR : (pair + 1) * PAIR] = spread[16 * pair : 16 * pair + 16]


def window(cell_row, cell_col, query):
    query_row = (query >> 4) + RADIUS
    query_col = (query & (SIDE - 1)) + RADIUS
    near = (jnp.abs(cell_row - query_row) <= RADIUS) & (jnp.abs(cell_col - query_col) <= RADIUS)
    return jnp.where(near, 0.0, -1e30)


def centre_bias(bias_ref):
    query = lax.broadcasted_iota(jnp.int32, (CELLS, CELLS), 1)
    cell = lax.broadcasted_iota(jnp.int32, (CELLS, CELLS), 0)
    bias_ref[...] = window((cell >> 4) + RADIUS, (cell & (SIDE - 1)) + RADIUS, query)


def strip_bias(kind, bias_ref):
    query = lax.broadcasted_iota(jnp.int32, (STRIP, CELLS), 1)
    cell = lax.broadcasted_iota(jnp.int32, (STRIP, CELLS), 0)
    depth = cell >> 4
    along = cell & (SIDE - 1)
    last = SIDE + 2 * RADIUS - 1
    if kind:
        first, second = (last - RADIUS - along, depth), (RADIUS + along, last - depth)
    else:
        first, second = (depth, RADIUS + along), (last - depth, last - RADIUS - along)
    in_first = first_half(query, kind)
    row = jnp.where(in_first, first[0], second[0])
    col = jnp.where(in_first, first[1], second[1])
    bias_ref[...] = window(row, col, query)


def first_half(query, kind):
    return (query & (SIDE - 1)) < SIDE // 2 if kind else query < CELLS // 2


def one_head(block, head):
    lane = lax.broadcasted_iota(jnp.int32, block.shape, 1)
    kept = (lane >= HEAD_DIM) if head else (lane < HEAD_DIM)
    return jnp.where(kept, block, jnp.zeros_like(block))


def halves(block, kind):
    kept = first_half(lax.broadcasted_iota(jnp.int32, block.shape, 0), kind)
    zero = jnp.zeros_like(block)
    return jnp.concatenate([jnp.where(kept, block, zero), jnp.where(kept, zero, block)], axis=1)


def by_half(stacked, kind):
    rows = stacked.shape[0] // 2
    kept = first_half(lax.broadcasted_iota(jnp.int32, (rows, CELLS), 1), kind)
    return jnp.where(kept, stacked[:rows], stacked[rows:])


def side_blocks(strips, part, kind, cols):
    tile = lax.axis_index("tile")
    second, first = strips
    straight = (tile if kind else lax.div(tile, lax.axis_size("tile") // 4)) & 1 == 0
    first, second = first[part, :, cols], second[part, :, cols]
    return jnp.where(straight, first, second), jnp.where(straight, second, first)


def side_cells(strips, part, kind, cols):
    return jnp.concatenate(side_blocks(strips, part, kind, cols), axis=1)


def halves(block, kind):
    kept = first_half(lax.broadcasted_iota(jnp.int32, block.shape, 0), kind)
    zero = jnp.zeros_like(block)
    return jnp.concatenate([jnp.where(kept, block, zero), jnp.where(kept, zero, block)], axis=1)


def by_half(stacked, kind):
    rows = stacked.shape[0] // 2
    kept = first_half(lax.broadcasted_iota(jnp.int32, (rows, CELLS), 1), kind)
    return jnp.where(kept, stacked[:rows], stacked[rows:])


def side_blocks(strips, part, kind, cols):
    tile = lax.axis_index("tile")
    second, first = strips
    straight = (tile if kind else lax.div(tile, lax.axis_size("tile") // 4)) & 1 == 0
    first, second = first[part, :, cols], second[part, :, cols]
    return jnp.where(straight, first, second), jnp.where(straight, second, first)


def side_cells(strips, part, kind, cols):
    return jnp.concatenate(side_blocks(strips, part, kind, cols), axis=1)


def side_products(cells, rows_head):
    return [mm_nt(cells[kind], halves(rows_head, kind)) for kind in range(2)]


def turned_sides(strips, part, kind, cols):
    return [block.T for block in side_blocks(strips, part, kind, cols)]


def pair_cols(pair):
    return pl.ds(pl.multiple_of(pair * PAIR, PAIR), PAIR)


def head_rows(turned, head):
    return turned[head * HEAD_DIM : (head + 1) * HEAD_DIM]


def over_side(turned, head, kind, sides):
    return by_half(mm(jnp.concatenate([head_rows(t, head) for t in turned], axis=0), sides), kind)


SCORE_SCALE = HEAD_DIM ** (-0.5)
LOG_SCALE = SCORE_SCALE * math.log2(math.e)


def lanes_of(head):
    return slice(head * CELLS, (head + 1) * CELLS)


def centre_kernel(
    query_ref, key_ref, value_ref, dout_ref,
    raw_ref, stats_ref, sums_ref, product_ref, query_out, key_out, bias_ref,
):
    centre_bias(bias_ref)

    def step(pair, carry):
        cols = pair_cols(pair)
        query, key, value, dout = (ref[:, cols] for ref in (query_ref, key_ref, value_ref, dout_ref))
        turned = value.T
        for head in range(2):
            lanes = lanes_of(head)
            scores = mm_nt(key, one_head(query, head)) + bias_ref[...]
            top = jnp.max(scores, axis=0, keepdims=True)
            raw = jnp.exp2((scores - top) * LOG_SCALE)
            raw_ref[pair, :, lanes] = raw
            stats_ref[pair, 0:1, lanes] = top
            stats_ref[pair, 1:2, lanes] = jnp.sum(raw, axis=0, keepdims=True)
            sums_ref[pair, :, lanes] = mm(head_rows(turned, head), raw.astype(jnp.bfloat16))
            product_ref[pair, :, lanes] = mm_nt(value, one_head(dout, head))
        query_out[:, cols] = query
        key_out[:, cols] = key
        return carry

    lax.fori_loop(0, raw_ref.shape[0], step, 0)


def column_kernel(
    first_ref, second_ref, query_ref, dout_ref, raw_ref, stats_ref, sums_ref, product_ref, bias_ref
):
    strips = (first_ref, second_ref)
    strip_bias(0, bias_ref)

    def step(pair, carry):
        cols = pair_cols(pair)
        keys = side_cells(strips, 0, 0, cols)
        values = side_cells(strips, 1, 0, cols)
        turned = turned_sides(strips, 1, 0, cols)
        for head in range(2):
            lanes = lanes_of(head)
            scores = mm_nt(keys, halves(one_head(query_ref[:, cols], head), 0)) + bias_ref[...]
            top = jnp.max(scores, axis=0, keepdims=True)
            raw = jnp.exp2((scores - top) * LOG_SCALE)
            raw_ref[pair, :, lanes] = raw
            stats_ref[pair, 0:1, lanes] = top
            stats_ref[pair, 1:2, lanes] = jnp.sum(raw, axis=0, keepdims=True)
            sums_ref[pair, :, lanes] = over_side(turned, head, 0, raw.astype(jnp.bfloat16))
            product_ref[pair, :, lanes] = mm_nt(values, halves(one_head(dout_ref[:, cols], head), 0))
        return carry

    lax.fori_loop(0, raw_ref.shape[0], step, 0)


def row_kernel(
    first_ref, second_ref, query_ref, dout_turned_ref, centre_stats_ref, centre_sums_ref, stats_ref, sums_ref,
    raw_ref, attention_ref, rows_ref, factors_ref, bias_ref,
):
    strips = (first_ref, second_ref)
    strip_bias(1, bias_ref)

    def step(pair, carry):
        cols = pair_cols(pair)
        keys = side_cells(strips, 0, 1, cols)
        turned = turned_sides(strips, 1, 1, cols)
        parts = []
        for head in range(2):
            lanes = lanes_of(head)
            scores = mm_nt(keys, halves(one_head(query_ref[:, cols], head), 1)) + bias_ref[...]
            tops = [ref[pair, 0:1, lanes] for ref in (centre_stats_ref, stats_ref)]
            top = jnp.maximum(jnp.max(scores, axis=0, keepdims=True), jnp.maximum(*tops))
            raw = jnp.exp2((scores - top) * LOG_SCALE)
            raw_ref[pair, :, lanes] = raw
            lifted = [jnp.exp2((t - top) * LOG_SCALE) for t in tops]
            total = jnp.sum(raw, axis=0, keepdims=True)
            total += lifted[0] * centre_stats_ref[pair, 1:2, lanes] + lifted[1] * stats_ref[pair, 1:2, lanes]
            inverse = 1.0 / total
            factors = [l * inverse for l in lifted]
            part = over_side(turned, head, 1, raw.astype(jnp.bfloat16)) * inverse
            part += factors[0] * centre_sums_ref[pair, :, lanes] + factors[1] * sums_ref[pair, :, lanes]
            parts.append(part)
            place = pl.ds(2 * pair + head, 1)
            features = pl.ds(pl.multiple_of((2 * pair + head) * HEAD_DIM, HEAD_DIM), HEAD_DIM)
            product = dout_turned_ref[features, :].astype(jnp.float32) * part
            rows_ref[0, place, :] = top
            rows_ref[1, place, :] = inverse
            rows_ref[2, place, :] = jnp.sum(product, axis=0, keepdims=True)
            factors_ref[0, place, :] = factors[0]
            factors_ref[1, place, :] = factors[1]
        attention_ref[:, cols] = jnp.concatenate(parts, axis=0).T.astype(jnp.bfloat16)
        return carry

    lax.fori_loop(0, raw_ref.shape[0], step, 0, unroll=True)


def backward_kernel(
    fourth_ref, third_ref, second_ref, first_ref, query_ref, key_ref, dout_ref, centre_raw_ref, column_raw_ref,
    row_raw_ref, centre_product_ref, column_product_ref, rows_ref, factors_ref, unused_ref,
    grad_query_ref, centre_ref, first_out, second_out,
):
    columns, rows = (third_ref, fourth_ref), (first_ref, second_ref)
    straight = lax.axis_index("tile") & 1 == 0

    def step(pair, carry):
        cols = pair_cols(pair)
        query = query_ref[:, cols]
        dout = dout_ref[:, cols]
        turned_centre = key_ref[:, cols].T
        turned_columns = turned_sides(columns, 0, 0, cols)
        turned_rows = turned_sides(rows, 0, 1, cols)
        row_values = side_cells(rows, 1, 1, cols)
        parts = []
        centre_scores = []
        centre_weights = []
        row_scores = []
        row_weights = []
        query_halves = []
        dout_halves = []
        for head in range(2):
            lanes = lanes_of(head)
            place = pl.ds(2 * pair + head, 1)
            delta = rows_ref[2, place, :]
            query_halves.append(halves(one_head(query, head), 1))
            dout_halves.append(halves(one_head(dout, head), 1))
            row_product = mm_nt(row_values, dout_halves[-1])

            def dscore(weights, product):
                return (weights * (product - delta)).astype(jnp.bfloat16)

            weights = centre_raw_ref[pair, :, lanes] * factors_ref[0, place, :]
            centre_weights.append(weights.astype(jnp.bfloat16))
            centre_scores.append(dscore(weights, centre_product_ref[pair, :, lanes]))
            column_weights = column_raw_ref[pair, :, lanes] * factors_ref[1, place, :]
            column_score = dscore(column_weights, column_product_ref[pair, :, lanes])
            weights = row_raw_ref[pair, :, lanes] * rows_ref[1, place, :]
            row_weights.append(weights.astype(jnp.bfloat16))
            row_score = dscore(weights, row_product)
            row_scores.append(row_score)
            part = mm(head_rows(turned_centre, head), centre_scores[-1])
            part += over_side(turned_columns, head, 0, column_score) + over_side(turned_rows, head, 1, row_score)
            parts.append(part)
        grad_query = jnp.concatenate(parts, axis=0).T * SCORE_SCALE
        grad_query_ref[:, cols] = grad_query.astype(jnp.bfloat16)
        grad_key, grad_value = joint_mm(
            jnp.concatenate(centre_scores, axis=1),
            jnp.concatenate(centre_weights, axis=1),
            both_heads(query),
            both_heads(dout),
        )
        centre_ref[0, :, cols] = grad_key * SCORE_SCALE
        centre_ref[1, :, cols] = grad_value
        west_east = (
            mm(jnp.concatenate(row_scores, axis=1), jnp.concatenate(query_halves, axis=0)) * SCORE_SCALE,
            mm(jnp.concatenate(row_weights, axis=1), jnp.concatenate(dout_halves, axis=0)),
        )
        for part, grads in enumerate(west_east):
            grads = grads.astype(jnp.bfloat16)
            west, east = grads[:, :PAIR], grads[:, PAIR:]
            first_out[part, :, cols] = jnp.where(straight, east, west)
            second_out[part, :, cols] = jnp.where(straight, west, east)
        return carry

    lax.fori_loop(0, centre_raw_ref.shape[0], step, 0)


def joint_mm(first, second, first_rows, second_rows):
    rows = first.shape[0]
    product = mm(jnp.concatenate([first, second], axis=0), jnp.concatenate([first_rows, second_rows], axis=1))
    return product[:rows, :PAIR], product[rows:, PAIR:]


def both_heads(block):
    return jnp.concatenate([one_head(block, head) for head in range(2)], axis=0)


def padded(block):
    return jnp.concatenate([block, jnp.zeros((LANES - block.shape[0], block.shape[1]), block.dtype)], axis=0)


def statistics(rows):
    first = 0
    for count in PARTS:
        heads = []
        for head in range(2):
            parts = [rows[2 * index + head : 2 * index + head + 1] for index in range(first, first + count)]
            heads.append(functools.reduce(jnp.add, parts))
        first += count
        yield jnp.concatenate(heads, axis=1)


def side_kernel(columns, rotations_ref, centre_ref, *refs):
    picked, rims, arrived = refs[:2], refs[2:4], refs[4:6]
    keys_ref, values_ref, chosen_ref, bias_ref, keys_done, values_done, sems = refs[6:]
    cell = lax.broadcasted_iota(jnp.int32, (STRIP, LANES), 0)
    query = lax.broadcasted_iota(jnp.int32, (STRIP, LANES), 1)
    near = jnp.abs((cell & (SIDE - 1)) - (query & (SIDE - 1))) <= RADIUS
    near = near & ((cell >> 4) >= (query >> 4)) & (query < STRIP)
    bias_ref[...] = jnp.where(near, 0.0, -1e30)
    token = lax.broadcasted_iota(jnp.int32, (CELLS, LANES), 0)
    place = lax.broadcasted_iota(jnp.int32, (CELLS, LANES), 1)
    for index, slot in enumerate(SIDE_ORDER):
        side = slot_side(slot, columns)
        wanted = jnp.where(place < STRIP, strip_token(side, rotations_ref[0, side], place), -1)
        chosen = jnp.where(token == wanted, 1.0, 0.0).astype(jnp.bfloat16)
        chosen_ref[:, index * LANES : (index + 1) * LANES] = chosen

    copies = []
    for pair in range(keys_ref.shape[1] // PAIR):
        cols = slice(pair * PAIR, (pair + 1) * PAIR)
        grads = []
        bias = jnp.concatenate([bias_ref[...]] * 2, axis=1)
        for picked_ref, rim_ref in zip(picked, rims):
            query = both_heads(padded(rim_ref[:STRIP, cols]))
            dout = both_heads(padded(rim_ref[STRIP : 2 * STRIP, cols]))
            top, inverse, delta = statistics(rim_ref[2 * STRIP :, cols].astype(jnp.float32))
            scores = mm_nt(picked_ref[0, :, cols], query) + bias
            weights = jnp.exp2((scores - top) * LOG_SCALE) * inverse
            product = mm_nt(picked_ref[1, :, cols], dout)
            dscore = (weights * (product - delta)).astype(jnp.bfloat16)
            grad = jnp.concatenate([mm(dscore, query) * SCORE_SCALE, mm(weights.astype(jnp.bfloat16), dout)], axis=1)
            grads.append(padded(grad.astype(jnp.bfloat16)))
        for ref in arrived:
            grads.append(padded(jnp.concatenate([ref[0, :, cols], ref[1, :, cols]], axis=1)))
        total = mm(chosen_ref[...], jnp.concatenate(grads, axis=0))
        keys_done[:, cols] = (centre_ref[0, :, cols] + total[:, :PAIR]).astype(jnp.bfloat16)
        values_done[:, cols] = (centre_ref[1, :, cols] + total[:, PAIR:]).astype(jnp.bfloat16)
        for index, (done, out_ref) in enumerate(((keys_done, keys_ref), (values_done, values_ref))):
            copy = pltpu.make_async_copy(done.at[:, cols], out_ref.at[:, cols], sems.at[2 * pair + index])
            copy.start()
            copies.append(copy)
    for copy in copies:
        copy.wait()


def call(kernel, name, out_shape, operands, scratch=(), smem=0, unused=0, gflop=0.1, out_space=pltpu.VMEM):
    specs = [pl.BlockSpec(memory_space=pltpu.SMEM)] * smem
    specs += [pl.BlockSpec(memory_space=pltpu.VMEM)] * (len(operands) - smem - unused)
    specs += [pl.BlockSpec(memory_space=pl.ANY)] * unused
    single = not isinstance(out_shape, list)
    outs = pl.BlockSpec(memory_space=out_space)
    return pl.pallas_call(
        kernel,
        out_shape=out_shape,
        in_specs=specs,
        out_specs=outs if single else [outs] * len(out_shape),
        scratch_shapes=list(scratch),
        compiler_params=pltpu.CompilerParams(vmem_limit_bytes=VMEM_LIMIT),
        cost_estimate=pl.CostEstimate(flops=int(gflop * 1e9), bytes_accessed=1 << 20, transcendentals=0),
        name=name,
    )(*operands)


def in_hbm(array):
    return pltpu.with_memory_space_constraint(array, pltpu.HBM)


def across(block, distances):
    heads = lax.axis_size("head")
    devices = [(tile, head) for tile in range(lax.axis_size("tile")) for head in range(heads)]
    route = [(tile * heads + head, (tile ^ distances[head % 2]) * heads + head) for tile, head in devices]
    return lax.ppermute(block, ("tile", "head"), route)


def exchanged(blocks, stride):
    terms = list(blocks[:1])
    for distance in range(1, len(blocks)):
        route = [(tile, tile ^ (distance * stride)) for tile in range(lax.axis_size("tile"))]
        terms.append(lax.ppermute(blocks[distance], "tile", route))
    return terms


def with_partners(blocks, slots):
    tile_count = lax.axis_size("tile")
    routes = {s: [(tile, partner(tile, tile_count, s)) for tile in range(tile_count)] for s in slots}
    return {s: lax.ppermute(blocks[s], "tile", routes[s]) for s in slots}


def shards(queries, keys, values, grad_output, out_weight, rotations):
    tile_count = lax.axis_size("tile")
    token_count, features = queries.shape
    model = out_weight.shape[0]
    pairs = features // PAIR
    far = tile_count // NEAR
    chunk = model // tile_count
    heads = lax.axis_size("head")
    columns = tile_count // 4
    queries, keys, values, out_weight, rotations = (
        in_hbm(a) for a in (queries, keys, values, out_weight, rotations)
    )

    def bf16(*shape):
        return jax.ShapeDtypeStruct(shape, jnp.bfloat16)

    def f32(*shape):
        return jax.ShapeDtypeStruct(shape, jnp.float32)

    strip_types = [bf16(2, STRIP, features)] * 4
    picked = call(
        functools.partial(pick_kernel, columns), "pick_strips", strip_types, (rotations, keys, values), smem=1
    )
    grad_output, *picked = lax.optimization_barrier((grad_output, *picked))
    strips = with_partners(picked, (3, 2, 1, 0))
    strips = [strips[s] for s in range(4)]

    cotangents = [
        lax.ppermute(grad_output, "head", [((h + k) % heads, h) for h in range(heads)]) for k in range(1, heads)
    ]
    dout, dout_turned, turned, turned_sent = call(
        functools.partial(cotangent_kernel, heads),
        "cotangent",
        [bf16(CELLS, features), bf16(features, CELLS)] + [bf16(2, far, chunk, CELLS)] * 2,
        (in_hbm(grad_output), *cotangents, out_weight),
        gflop=1.0,
    )
    turned_arrived = across(turned_sent, (1, 2))
    part_types = [f32(pairs, 2, 2 * CELLS), f32(pairs, HEAD_DIM, 2 * CELLS)]
    raw_centre, stats_centre, sums_centre, product_centre, queries, keys = call(
        centre_kernel,
        "centre",
        [f32(pairs, CELLS, 2 * CELLS)] + part_types + [f32(pairs, CELLS, 2 * CELLS)] + [bf16(CELLS, features)] * 2,
        (queries, keys, values, dout),
        scratch=[pltpu.VMEM((CELLS, CELLS), jnp.float32)],
        gflop=3.0,
    )
    strip_scratch = [pltpu.VMEM((STRIP, CELLS), jnp.float32)]
    raw_columns, stats_columns, sums_columns, product_columns = call(
        column_kernel,
        "columns",
        [f32(pairs, STRIP, 2 * CELLS)] + part_types + [f32(pairs, STRIP, 2 * CELLS)],
        (strips[2], strips[3], queries, dout),
        scratch=strip_scratch,
        gflop=2.0,
    )
    raw_rows, attention, rows, factors = call(
        row_kernel,
        "rows",
        [f32(pairs, STRIP, 2 * CELLS), bf16(CELLS, features)] + [f32(k, 2 * pairs, CELLS) for k in (3, 2)],
        (strips[0], strips[1], queries, dout_turned, stats_centre, sums_centre, stats_columns, sums_columns),
        scratch=strip_scratch,
    )
    attention_arrived = across(attention, (1, 2))
    rims = call(
        functools.partial(rim_kernel, columns),
        "rims",
        [bf16(2 * STRIP + 16, features)] * 2,
        (queries, dout, rows, turned_arrived),
        unused=1,
    )
    rims = dict(enumerate(rims, 2))
    rims_arrived = with_partners(rims, (3, 2))
    grad_queries, centre, *backs = call(
        backward_kernel,
        "backward",
        [bf16(CELLS, features), f32(2, CELLS, features)] + strip_types[:2],
        (
            *strips[::-1], queries, keys, dout, raw_centre, raw_columns, raw_rows, product_centre, product_columns,
            rows, factors, rims[3],
        ),
        unused=1,
        gflop=3.0,
    )
    kept, sent = call(
        partial_kernel,
        "partial",
        [f32(far, chunk, features), bf16(far, chunk, features)],
        (attention, attention_arrived, turned, turned_arrived, centre),
        unused=1,
    )
    terms = [kept, across(sent, (2, 1))]
    backs = dict(enumerate(lax.optimization_barrier((*backs, sent))[:2]))
    backs_arrived = with_partners(backs, (0, 1))

    here = call(
        mark_kernel,
        "rims_here",
        f32(8, LANES),
        (centre, rims_arrived[3], rims_arrived[2]),
        unused=3,
        gflop=3.0,
    )
    stride = NEAR
    while stride < tile_count:
        ways = min(NEAR, tile_count // stride)
        sums = call(
            functools.partial(sum_kernel, len(terms)),
            "plane_sum",
            [bf16(tile_count // stride // ways, chunk, features)] * ways,
            (*terms, here),
            unused=1,
        )
        terms = exchanged(sums, stride)
        stride *= ways

    grad_keys, grad_values = call(
        functools.partial(side_kernel, columns),
        "sides",
        [bf16(CELLS, features)] * 2,
        (
            rotations, centre, picked[3], picked[2], rims_arrived[3], rims_arrived[2], backs_arrived[1], backs_arrived[0]
        ),
        scratch=[pltpu.VMEM((CELLS, 4 * LANES), jnp.bfloat16), pltpu.VMEM((STRIP, LANES), jnp.float32)]
        + [pltpu.VMEM((CELLS, features), jnp.bfloat16)] * 2
        + [pltpu.SemaphoreType.DMA((2 * pairs,))],
        smem=1,
        gflop=3.0,
        out_space=pl.ANY,
    )
    grad_out_weight = call(
        functools.partial(weight_kernel, 1.0 / math.sqrt(token_count * tile_count)),
        "weight_sum",
        f32(chunk, features),
        terms,
    )
    return (grad_queries, grad_keys, grad_values, grad_out_weight)


def solution(mesh):
    placed = (
        P("tile", "head"),
        P("tile", "head"),
        P("tile", "head"),
        P("tile", "head"),
        P(None, "head"),
        P("tile", None),
    )
    return jax.shard_map(
        shards,
        mesh=mesh,
        in_specs=placed,
        out_specs=(P("tile", "head"), P("tile", "head"), P("tile", "head"), P("tile", "head")),
        check_vma=False,
    )
```

```python
import functools
import math

import jax
import jax.numpy as jnp
from jax import lax
from jax.experimental import pallas as pl
from jax.experimental.pallas import tpu as pltpu
from jax.sharding import PartitionSpec as P

HEAD_DIM = 64
RADIUS = 6
SIDE = 16
CELLS = SIDE * SIDE
STRIP = RADIUS * SIDE
NEAR = 4
LANES = 128
PAIR = 2 * HEAD_DIM
VMEM_LIMIT = 32 * 1024 * 1024
NT = (((1,), (1,)), ((), ()))


def mm(a, b):
    return jnp.dot(a, b, preferred_element_type=jnp.float32)


def mm_nt(a, b):
    return lax.dot_general(a, b, NT, preferred_element_type=jnp.float32)


def strip_token(side_index, rotation, cell):
    turn = lax.rem(side_index + 6 - rotation, 4)
    depth = cell >> 4
    along = cell & (SIDE - 1)
    far = SIDE - 1 - along
    near_rim = RADIUS - 1 - depth
    far_rim = SIDE - RADIUS + depth
    row = jnp.where(turn == 0, far_rim, jnp.where(turn == 1, along, jnp.where(turn == 2, near_rim, far)))
    col = jnp.where(turn == 0, along, jnp.where(turn == 1, near_rim, jnp.where(turn == 2, far, far_rim)))
    return row * SIDE + col


def slot_side(slot, columns):
    tile = lax.axis_index("tile")
    if slot < 2:
        return jnp.where((tile + slot) & 1 == 0, 1, 3)
    return jnp.where((lax.div(tile, columns) + slot) & 1 == 0, 2, 0)


def partner(tile, tile_count, slot):
    columns = tile_count // 4
    if slot < 2:
        return (tile + (1 if (tile + slot) % 2 == 0 else -1)) % tile_count
    return (tile + (columns if (tile // columns + slot) % 2 == 0 else -columns)) % tile_count


def pick_kernel(columns, rotations_ref, keys_ref, values_ref, *out_refs):
    cell = lax.broadcasted_iota(jnp.int32, (STRIP, CELLS), 0)
    token = lax.broadcasted_iota(jnp.int32, (STRIP, CELLS), 1)
    for slot, out_ref in enumerate(out_refs):
        side = slot_side(slot, columns)
        wanted = strip_token(side, rotations_ref[0, side], cell)
        chosen = jnp.where(token == wanted, 1.0, 0.0).astype(jnp.bfloat16)
        out_ref[0] = mm(chosen, keys_ref[...]).astype(jnp.bfloat16)
        out_ref[1] = mm(chosen, values_ref[...]).astype(jnp.bfloat16)


def weight_kernel(scale, *refs):
    total = refs[0][0].astype(jnp.float32)
    for ref in refs[1:-1]:
        total += ref[0].astype(jnp.float32)
    refs[-1][...] = total * scale


def partial_kernel(attention_ref, arrived_ref, turned_ref, turned_arrived_ref, unused_ref, kept_ref, sent_ref):
    for index, out_ref in enumerate((kept_ref, sent_ref)):
        total = None
        for turned_part, attention_part in ((turned_ref, attention_ref), (turned_arrived_ref, arrived_ref)):
            turned = turned_part[index]
            turned = turned.reshape(turned.shape[0] * turned.shape[1], turned.shape[2])
            term = mm(turned, attention_part[...])
            total = term if total is None else total + term
        out_ref[...] = total.astype(out_ref.dtype).reshape(out_ref.shape)


def mark_kernel(*refs):
    refs[-1][...] = jnp.zeros(refs[-1].shape, refs[-1].dtype)


def sum_kernel(count, *refs):
    terms, outs = refs[:count], refs[count + 1 :]
    for q in range(terms[0].shape[0]):
        total = terms[0][q].astype(jnp.float32)
        for ref in terms[1:]:
            total += ref[q].astype(jnp.float32)
        outs[q % len(outs)][q // len(outs)] = total.astype(jnp.bfloat16)


def rim_token(side_index, place):
    depth = place >> 4
    along = place & (SIDE - 1)
    last = SIDE - 1
    north, east, south = side_index == 0, side_index == 1, side_index == 2
    row = jnp.where(north, depth, jnp.where(east, along, jnp.where(south, last - depth, last - along)))
    col = jnp.where(north, along, jnp.where(east, last - depth, jnp.where(south, last - along, depth)))
    return row * SIDE + col


def cotangent_kernel(heads, *refs):
    blocks, out_weight_ref, outs = refs[:heads], refs[heads], refs[heads + 1 :]
    dout_ref, dout_turned_ref, turned_ref, turned_sent_ref = outs
    head = lax.axis_index("head")
    axis = head & 1
    tile = lax.axis_index("tile")
    chunk = turned_ref.shape[2]
    width = blocks[0].shape[1]
    total = None
    for distance, block_ref in enumerate(blocks):
        owner = lax.rem(head + distance, heads)
        start = pl.multiple_of(owner * width, width)
        block = block_ref[...]
        term = mm(block, out_weight_ref[pl.ds(start, width), :])
        total = term if total is None else total + term
        turned = block.T
        first = owner * (width // chunk)
        for index in range(width // chunk):
            target = (first + index) ^ tile
            rows = turned[index * chunk : (index + 1) * chunk]
            for parity, out_ref in enumerate((turned_ref, turned_sent_ref)):

                @pl.when((target >> axis) & 1 == parity)
                def _():
                    out_ref[(target >> (1 - axis)) & 1, target >> 2] = rows

    dout = total.astype(jnp.bfloat16)
    dout_ref[...] = dout
    dout_turned_ref[...] = dout.T


def split(exact, count):
    parts = []
    for _ in range(count):
        part = exact.astype(jnp.bfloat16).astype(jnp.float32)
        parts.append(part)
        exact = exact - part
    return parts


PARTS = (3, 2, 2)
SIDE_ORDER = (3, 2, 1, 0)


def rim_kernel(columns, query_ref, dout_ref, rows_ref, unused_ref, *rim_refs):
    place = lax.broadcasted_iota(jnp.int32, (LANES, CELLS), 0)
    token = lax.broadcasted_iota(jnp.int32, (LANES, CELLS), 1)
    parts = [part for kind, count in enumerate(PARTS) for part in split(rows_ref[kind], count)]
    pairs = rows_ref.shape[1] // 2
    filler = jnp.zeros((16 - 2 * len(parts), CELLS), jnp.float32)
    rows = [
        jnp.concatenate([part[2 * pair : 2 * pair + 2] for part in parts] + [filler], axis=0) for pair in range(pairs)
    ]
    rows = jnp.concatenate(rows, axis=0).astype(jnp.bfloat16)
    for slot, rim_ref in enumerate(rim_refs, 2):
        wanted = rim_token(slot_side(slot, columns), place)
        chosen = jnp.where((token == wanted) & (place < STRIP), 1.0, 0.0).astype(jnp.bfloat16)
        rim_ref[:STRIP] = mm(chosen[:STRIP], query_ref[...]).astype(jnp.bfloat16)
        rim_ref[STRIP : 2 * STRIP] = mm(chosen[:STRIP], dout_ref[...]).astype(jnp.bfloat16)
        spread = mm_nt(rows, chosen).astype(jnp.bfloat16)
        for pair in range(pairs):
            rim_ref[2 * STRIP :, pair * PAIR : (pair + 1) * PAIR] = spread[16 * pair : 16 * pair + 16]


def window(cell_row, cell_col, query):
    query_row = (query >> 4) + RADIUS
    query_col = (query & (SIDE - 1)) + RADIUS
    near = (jnp.abs(cell_row - query_row) <= RADIUS) & (jnp.abs(cell_col - query_col) <= RADIUS)
    return jnp.where(near, 0.0, -1e30)


def centre_bias(bias_ref):
    query = lax.broadcasted_iota(jnp.int32, (CELLS, CELLS), 1)
    cell = lax.broadcasted_iota(jnp.int32, (CELLS, CELLS), 0)
    bias_ref[...] = window((cell >> 4) + RADIUS, (cell & (SIDE - 1)) + RADIUS, query)


def strip_bias(kind, bias_ref):
    query = lax.broadcasted_iota(jnp.int32, (STRIP, CELLS), 1)
    cell = lax.broadcasted_iota(jnp.int32, (STRIP, CELLS), 0)
    depth = cell >> 4
    along = cell & (SIDE - 1)
    last = SIDE + 2 * RADIUS - 1
    if kind:
        first, second = (last - RADIUS - along, depth), (RADIUS + along, last - depth)
    else:
        first, second = (depth, RADIUS + along), (last - depth, last - RADIUS - along)
    in_first = first_half(query, kind)
    row = jnp.where(in_first, first[0], second[0])
    col = jnp.where(in_first, first[1], second[1])
    bias_ref[...] = window(row, col, query)


def first_half(query, kind):
    return (query & (SIDE - 1)) < SIDE // 2 if kind else query < CELLS // 2


def one_head(block, head):
    lane = lax.broadcasted_iota(jnp.int32, block.shape, 1)
    kept = (lane >= HEAD_DIM) if head else (lane < HEAD_DIM)
    return jnp.where(kept, block, jnp.zeros_like(block))


def halves(block, kind):
    kept = first_half(lax.broadcasted_iota(jnp.int32, block.shape, 0), kind)
    zero = jnp.zeros_like(block)
    return jnp.concatenate([jnp.where(kept, block, zero), jnp.where(kept, zero, block)], axis=1)


def by_half(stacked, kind):
    rows = stacked.shape[0] // 2
    kept = first_half(lax.broadcasted_iota(jnp.int32, (rows, CELLS), 1), kind)
    return jnp.where(kept, stacked[:rows], stacked[rows:])


def side_blocks(strips, part, kind, cols):
    tile = lax.axis_index("tile")
    second, first = strips
    straight = (tile if kind else lax.div(tile, lax.axis_size("tile") // 4)) & 1 == 0
    first, second = first[part, :, cols], second[part, :, cols]
    return jnp.where(straight, first, second), jnp.where(straight, second, first)


def side_cells(strips, part, kind, cols):
    return jnp.concatenate(side_blocks(strips, part, kind, cols), axis=1)


def halves(block, kind):
    kept = first_half(lax.broadcasted_iota(jnp.int32, block.shape, 0), kind)
    zero = jnp.zeros_like(block)
    return jnp.concatenate([jnp.where(kept, block, zero), jnp.where(kept, zero, block)], axis=1)


def by_half(stacked, kind):
    rows = stacked.shape[0] // 2
    kept = first_half(lax.broadcasted_iota(jnp.int32, (rows, CELLS), 1), kind)
    return jnp.where(kept, stacked[:rows], stacked[rows:])


def side_blocks(strips, part, kind, cols):
    tile = lax.axis_index("tile")
    second, first = strips
    straight = (tile if kind else lax.div(tile, lax.axis_size("tile") // 4)) & 1 == 0
    first, second = first[part, :, cols], second[part, :, cols]
    return jnp.where(straight, first, second), jnp.where(straight, second, first)


def side_cells(strips, part, kind, cols):
    return jnp.concatenate(side_blocks(strips, part, kind, cols), axis=1)


def side_products(cells, rows_head):
    return [mm_nt(cells[kind], halves(rows_head, kind)) for kind in range(2)]


def turned_sides(strips, part, kind, cols):
    return [block.T for block in side_blocks(strips, part, kind, cols)]


def pair_cols(pair):
    return pl.ds(pl.multiple_of(pair * PAIR, PAIR), PAIR)


def head_rows(turned, head):
    return turned[head * HEAD_DIM : (head + 1) * HEAD_DIM]


def over_side(turned, head, kind, sides):
    return by_half(mm(jnp.concatenate([head_rows(t, head) for t in turned], axis=0), sides), kind)


SCORE_SCALE = HEAD_DIM ** (-0.5)
LOG_SCALE = SCORE_SCALE * math.log2(math.e)


def lanes_of(head):
    return slice(head * CELLS, (head + 1) * CELLS)


def centre_kernel(
    query_ref, key_ref, value_ref, dout_ref,
    raw_ref, stats_ref, sums_ref, product_ref, query_out, key_out, bias_ref,
):
    centre_bias(bias_ref)

    def step(pair, carry):
        cols = pair_cols(pair)
        query, key, value, dout = (ref[:, cols] for ref in (query_ref, key_ref, value_ref, dout_ref))
        turned = value.T
        for head in range(2):
            lanes = lanes_of(head)
            scores = mm_nt(key, one_head(query, head)) + bias_ref[...]
            top = jnp.max(scores, axis=0, keepdims=True)
            raw = jnp.exp2((scores - top) * LOG_SCALE)
            raw_ref[pair, :, lanes] = raw
            stats_ref[pair, 0:1, lanes] = top
            stats_ref[pair, 1:2, lanes] = jnp.sum(raw, axis=0, keepdims=True)
            sums_ref[pair, :, lanes] = mm(head_rows(turned, head), raw.astype(jnp.bfloat16))
            product_ref[pair, :, lanes] = mm_nt(value, one_head(dout, head))
        query_out[:, cols] = query
        key_out[:, cols] = key
        return carry

    lax.fori_loop(0, raw_ref.shape[0], step, 0)


def column_kernel(
    first_ref, second_ref, query_ref, dout_ref, raw_ref, stats_ref, sums_ref, product_ref, bias_ref
):
    strips = (first_ref, second_ref)
    strip_bias(0, bias_ref)

    def step(pair, carry):
        cols = pair_cols(pair)
        keys = side_cells(strips, 0, 0, cols)
        values = side_cells(strips, 1, 0, cols)
        turned = turned_sides(strips, 1, 0, cols)
        for head in range(2):
            lanes = lanes_of(head)
            scores = mm_nt(keys, halves(one_head(query_ref[:, cols], head), 0)) + bias_ref[...]
            top = jnp.max(scores, axis=0, keepdims=True)
            raw = jnp.exp2((scores - top) * LOG_SCALE)
            raw_ref[pair, :, lanes] = raw
            stats_ref[pair, 0:1, lanes] = top
            stats_ref[pair, 1:2, lanes] = jnp.sum(raw, axis=0, keepdims=True)
            sums_ref[pair, :, lanes] = over_side(turned, head, 0, raw.astype(jnp.bfloat16))
            product_ref[pair, :, lanes] = mm_nt(values, halves(one_head(dout_ref[:, cols], head), 0))
        return carry

    lax.fori_loop(0, raw_ref.shape[0], step, 0)


def row_kernel(
    first_ref, second_ref, query_ref, dout_turned_ref, centre_stats_ref, centre_sums_ref, stats_ref, sums_ref,
    raw_ref, attention_ref, rows_ref, factors_ref, bias_ref,
):
    strips = (first_ref, second_ref)
    strip_bias(1, bias_ref)

    def step(pair, carry):
        cols = pair_cols(pair)
        keys = side_cells(strips, 0, 1, cols)
        turned = turned_sides(strips, 1, 1, cols)
        parts = []
        for head in range(2):
            lanes = lanes_of(head)
            scores = mm_nt(keys, halves(one_head(query_ref[:, cols], head), 1)) + bias_ref[...]
            tops = [ref[pair, 0:1, lanes] for ref in (centre_stats_ref, stats_ref)]
            top = jnp.maximum(jnp.max(scores, axis=0, keepdims=True), jnp.maximum(*tops))
            raw = jnp.exp2((scores - top) * LOG_SCALE)
            raw_ref[pair, :, lanes] = raw
            lifted = [jnp.exp2((t - top) * LOG_SCALE) for t in tops]
            total = jnp.sum(raw, axis=0, keepdims=True)
            total += lifted[0] * centre_stats_ref[pair, 1:2, lanes] + lifted[1] * stats_ref[pair, 1:2, lanes]
            inverse = 1.0 / total
            factors = [l * inverse for l in lifted]
            part = over_side(turned, head, 1, raw.astype(jnp.bfloat16)) * inverse
            part += factors[0] * centre_sums_ref[pair, :, lanes] + factors[1] * sums_ref[pair, :, lanes]
            parts.append(part)
            place = pl.ds(2 * pair + head, 1)
            features = pl.ds(pl.multiple_of((2 * pair + head) * HEAD_DIM, HEAD_DIM), HEAD_DIM)
            product = dout_turned_ref[features, :].astype(jnp.float32) * part
            rows_ref[0, place, :] = top
            rows_ref[1, place, :] = inverse
            rows_ref[2, place, :] = jnp.sum(product, axis=0, keepdims=True)
            factors_ref[0, place, :] = factors[0]
            factors_ref[1, place, :] = factors[1]
        attention_ref[:, cols] = jnp.concatenate(parts, axis=0).T.astype(jnp.bfloat16)
        return carry

    lax.fori_loop(0, raw_ref.shape[0], step, 0, unroll=True)


def backward_kernel(
    fourth_ref, third_ref, second_ref, first_ref, query_ref, key_ref, dout_ref, centre_raw_ref, column_raw_ref,
    row_raw_ref, centre_product_ref, column_product_ref, rows_ref, factors_ref, unused_ref,
    grad_query_ref, centre_ref, first_out, second_out,
):
    columns, rows = (third_ref, fourth_ref), (first_ref, second_ref)
    straight = lax.axis_index("tile") & 1 == 0

    def step(pair, carry):
        cols = pair_cols(pair)
        query = query_ref[:, cols]
        dout = dout_ref[:, cols]
        turned_centre = key_ref[:, cols].T
        turned_columns = turned_sides(columns, 0, 0, cols)
        turned_rows = turned_sides(rows, 0, 1, cols)
        row_values = side_cells(rows, 1, 1, cols)
        parts = []
        centre_scores = []
        centre_weights = []
        row_scores = []
        row_weights = []
        query_halves = []
        dout_halves = []
        for head in range(2):
            lanes = lanes_of(head)
            place = pl.ds(2 * pair + head, 1)
            delta = rows_ref[2, place, :]
            query_halves.append(halves(one_head(query, head), 1))
            dout_halves.append(halves(one_head(dout, head), 1))
            row_product = mm_nt(row_values, dout_halves[-1])

            def dscore(weights, product):
                return (weights * (product - delta)).astype(jnp.bfloat16)

            weights = centre_raw_ref[pair, :, lanes] * factors_ref[0, place, :]
            centre_weights.append(weights.astype(jnp.bfloat16))
            centre_scores.append(dscore(weights, centre_product_ref[pair, :, lanes]))
            column_weights = column_raw_ref[pair, :, lanes] * factors_ref[1, place, :]
            column_score = dscore(column_weights, column_product_ref[pair, :, lanes])
            weights = row_raw_ref[pair, :, lanes] * rows_ref[1, place, :]
            row_weights.append(weights.astype(jnp.bfloat16))
            row_score = dscore(weights, row_product)
            row_scores.append(row_score)
            part = mm(head_rows(turned_centre, head), centre_scores[-1])
            part += over_side(turned_columns, head, 0, column_score) + over_side(turned_rows, head, 1, row_score)
            parts.append(part)
        grad_query = jnp.concatenate(parts, axis=0).T * SCORE_SCALE
        grad_query_ref[:, cols] = grad_query.astype(jnp.bfloat16)
        grad_key, grad_value = joint_mm(
            jnp.concatenate(centre_scores, axis=1),
            jnp.concatenate(centre_weights, axis=1),
            both_heads(query),
            both_heads(dout),
        )
        centre_ref[0, :, cols] = grad_key * SCORE_SCALE
        centre_ref[1, :, cols] = grad_value
        west_east = (
            mm(jnp.concatenate(row_scores, axis=1), jnp.concatenate(query_halves, axis=0)) * SCORE_SCALE,
            mm(jnp.concatenate(row_weights, axis=1), jnp.concatenate(dout_halves, axis=0)),
        )
        for part, grads in enumerate(west_east):
            grads = grads.astype(jnp.bfloat16)
            west, east = grads[:, :PAIR], grads[:, PAIR:]
            first_out[part, :, cols] = jnp.where(straight, east, west)
            second_out[part, :, cols] = jnp.where(straight, west, east)
        return carry

    lax.fori_loop(0, centre_raw_ref.shape[0], step, 0)


def joint_mm(first, second, first_rows, second_rows):
    rows = first.shape[0]
    product = mm(jnp.concatenate([first, second], axis=0), jnp.concatenate([first_rows, second_rows], axis=1))
    return product[:rows, :PAIR], product[rows:, PAIR:]


def both_heads(block):
    return jnp.concatenate([one_head(block, head) for head in range(2)], axis=0)


def padded(block):
    return jnp.concatenate([block, jnp.zeros((LANES - block.shape[0], block.shape[1]), block.dtype)], axis=0)


def statistics(rows):
    first = 0
    for count in PARTS:
        heads = []
        for head in range(2):
            parts = [rows[2 * index + head : 2 * index + head + 1] for index in range(first, first + count)]
            heads.append(functools.reduce(jnp.add, parts))
        first += count
        yield jnp.concatenate(heads, axis=1)


def choose_strips(slots, columns, rotations_ref, chosen_ref):
    token = lax.broadcasted_iota(jnp.int32, (CELLS, LANES), 0)
    place = lax.broadcasted_iota(jnp.int32, (CELLS, LANES), 1)
    for index, slot in enumerate(slots):
        side = slot_side(slot, columns)
        wanted = jnp.where(place < STRIP, strip_token(side, rotations_ref[0, side], place), -1)
        chosen = jnp.where(token == wanted, 1.0, 0.0).astype(jnp.bfloat16)
        chosen_ref[:, index * LANES : (index + 1) * LANES] = chosen


def side_kernel(columns, rotations_ref, centre_ref, *refs):
    picked, rims = refs[:2], refs[2:4]
    unused_ref, total_ref, chosen_ref, bias_ref = refs[4:]
    cell = lax.broadcasted_iota(jnp.int32, (STRIP, LANES), 0)
    query = lax.broadcasted_iota(jnp.int32, (STRIP, LANES), 1)
    near = jnp.abs((cell & (SIDE - 1)) - (query & (SIDE - 1))) <= RADIUS
    near = near & ((cell >> 4) >= (query >> 4)) & (query < STRIP)
    bias_ref[...] = jnp.where(near, 0.0, -1e30)
    choose_strips((3, 2), columns, rotations_ref, chosen_ref)
    for pair in range(total_ref.shape[2] // PAIR):
        cols = slice(pair * PAIR, (pair + 1) * PAIR)
        grads = []
        bias = jnp.concatenate([bias_ref[...]] * 2, axis=1)
        for picked_ref, rim_ref in zip(picked, rims):
            query = both_heads(padded(rim_ref[:STRIP, cols]))
            dout = both_heads(padded(rim_ref[STRIP : 2 * STRIP, cols]))
            top, inverse, delta = statistics(rim_ref[2 * STRIP :, cols].astype(jnp.float32))
            scores = mm_nt(picked_ref[0, :, cols], query) + bias
            weights = jnp.exp2((scores - top) * LOG_SCALE) * inverse
            product = mm_nt(picked_ref[1, :, cols], dout)
            dscore = (weights * (product - delta)).astype(jnp.bfloat16)
            grad = jnp.concatenate([mm(dscore, query) * SCORE_SCALE, mm(weights.astype(jnp.bfloat16), dout)], axis=1)
            grads.append(padded(grad.astype(jnp.bfloat16)))
        total = mm(chosen_ref[...], jnp.concatenate(grads, axis=0))
        total_ref[0, :, cols] = centre_ref[0, :, cols] + total[:, :PAIR]
        total_ref[1, :, cols] = centre_ref[1, :, cols] + total[:, PAIR:]


def merge_kernel(columns, rotations_ref, centre_ref, second_ref, first_ref, unused_ref, *refs):
    keys_ref, values_ref, chosen_ref, keys_done, values_done, sems = refs
    choose_strips((1, 0), columns, rotations_ref, chosen_ref)
    copies = []
    for pair in range(keys_ref.shape[1] // PAIR):
        cols = slice(pair * PAIR, (pair + 1) * PAIR)
        grads = [padded(jnp.concatenate([ref[0, :, cols], ref[1, :, cols]], axis=1)) for ref in (second_ref, first_ref)]
        total = mm(chosen_ref[...], jnp.concatenate(grads, axis=0))
        keys_done[:, cols] = (centre_ref[0, :, cols] + total[:, :PAIR]).astype(jnp.bfloat16)
        values_done[:, cols] = (centre_ref[1, :, cols] + total[:, PAIR:]).astype(jnp.bfloat16)
        for index, (done, out_ref) in enumerate(((keys_done, keys_ref), (values_done, values_ref))):
            copy = pltpu.make_async_copy(done.at[:, cols], out_ref.at[:, cols], sems.at[2 * pair + index])
            copy.start()
            copies.append(copy)
    for copy in copies:
        copy.wait()


def call(kernel, name, out_shape, operands, scratch=(), smem=0, unused=0, gflop=0.1, out_space=pltpu.VMEM):
    specs = [pl.BlockSpec(memory_space=pltpu.SMEM)] * smem
    specs += [pl.BlockSpec(memory_space=pltpu.VMEM)] * (len(operands) - smem - unused)
    specs += [pl.BlockSpec(memory_space=pl.ANY)] * unused
    single = not isinstance(out_shape, list)
    outs = pl.BlockSpec(memory_space=out_space)
    return pl.pallas_call(
        kernel,
        out_shape=out_shape,
        in_specs=specs,
        out_specs=outs if single else [outs] * len(out_shape),
        scratch_shapes=list(scratch),
        compiler_params=pltpu.CompilerParams(vmem_limit_bytes=VMEM_LIMIT),
        cost_estimate=pl.CostEstimate(flops=int(gflop * 1e9), bytes_accessed=1 << 20, transcendentals=0),
        name=name,
    )(*operands)


def in_hbm(array):
    return pltpu.with_memory_space_constraint(array, pltpu.HBM)


def across(block, distances):
    heads = lax.axis_size("head")
    devices = [(tile, head) for tile in range(lax.axis_size("tile")) for head in range(heads)]
    route = [(tile * heads + head, (tile ^ distances[head % 2]) * heads + head) for tile, head in devices]
    return lax.ppermute(block, ("tile", "head"), route)


def exchanged(blocks, stride):
    terms = list(blocks[:1])
    for distance in range(1, len(blocks)):
        route = [(tile, tile ^ (distance * stride)) for tile in range(lax.axis_size("tile"))]
        terms.append(lax.ppermute(blocks[distance], "tile", route))
    return terms


def with_partners(blocks, slots):
    tile_count = lax.axis_size("tile")
    routes = {s: [(tile, partner(tile, tile_count, s)) for tile in range(tile_count)] for s in slots}
    return {s: lax.ppermute(blocks[s], "tile", routes[s]) for s in slots}


def shards(queries, keys, values, grad_output, out_weight, rotations):
    tile_count = lax.axis_size("tile")
    token_count, features = queries.shape
    model = out_weight.shape[0]
    pairs = features // PAIR
    far = tile_count // NEAR
    chunk = model // tile_count
    heads = lax.axis_size("head")
    columns = tile_count // 4
    queries, keys, values, out_weight, rotations = (
        in_hbm(a) for a in (queries, keys, values, out_weight, rotations)
    )

    def bf16(*shape):
        return jax.ShapeDtypeStruct(shape, jnp.bfloat16)

    def f32(*shape):
        return jax.ShapeDtypeStruct(shape, jnp.float32)

    strip_types = [bf16(2, STRIP, features)] * 4
    picked = call(
        functools.partial(pick_kernel, columns), "pick_strips", strip_types, (rotations, keys, values), smem=1
    )
    grad_output, *picked = lax.optimization_barrier((grad_output, *picked))
    strips = with_partners(picked, (3, 2, 1, 0))
    strips = [strips[s] for s in range(4)]

    cotangents = [
        lax.ppermute(grad_output, "head", [((h + k) % heads, h) for h in range(heads)]) for k in range(1, heads)
    ]
    dout, dout_turned, turned, turned_sent = call(
        functools.partial(cotangent_kernel, heads),
        "cotangent",
        [bf16(CELLS, features), bf16(features, CELLS)] + [bf16(2, far, chunk, CELLS)] * 2,
        (in_hbm(grad_output), *cotangents, out_weight),
        gflop=1.0,
    )
    turned_arrived = across(turned_sent, (1, 2))
    part_types = [f32(pairs, 2, 2 * CELLS), f32(pairs, HEAD_DIM, 2 * CELLS)]
    raw_centre, stats_centre, sums_centre, product_centre, queries, keys = call(
        centre_kernel,
        "centre",
        [f32(pairs, CELLS, 2 * CELLS)] + part_types + [f32(pairs, CELLS, 2 * CELLS)] + [bf16(CELLS, features)] * 2,
        (queries, keys, values, dout),
        scratch=[pltpu.VMEM((CELLS, CELLS), jnp.float32)],
        gflop=3.0,
    )
    strip_scratch = [pltpu.VMEM((STRIP, CELLS), jnp.float32)]
    raw_columns, stats_columns, sums_columns, product_columns = call(
        column_kernel,
        "columns",
        [f32(pairs, STRIP, 2 * CELLS)] + part_types + [f32(pairs, STRIP, 2 * CELLS)],
        (strips[2], strips[3], queries, dout),
        scratch=strip_scratch,
        gflop=2.0,
    )
    raw_rows, attention, rows, factors = call(
        row_kernel,
        "rows",
        [f32(pairs, STRIP, 2 * CELLS), bf16(CELLS, features)] + [f32(k, 2 * pairs, CELLS) for k in (3, 2)],
        (strips[0], strips[1], queries, dout_turned, stats_centre, sums_centre, stats_columns, sums_columns),
        scratch=strip_scratch,
    )
    attention_arrived = across(attention, (1, 2))
    rims = call(
        functools.partial(rim_kernel, columns),
        "rims",
        [bf16(2 * STRIP + 16, features)] * 2,
        (queries, dout, rows, turned_arrived),
        unused=1,
    )
    rims = dict(enumerate(rims, 2))
    rims_arrived = with_partners(rims, (3, 2))
    grad_queries, centre, *backs = call(
        backward_kernel,
        "backward",
        [bf16(CELLS, features), f32(2, CELLS, features)] + strip_types[:2],
        (
            *strips[::-1], queries, keys, dout, raw_centre, raw_columns, raw_rows, product_centre, product_columns,
            rows, factors, rims[3],
        ),
        unused=1,
        gflop=3.0,
    )
    kept, sent = call(
        partial_kernel,
        "partial",
        [f32(far, chunk, features), bf16(far, chunk, features)],
        (attention, attention_arrived, turned, turned_arrived, centre),
        unused=1,
    )
    terms = [kept, across(sent, (2, 1))]
    backs = dict(enumerate(lax.optimization_barrier((*backs, sent))[:2]))
    backs_arrived = with_partners(backs, (0, 1))

    here = call(
        mark_kernel,
        "rims_here",
        f32(8, LANES),
        (centre, rims_arrived[3], rims_arrived[2]),
        unused=3,
        gflop=3.0,
    )
    side_scratch = [pltpu.VMEM((CELLS, 2 * LANES), jnp.bfloat16)]
    stride = NEAR
    while stride < tile_count:
        sums = call(
            functools.partial(sum_kernel, len(terms)),
            "plane_sum",
            [bf16(tile_count // stride // 2, chunk, features)] * 2,
            (*terms, here),
            unused=1,
        )
        if stride == NEAR:
            here = call(
                functools.partial(side_kernel, columns),
                "sides",
                f32(2, CELLS, features),
                (rotations, centre, picked[3], picked[2], rims_arrived[3], rims_arrived[2], sums[1]),
                scratch=side_scratch + [pltpu.VMEM((STRIP, LANES), jnp.float32)],
                smem=1,
                unused=1,
                gflop=3.0,
            )
        terms = exchanged(sums, stride)
        stride *= 2
    grad_keys, grad_values = call(
        functools.partial(merge_kernel, columns),
        "merge",
        [bf16(CELLS, features)] * 2,
        (rotations, here, backs_arrived[1], backs_arrived[0], sums[1]),
        scratch=side_scratch
        + [pltpu.VMEM((CELLS, features), jnp.bfloat16)] * 2
        + [pltpu.SemaphoreType.DMA((2 * pairs,))],
        smem=1,
        unused=1,
        gflop=3.0,
        out_space=pl.ANY,
    )
    grad_out_weight = call(
        functools.partial(weight_kernel, 1.0 / math.sqrt(token_count * tile_count)),
        "weight_sum",
        f32(chunk, features),
        terms,
    )
    return (grad_queries, grad_keys, grad_values, grad_out_weight)


def solution(mesh):
    placed = (
        P("tile", "head"),
        P("tile", "head"),
        P("tile", "head"),
        P("tile", "head"),
        P(None, "head"),
        P("tile", None),
    )
    return jax.shard_map(
        shards,
        mesh=mesh,
        in_specs=placed,
        out_specs=(P("tile", "head"), P("tile", "head"), P("tile", "head"), P("tile", "head")),
        check_vma=False,
    )
```

```python
import functools
import math

import jax
import jax.numpy as jnp
from jax import lax
from jax.experimental import pallas as pl
from jax.experimental.pallas import tpu as pltpu
from jax.sharding import PartitionSpec as P

HEAD_DIM = 64
RADIUS = 6
SIDE = 16
CELLS = SIDE * SIDE
STRIP = RADIUS * SIDE
NEAR = 4
LANES = 128
PAIR = 2 * HEAD_DIM
VMEM_LIMIT = 32 * 1024 * 1024
NT = (((1,), (1,)), ((), ()))


def mm(a, b):
    return jnp.dot(a, b, preferred_element_type=jnp.float32)


def mm_nt(a, b):
    return lax.dot_general(a, b, NT, preferred_element_type=jnp.float32)


def strip_token(side_index, rotation, cell):
    turn = lax.rem(side_index + 6 - rotation, 4)
    depth = cell >> 4
    along = cell & (SIDE - 1)
    far = SIDE - 1 - along
    near_rim = RADIUS - 1 - depth
    far_rim = SIDE - RADIUS + depth
    row = jnp.where(turn == 0, far_rim, jnp.where(turn == 1, along, jnp.where(turn == 2, near_rim, far)))
    col = jnp.where(turn == 0, along, jnp.where(turn == 1, near_rim, jnp.where(turn == 2, far, far_rim)))
    return row * SIDE + col


def slot_side(slot, columns):
    tile = lax.axis_index("tile")
    if slot < 2:
        return jnp.where((tile + slot) & 1 == 0, 1, 3)
    return jnp.where((lax.div(tile, columns) + slot) & 1 == 0, 2, 0)


def partner(tile, tile_count, slot):
    columns = tile_count // 4
    if slot < 2:
        return (tile + (1 if (tile + slot) % 2 == 0 else -1)) % tile_count
    return (tile + (columns if (tile // columns + slot) % 2 == 0 else -columns)) % tile_count


def pick_kernel(columns, rotations_ref, keys_ref, values_ref, *out_refs):
    cell = lax.broadcasted_iota(jnp.int32, (STRIP, CELLS), 0)
    token = lax.broadcasted_iota(jnp.int32, (STRIP, CELLS), 1)
    for slot, out_ref in enumerate(out_refs):
        side = slot_side(slot, columns)
        wanted = strip_token(side, rotations_ref[0, side], cell)
        chosen = jnp.where(token == wanted, 1.0, 0.0).astype(jnp.bfloat16)
        out_ref[0] = mm(chosen, keys_ref[...]).astype(jnp.bfloat16)
        out_ref[1] = mm(chosen, values_ref[...]).astype(jnp.bfloat16)


def weight_kernel(scale, *refs):
    total = refs[0][0].astype(jnp.float32)
    for ref in refs[1:-1]:
        total += ref[0].astype(jnp.float32)
    refs[-1][...] = total * scale


def partial_kernel(*refs):
    own, arrived, (turned_ref, turned_arrived_ref, _, kept_ref, sent_ref) = refs[:2], refs[2:4], refs[4:]
    for index, out_ref in enumerate((kept_ref, sent_ref)):
        half = out_ref.shape[2] // 2
        for side in range(2):
            total = None
            for turned_part, attention_part in ((turned_ref, own[side]), (turned_arrived_ref, arrived[side])):
                turned = turned_part[index]
                turned = turned.reshape(turned.shape[0] * turned.shape[1], turned.shape[2])
                term = mm(turned, attention_part[...])
                total = term if total is None else total + term
            total = total.astype(out_ref.dtype).reshape(out_ref.shape[0], out_ref.shape[1], half)
            out_ref[:, :, side * half : (side + 1) * half] = total


def sum_kernel(count, *refs):
    terms, outs = refs[:count], refs[count + 3 :]
    for q in range(terms[0].shape[0]):
        total = terms[0][q].astype(jnp.float32)
        for ref in terms[1:]:
            total += ref[q].astype(jnp.float32)
        outs[q % len(outs)][q // len(outs)] = total.astype(jnp.bfloat16)


def rim_token(side_index, place):
    depth = place >> 4
    along = place & (SIDE - 1)
    last = SIDE - 1
    north, east, south = side_index == 0, side_index == 1, side_index == 2
    row = jnp.where(north, depth, jnp.where(east, along, jnp.where(south, last - depth, last - along)))
    col = jnp.where(north, along, jnp.where(east, last - depth, jnp.where(south, last - along, depth)))
    return row * SIDE + col


def cotangent_kernel(heads, *refs):
    blocks, out_weight_ref, outs = refs[:heads], refs[heads], refs[heads + 1 :]
    dout_ref, dout_turned_ref, turned_ref, turned_sent_ref = outs
    head = lax.axis_index("head")
    axis = head & 1
    tile = lax.axis_index("tile")
    chunk = turned_ref.shape[2]
    width = blocks[0].shape[1]
    total = None
    for distance, block_ref in enumerate(blocks):
        owner = lax.rem(head + distance, heads)
        start = pl.multiple_of(owner * width, width)
        block = block_ref[...]
        term = mm(block, out_weight_ref[pl.ds(start, width), :])
        total = term if total is None else total + term
        turned = block.T
        first = owner * (width // chunk)
        for index in range(width // chunk):
            target = (first + index) ^ tile
            rows = turned[index * chunk : (index + 1) * chunk]
            for parity, out_ref in enumerate((turned_ref, turned_sent_ref)):

                @pl.when((target >> axis) & 1 == parity)
                def _():
                    out_ref[(target >> (1 - axis)) & 1, target >> 2] = rows

    dout = total.astype(jnp.bfloat16)
    dout_ref[...] = dout
    dout_turned_ref[...] = dout.T


def split(exact, count):
    parts = []
    for _ in range(count):
        part = exact.astype(jnp.bfloat16).astype(jnp.float32)
        parts.append(part)
        exact = exact - part
    return parts


PARTS = (3, 2, 2)
SIDE_ORDER = (3, 2, 0, 1)


def rim_kernel(columns, query_ref, dout_ref, rows_ref, unused_ref, *rim_refs):
    place = lax.broadcasted_iota(jnp.int32, (LANES, CELLS), 0)
    token = lax.broadcasted_iota(jnp.int32, (LANES, CELLS), 1)
    parts = [part for kind, count in enumerate(PARTS) for part in split(rows_ref[kind], count)]
    pairs = rows_ref.shape[1] // 2
    filler = jnp.zeros((16 - 2 * len(parts), CELLS), jnp.float32)
    rows = [
        jnp.concatenate([part[2 * pair : 2 * pair + 2] for part in parts] + [filler], axis=0) for pair in range(pairs)
    ]
    rows = jnp.concatenate(rows, axis=0).astype(jnp.bfloat16)
    for slot, rim_ref in enumerate(rim_refs):
        wanted = rim_token(slot_side(slot, columns), place)
        chosen = jnp.where((token == wanted) & (place < STRIP), 1.0, 0.0).astype(jnp.bfloat16)
        rim_ref[:STRIP] = mm(chosen[:STRIP], query_ref[...]).astype(jnp.bfloat16)
        rim_ref[STRIP : 2 * STRIP] = mm(chosen[:STRIP], dout_ref[...]).astype(jnp.bfloat16)
        spread = mm_nt(rows, chosen).astype(jnp.bfloat16)
        for pair in range(pairs):
            rim_ref[2 * STRIP :, pair * PAIR : (pair + 1) * PAIR] = spread[16 * pair : 16 * pair + 16]


def window(cell_row, cell_col, query):
    query_row = (query >> 4) + RADIUS
    query_col = (query & (SIDE - 1)) + RADIUS
    near = (jnp.abs(cell_row - query_row) <= RADIUS) & (jnp.abs(cell_col - query_col) <= RADIUS)
    return jnp.where(near, 0.0, -1e30)


def centre_bias(bias_ref):
    query = lax.broadcasted_iota(jnp.int32, (CELLS, CELLS), 1)
    cell = lax.broadcasted_iota(jnp.int32, (CELLS, CELLS), 0)
    bias_ref[...] = window((cell >> 4) + RADIUS, (cell & (SIDE - 1)) + RADIUS, query)


def strip_bias(kind, bias_ref):
    query = lax.broadcasted_iota(jnp.int32, (STRIP, CELLS), 1)
    cell = lax.broadcasted_iota(jnp.int32, (STRIP, CELLS), 0)
    depth = cell >> 4
    along = cell & (SIDE - 1)
    last = SIDE + 2 * RADIUS - 1
    if kind:
        first, second = (last - RADIUS - along, depth), (RADIUS + along, last - depth)
    else:
        first, second = (depth, RADIUS + along), (last - depth, last - RADIUS - along)
    in_first = first_half(query, kind)
    row = jnp.where(in_first, first[0], second[0])
    col = jnp.where(in_first, first[1], second[1])
    bias_ref[...] = window(row, col, query)


def first_half(query, kind):
    return (query & (SIDE - 1)) < SIDE // 2 if kind else query < CELLS // 2


def one_head(block, head):
    lane = lax.broadcasted_iota(jnp.int32, block.shape, 1)
    kept = (lane >= HEAD_DIM) if head else (lane < HEAD_DIM)
    return jnp.where(kept, block, jnp.zeros_like(block))


def halves(block, kind):
    kept = first_half(lax.broadcasted_iota(jnp.int32, block.shape, 0), kind)
    zero = jnp.zeros_like(block)
    return jnp.concatenate([jnp.where(kept, block, zero), jnp.where(kept, zero, block)], axis=1)


def by_half(stacked, kind):
    rows = stacked.shape[0] // 2
    kept = first_half(lax.broadcasted_iota(jnp.int32, (rows, CELLS), 1), kind)
    return jnp.where(kept, stacked[:rows], stacked[rows:])


def side_blocks(strips, part, kind, cols):
    tile = lax.axis_index("tile")
    second, first = strips
    straight = (tile if kind else lax.div(tile, lax.axis_size("tile") // 4)) & 1 == 0
    first, second = first[part, :, cols], second[part, :, cols]
    return jnp.where(straight, first, second), jnp.where(straight, second, first)


def side_cells(strips, part, kind, cols):
    return jnp.concatenate(side_blocks(strips, part, kind, cols), axis=1)


def halves(block, kind):
    kept = first_half(lax.broadcasted_iota(jnp.int32, block.shape, 0), kind)
    zero = jnp.zeros_like(block)
    return jnp.concatenate([jnp.where(kept, block, zero), jnp.where(kept, zero, block)], axis=1)


def by_half(stacked, kind):
    rows = stacked.shape[0] // 2
    kept = first_half(lax.broadcasted_iota(jnp.int32, (rows, CELLS), 1), kind)
    return jnp.where(kept, stacked[:rows], stacked[rows:])


def side_blocks(strips, part, kind, cols):
    tile = lax.axis_index("tile")
    second, first = strips
    straight = (tile if kind else lax.div(tile, lax.axis_size("tile") // 4)) & 1 == 0
    first, second = first[part, :, cols], second[part, :, cols]
    return jnp.where(straight, first, second), jnp.where(straight, second, first)


def side_cells(strips, part, kind, cols):
    return jnp.concatenate(side_blocks(strips, part, kind, cols), axis=1)


def side_products(cells, rows_head):
    return [mm_nt(cells[kind], halves(rows_head, kind)) for kind in range(2)]


def turned_sides(strips, part, kind, cols):
    return [block.T for block in side_blocks(strips, part, kind, cols)]


def pair_cols(pair):
    return pl.ds(pl.multiple_of(pair * PAIR, PAIR), PAIR)


def head_rows(turned, head):
    return turned[head * HEAD_DIM : (head + 1) * HEAD_DIM]


def over_side(turned, head, kind, sides):
    return by_half(mm(jnp.concatenate([head_rows(t, head) for t in turned], axis=0), sides), kind)


SCORE_SCALE = HEAD_DIM ** (-0.5)
LOG_SCALE = SCORE_SCALE * math.log2(math.e)


def lanes_of(head):
    return slice(head * CELLS, (head + 1) * CELLS)


def centre_kernel(
    query_ref, key_ref, value_ref, dout_ref,
    raw_ref, stats_ref, sums_ref, product_ref, query_out, key_out, bias_ref,
):
    centre_bias(bias_ref)

    def step(pair, carry):
        cols = pair_cols(pair)
        query, key, value, dout = (ref[:, cols] for ref in (query_ref, key_ref, value_ref, dout_ref))
        turned = value.T
        for head in range(2):
            lanes = lanes_of(head)
            scores = mm_nt(key, one_head(query, head)) + bias_ref[...]
            top = jnp.max(scores, axis=0, keepdims=True)
            raw = jnp.exp2((scores - top) * LOG_SCALE)
            raw_ref[pair, :, lanes] = raw
            stats_ref[pair, 0:1, lanes] = top
            stats_ref[pair, 1:2, lanes] = jnp.sum(raw, axis=0, keepdims=True)
            sums_ref[pair, :, lanes] = mm(head_rows(turned, head), raw.astype(jnp.bfloat16))
            product_ref[pair, :, lanes] = mm_nt(value, one_head(dout, head))
        query_out[:, cols] = query
        key_out[:, cols] = key
        return carry

    lax.fori_loop(0, raw_ref.shape[0], step, 0)


def column_kernel(
    first_ref, second_ref, query_ref, dout_ref, raw_ref, stats_ref, sums_ref, product_ref, bias_ref
):
    strips = (first_ref, second_ref)
    strip_bias(0, bias_ref)

    def step(pair, carry):
        cols = pair_cols(pair)
        keys = side_cells(strips, 0, 0, cols)
        values = side_cells(strips, 1, 0, cols)
        turned = turned_sides(strips, 1, 0, cols)
        for head in range(2):
            lanes = lanes_of(head)
            scores = mm_nt(keys, halves(one_head(query_ref[:, cols], head), 0)) + bias_ref[...]
            top = jnp.max(scores, axis=0, keepdims=True)
            raw = jnp.exp2((scores - top) * LOG_SCALE)
            raw_ref[pair, :, lanes] = raw
            stats_ref[pair, 0:1, lanes] = top
            stats_ref[pair, 1:2, lanes] = jnp.sum(raw, axis=0, keepdims=True)
            sums_ref[pair, :, lanes] = over_side(turned, head, 0, raw.astype(jnp.bfloat16))
            product_ref[pair, :, lanes] = mm_nt(values, halves(one_head(dout_ref[:, cols], head), 0))
        return carry

    lax.fori_loop(0, raw_ref.shape[0], step, 0)


def row_kernel(
    first_ref, second_ref, query_ref, dout_turned_ref, centre_stats_ref, centre_sums_ref, stats_ref, sums_ref,
    raw_ref, left_ref, right_ref, rows_ref, factors_ref, bias_ref,
):
    strips = (first_ref, second_ref)
    strip_bias(1, bias_ref)

    def step(pair):
        cols = slice(pair * PAIR, (pair + 1) * PAIR)
        keys = side_cells(strips, 0, 1, cols)
        turned = turned_sides(strips, 1, 1, cols)
        parts = []
        for head in range(2):
            lanes = lanes_of(head)
            scores = mm_nt(keys, halves(one_head(query_ref[:, cols], head), 1)) + bias_ref[...]
            tops = [ref[pair, 0:1, lanes] for ref in (centre_stats_ref, stats_ref)]
            top = jnp.maximum(jnp.max(scores, axis=0, keepdims=True), jnp.maximum(*tops))
            raw = jnp.exp2((scores - top) * LOG_SCALE)
            raw_ref[pair, :, lanes] = raw
            lifted = [jnp.exp2((t - top) * LOG_SCALE) for t in tops]
            total = jnp.sum(raw, axis=0, keepdims=True)
            total += lifted[0] * centre_stats_ref[pair, 1:2, lanes] + lifted[1] * stats_ref[pair, 1:2, lanes]
            inverse = 1.0 / total
            factors = [l * inverse for l in lifted]
            part = over_side(turned, head, 1, raw.astype(jnp.bfloat16)) * inverse
            part += factors[0] * centre_sums_ref[pair, :, lanes] + factors[1] * sums_ref[pair, :, lanes]
            parts.append(part)
            place = slice(2 * pair + head, 2 * pair + head + 1)
            features = slice((2 * pair + head) * HEAD_DIM, (2 * pair + head + 1) * HEAD_DIM)
            product = dout_turned_ref[features, :].astype(jnp.float32) * part
            rows_ref[0, place, :] = top
            rows_ref[1, place, :] = inverse
            rows_ref[2, place, :] = jnp.sum(product, axis=0, keepdims=True)
            factors_ref[0, place, :] = factors[0]
            factors_ref[1, place, :] = factors[1]
        attention = jnp.concatenate(parts, axis=0).T.astype(jnp.bfloat16)
        half = raw_ref.shape[0] // 2
        attention_ref = left_ref if pair < half else right_ref
        attention_ref[:, pair % half * PAIR : (pair % half + 1) * PAIR] = attention

    for pair in range(raw_ref.shape[0]):
        step(pair)


def backward_kernel(
    fourth_ref, third_ref, second_ref, first_ref, query_ref, key_ref, dout_ref, centre_raw_ref, column_raw_ref,
    row_raw_ref, centre_product_ref, column_product_ref, rows_ref, factors_ref, unused_ref,
    grad_query_ref, centre_ref,
):
    columns, rows = (third_ref, fourth_ref), (first_ref, second_ref)

    def step(pair, carry):
        cols = pair_cols(pair)
        query = query_ref[:, cols]
        dout = dout_ref[:, cols]
        turned_centre = key_ref[:, cols].T
        turned_columns = turned_sides(columns, 0, 0, cols)
        turned_rows = turned_sides(rows, 0, 1, cols)
        row_values = side_cells(rows, 1, 1, cols)
        parts = []
        centre_scores = []
        centre_weights = []
        for head in range(2):
            lanes = lanes_of(head)
            place = pl.ds(2 * pair + head, 1)
            delta = rows_ref[2, place, :]
            row_product = mm_nt(row_values, halves(one_head(dout, head), 1))

            def dscore(weights, product):
                return (weights * (product - delta)).astype(jnp.bfloat16)

            weights = centre_raw_ref[pair, :, lanes] * factors_ref[0, place, :]
            centre_weights.append(weights.astype(jnp.bfloat16))
            centre_scores.append(dscore(weights, centre_product_ref[pair, :, lanes]))
            column_weights = column_raw_ref[pair, :, lanes] * factors_ref[1, place, :]
            column_score = dscore(column_weights, column_product_ref[pair, :, lanes])
            row_score = dscore(row_raw_ref[pair, :, lanes] * rows_ref[1, place, :], row_product)
            part = mm(head_rows(turned_centre, head), centre_scores[-1])
            part += over_side(turned_columns, head, 0, column_score) + over_side(turned_rows, head, 1, row_score)
            parts.append(part)
        grad_query = jnp.concatenate(parts, axis=0).T * SCORE_SCALE
        grad_query_ref[:, cols] = grad_query.astype(jnp.bfloat16)
        grad_key, grad_value = joint_mm(
            jnp.concatenate(centre_scores, axis=1),
            jnp.concatenate(centre_weights, axis=1),
            both_heads(query),
            both_heads(dout),
        )
        centre_ref[0, :, cols] = grad_key * SCORE_SCALE
        centre_ref[1, :, cols] = grad_value
        return carry

    lax.fori_loop(0, centre_raw_ref.shape[0], step, 0)


def joint_mm(first, second, first_rows, second_rows):
    rows = first.shape[0]
    product = mm(jnp.concatenate([first, second], axis=0), jnp.concatenate([first_rows, second_rows], axis=1))
    return product[:rows, :PAIR], product[rows:, PAIR:]


def both_heads(block):
    return jnp.concatenate([one_head(block, head) for head in range(2)], axis=0)


def padded(block):
    return jnp.concatenate([block, jnp.zeros((LANES - block.shape[0], block.shape[1]), block.dtype)], axis=0)


def statistics(rows):
    first = 0
    for count in PARTS:
        heads = []
        for head in range(2):
            parts = [rows[2 * index + head : 2 * index + head + 1] for index in range(first, first + count)]
            heads.append(functools.reduce(jnp.add, parts))
        first += count
        yield jnp.concatenate(heads, axis=1)


def side_kernel(columns, rotations_ref, centre_ref, *refs):
    picked, rims = refs[:4], refs[4:8]
    keys_ref, values_ref, chosen_ref, bias_ref, keys_done, values_done, sems = refs[8:]
    cell = lax.broadcasted_iota(jnp.int32, (STRIP, LANES), 0)
    query = lax.broadcasted_iota(jnp.int32, (STRIP, LANES), 1)
    near = jnp.abs((cell & (SIDE - 1)) - (query & (SIDE - 1))) <= RADIUS
    near = near & ((cell >> 4) >= (query >> 4)) & (query < STRIP)
    bias_ref[...] = jnp.where(near, 0.0, -1e30)
    token = lax.broadcasted_iota(jnp.int32, (CELLS, LANES), 0)
    place = lax.broadcasted_iota(jnp.int32, (CELLS, LANES), 1)
    for index, slot in enumerate(SIDE_ORDER):
        side = slot_side(slot, columns)
        wanted = jnp.where(place < STRIP, strip_token(side, rotations_ref[0, side], place), -1)
        chosen = jnp.where(token == wanted, 1.0, 0.0).astype(jnp.bfloat16)
        chosen_ref[:, index * LANES : (index + 1) * LANES] = chosen

    copies = []
    for pair in range(keys_ref.shape[1] // PAIR):
        cols = slice(pair * PAIR, (pair + 1) * PAIR)
        grads = []
        bias = jnp.concatenate([bias_ref[...]] * 2, axis=1)
        for picked_ref, rim_ref in zip(picked, rims):
            query = both_heads(padded(rim_ref[:STRIP, cols]))
            dout = both_heads(padded(rim_ref[STRIP : 2 * STRIP, cols]))
            top, inverse, delta = statistics(rim_ref[2 * STRIP :, cols].astype(jnp.float32))
            scores = mm_nt(picked_ref[0, :, cols], query) + bias
            weights = jnp.exp2((scores - top) * LOG_SCALE) * inverse
            product = mm_nt(picked_ref[1, :, cols], dout)
            dscore = (weights * (product - delta)).astype(jnp.bfloat16)
            grad = jnp.concatenate([mm(dscore, query) * SCORE_SCALE, mm(weights.astype(jnp.bfloat16), dout)], axis=1)
            grads.append(padded(grad.astype(jnp.bfloat16)))
        total = mm(chosen_ref[...], jnp.concatenate(grads, axis=0))
        keys_done[:, cols] = (centre_ref[0, :, cols] + total[:, :PAIR]).astype(jnp.bfloat16)
        values_done[:, cols] = (centre_ref[1, :, cols] + total[:, PAIR:]).astype(jnp.bfloat16)
        for index, (done, out_ref) in enumerate(((keys_done, keys_ref), (values_done, values_ref))):
            copy = pltpu.make_async_copy(done.at[:, cols], out_ref.at[:, cols], sems.at[2 * pair + index])
            copy.start()
            copies.append(copy)
    for copy in copies:
        copy.wait()


def call(kernel, name, out_shape, operands, scratch=(), smem=0, unused=0, gflop=0.1, out_space=pltpu.VMEM):
    specs = [pl.BlockSpec(memory_space=pltpu.SMEM)] * smem
    specs += [pl.BlockSpec(memory_space=pltpu.VMEM)] * (len(operands) - smem - unused)
    specs += [pl.BlockSpec(memory_space=pl.ANY)] * unused
    single = not isinstance(out_shape, list)
    outs = pl.BlockSpec(memory_space=out_space)
    return pl.pallas_call(
        kernel,
        out_shape=out_shape,
        in_specs=specs,
        out_specs=outs if single else [outs] * len(out_shape),
        scratch_shapes=list(scratch),
        compiler_params=pltpu.CompilerParams(vmem_limit_bytes=VMEM_LIMIT),
        cost_estimate=pl.CostEstimate(flops=int(gflop * 1e9), bytes_accessed=1 << 20, transcendentals=0),
        name=name,
    )(*operands)


def in_hbm(array):
    return pltpu.with_memory_space_constraint(array, pltpu.HBM)


def across(block, distances):
    heads = lax.axis_size("head")
    devices = [(tile, head) for tile in range(lax.axis_size("tile")) for head in range(heads)]
    route = [(tile * heads + head, (tile ^ distances[head % 2]) * heads + head) for tile, head in devices]
    return lax.ppermute(block, ("tile", "head"), route)


def exchanged(blocks, stride):
    terms = list(blocks[:1])
    for distance in (2, 3, 1) if len(blocks) == 4 else (1,):
        route = [(tile, tile ^ (distance * stride)) for tile in range(lax.axis_size("tile"))]
        terms.append(lax.ppermute(blocks[distance], "tile", route))
    return terms


def with_partners(blocks, slots):
    tile_count = lax.axis_size("tile")
    routes = {s: [(tile, partner(tile, tile_count, s)) for tile in range(tile_count)] for s in slots}
    return {s: lax.ppermute(blocks[s], "tile", routes[s]) for s in slots}


def shards(queries, keys, values, grad_output, out_weight, rotations):
    tile_count = lax.axis_size("tile")
    token_count, features = queries.shape
    model = out_weight.shape[0]
    pairs = features // PAIR
    far = tile_count // NEAR
    chunk = model // tile_count
    heads = lax.axis_size("head")
    columns = tile_count // 4
    queries, keys, values, out_weight, rotations = (
        in_hbm(a) for a in (queries, keys, values, out_weight, rotations)
    )

    def bf16(*shape):
        return jax.ShapeDtypeStruct(shape, jnp.bfloat16)

    def f32(*shape):
        return jax.ShapeDtypeStruct(shape, jnp.float32)

    strip_types = [bf16(2, STRIP, features)] * 4
    picked = call(
        functools.partial(pick_kernel, columns), "pick_strips", strip_types, (rotations, keys, values), smem=1
    )
    grad_output, *picked = lax.optimization_barrier((grad_output, *picked))
    strips = with_partners(picked, (3, 2, 1, 0))
    strips = [strips[s] for s in range(4)]

    cotangents = [
        lax.ppermute(grad_output, "head", [((h + k) % heads, h) for h in range(heads)]) for k in range(1, heads)
    ]
    dout, dout_turned, turned, turned_sent = call(
        functools.partial(cotangent_kernel, heads),
        "cotangent",
        [bf16(CELLS, features), bf16(features, CELLS)] + [bf16(2, far, chunk, CELLS)] * 2,
        (in_hbm(grad_output), *cotangents, out_weight),
        gflop=1.0,
    )
    turned_arrived = across(turned_sent, (1, 2))
    part_types = [f32(pairs, 2, 2 * CELLS), f32(pairs, HEAD_DIM, 2 * CELLS)]
    raw_centre, stats_centre, sums_centre, product_centre, queries, keys = call(
        centre_kernel,
        "centre",
        [f32(pairs, CELLS, 2 * CELLS)] + part_types + [f32(pairs, CELLS, 2 * CELLS)] + [bf16(CELLS, features)] * 2,
        (queries, keys, values, dout),
        scratch=[pltpu.VMEM((CELLS, CELLS), jnp.float32)],
        gflop=3.0,
    )
    strip_scratch = [pltpu.VMEM((STRIP, CELLS), jnp.float32)]
    raw_columns, stats_columns, sums_columns, product_columns = call(
        column_kernel,
        "columns",
        [f32(pairs, STRIP, 2 * CELLS)] + part_types + [f32(pairs, STRIP, 2 * CELLS)],
        (strips[2], strips[3], queries, dout),
        scratch=strip_scratch,
        gflop=2.0,
    )
    raw_rows, left, right, rows, factors = call(
        row_kernel,
        "rows",
        [f32(pairs, STRIP, 2 * CELLS)]
        + [bf16(CELLS, features // 2)] * 2
        + [f32(k, 2 * pairs, CELLS) for k in (3, 2)],
        (strips[0], strips[1], queries, dout_turned, stats_centre, sums_centre, stats_columns, sums_columns),
        scratch=strip_scratch,
    )
    gathered = [across(half, (1, 2)) for half in (left, right)]
    rims = call(
        functools.partial(rim_kernel, columns),
        "rims",
        [bf16(2 * STRIP + 16, features)] * 4,
        (queries, dout, rows, turned_arrived),
        unused=1,
    )
    rims_arrived = with_partners(rims, (3, 2))
    kept, sent = call(
        partial_kernel,
        "partial",
        [f32(far, chunk, features), bf16(far, chunk, features)],
        (left, right, *gathered, turned, turned_arrived, rims[0]),
        unused=1,
    )
    terms = [kept, across(sent, (2, 1))]
    rims = lax.optimization_barrier((*rims, sent))[:4]
    rims_arrived |= with_partners(rims, (0, 1))
    grad_queries, centre = call(
        backward_kernel,
        "backward",
        [bf16(CELLS, features), f32(2, CELLS, features)],
        (
            *strips[::-1], queries, keys, dout, raw_centre, raw_columns, raw_rows, product_centre, product_columns,
            rows, factors, sent,
        ),
        unused=1,
        gflop=3.0,
    )
    stride = NEAR
    while stride < tile_count:
        ways = min(NEAR, tile_count // stride)
        sums = call(
            functools.partial(sum_kernel, len(terms)),
            "plane_sum",
            [bf16(tile_count // stride // ways, chunk, features)] * ways,
            (*terms, centre, rims_arrived[3], rims_arrived[2]),
            unused=3,
        )
        terms = exchanged(sums, stride)
        stride *= ways

    grad_keys, grad_values = call(
        functools.partial(side_kernel, columns),
        "sides",
        [bf16(CELLS, features)] * 2,
        (rotations, centre, *(picked[s] for s in SIDE_ORDER), *(rims_arrived[s] for s in SIDE_ORDER)),
        scratch=[pltpu.VMEM((CELLS, 4 * LANES), jnp.bfloat16), pltpu.VMEM((STRIP, LANES), jnp.float32)]
        + [pltpu.VMEM((CELLS, features), jnp.bfloat16)] * 2
        + [pltpu.SemaphoreType.DMA((2 * pairs,))],
        smem=1,
        gflop=3.0,
        out_space=pl.ANY,
    )
    grad_out_weight = call(
        functools.partial(weight_kernel, 1.0 / math.sqrt(token_count * tile_count)),
        "weight_sum",
        f32(chunk, features),
        terms,
    )
    return (grad_queries, grad_keys, grad_values, grad_out_weight)


def solution(mesh):
    placed = (
        P("tile", "head"),
        P("tile", "head"),
        P("tile", "head"),
        P("tile", "head"),
        P(None, "head"),
        P("tile", None),
    )
    return jax.shard_map(
        shards,
        mesh=mesh,
        in_specs=placed,
        out_specs=(P("tile", "head"), P("tile", "head"), P("tile", "head"), P("tile", "head")),
        check_vma=False,
    )
```

```python
import functools
import math

import jax
import jax.numpy as jnp
from jax import lax
from jax.experimental import pallas as pl
from jax.experimental.pallas import tpu as pltpu
from jax.sharding import PartitionSpec as P

HEAD_DIM = 64
RADIUS = 6
SIDE = 16
CELLS = SIDE * SIDE
STRIP = RADIUS * SIDE
NEAR = 4
LANES = 128
PAIR = 2 * HEAD_DIM
VMEM_LIMIT = 32 * 1024 * 1024
NT = (((1,), (1,)), ((), ()))


def mm(a, b):
    return jnp.dot(a, b, preferred_element_type=jnp.float32)


def mm_nt(a, b):
    return lax.dot_general(a, b, NT, preferred_element_type=jnp.float32)


def strip_token(side_index, rotation, cell):
    turn = lax.rem(side_index + 6 - rotation, 4)
    depth = cell >> 4
    along = cell & (SIDE - 1)
    far = SIDE - 1 - along
    near_rim = RADIUS - 1 - depth
    far_rim = SIDE - RADIUS + depth
    row = jnp.where(turn == 0, far_rim, jnp.where(turn == 1, along, jnp.where(turn == 2, near_rim, far)))
    col = jnp.where(turn == 0, along, jnp.where(turn == 1, near_rim, jnp.where(turn == 2, far, far_rim)))
    return row * SIDE + col


def slot_side(slot, columns):
    tile = lax.axis_index("tile")
    if slot < 2:
        return jnp.where((tile + slot) & 1 == 0, 1, 3)
    return jnp.where((lax.div(tile, columns) + slot) & 1 == 0, 2, 0)


def partner(tile, tile_count, slot):
    columns = tile_count // 4
    if slot < 2:
        return (tile + (1 if (tile + slot) % 2 == 0 else -1)) % tile_count
    return (tile + (columns if (tile // columns + slot) % 2 == 0 else -columns)) % tile_count


def pick_kernel(columns, rotations_ref, keys_ref, values_ref, *out_refs):
    cell = lax.broadcasted_iota(jnp.int32, (STRIP, CELLS), 0)
    token = lax.broadcasted_iota(jnp.int32, (STRIP, CELLS), 1)
    for slot, out_ref in enumerate(out_refs):
        side = slot_side(slot, columns)
        wanted = strip_token(side, rotations_ref[0, side], cell)
        chosen = jnp.where(token == wanted, 1.0, 0.0).astype(jnp.bfloat16)
        out_ref[0] = mm(chosen, keys_ref[...]).astype(jnp.bfloat16)
        out_ref[1] = mm(chosen, values_ref[...]).astype(jnp.bfloat16)


def weight_kernel(scale, *refs):
    total = refs[0][0].astype(jnp.float32)
    for ref in refs[1:-1]:
        total += ref[0].astype(jnp.float32)
    refs[-1][...] = total * scale


def partial_kernel(attention_ref, arrived_ref, turned_ref, turned_arrived_ref, unused_ref, kept_ref, sent_ref):
    for index, out_ref in enumerate((kept_ref, sent_ref)):
        total = None
        for turned_part, attention_part in ((turned_ref, attention_ref), (turned_arrived_ref, arrived_ref)):
            turned = turned_part[index]
            turned = turned.reshape(turned.shape[0] * turned.shape[1], turned.shape[2])
            term = mm(turned, attention_part[...])
            total = term if total is None else total + term
        out_ref[...] = total.astype(out_ref.dtype).reshape(out_ref.shape)


def sum_kernel(count, *refs):
    terms, outs = refs[:count], refs[count + 3 :]
    for q in range(terms[0].shape[0]):
        total = terms[0][q].astype(jnp.float32)
        for ref in terms[1:]:
            total += ref[q].astype(jnp.float32)
        outs[q % len(outs)][q // len(outs)] = total.astype(jnp.bfloat16)


def rim_token(side_index, place):
    depth = place >> 4
    along = place & (SIDE - 1)
    last = SIDE - 1
    north, east, south = side_index == 0, side_index == 1, side_index == 2
    row = jnp.where(north, depth, jnp.where(east, along, jnp.where(south, last - depth, last - along)))
    col = jnp.where(north, along, jnp.where(east, last - depth, jnp.where(south, last - along, depth)))
    return row * SIDE + col


def cotangent_kernel(heads, *refs):
    blocks, out_weight_ref, outs = refs[:heads], refs[heads], refs[heads + 1 :]
    dout_ref, dout_turned_ref, turned_ref, turned_sent_ref = outs
    head = lax.axis_index("head")
    axis = head & 1
    tile = lax.axis_index("tile")
    chunk = turned_ref.shape[2]
    width = blocks[0].shape[1]
    total = None
    for distance, block_ref in enumerate(blocks):
        owner = lax.rem(head + distance, heads)
        start = pl.multiple_of(owner * width, width)
        block = block_ref[...]
        term = mm(block, out_weight_ref[pl.ds(start, width), :])
        total = term if total is None else total + term
        turned = block.T
        first = owner * (width // chunk)
        for index in range(width // chunk):
            target = (first + index) ^ tile
            rows = turned[index * chunk : (index + 1) * chunk]
            for parity, out_ref in enumerate((turned_ref, turned_sent_ref)):

                @pl.when((target >> axis) & 1 == parity)
                def _():
                    out_ref[(target >> (1 - axis)) & 1, target >> 2] = rows

    dout = total.astype(jnp.bfloat16)
    dout_ref[...] = dout
    dout_turned_ref[...] = dout.T


def split(exact, count):
    parts = []
    for _ in range(count):
        part = exact.astype(jnp.bfloat16).astype(jnp.float32)
        parts.append(part)
        exact = exact - part
    return parts


PARTS = (3, 2, 2)
SIDE_ORDER = (3, 2, 1, 0)


def rim_kernel(columns, query_ref, dout_ref, rows_ref, unused_ref, *rim_refs):
    place = lax.broadcasted_iota(jnp.int32, (LANES, CELLS), 0)
    token = lax.broadcasted_iota(jnp.int32, (LANES, CELLS), 1)
    parts = [part for kind, count in enumerate(PARTS) for part in split(rows_ref[kind], count)]
    pairs = rows_ref.shape[1] // 2
    filler = jnp.zeros((16 - 2 * len(parts), CELLS), jnp.float32)
    rows = [
        jnp.concatenate([part[2 * pair : 2 * pair + 2] for part in parts] + [filler], axis=0) for pair in range(pairs)
    ]
    rows = jnp.concatenate(rows, axis=0).astype(jnp.bfloat16)
    for slot, rim_ref in enumerate(rim_refs):
        wanted = rim_token(slot_side(slot, columns), place)
        chosen = jnp.where((token == wanted) & (place < STRIP), 1.0, 0.0).astype(jnp.bfloat16)
        rim_ref[:STRIP] = mm(chosen[:STRIP], query_ref[...]).astype(jnp.bfloat16)
        rim_ref[STRIP : 2 * STRIP] = mm(chosen[:STRIP], dout_ref[...]).astype(jnp.bfloat16)
        spread = mm_nt(rows, chosen).astype(jnp.bfloat16)
        for pair in range(pairs):
            rim_ref[2 * STRIP :, pair * PAIR : (pair + 1) * PAIR] = spread[16 * pair : 16 * pair + 16]


def window(cell_row, cell_col, query):
    query_row = (query >> 4) + RADIUS
    query_col = (query & (SIDE - 1)) + RADIUS
    near = (jnp.abs(cell_row - query_row) <= RADIUS) & (jnp.abs(cell_col - query_col) <= RADIUS)
    return jnp.where(near, 0.0, -1e30)


def centre_bias(bias_ref):
    query = lax.broadcasted_iota(jnp.int32, (CELLS, CELLS), 1)
    cell = lax.broadcasted_iota(jnp.int32, (CELLS, CELLS), 0)
    bias_ref[...] = window((cell >> 4) + RADIUS, (cell & (SIDE - 1)) + RADIUS, query)


def strip_bias(kind, bias_ref):
    query = lax.broadcasted_iota(jnp.int32, (STRIP, CELLS), 1)
    cell = lax.broadcasted_iota(jnp.int32, (STRIP, CELLS), 0)
    depth = cell >> 4
    along = cell & (SIDE - 1)
    last = SIDE + 2 * RADIUS - 1
    if kind:
        first, second = (last - RADIUS - along, depth), (RADIUS + along, last - depth)
    else:
        first, second = (depth, RADIUS + along), (last - depth, last - RADIUS - along)
    in_first = first_half(query, kind)
    row = jnp.where(in_first, first[0], second[0])
    col = jnp.where(in_first, first[1], second[1])
    bias_ref[...] = window(row, col, query)


def first_half(query, kind):
    return (query & (SIDE - 1)) < SIDE // 2 if kind else query < CELLS // 2


def one_head(block, head):
    lane = lax.broadcasted_iota(jnp.int32, block.shape, 1)
    kept = (lane >= HEAD_DIM) if head else (lane < HEAD_DIM)
    return jnp.where(kept, block, jnp.zeros_like(block))


def halves(block, kind):
    kept = first_half(lax.broadcasted_iota(jnp.int32, block.shape, 0), kind)
    zero = jnp.zeros_like(block)
    return jnp.concatenate([jnp.where(kept, block, zero), jnp.where(kept, zero, block)], axis=1)


def by_half(stacked, kind):
    rows = stacked.shape[0] // 2
    kept = first_half(lax.broadcasted_iota(jnp.int32, (rows, CELLS), 1), kind)
    return jnp.where(kept, stacked[:rows], stacked[rows:])


def side_blocks(strips, part, kind, cols):
    tile = lax.axis_index("tile")
    second, first = strips
    straight = (tile if kind else lax.div(tile, lax.axis_size("tile") // 4)) & 1 == 0
    first, second = first[part, :, cols], second[part, :, cols]
    return jnp.where(straight, first, second), jnp.where(straight, second, first)


def side_cells(strips, part, kind, cols):
    return jnp.concatenate(side_blocks(strips, part, kind, cols), axis=1)


def halves(block, kind):
    kept = first_half(lax.broadcasted_iota(jnp.int32, block.shape, 0), kind)
    zero = jnp.zeros_like(block)
    return jnp.concatenate([jnp.where(kept, block, zero), jnp.where(kept, zero, block)], axis=1)


def by_half(stacked, kind):
    rows = stacked.shape[0] // 2
    kept = first_half(lax.broadcasted_iota(jnp.int32, (rows, CELLS), 1), kind)
    return jnp.where(kept, stacked[:rows], stacked[rows:])


def side_blocks(strips, part, kind, cols):
    tile = lax.axis_index("tile")
    second, first = strips
    straight = (tile if kind else lax.div(tile, lax.axis_size("tile") // 4)) & 1 == 0
    first, second = first[part, :, cols], second[part, :, cols]
    return jnp.where(straight, first, second), jnp.where(straight, second, first)


def side_cells(strips, part, kind, cols):
    return jnp.concatenate(side_blocks(strips, part, kind, cols), axis=1)


def side_products(cells, rows_head):
    return [mm_nt(cells[kind], halves(rows_head, kind)) for kind in range(2)]


def turned_sides(strips, part, kind, cols):
    return [block.T for block in side_blocks(strips, part, kind, cols)]


def pair_cols(pair):
    return pl.ds(pl.multiple_of(pair * PAIR, PAIR), PAIR)


def head_rows(turned, head):
    return turned[head * HEAD_DIM : (head + 1) * HEAD_DIM]


def over_side(turned, head, kind, sides):
    return by_half(mm(jnp.concatenate([head_rows(t, head) for t in turned], axis=0), sides), kind)


SCORE_SCALE = HEAD_DIM ** (-0.5)
LOG_SCALE = SCORE_SCALE * math.log2(math.e)


def lanes_of(head):
    return slice(head * CELLS, (head + 1) * CELLS)


def centre_kernel(
    query_ref, key_ref, value_ref, dout_ref,
    raw_ref, stats_ref, sums_ref, product_ref, query_out, key_out, bias_ref,
):
    centre_bias(bias_ref)

    def step(pair, carry):
        cols = pair_cols(pair)
        query, key, value, dout = (ref[:, cols] for ref in (query_ref, key_ref, value_ref, dout_ref))
        turned = value.T
        for head in range(2):
            lanes = lanes_of(head)
            scores = mm_nt(key, one_head(query, head)) + bias_ref[...]
            top = jnp.max(scores, axis=0, keepdims=True)
            raw = jnp.exp2((scores - top) * LOG_SCALE)
            raw_ref[pair, :, lanes] = raw
            stats_ref[pair, 0:1, lanes] = top
            stats_ref[pair, 1:2, lanes] = jnp.sum(raw, axis=0, keepdims=True)
            sums_ref[pair, :, lanes] = mm(head_rows(turned, head), raw.astype(jnp.bfloat16))
            product_ref[pair, :, lanes] = mm_nt(value, one_head(dout, head))
        query_out[:, cols] = query
        key_out[:, cols] = key
        return carry

    lax.fori_loop(0, raw_ref.shape[0], step, 0)


def column_kernel(
    first_ref, second_ref, query_ref, dout_ref, raw_ref, stats_ref, sums_ref, product_ref, bias_ref
):
    strips = (first_ref, second_ref)
    strip_bias(0, bias_ref)

    def step(pair, carry):
        cols = pair_cols(pair)
        keys = side_cells(strips, 0, 0, cols)
        values = side_cells(strips, 1, 0, cols)
        turned = turned_sides(strips, 1, 0, cols)
        for head in range(2):
            lanes = lanes_of(head)
            scores = mm_nt(keys, halves(one_head(query_ref[:, cols], head), 0)) + bias_ref[...]
            top = jnp.max(scores, axis=0, keepdims=True)
            raw = jnp.exp2((scores - top) * LOG_SCALE)
            raw_ref[pair, :, lanes] = raw
            stats_ref[pair, 0:1, lanes] = top
            stats_ref[pair, 1:2, lanes] = jnp.sum(raw, axis=0, keepdims=True)
            sums_ref[pair, :, lanes] = over_side(turned, head, 0, raw.astype(jnp.bfloat16))
            product_ref[pair, :, lanes] = mm_nt(values, halves(one_head(dout_ref[:, cols], head), 0))
        return carry

    lax.fori_loop(0, raw_ref.shape[0], step, 0)


def row_kernel(
    first_ref, second_ref, query_ref, dout_turned_ref, centre_stats_ref, centre_sums_ref, stats_ref, sums_ref,
    raw_ref, attention_ref, rows_ref, factors_ref, bias_ref,
):
    strips = (first_ref, second_ref)
    strip_bias(1, bias_ref)

    def step(pair, carry):
        cols = pair_cols(pair)
        keys = side_cells(strips, 0, 1, cols)
        turned = turned_sides(strips, 1, 1, cols)
        parts = []
        for head in range(2):
            lanes = lanes_of(head)
            scores = mm_nt(keys, halves(one_head(query_ref[:, cols], head), 1)) + bias_ref[...]
            tops = [ref[pair, 0:1, lanes] for ref in (centre_stats_ref, stats_ref)]
            top = jnp.maximum(jnp.max(scores, axis=0, keepdims=True), jnp.maximum(*tops))
            raw = jnp.exp2((scores - top) * LOG_SCALE)
            raw_ref[pair, :, lanes] = raw
            lifted = [jnp.exp2((t - top) * LOG_SCALE) for t in tops]
            total = jnp.sum(raw, axis=0, keepdims=True)
            total += lifted[0] * centre_stats_ref[pair, 1:2, lanes] + lifted[1] * stats_ref[pair, 1:2, lanes]
            inverse = 1.0 / total
            factors = [l * inverse for l in lifted]
            part = over_side(turned, head, 1, raw.astype(jnp.bfloat16)) * inverse
            part += factors[0] * centre_sums_ref[pair, :, lanes] + factors[1] * sums_ref[pair, :, lanes]
            parts.append(part)
            place = pl.ds(2 * pair + head, 1)
            features = pl.ds(pl.multiple_of((2 * pair + head) * HEAD_DIM, HEAD_DIM), HEAD_DIM)
            product = dout_turned_ref[features, :].astype(jnp.float32) * part
            rows_ref[0, place, :] = top
            rows_ref[1, place, :] = inverse
            rows_ref[2, place, :] = jnp.sum(product, axis=0, keepdims=True)
            factors_ref[0, place, :] = factors[0]
            factors_ref[1, place, :] = factors[1]
        attention_ref[:, cols] = jnp.concatenate(parts, axis=0).T.astype(jnp.bfloat16)
        return carry

    lax.fori_loop(0, raw_ref.shape[0], step, 0, unroll=True)


def backward_kernel(
    fourth_ref, third_ref, second_ref, first_ref, query_ref, key_ref, dout_ref, centre_raw_ref, column_raw_ref,
    row_raw_ref, centre_product_ref, column_product_ref, rows_ref, factors_ref, unused_ref,
    grad_query_ref, centre_ref,
):
    columns, rows = (third_ref, fourth_ref), (first_ref, second_ref)

    def step(pair, carry):
        cols = pair_cols(pair)
        query = query_ref[:, cols]
        dout = dout_ref[:, cols]
        turned_centre = key_ref[:, cols].T
        turned_columns = turned_sides(columns, 0, 0, cols)
        turned_rows = turned_sides(rows, 0, 1, cols)
        row_values = side_cells(rows, 1, 1, cols)
        parts = []
        centre_scores = []
        centre_weights = []
        for head in range(2):
            lanes = lanes_of(head)
            place = pl.ds(2 * pair + head, 1)
            delta = rows_ref[2, place, :]
            row_product = mm_nt(row_values, halves(one_head(dout, head), 1))

            def dscore(weights, product):
                return (weights * (product - delta)).astype(jnp.bfloat16)

            weights = centre_raw_ref[pair, :, lanes] * factors_ref[0, place, :]
            centre_weights.append(weights.astype(jnp.bfloat16))
            centre_scores.append(dscore(weights, centre_product_ref[pair, :, lanes]))
            column_weights = column_raw_ref[pair, :, lanes] * factors_ref[1, place, :]
            column_score = dscore(column_weights, column_product_ref[pair, :, lanes])
            row_score = dscore(row_raw_ref[pair, :, lanes] * rows_ref[1, place, :], row_product)
            part = mm(head_rows(turned_centre, head), centre_scores[-1])
            part += over_side(turned_columns, head, 0, column_score) + over_side(turned_rows, head, 1, row_score)
            parts.append(part)
        grad_query = jnp.concatenate(parts, axis=0).T * SCORE_SCALE
        grad_query_ref[:, cols] = grad_query.astype(jnp.bfloat16)
        grad_key, grad_value = joint_mm(
            jnp.concatenate(centre_scores, axis=1),
            jnp.concatenate(centre_weights, axis=1),
            both_heads(query),
            both_heads(dout),
        )
        centre_ref[0, :, cols] = grad_key * SCORE_SCALE
        centre_ref[1, :, cols] = grad_value
        return carry

    lax.fori_loop(0, centre_raw_ref.shape[0], step, 0)


def joint_mm(first, second, first_rows, second_rows):
    rows = first.shape[0]
    product = mm(jnp.concatenate([first, second], axis=0), jnp.concatenate([first_rows, second_rows], axis=1))
    return product[:rows, :PAIR], product[rows:, PAIR:]


def both_heads(block):
    return jnp.concatenate([one_head(block, head) for head in range(2)], axis=0)


def padded(block):
    return jnp.concatenate([block, jnp.zeros((LANES - block.shape[0], block.shape[1]), block.dtype)], axis=0)


def statistics(rows):
    first = 0
    for count in PARTS:
        heads = []
        for head in range(2):
            parts = [rows[2 * index + head : 2 * index + head + 1] for index in range(first, first + count)]
            heads.append(functools.reduce(jnp.add, parts))
        first += count
        yield jnp.concatenate(heads, axis=1)


def side_kernel(columns, rotations_ref, centre_ref, *refs):
    picked, rims = refs[:4], refs[4:8]
    keys_ref, values_ref, chosen_ref, bias_ref, keys_done, values_done, sems = refs[8:]
    cell = lax.broadcasted_iota(jnp.int32, (STRIP, LANES), 0)
    query = lax.broadcasted_iota(jnp.int32, (STRIP, LANES), 1)
    near = jnp.abs((cell & (SIDE - 1)) - (query & (SIDE - 1))) <= RADIUS
    near = near & ((cell >> 4) >= (query >> 4)) & (query < STRIP)
    bias_ref[...] = jnp.where(near, 0.0, -1e30)
    token = lax.broadcasted_iota(jnp.int32, (CELLS, LANES), 0)
    place = lax.broadcasted_iota(jnp.int32, (CELLS, LANES), 1)
    for index, slot in enumerate(SIDE_ORDER):
        side = slot_side(slot, columns)
        wanted = jnp.where(place < STRIP, strip_token(side, rotations_ref[0, side], place), -1)
        chosen = jnp.where(token == wanted, 1.0, 0.0).astype(jnp.bfloat16)
        chosen_ref[:, index * LANES : (index + 1) * LANES] = chosen

    copies = []
    for pair in range(keys_ref.shape[1] // PAIR):
        cols = slice(pair * PAIR, (pair + 1) * PAIR)
        grads = []
        bias = jnp.concatenate([bias_ref[...]] * 2, axis=1)
        for picked_ref, rim_ref in zip(picked, rims):
            query = both_heads(padded(rim_ref[:STRIP, cols]))
            dout = both_heads(padded(rim_ref[STRIP : 2 * STRIP, cols]))
            top, inverse, delta = statistics(rim_ref[2 * STRIP :, cols].astype(jnp.float32))
            scores = mm_nt(picked_ref[0, :, cols], query) + bias
            weights = jnp.exp2((scores - top) * LOG_SCALE) * inverse
            product = mm_nt(picked_ref[1, :, cols], dout)
            dscore = (weights * (product - delta)).astype(jnp.bfloat16)
            grad = jnp.concatenate([mm(dscore, query) * SCORE_SCALE, mm(weights.astype(jnp.bfloat16), dout)], axis=1)
            grads.append(padded(grad.astype(jnp.bfloat16)))
        total = mm(chosen_ref[...], jnp.concatenate(grads, axis=0))
        keys_done[:, cols] = (centre_ref[0, :, cols] + total[:, :PAIR]).astype(jnp.bfloat16)
        values_done[:, cols] = (centre_ref[1, :, cols] + total[:, PAIR:]).astype(jnp.bfloat16)
        for index, (done, out_ref) in enumerate(((keys_done, keys_ref), (values_done, values_ref))):
            copy = pltpu.make_async_copy(done.at[:, cols], out_ref.at[:, cols], sems.at[2 * pair + index])
            copy.start()
            copies.append(copy)
    for copy in copies:
        copy.wait()


def call(kernel, name, out_shape, operands, scratch=(), smem=0, unused=0, gflop=0.1, out_space=pltpu.VMEM):
    specs = [pl.BlockSpec(memory_space=pltpu.SMEM)] * smem
    specs += [pl.BlockSpec(memory_space=pltpu.VMEM)] * (len(operands) - smem - unused)
    specs += [pl.BlockSpec(memory_space=pl.ANY)] * unused
    single = not isinstance(out_shape, list)
    outs = pl.BlockSpec(memory_space=out_space)
    return pl.pallas_call(
        kernel,
        out_shape=out_shape,
        in_specs=specs,
        out_specs=outs if single else [outs] * len(out_shape),
        scratch_shapes=list(scratch),
        compiler_params=pltpu.CompilerParams(vmem_limit_bytes=VMEM_LIMIT),
        cost_estimate=pl.CostEstimate(flops=int(gflop * 1e9), bytes_accessed=1 << 20, transcendentals=0),
        name=name,
    )(*operands)


def in_hbm(array):
    return pltpu.with_memory_space_constraint(array, pltpu.HBM)


def across(block, distances):
    heads = lax.axis_size("head")
    devices = [(tile, head) for tile in range(lax.axis_size("tile")) for head in range(heads)]
    route = [(tile * heads + head, (tile ^ distances[head % 2]) * heads + head) for tile, head in devices]
    return lax.ppermute(block, ("tile", "head"), route)


def exchanged(blocks, stride):
    terms = list(blocks[:1])
    for distance in range(1, len(blocks)):
        route = [(tile, tile ^ (distance * stride)) for tile in range(lax.axis_size("tile"))]
        terms.append(lax.ppermute(blocks[distance], "tile", route))
    return terms


def with_partners(blocks, slots):
    tile_count = lax.axis_size("tile")
    routes = {s: [(tile, partner(tile, tile_count, s)) for tile in range(tile_count)] for s in slots}
    return {s: lax.ppermute(blocks[s], "tile", routes[s]) for s in slots}


def shards(queries, keys, values, grad_output, out_weight, rotations):
    tile_count = lax.axis_size("tile")
    token_count, features = queries.shape
    model = out_weight.shape[0]
    pairs = features // PAIR
    far = tile_count // NEAR
    chunk = model // tile_count
    heads = lax.axis_size("head")
    columns = tile_count // 4
    queries, keys, values, out_weight, rotations = (
        in_hbm(a) for a in (queries, keys, values, out_weight, rotations)
    )

    def bf16(*shape):
        return jax.ShapeDtypeStruct(shape, jnp.bfloat16)

    def f32(*shape):
        return jax.ShapeDtypeStruct(shape, jnp.float32)

    strip_types = [bf16(2, STRIP, features)] * 4
    picked = call(
        functools.partial(pick_kernel, columns), "pick_strips", strip_types, (rotations, keys, values), smem=1
    )
    grad_output, *picked = lax.optimization_barrier((grad_output, *picked))
    strips = with_partners(picked, (3, 2, 1, 0))
    strips = [strips[s] for s in range(4)]

    cotangents = [
        lax.ppermute(grad_output, "head", [((h + k) % heads, h) for h in range(heads)]) for k in range(1, heads)
    ]
    dout, dout_turned, turned, turned_sent = call(
        functools.partial(cotangent_kernel, heads),
        "cotangent",
        [bf16(CELLS, features), bf16(features, CELLS)] + [bf16(2, far, chunk, CELLS)] * 2,
        (in_hbm(grad_output), *cotangents, out_weight),
        gflop=1.0,
    )
    turned_arrived = across(turned_sent, (1, 2))
    part_types = [f32(pairs, 2, 2 * CELLS), f32(pairs, HEAD_DIM, 2 * CELLS)]
    raw_centre, stats_centre, sums_centre, product_centre, queries, keys = call(
        centre_kernel,
        "centre",
        [f32(pairs, CELLS, 2 * CELLS)] + part_types + [f32(pairs, CELLS, 2 * CELLS)] + [bf16(CELLS, features)] * 2,
        (queries, keys, values, dout),
        scratch=[pltpu.VMEM((CELLS, CELLS), jnp.float32)],
        gflop=3.0,
    )
    strip_scratch = [pltpu.VMEM((STRIP, CELLS), jnp.float32)]
    raw_columns, stats_columns, sums_columns, product_columns = call(
        column_kernel,
        "columns",
        [f32(pairs, STRIP, 2 * CELLS)] + part_types + [f32(pairs, STRIP, 2 * CELLS)],
        (strips[2], strips[3], queries, dout),
        scratch=strip_scratch,
        gflop=2.0,
    )
    raw_rows, attention, rows, factors = call(
        row_kernel,
        "rows",
        [f32(pairs, STRIP, 2 * CELLS), bf16(CELLS, features)] + [f32(k, 2 * pairs, CELLS) for k in (3, 2)],
        (strips[0], strips[1], queries, dout_turned, stats_centre, sums_centre, stats_columns, sums_columns),
        scratch=strip_scratch,
    )
    attention_arrived = across(attention, (1, 2))
    rims = call(
        functools.partial(rim_kernel, columns),
        "rims",
        [bf16(2 * STRIP + 16, features)] * 4,
        (queries, dout, rows, turned_arrived),
        unused=1,
    )
    rims_arrived = with_partners(rims, (3, 2, 1))
    kept, sent = call(
        partial_kernel,
        "partial",
        [f32(far, chunk, features), bf16(far, chunk, features)],
        (attention, attention_arrived, turned, turned_arrived, rims[0]),
        unused=1,
    )
    terms = [kept, across(sent, (2, 1))]
    rims = lax.optimization_barrier((*rims, sent))[:4]
    rims_arrived |= with_partners(rims, (0,))
    grad_queries, centre = call(
        backward_kernel,
        "backward",
        [bf16(CELLS, features), f32(2, CELLS, features)],
        (
            *strips[::-1], queries, keys, dout, raw_centre, raw_columns, raw_rows, product_centre, product_columns,
            rows, factors, sent,
        ),
        unused=1,
        gflop=3.0,
    )
    stride = NEAR
    while stride < tile_count:
        ways = min(NEAR, tile_count // stride)
        sums = call(
            functools.partial(sum_kernel, len(terms)),
            "plane_sum",
            [bf16(tile_count // stride // ways, chunk, features)] * ways,
            (*terms, centre, rims_arrived[3], rims_arrived[2]),
            unused=3,
        )
        terms = exchanged(sums, stride)
        stride *= ways

    grad_keys, grad_values = call(
        functools.partial(side_kernel, columns),
        "sides",
        [bf16(CELLS, features)] * 2,
        (rotations, centre, *(picked[s] for s in SIDE_ORDER), *(rims_arrived[s] for s in SIDE_ORDER)),
        scratch=[pltpu.VMEM((CELLS, 4 * LANES), jnp.bfloat16), pltpu.VMEM((STRIP, LANES), jnp.float32)]
        + [pltpu.VMEM((CELLS, features), jnp.bfloat16)] * 2
        + [pltpu.SemaphoreType.DMA((2 * pairs,))],
        smem=1,
        gflop=3.0,
        out_space=pl.ANY,
    )
    grad_out_weight = call(
        functools.partial(weight_kernel, 1.0 / math.sqrt(token_count * tile_count)),
        "weight_sum",
        f32(chunk, features),
        terms,
    )
    return (grad_queries, grad_keys, grad_values, grad_out_weight)


def solution(mesh):
    placed = (
        P("tile", "head"),
        P("tile", "head"),
        P("tile", "head"),
        P("tile", "head"),
        P(None, "head"),
        P("tile", None),
    )
    return jax.shard_map(
        shards,
        mesh=mesh,
        in_specs=placed,
        out_specs=(P("tile", "head"), P("tile", "head"), P("tile", "head"), P("tile", "head")),
        check_vma=False,
    )
```

```python
import functools
import math

import jax
import jax.numpy as jnp
from jax import lax
from jax.experimental import pallas as pl
from jax.experimental.pallas import tpu as pltpu
from jax.sharding import PartitionSpec as P

HEAD_DIM = 64
RADIUS = 6
SIDE = 16
CELLS = SIDE * SIDE
STRIP = RADIUS * SIDE
NEAR = 4
LANES = 128
PAIR = 2 * HEAD_DIM
VMEM_LIMIT = 32 * 1024 * 1024
NT = (((1,), (1,)), ((), ()))


def mm(a, b):
    return jnp.dot(a, b, preferred_element_type=jnp.float32)


def mm_nt(a, b):
    return lax.dot_general(a, b, NT, preferred_element_type=jnp.float32)


def strip_token(side_index, rotation, cell):
    turn = lax.rem(side_index + 6 - rotation, 4)
    depth = cell >> 4
    along = cell & (SIDE - 1)
    far = SIDE - 1 - along
    near_rim = RADIUS - 1 - depth
    far_rim = SIDE - RADIUS + depth
    row = jnp.where(turn == 0, far_rim, jnp.where(turn == 1, along, jnp.where(turn == 2, near_rim, far)))
    col = jnp.where(turn == 0, along, jnp.where(turn == 1, near_rim, jnp.where(turn == 2, far, far_rim)))
    return row * SIDE + col


def slot_side(slot, columns):
    tile = lax.axis_index("tile")
    if slot < 2:
        return jnp.where((tile + slot) & 1 == 0, 1, 3)
    return jnp.where((lax.div(tile, columns) + slot) & 1 == 0, 2, 0)


def partner(tile, tile_count, slot):
    columns = tile_count // 4
    if slot < 2:
        return (tile + (1 if (tile + slot) % 2 == 0 else -1)) % tile_count
    return (tile + (columns if (tile // columns + slot) % 2 == 0 else -columns)) % tile_count


def pick_kernel(columns, rotations_ref, keys_ref, values_ref, *out_refs):
    cell = lax.broadcasted_iota(jnp.int32, (STRIP, CELLS), 0)
    token = lax.broadcasted_iota(jnp.int32, (STRIP, CELLS), 1)
    for slot, out_ref in enumerate(out_refs):
        side = slot_side(slot, columns)
        wanted = strip_token(side, rotations_ref[0, side], cell)
        chosen = jnp.where(token == wanted, 1.0, 0.0).astype(jnp.bfloat16)
        out_ref[0] = mm(chosen, keys_ref[...]).astype(jnp.bfloat16)
        out_ref[1] = mm(chosen, values_ref[...]).astype(jnp.bfloat16)


def weight_kernel(scale, *refs):
    total = refs[0][0].astype(jnp.float32)
    for ref in refs[1:-1]:
        total += ref[0].astype(jnp.float32)
    refs[-1][...] = total * scale


def partial_kernel(attention_ref, arrived_ref, turned_ref, turned_arrived_ref, unused_ref, kept_ref, sent_ref):
    for index, out_ref in enumerate((kept_ref, sent_ref)):
        total = None
        for turned_part, attention_part in ((turned_ref, attention_ref), (turned_arrived_ref, arrived_ref)):
            turned = turned_part[index]
            turned = turned.reshape(turned.shape[0] * turned.shape[1], turned.shape[2])
            term = mm(turned, attention_part[...])
            total = term if total is None else total + term
        out_ref[...] = total.astype(out_ref.dtype).reshape(out_ref.shape)


def sum_kernel(count, *refs):
    terms, outs = refs[:count], refs[count + 3 :]
    for q in range(terms[0].shape[0]):
        total = terms[0][q].astype(jnp.float32)
        for ref in terms[1:]:
            total += ref[q].astype(jnp.float32)
        outs[q % len(outs)][q // len(outs)] = total.astype(jnp.bfloat16)


def rim_token(side_index, place):
    depth = place >> 4
    along = place & (SIDE - 1)
    last = SIDE - 1
    north, east, south = side_index == 0, side_index == 1, side_index == 2
    row = jnp.where(north, depth, jnp.where(east, along, jnp.where(south, last - depth, last - along)))
    col = jnp.where(north, along, jnp.where(east, last - depth, jnp.where(south, last - along, depth)))
    return row * SIDE + col


def cotangent_kernel(heads, *refs):
    blocks, out_weight_ref, outs = refs[:heads], refs[heads], refs[heads + 1 :]
    dout_ref, dout_turned_ref, turned_ref, turned_sent_ref = outs
    head = lax.axis_index("head")
    axis = 1 - (head & 1)
    tile = lax.axis_index("tile")
    chunk = turned_ref.shape[2]
    width = blocks[0].shape[1]
    total = None
    for distance, block_ref in enumerate(blocks):
        owner = lax.rem(head + distance, heads)
        start = pl.multiple_of(owner * width, width)
        block = block_ref[...]
        term = mm(block, out_weight_ref[pl.ds(start, width), :])
        total = term if total is None else total + term
        turned = block.T
        first = owner * (width // chunk)
        for index in range(width // chunk):
            target = (first + index) ^ tile
            rows = turned[index * chunk : (index + 1) * chunk]
            for parity, out_ref in enumerate((turned_ref, turned_sent_ref)):

                @pl.when((target >> axis) & 1 == parity)
                def _():
                    out_ref[(target >> (1 - axis)) & 1, target >> 2] = rows

    dout = total.astype(jnp.bfloat16)
    dout_ref[...] = dout
    dout_turned_ref[...] = dout.T


def split(exact, count):
    parts = []
    for _ in range(count):
        part = exact.astype(jnp.bfloat16).astype(jnp.float32)
        parts.append(part)
        exact = exact - part
    return parts


PARTS = (3, 2, 2)
SIDE_ORDER = (3, 2, 1, 0)


def rim_kernel(columns, query_ref, dout_ref, rows_ref, unused_ref, *rim_refs):
    place = lax.broadcasted_iota(jnp.int32, (LANES, CELLS), 0)
    token = lax.broadcasted_iota(jnp.int32, (LANES, CELLS), 1)
    parts = [part for kind, count in enumerate(PARTS) for part in split(rows_ref[kind], count)]
    pairs = rows_ref.shape[1] // 2
    filler = jnp.zeros((16 - 2 * len(parts), CELLS), jnp.float32)
    rows = [
        jnp.concatenate([part[2 * pair : 2 * pair + 2] for part in parts] + [filler], axis=0) for pair in range(pairs)
    ]
    rows = jnp.concatenate(rows, axis=0).astype(jnp.bfloat16)
    for slot, rim_ref in enumerate(rim_refs):
        wanted = rim_token(slot_side(slot, columns), place)
        chosen = jnp.where((token == wanted) & (place < STRIP), 1.0, 0.0).astype(jnp.bfloat16)
        rim_ref[:STRIP] = mm(chosen[:STRIP], query_ref[...]).astype(jnp.bfloat16)
        rim_ref[STRIP : 2 * STRIP] = mm(chosen[:STRIP], dout_ref[...]).astype(jnp.bfloat16)
        spread = mm_nt(rows, chosen).astype(jnp.bfloat16)
        for pair in range(pairs):
            rim_ref[2 * STRIP :, pair * PAIR : (pair + 1) * PAIR] = spread[16 * pair : 16 * pair + 16]


def window(cell_row, cell_col, query):
    query_row = (query >> 4) + RADIUS
    query_col = (query & (SIDE - 1)) + RADIUS
    near = (jnp.abs(cell_row - query_row) <= RADIUS) & (jnp.abs(cell_col - query_col) <= RADIUS)
    return jnp.where(near, 0.0, -1e30)


def centre_bias(bias_ref):
    query = lax.broadcasted_iota(jnp.int32, (CELLS, CELLS), 1)
    cell = lax.broadcasted_iota(jnp.int32, (CELLS, CELLS), 0)
    bias_ref[...] = window((cell >> 4) + RADIUS, (cell & (SIDE - 1)) + RADIUS, query)


def strip_bias(kind, bias_ref):
    query = lax.broadcasted_iota(jnp.int32, (STRIP, CELLS), 1)
    cell = lax.broadcasted_iota(jnp.int32, (STRIP, CELLS), 0)
    depth = cell >> 4
    along = cell & (SIDE - 1)
    last = SIDE + 2 * RADIUS - 1
    if kind:
        first, second = (last - RADIUS - along, depth), (RADIUS + along, last - depth)
    else:
        first, second = (depth, RADIUS + along), (last - depth, last - RADIUS - along)
    in_first = first_half(query, kind)
    row = jnp.where(in_first, first[0], second[0])
    col = jnp.where(in_first, first[1], second[1])
    bias_ref[...] = window(row, col, query)


def first_half(query, kind):
    return (query & (SIDE - 1)) < SIDE // 2 if kind else query < CELLS // 2


def one_head(block, head):
    lane = lax.broadcasted_iota(jnp.int32, block.shape, 1)
    kept = (lane >= HEAD_DIM) if head else (lane < HEAD_DIM)
    return jnp.where(kept, block, jnp.zeros_like(block))


def halves(block, kind):
    kept = first_half(lax.broadcasted_iota(jnp.int32, block.shape, 0), kind)
    zero = jnp.zeros_like(block)
    return jnp.concatenate([jnp.where(kept, block, zero), jnp.where(kept, zero, block)], axis=1)


def by_half(stacked, kind):
    rows = stacked.shape[0] // 2
    kept = first_half(lax.broadcasted_iota(jnp.int32, (rows, CELLS), 1), kind)
    return jnp.where(kept, stacked[:rows], stacked[rows:])


def side_blocks(strips, part, kind, cols):
    tile = lax.axis_index("tile")
    second, first = strips
    straight = (tile if kind else lax.div(tile, lax.axis_size("tile") // 4)) & 1 == 0
    first, second = first[part, :, cols], second[part, :, cols]
    return jnp.where(straight, first, second), jnp.where(straight, second, first)


def side_cells(strips, part, kind, cols):
    return jnp.concatenate(side_blocks(strips, part, kind, cols), axis=1)


def halves(block, kind):
    kept = first_half(lax.broadcasted_iota(jnp.int32, block.shape, 0), kind)
    zero = jnp.zeros_like(block)
    return jnp.concatenate([jnp.where(kept, block, zero), jnp.where(kept, zero, block)], axis=1)


def by_half(stacked, kind):
    rows = stacked.shape[0] // 2
    kept = first_half(lax.broadcasted_iota(jnp.int32, (rows, CELLS), 1), kind)
    return jnp.where(kept, stacked[:rows], stacked[rows:])


def side_blocks(strips, part, kind, cols):
    tile = lax.axis_index("tile")
    second, first = strips
    straight = (tile if kind else lax.div(tile, lax.axis_size("tile") // 4)) & 1 == 0
    first, second = first[part, :, cols], second[part, :, cols]
    return jnp.where(straight, first, second), jnp.where(straight, second, first)


def side_cells(strips, part, kind, cols):
    return jnp.concatenate(side_blocks(strips, part, kind, cols), axis=1)


def side_products(cells, rows_head):
    return [mm_nt(cells[kind], halves(rows_head, kind)) for kind in range(2)]


def turned_sides(strips, part, kind, cols):
    return [block.T for block in side_blocks(strips, part, kind, cols)]


def pair_cols(pair):
    return pl.ds(pl.multiple_of(pair * PAIR, PAIR), PAIR)


def head_rows(turned, head):
    return turned[head * HEAD_DIM : (head + 1) * HEAD_DIM]


def over_side(turned, head, kind, sides):
    return by_half(mm(jnp.concatenate([head_rows(t, head) for t in turned], axis=0), sides), kind)


SCORE_SCALE = HEAD_DIM ** (-0.5)
LOG_SCALE = SCORE_SCALE * math.log2(math.e)


def lanes_of(head):
    return slice(head * CELLS, (head + 1) * CELLS)


def centre_kernel(
    query_ref, key_ref, value_ref, dout_ref,
    raw_ref, stats_ref, sums_ref, product_ref, query_out, key_out, bias_ref,
):
    centre_bias(bias_ref)

    def step(pair, carry):
        cols = pair_cols(pair)
        query, key, value, dout = (ref[:, cols] for ref in (query_ref, key_ref, value_ref, dout_ref))
        turned = value.T
        for head in range(2):
            lanes = lanes_of(head)
            scores = mm_nt(key, one_head(query, head)) + bias_ref[...]
            top = jnp.max(scores, axis=0, keepdims=True)
            raw = jnp.exp2((scores - top) * LOG_SCALE)
            raw_ref[pair, :, lanes] = raw
            stats_ref[pair, 0:1, lanes] = top
            stats_ref[pair, 1:2, lanes] = jnp.sum(raw, axis=0, keepdims=True)
            sums_ref[pair, :, lanes] = mm(head_rows(turned, head), raw.astype(jnp.bfloat16))
            product_ref[pair, :, lanes] = mm_nt(value, one_head(dout, head))
        query_out[:, cols] = query
        key_out[:, cols] = key
        return carry

    lax.fori_loop(0, raw_ref.shape[0], step, 0)


def column_kernel(
    first_ref, second_ref, query_ref, dout_ref, raw_ref, stats_ref, sums_ref, product_ref, bias_ref
):
    strips = (first_ref, second_ref)
    strip_bias(0, bias_ref)

    def step(pair, carry):
        cols = pair_cols(pair)
        keys = side_cells(strips, 0, 0, cols)
        values = side_cells(strips, 1, 0, cols)
        turned = turned_sides(strips, 1, 0, cols)
        for head in range(2):
            lanes = lanes_of(head)
            scores = mm_nt(keys, halves(one_head(query_ref[:, cols], head), 0)) + bias_ref[...]
            top = jnp.max(scores, axis=0, keepdims=True)
            raw = jnp.exp2((scores - top) * LOG_SCALE)
            raw_ref[pair, :, lanes] = raw
            stats_ref[pair, 0:1, lanes] = top
            stats_ref[pair, 1:2, lanes] = jnp.sum(raw, axis=0, keepdims=True)
            sums_ref[pair, :, lanes] = over_side(turned, head, 0, raw.astype(jnp.bfloat16))
            product_ref[pair, :, lanes] = mm_nt(values, halves(one_head(dout_ref[:, cols], head), 0))
        return carry

    lax.fori_loop(0, raw_ref.shape[0], step, 0)


def row_kernel(
    first_ref, second_ref, query_ref, dout_turned_ref, centre_stats_ref, centre_sums_ref, stats_ref, sums_ref,
    raw_ref, attention_ref, rows_ref, factors_ref, bias_ref,
):
    strips = (first_ref, second_ref)
    strip_bias(1, bias_ref)

    def step(pair, carry):
        cols = pair_cols(pair)
        keys = side_cells(strips, 0, 1, cols)
        turned = turned_sides(strips, 1, 1, cols)
        parts = []
        for head in range(2):
            lanes = lanes_of(head)
            scores = mm_nt(keys, halves(one_head(query_ref[:, cols], head), 1)) + bias_ref[...]
            tops = [ref[pair, 0:1, lanes] for ref in (centre_stats_ref, stats_ref)]
            top = jnp.maximum(jnp.max(scores, axis=0, keepdims=True), jnp.maximum(*tops))
            raw = jnp.exp2((scores - top) * LOG_SCALE)
            raw_ref[pair, :, lanes] = raw
            lifted = [jnp.exp2((t - top) * LOG_SCALE) for t in tops]
            total = jnp.sum(raw, axis=0, keepdims=True)
            total += lifted[0] * centre_stats_ref[pair, 1:2, lanes] + lifted[1] * stats_ref[pair, 1:2, lanes]
            inverse = 1.0 / total
            factors = [l * inverse for l in lifted]
            part = over_side(turned, head, 1, raw.astype(jnp.bfloat16)) * inverse
            part += factors[0] * centre_sums_ref[pair, :, lanes] + factors[1] * sums_ref[pair, :, lanes]
            parts.append(part)
            place = pl.ds(2 * pair + head, 1)
            features = pl.ds(pl.multiple_of((2 * pair + head) * HEAD_DIM, HEAD_DIM), HEAD_DIM)
            product = dout_turned_ref[features, :].astype(jnp.float32) * part
            rows_ref[0, place, :] = top
            rows_ref[1, place, :] = inverse
            rows_ref[2, place, :] = jnp.sum(product, axis=0, keepdims=True)
            factors_ref[0, place, :] = factors[0]
            factors_ref[1, place, :] = factors[1]
        attention_ref[:, cols] = jnp.concatenate(parts, axis=0).T.astype(jnp.bfloat16)
        return carry

    lax.fori_loop(0, raw_ref.shape[0], step, 0, unroll=True)


def backward_kernel(
    fourth_ref, third_ref, second_ref, first_ref, query_ref, key_ref, dout_ref, centre_raw_ref, column_raw_ref,
    row_raw_ref, centre_product_ref, column_product_ref, rows_ref, factors_ref, unused_ref,
    grad_query_ref, centre_ref,
):
    columns, rows = (third_ref, fourth_ref), (first_ref, second_ref)

    def step(pair, carry):
        cols = pair_cols(pair)
        query = query_ref[:, cols]
        dout = dout_ref[:, cols]
        turned_centre = key_ref[:, cols].T
        turned_columns = turned_sides(columns, 0, 0, cols)
        turned_rows = turned_sides(rows, 0, 1, cols)
        row_values = side_cells(rows, 1, 1, cols)
        parts = []
        centre_scores = []
        centre_weights = []
        for head in range(2):
            lanes = lanes_of(head)
            place = pl.ds(2 * pair + head, 1)
            delta = rows_ref[2, place, :]
            row_product = mm_nt(row_values, halves(one_head(dout, head), 1))

            def dscore(weights, product):
                return (weights * (product - delta)).astype(jnp.bfloat16)

            weights = centre_raw_ref[pair, :, lanes] * factors_ref[0, place, :]
            centre_weights.append(weights.astype(jnp.bfloat16))
            centre_scores.append(dscore(weights, centre_product_ref[pair, :, lanes]))
            column_weights = column_raw_ref[pair, :, lanes] * factors_ref[1, place, :]
            column_score = dscore(column_weights, column_product_ref[pair, :, lanes])
            row_score = dscore(row_raw_ref[pair, :, lanes] * rows_ref[1, place, :], row_product)
            part = mm(head_rows(turned_centre, head), centre_scores[-1])
            part += over_side(turned_columns, head, 0, column_score) + over_side(turned_rows, head, 1, row_score)
            parts.append(part)
        grad_query = jnp.concatenate(parts, axis=0).T * SCORE_SCALE
        grad_query_ref[:, cols] = grad_query.astype(jnp.bfloat16)
        grad_key, grad_value = joint_mm(
            jnp.concatenate(centre_scores, axis=1),
            jnp.concatenate(centre_weights, axis=1),
            both_heads(query),
            both_heads(dout),
        )
        centre_ref[0, :, cols] = grad_key * SCORE_SCALE
        centre_ref[1, :, cols] = grad_value
        return carry

    lax.fori_loop(0, centre_raw_ref.shape[0], step, 0)


def joint_mm(first, second, first_rows, second_rows):
    rows = first.shape[0]
    product = mm(jnp.concatenate([first, second], axis=0), jnp.concatenate([first_rows, second_rows], axis=1))
    return product[:rows, :PAIR], product[rows:, PAIR:]


def both_heads(block):
    return jnp.concatenate([one_head(block, head) for head in range(2)], axis=0)


def padded(block):
    return jnp.concatenate([block, jnp.zeros((LANES - block.shape[0], block.shape[1]), block.dtype)], axis=0)


def statistics(rows):
    first = 0
    for count in PARTS:
        heads = []
        for head in range(2):
            parts = [rows[2 * index + head : 2 * index + head + 1] for index in range(first, first + count)]
            heads.append(functools.reduce(jnp.add, parts))
        first += count
        yield jnp.concatenate(heads, axis=1)


def side_kernel(columns, rotations_ref, centre_ref, *refs):
    picked, rims = refs[:4], refs[4:8]
    keys_ref, values_ref, chosen_ref, bias_ref, keys_done, values_done, sems = refs[8:]
    cell = lax.broadcasted_iota(jnp.int32, (STRIP, LANES), 0)
    query = lax.broadcasted_iota(jnp.int32, (STRIP, LANES), 1)
    near = jnp.abs((cell & (SIDE - 1)) - (query & (SIDE - 1))) <= RADIUS
    near = near & ((cell >> 4) >= (query >> 4)) & (query < STRIP)
    bias_ref[...] = jnp.where(near, 0.0, -1e30)
    token = lax.broadcasted_iota(jnp.int32, (CELLS, LANES), 0)
    place = lax.broadcasted_iota(jnp.int32, (CELLS, LANES), 1)
    for index, slot in enumerate(SIDE_ORDER):
        side = slot_side(slot, columns)
        wanted = jnp.where(place < STRIP, strip_token(side, rotations_ref[0, side], place), -1)
        chosen = jnp.where(token == wanted, 1.0, 0.0).astype(jnp.bfloat16)
        chosen_ref[:, index * LANES : (index + 1) * LANES] = chosen

    copies = []
    for pair in range(keys_ref.shape[1] // PAIR):
        cols = slice(pair * PAIR, (pair + 1) * PAIR)
        grads = []
        bias = jnp.concatenate([bias_ref[...]] * 2, axis=1)
        for picked_ref, rim_ref in zip(picked, rims):
            query = both_heads(padded(rim_ref[:STRIP, cols]))
            dout = both_heads(padded(rim_ref[STRIP : 2 * STRIP, cols]))
            top, inverse, delta = statistics(rim_ref[2 * STRIP :, cols].astype(jnp.float32))
            scores = mm_nt(picked_ref[0, :, cols], query) + bias
            weights = jnp.exp2((scores - top) * LOG_SCALE) * inverse
            product = mm_nt(picked_ref[1, :, cols], dout)
            dscore = (weights * (product - delta)).astype(jnp.bfloat16)
            grad = jnp.concatenate([mm(dscore, query) * SCORE_SCALE, mm(weights.astype(jnp.bfloat16), dout)], axis=1)
            grads.append(padded(grad.astype(jnp.bfloat16)))
        total = mm(chosen_ref[...], jnp.concatenate(grads, axis=0))
        keys_done[:, cols] = (centre_ref[0, :, cols] + total[:, :PAIR]).astype(jnp.bfloat16)
        values_done[:, cols] = (centre_ref[1, :, cols] + total[:, PAIR:]).astype(jnp.bfloat16)
        for index, (done, out_ref) in enumerate(((keys_done, keys_ref), (values_done, values_ref))):
            copy = pltpu.make_async_copy(done.at[:, cols], out_ref.at[:, cols], sems.at[2 * pair + index])
            copy.start()
            copies.append(copy)
    for copy in copies:
        copy.wait()


def call(kernel, name, out_shape, operands, scratch=(), smem=0, unused=0, gflop=0.1, out_space=pltpu.VMEM):
    specs = [pl.BlockSpec(memory_space=pltpu.SMEM)] * smem
    specs += [pl.BlockSpec(memory_space=pltpu.VMEM)] * (len(operands) - smem - unused)
    specs += [pl.BlockSpec(memory_space=pl.ANY)] * unused
    single = not isinstance(out_shape, list)
    outs = pl.BlockSpec(memory_space=out_space)
    return pl.pallas_call(
        kernel,
        out_shape=out_shape,
        in_specs=specs,
        out_specs=outs if single else [outs] * len(out_shape),
        scratch_shapes=list(scratch),
        compiler_params=pltpu.CompilerParams(vmem_limit_bytes=VMEM_LIMIT),
        cost_estimate=pl.CostEstimate(flops=int(gflop * 1e9), bytes_accessed=1 << 20, transcendentals=0),
        name=name,
    )(*operands)


def in_hbm(array):
    return pltpu.with_memory_space_constraint(array, pltpu.HBM)


def across(block, distances):
    heads = lax.axis_size("head")
    devices = [(tile, head) for tile in range(lax.axis_size("tile")) for head in range(heads)]
    route = [(tile * heads + head, (tile ^ distances[head % 2]) * heads + head) for tile, head in devices]
    return lax.ppermute(block, ("tile", "head"), route)


def exchanged(blocks, stride):
    terms = list(blocks[:1])
    for distance in range(1, len(blocks)):
        route = [(tile, tile ^ (distance * stride)) for tile in range(lax.axis_size("tile"))]
        terms.append(lax.ppermute(blocks[distance], "tile", route))
    return terms


def with_partners(blocks, slots):
    tile_count = lax.axis_size("tile")
    routes = {s: [(tile, partner(tile, tile_count, s)) for tile in range(tile_count)] for s in slots}
    return {s: lax.ppermute(blocks[s], "tile", routes[s]) for s in slots}


def shards(queries, keys, values, grad_output, out_weight, rotations):
    tile_count = lax.axis_size("tile")
    token_count, features = queries.shape
    model = out_weight.shape[0]
    pairs = features // PAIR
    far = tile_count // NEAR
    chunk = model // tile_count
    heads = lax.axis_size("head")
    columns = tile_count // 4
    queries, keys, values, out_weight, rotations = (
        in_hbm(a) for a in (queries, keys, values, out_weight, rotations)
    )

    def bf16(*shape):
        return jax.ShapeDtypeStruct(shape, jnp.bfloat16)

    def f32(*shape):
        return jax.ShapeDtypeStruct(shape, jnp.float32)

    strip_types = [bf16(2, STRIP, features)] * 4
    picked = call(
        functools.partial(pick_kernel, columns), "pick_strips", strip_types, (rotations, keys, values), smem=1
    )
    grad_output, *picked = lax.optimization_barrier((grad_output, *picked))
    strips = with_partners(picked, (3, 2, 1, 0))
    strips = [strips[s] for s in range(4)]

    cotangents = [
        lax.ppermute(grad_output, "head", [((h + k) % heads, h) for h in range(heads)]) for k in range(1, heads)
    ]
    dout, dout_turned, turned, turned_sent = call(
        functools.partial(cotangent_kernel, heads),
        "cotangent",
        [bf16(CELLS, features), bf16(features, CELLS)] + [bf16(2, far, chunk, CELLS)] * 2,
        (in_hbm(grad_output), *cotangents, out_weight),
        gflop=1.0,
    )
    turned_arrived = across(turned_sent, (2, 1))
    part_types = [f32(pairs, 2, 2 * CELLS), f32(pairs, HEAD_DIM, 2 * CELLS)]
    raw_centre, stats_centre, sums_centre, product_centre, queries, keys = call(
        centre_kernel,
        "centre",
        [f32(pairs, CELLS, 2 * CELLS)] + part_types + [f32(pairs, CELLS, 2 * CELLS)] + [bf16(CELLS, features)] * 2,
        (queries, keys, values, dout),
        scratch=[pltpu.VMEM((CELLS, CELLS), jnp.float32)],
        gflop=3.0,
    )
    strip_scratch = [pltpu.VMEM((STRIP, CELLS), jnp.float32)]
    raw_columns, stats_columns, sums_columns, product_columns = call(
        column_kernel,
        "columns",
        [f32(pairs, STRIP, 2 * CELLS)] + part_types + [f32(pairs, STRIP, 2 * CELLS)],
        (strips[2], strips[3], queries, dout),
        scratch=strip_scratch,
        gflop=2.0,
    )
    raw_rows, attention, rows, factors = call(
        row_kernel,
        "rows",
        [f32(pairs, STRIP, 2 * CELLS), bf16(CELLS, features)] + [f32(k, 2 * pairs, CELLS) for k in (3, 2)],
        (strips[0], strips[1], queries, dout_turned, stats_centre, sums_centre, stats_columns, sums_columns),
        scratch=strip_scratch,
    )
    attention_arrived = across(attention, (2, 1))
    rims = call(
        functools.partial(rim_kernel, columns),
        "rims",
        [bf16(2 * STRIP + 16, features)] * 4,
        (queries, dout, rows, turned_arrived),
        unused=1,
    )
    rims_arrived = with_partners(rims, (3, 2))
    kept, sent = call(
        partial_kernel,
        "partial",
        [f32(far, chunk, features), bf16(far, chunk, features)],
        (attention, attention_arrived, turned, turned_arrived, rims[0]),
        unused=1,
    )
    terms = [kept, across(sent, (1, 2))]
    rims = lax.optimization_barrier((*rims, sent))[:4]
    rims_arrived |= with_partners(rims, (1, 0))
    grad_queries, centre = call(
        backward_kernel,
        "backward",
        [bf16(CELLS, features), f32(2, CELLS, features)],
        (
            *strips[::-1], queries, keys, dout, raw_centre, raw_columns, raw_rows, product_centre, product_columns,
            rows, factors, sent,
        ),
        unused=1,
        gflop=3.0,
    )
    stride = NEAR
    while stride < tile_count:
        ways = min(NEAR, tile_count // stride)
        sums = call(
            functools.partial(sum_kernel, len(terms)),
            "plane_sum",
            [bf16(tile_count // stride // ways, chunk, features)] * ways,
            (*terms, centre, rims_arrived[3], rims_arrived[2]),
            unused=3,
        )
        terms = exchanged(sums, stride)
        stride *= ways

    grad_keys, grad_values = call(
        functools.partial(side_kernel, columns),
        "sides",
        [bf16(CELLS, features)] * 2,
        (rotations, centre, *(picked[s] for s in SIDE_ORDER), *(rims_arrived[s] for s in SIDE_ORDER)),
        scratch=[pltpu.VMEM((CELLS, 4 * LANES), jnp.bfloat16), pltpu.VMEM((STRIP, LANES), jnp.float32)]
        + [pltpu.VMEM((CELLS, features), jnp.bfloat16)] * 2
        + [pltpu.SemaphoreType.DMA((2 * pairs,))],
        smem=1,
        gflop=3.0,
        out_space=pl.ANY,
    )
    grad_out_weight = call(
        functools.partial(weight_kernel, 1.0 / math.sqrt(token_count * tile_count)),
        "weight_sum",
        f32(chunk, features),
        terms,
    )
    return (grad_queries, grad_keys, grad_values, grad_out_weight)


def solution(mesh):
    placed = (
        P("tile", "head"),
        P("tile", "head"),
        P("tile", "head"),
        P("tile", "head"),
        P(None, "head"),
        P("tile", None),
    )
    return jax.shard_map(
        shards,
        mesh=mesh,
        in_specs=placed,
        out_specs=(P("tile", "head"), P("tile", "head"), P("tile", "head"), P("tile", "head")),
        check_vma=False,
    )
```

```python
import functools
import math

import jax
import jax.numpy as jnp
from jax import lax
from jax.experimental import pallas as pl
from jax.experimental.pallas import tpu as pltpu
from jax.sharding import PartitionSpec as P

HEAD_DIM = 64
RADIUS = 6
SIDE = 16
CELLS = SIDE * SIDE
STRIP = RADIUS * SIDE
NEAR = 4
LANES = 128
PAIR = 2 * HEAD_DIM
VMEM_LIMIT = 32 * 1024 * 1024
NT = (((1,), (1,)), ((), ()))


def mm(a, b):
    return jnp.dot(a, b, preferred_element_type=jnp.float32)


def mm_nt(a, b):
    return lax.dot_general(a, b, NT, preferred_element_type=jnp.float32)


def strip_token(side_index, rotation, cell):
    turn = lax.rem(side_index + 6 - rotation, 4)
    depth = cell >> 4
    along = cell & (SIDE - 1)
    far = SIDE - 1 - along
    near_rim = RADIUS - 1 - depth
    far_rim = SIDE - RADIUS + depth
    row = jnp.where(turn == 0, far_rim, jnp.where(turn == 1, along, jnp.where(turn == 2, near_rim, far)))
    col = jnp.where(turn == 0, along, jnp.where(turn == 1, near_rim, jnp.where(turn == 2, far, far_rim)))
    return row * SIDE + col


def slot_side(slot, columns):
    tile = lax.axis_index("tile")
    if slot < 2:
        return jnp.where((tile + slot) & 1 == 0, 1, 3)
    return jnp.where((lax.div(tile, columns) + slot) & 1 == 0, 2, 0)


def partner(tile, tile_count, slot):
    columns = tile_count // 4
    if slot < 2:
        return (tile + (1 if (tile + slot) % 2 == 0 else -1)) % tile_count
    return (tile + (columns if (tile // columns + slot) % 2 == 0 else -columns)) % tile_count


def pick_kernel(columns, rotations_ref, keys_ref, values_ref, *refs):
    out_refs, (pair_ref, chosen_ref, sems) = refs[:4], refs[4:]
    copies = [
        pltpu.make_async_copy(ref, pair_ref.at[part], sems.at[part]) for part, ref in enumerate((keys_ref, values_ref))
    ]
    for copy in copies:
        copy.start()
    cell = lax.broadcasted_iota(jnp.int32, (STRIP, CELLS), 0)
    token = lax.broadcasted_iota(jnp.int32, (STRIP, CELLS), 1)
    for slot in range(4):
        side = slot_side(slot, columns)
        wanted = strip_token(side, rotations_ref[0, side], cell)
        chosen_ref[slot * STRIP : (slot + 1) * STRIP] = jnp.where(token == wanted, 1.0, 0.0).astype(jnp.bfloat16)
    for part, copy in enumerate(copies):
        copy.wait()
        picked = mm(chosen_ref[...], pair_ref[part]).astype(jnp.bfloat16)
        for slot, out_ref in enumerate(out_refs):
            out_ref[part] = picked[slot * STRIP : (slot + 1) * STRIP]


def weight_kernel(scale, *refs):
    total = refs[0][0].astype(jnp.float32)
    for ref in refs[1:-1]:
        total += ref[0].astype(jnp.float32)
    refs[-1][...] = total * scale


def partial_kernel(attention_ref, arrived_ref, turned_ref, turned_arrived_ref, unused_ref, kept_ref, sent_ref):
    for index, out_ref in enumerate((kept_ref, sent_ref)):
        total = None
        for turned_part, attention_part in ((turned_ref, attention_ref), (turned_arrived_ref, arrived_ref)):
            turned = turned_part[index]
            turned = turned.reshape(turned.shape[0] * turned.shape[1], turned.shape[2])
            term = mm(turned, attention_part[...])
            total = term if total is None else total + term
        out_ref[...] = total.astype(out_ref.dtype).reshape(out_ref.shape)


def sum_kernel(count, *refs):
    terms, outs = refs[:count], refs[count + 3 :]
    for q in range(terms[0].shape[0]):
        total = terms[0][q].astype(jnp.float32)
        for ref in terms[1:]:
            total += ref[q].astype(jnp.float32)
        outs[q % len(outs)][q // len(outs)] = total.astype(jnp.bfloat16)


def rim_token(side_index, place):
    depth = place >> 4
    along = place & (SIDE - 1)
    last = SIDE - 1
    north, east, south = side_index == 0, side_index == 1, side_index == 2
    row = jnp.where(north, depth, jnp.where(east, along, jnp.where(south, last - depth, last - along)))
    col = jnp.where(north, along, jnp.where(east, last - depth, jnp.where(south, last - along, depth)))
    return row * SIDE + col


def cotangent_kernel(heads, *refs):
    blocks, out_weight_ref, outs = refs[:heads], refs[heads], refs[heads + 1 :]
    dout_ref, dout_turned_ref, turned_ref, turned_sent_ref = outs
    head = lax.axis_index("head")
    axis = head & 1
    tile = lax.axis_index("tile")
    chunk = turned_ref.shape[2]
    width = blocks[0].shape[1]
    total = None
    for distance, block_ref in enumerate(blocks):
        owner = lax.rem(head + distance, heads)
        start = pl.multiple_of(owner * width, width)
        block = block_ref[...]
        term = mm(block, out_weight_ref[pl.ds(start, width), :])
        total = term if total is None else total + term
        turned = block.T
        first = owner * (width // chunk)
        for index in range(width // chunk):
            target = (first + index) ^ tile
            rows = turned[index * chunk : (index + 1) * chunk]
            for parity, out_ref in enumerate((turned_ref, turned_sent_ref)):

                @pl.when((target >> axis) & 1 == parity)
                def _():
                    out_ref[(target >> (1 - axis)) & 1, target >> 2] = rows

    dout = total.astype(jnp.bfloat16)
    dout_ref[...] = dout
    dout_turned_ref[...] = dout.T


def split(exact, count):
    parts = []
    for _ in range(count):
        part = exact.astype(jnp.bfloat16).astype(jnp.float32)
        parts.append(part)
        exact = exact - part
    return parts


PARTS = (3, 2, 2)
SIDE_ORDER = (3, 2, 1, 0)


def rim_kernel(query_ref, dout_ref, rows_ref, chosen_ref, unused_ref, *rim_refs):
    parts = [part for kind, count in enumerate(PARTS) for part in split(rows_ref[kind], count)]
    pairs = rows_ref.shape[1] // 2
    filler = jnp.zeros((16 - 2 * len(parts), CELLS), jnp.float32)
    rows = [
        jnp.concatenate([part[2 * pair : 2 * pair + 2] for part in parts] + [filler], axis=0) for pair in range(pairs)
    ]
    rows = jnp.concatenate(rows, axis=0).astype(jnp.bfloat16)
    for slot, rim_ref in enumerate(rim_refs):
        chosen = chosen_ref[slot]
        rim_ref[:STRIP] = mm(chosen[:STRIP], query_ref[...]).astype(jnp.bfloat16)
        rim_ref[STRIP : 2 * STRIP] = mm(chosen[:STRIP], dout_ref[...]).astype(jnp.bfloat16)
        spread = mm_nt(rows, chosen).astype(jnp.bfloat16)
        for pair in range(pairs):
            rim_ref[2 * STRIP :, pair * PAIR : (pair + 1) * PAIR] = spread[16 * pair : 16 * pair + 16]


def window(cell_row, cell_col, query):
    query_row = (query >> 4) + RADIUS
    query_col = (query & (SIDE - 1)) + RADIUS
    near = (jnp.abs(cell_row - query_row) <= RADIUS) & (jnp.abs(cell_col - query_col) <= RADIUS)
    return jnp.where(near, 0.0, -1e30)


def centre_bias(bias_ref):
    query = lax.broadcasted_iota(jnp.int32, (CELLS, CELLS), 1)
    cell = lax.broadcasted_iota(jnp.int32, (CELLS, CELLS), 0)
    bias_ref[...] = window((cell >> 4) + RADIUS, (cell & (SIDE - 1)) + RADIUS, query)


def strip_bias(kind, bias_ref):
    query = lax.broadcasted_iota(jnp.int32, (STRIP, CELLS), 1)
    cell = lax.broadcasted_iota(jnp.int32, (STRIP, CELLS), 0)
    depth = cell >> 4
    along = cell & (SIDE - 1)
    last = SIDE + 2 * RADIUS - 1
    if kind:
        first, second = (last - RADIUS - along, depth), (RADIUS + along, last - depth)
    else:
        first, second = (depth, RADIUS + along), (last - depth, last - RADIUS - along)
    in_first = first_half(query, kind)
    row = jnp.where(in_first, first[0], second[0])
    col = jnp.where(in_first, first[1], second[1])
    bias_ref[...] = window(row, col, query)


def first_half(query, kind):
    return (query & (SIDE - 1)) < SIDE // 2 if kind else query < CELLS // 2


def one_head(block, head):
    lane = lax.broadcasted_iota(jnp.int32, block.shape, 1)
    kept = (lane >= HEAD_DIM) if head else (lane < HEAD_DIM)
    return jnp.where(kept, block, jnp.zeros_like(block))


def halves(block, kind):
    kept = first_half(lax.broadcasted_iota(jnp.int32, block.shape, 0), kind)
    zero = jnp.zeros_like(block)
    return jnp.concatenate([jnp.where(kept, block, zero), jnp.where(kept, zero, block)], axis=1)


def by_half(stacked, kind):
    rows = stacked.shape[0] // 2
    kept = first_half(lax.broadcasted_iota(jnp.int32, (rows, CELLS), 1), kind)
    return jnp.where(kept, stacked[:rows], stacked[rows:])


def side_blocks(strips, part, kind, cols):
    tile = lax.axis_index("tile")
    second, first = strips
    straight = (tile if kind else lax.div(tile, lax.axis_size("tile") // 4)) & 1 == 0
    first, second = first[part, :, cols], second[part, :, cols]
    return jnp.where(straight, first, second), jnp.where(straight, second, first)


def side_cells(strips, part, kind, cols):
    return jnp.concatenate(side_blocks(strips, part, kind, cols), axis=1)


def halves(block, kind):
    kept = first_half(lax.broadcasted_iota(jnp.int32, block.shape, 0), kind)
    zero = jnp.zeros_like(block)
    return jnp.concatenate([jnp.where(kept, block, zero), jnp.where(kept, zero, block)], axis=1)


def by_half(stacked, kind):
    rows = stacked.shape[0] // 2
    kept = first_half(lax.broadcasted_iota(jnp.int32, (rows, CELLS), 1), kind)
    return jnp.where(kept, stacked[:rows], stacked[rows:])


def side_blocks(strips, part, kind, cols):
    tile = lax.axis_index("tile")
    second, first = strips
    straight = (tile if kind else lax.div(tile, lax.axis_size("tile") // 4)) & 1 == 0
    first, second = first[part, :, cols], second[part, :, cols]
    return jnp.where(straight, first, second), jnp.where(straight, second, first)


def side_cells(strips, part, kind, cols):
    return jnp.concatenate(side_blocks(strips, part, kind, cols), axis=1)


def side_products(cells, rows_head):
    return [mm_nt(cells[kind], halves(rows_head, kind)) for kind in range(2)]


def turned_sides(strips, part, kind, cols):
    return [block.T for block in side_blocks(strips, part, kind, cols)]


def pair_cols(pair):
    return pl.ds(pl.multiple_of(pair * PAIR, PAIR), PAIR)


def head_rows(turned, head):
    return turned[head * HEAD_DIM : (head + 1) * HEAD_DIM]


def over_side(turned, head, kind, sides):
    return by_half(mm(jnp.concatenate([head_rows(t, head) for t in turned], axis=0), sides), kind)


SCORE_SCALE = HEAD_DIM ** (-0.5)
LOG_SCALE = SCORE_SCALE * math.log2(math.e)


def lanes_of(head):
    return slice(head * CELLS, (head + 1) * CELLS)


def centre_kernel(
    query_ref, key_ref, value_ref, dout_ref,
    raw_ref, stats_ref, sums_ref, product_ref, query_out, key_out, bias_ref,
):
    centre_bias(bias_ref)

    def step(pair, carry):
        cols = pair_cols(pair)
        query, key, value, dout = (ref[:, cols] for ref in (query_ref, key_ref, value_ref, dout_ref))
        turned = value.T
        for head in range(2):
            lanes = lanes_of(head)
            scores = mm_nt(key, one_head(query, head)) + bias_ref[...]
            top = jnp.max(scores, axis=0, keepdims=True)
            raw = jnp.exp2((scores - top) * LOG_SCALE)
            raw_ref[pair, :, lanes] = raw
            stats_ref[pair, 0:1, lanes] = top
            stats_ref[pair, 1:2, lanes] = jnp.sum(raw, axis=0, keepdims=True)
            sums_ref[pair, :, lanes] = mm(head_rows(turned, head), raw.astype(jnp.bfloat16))
            product_ref[pair, :, lanes] = mm_nt(value, one_head(dout, head))
        query_out[:, cols] = query
        key_out[:, cols] = key
        return carry

    lax.fori_loop(0, raw_ref.shape[0], step, 0)


def column_kernel(
    columns, rotations_ref, first_ref, second_ref, query_ref, dout_ref,
    raw_ref, stats_ref, sums_ref, product_ref, row_bias_ref, rim_chosen_ref, chosen_ref, bias_ref,
):
    strips = (first_ref, second_ref)
    strip_bias(0, bias_ref)
    strip_bias(1, row_bias_ref)
    place = lax.broadcasted_iota(jnp.int32, (LANES, CELLS), 0)
    token = lax.broadcasted_iota(jnp.int32, (LANES, CELLS), 1)
    for slot in range(4):
        wanted = rim_token(slot_side(slot, columns), place)
        chosen = jnp.where((token == wanted) & (place < STRIP), 1.0, 0.0).astype(jnp.bfloat16)
        rim_chosen_ref[slot] = chosen
    place = lax.broadcasted_iota(jnp.int32, (CELLS, LANES), 1)
    token = lax.broadcasted_iota(jnp.int32, (CELLS, LANES), 0)
    for index, slot in enumerate(SIDE_ORDER):
        side = slot_side(slot, columns)
        wanted = jnp.where(place < STRIP, strip_token(side, rotations_ref[0, side], place), -1)
        chosen = jnp.where(token == wanted, 1.0, 0.0).astype(jnp.bfloat16)
        chosen_ref[:, index * LANES : (index + 1) * LANES] = chosen

    def step(pair, carry):
        cols = pair_cols(pair)
        keys = side_cells(strips, 0, 0, cols)
        values = side_cells(strips, 1, 0, cols)
        turned = turned_sides(strips, 1, 0, cols)
        for head in range(2):
            lanes = lanes_of(head)
            scores = mm_nt(keys, halves(one_head(query_ref[:, cols], head), 0)) + bias_ref[...]
            top = jnp.max(scores, axis=0, keepdims=True)
            raw = jnp.exp2((scores - top) * LOG_SCALE)
            raw_ref[pair, :, lanes] = raw
            stats_ref[pair, 0:1, lanes] = top
            stats_ref[pair, 1:2, lanes] = jnp.sum(raw, axis=0, keepdims=True)
            sums_ref[pair, :, lanes] = over_side(turned, head, 0, raw.astype(jnp.bfloat16))
            product_ref[pair, :, lanes] = mm_nt(values, halves(one_head(dout_ref[:, cols], head), 0))
        return carry

    lax.fori_loop(0, raw_ref.shape[0], step, 0)


def row_kernel(
    first_ref, second_ref, query_ref, dout_turned_ref, centre_stats_ref, centre_sums_ref, stats_ref, sums_ref, bias_ref,
    raw_ref, attention_ref, rows_ref, factors_ref,
):
    strips = (first_ref, second_ref)

    def step(pair, carry):
        cols = pair_cols(pair)
        keys = side_cells(strips, 0, 1, cols)
        turned = turned_sides(strips, 1, 1, cols)
        parts = []
        for head in range(2):
            lanes = lanes_of(head)
            scores = mm_nt(keys, halves(one_head(query_ref[:, cols], head), 1)) + bias_ref[...]
            tops = [ref[pair, 0:1, lanes] for ref in (centre_stats_ref, stats_ref)]
            top = jnp.maximum(jnp.max(scores, axis=0, keepdims=True), jnp.maximum(*tops))
            raw = jnp.exp2((scores - top) * LOG_SCALE)
            raw_ref[pair, :, lanes] = raw
            lifted = [jnp.exp2((t - top) * LOG_SCALE) for t in tops]
            total = jnp.sum(raw, axis=0, keepdims=True)
            total += lifted[0] * centre_stats_ref[pair, 1:2, lanes] + lifted[1] * stats_ref[pair, 1:2, lanes]
            inverse = 1.0 / total
            factors = [l * inverse for l in lifted]
            part = over_side(turned, head, 1, raw.astype(jnp.bfloat16)) * inverse
            part += factors[0] * centre_sums_ref[pair, :, lanes] + factors[1] * sums_ref[pair, :, lanes]
            parts.append(part)
            place = pl.ds(2 * pair + head, 1)
            features = pl.ds(pl.multiple_of((2 * pair + head) * HEAD_DIM, HEAD_DIM), HEAD_DIM)
            product = dout_turned_ref[features, :].astype(jnp.float32) * part
            rows_ref[0, place, :] = top
            rows_ref[1, place, :] = inverse
            rows_ref[2, place, :] = jnp.sum(product, axis=0, keepdims=True)
            factors_ref[0, place, :] = factors[0]
            factors_ref[1, place, :] = factors[1]
        attention_ref[:, cols] = jnp.concatenate(parts, axis=0).T.astype(jnp.bfloat16)
        return carry

    lax.fori_loop(0, raw_ref.shape[0], step, 0, unroll=True)


def backward_kernel(
    fourth_ref, third_ref, second_ref, first_ref, query_ref, key_ref, dout_ref, centre_raw_ref, column_raw_ref,
    row_raw_ref, centre_product_ref, column_product_ref, rows_ref, factors_ref, unused_ref,
    grad_query_ref, centre_ref,
):
    columns, rows = (third_ref, fourth_ref), (first_ref, second_ref)

    def step(pair, carry):
        cols = pair_cols(pair)
        query = query_ref[:, cols]
        dout = dout_ref[:, cols]
        turned_centre = key_ref[:, cols].T
        turned_columns = turned_sides(columns, 0, 0, cols)
        turned_rows = turned_sides(rows, 0, 1, cols)
        row_values = side_cells(rows, 1, 1, cols)
        parts = []
        centre_scores = []
        centre_weights = []
        for head in range(2):
            lanes = lanes_of(head)
            place = pl.ds(2 * pair + head, 1)
            delta = rows_ref[2, place, :]
            row_product = mm_nt(row_values, halves(one_head(dout, head), 1))

            def dscore(weights, product):
                return (weights * (product - delta)).astype(jnp.bfloat16)

            weights = centre_raw_ref[pair, :, lanes] * factors_ref[0, place, :]
            centre_weights.append(weights.astype(jnp.bfloat16))
            centre_scores.append(dscore(weights, centre_product_ref[pair, :, lanes]))
            column_weights = column_raw_ref[pair, :, lanes] * factors_ref[1, place, :]
            column_score = dscore(column_weights, column_product_ref[pair, :, lanes])
            row_score = dscore(row_raw_ref[pair, :, lanes] * rows_ref[1, place, :], row_product)
            part = mm(head_rows(turned_centre, head), centre_scores[-1])
            part += over_side(turned_columns, head, 0, column_score) + over_side(turned_rows, head, 1, row_score)
            parts.append(part)
        grad_query = jnp.concatenate(parts, axis=0).T * SCORE_SCALE
        grad_query_ref[:, cols] = grad_query.astype(jnp.bfloat16)
        grad_key, grad_value = joint_mm(
            jnp.concatenate(centre_scores, axis=1),
            jnp.concatenate(centre_weights, axis=1),
            both_heads(query),
            both_heads(dout),
        )
        centre_ref[0, :, cols] = grad_key * SCORE_SCALE
        centre_ref[1, :, cols] = grad_value
        return carry

    lax.fori_loop(0, centre_raw_ref.shape[0], step, 0)


def joint_mm(first, second, first_rows, second_rows):
    rows = first.shape[0]
    product = mm(jnp.concatenate([first, second], axis=0), jnp.concatenate([first_rows, second_rows], axis=1))
    return product[:rows, :PAIR], product[rows:, PAIR:]


def both_heads(block):
    return jnp.concatenate([one_head(block, head) for head in range(2)], axis=0)


def padded(block):
    return jnp.concatenate([block, jnp.zeros((LANES - block.shape[0], block.shape[1]), block.dtype)], axis=0)


def statistics(rows):
    first = 0
    for count in PARTS:
        heads = []
        for head in range(2):
            parts = [rows[2 * index + head : 2 * index + head + 1] for index in range(first, first + count)]
            heads.append(functools.reduce(jnp.add, parts))
        first += count
        yield jnp.concatenate(heads, axis=1)


def side_kernel(centre_ref, chosen_ref, *refs):
    picked, rims = refs[:4], refs[4:8]
    keys_ref, values_ref, bias_ref, keys_done, values_done, sems = refs[8:]
    cell = lax.broadcasted_iota(jnp.int32, (STRIP, LANES), 0)
    query = lax.broadcasted_iota(jnp.int32, (STRIP, LANES), 1)
    near = jnp.abs((cell & (SIDE - 1)) - (query & (SIDE - 1))) <= RADIUS
    near = near & ((cell >> 4) >= (query >> 4)) & (query < STRIP)
    bias_ref[...] = jnp.where(near, 0.0, -1e30)
    copies = []
    for pair in range(keys_ref.shape[1] // PAIR):
        cols = slice(pair * PAIR, (pair + 1) * PAIR)
        grads = []
        bias = jnp.concatenate([bias_ref[...]] * 2, axis=1)
        for picked_ref, rim_ref in zip(picked, rims):
            query = both_heads(padded(rim_ref[:STRIP, cols]))
            dout = both_heads(padded(rim_ref[STRIP : 2 * STRIP, cols]))
            top, inverse, delta = statistics(rim_ref[2 * STRIP :, cols].astype(jnp.float32))
            scores = mm_nt(picked_ref[0, :, cols], query) + bias
            weights = jnp.exp2((scores - top) * LOG_SCALE) * inverse
            product = mm_nt(picked_ref[1, :, cols], dout)
            dscore = (weights * (product - delta)).astype(jnp.bfloat16)
            grad = jnp.concatenate([mm(dscore, query) * SCORE_SCALE, mm(weights.astype(jnp.bfloat16), dout)], axis=1)
            grads.append(padded(grad.astype(jnp.bfloat16)))
        total = mm(chosen_ref[...], jnp.concatenate(grads, axis=0))
        keys_done[:, cols] = (centre_ref[0, :, cols] + total[:, :PAIR]).astype(jnp.bfloat16)
        values_done[:, cols] = (centre_ref[1, :, cols] + total[:, PAIR:]).astype(jnp.bfloat16)
        for index, (done, out_ref) in enumerate(((keys_done, keys_ref), (values_done, values_ref))):
            copy = pltpu.make_async_copy(done.at[:, cols], out_ref.at[:, cols], sems.at[2 * pair + index])
            copy.start()
            copies.append(copy)
    for copy in copies:
        copy.wait()


def call(kernel, name, out_shape, operands, scratch=(), smem=0, unused=0, gflop=0.1, out_space=pltpu.VMEM):
    specs = [pl.BlockSpec(memory_space=pltpu.SMEM)] * smem
    specs += [pl.BlockSpec(memory_space=pltpu.VMEM)] * (len(operands) - smem - unused)
    specs += [pl.BlockSpec(memory_space=pl.ANY)] * unused
    single = not isinstance(out_shape, list)
    outs = pl.BlockSpec(memory_space=out_space)
    return pl.pallas_call(
        kernel,
        out_shape=out_shape,
        in_specs=specs,
        out_specs=outs if single else [outs] * len(out_shape),
        scratch_shapes=list(scratch),
        compiler_params=pltpu.CompilerParams(vmem_limit_bytes=VMEM_LIMIT),
        cost_estimate=pl.CostEstimate(flops=int(gflop * 1e9), bytes_accessed=1 << 20, transcendentals=0),
        name=name,
    )(*operands)


def in_hbm(array):
    return pltpu.with_memory_space_constraint(array, pltpu.HBM)


def across(block, distances):
    heads = lax.axis_size("head")
    devices = [(tile, head) for tile in range(lax.axis_size("tile")) for head in range(heads)]
    route = [(tile * heads + head, (tile ^ distances[head % 2]) * heads + head) for tile, head in devices]
    return lax.ppermute(block, ("tile", "head"), route)


def exchanged(blocks, stride):
    terms = list(blocks[:1])
    for distance in range(1, len(blocks)):
        route = [(tile, tile ^ (distance * stride)) for tile in range(lax.axis_size("tile"))]
        terms.append(lax.ppermute(blocks[distance], "tile", route))
    return terms


def with_partners(blocks, slots):
    tile_count = lax.axis_size("tile")
    routes = {s: [(tile, partner(tile, tile_count, s)) for tile in range(tile_count)] for s in slots}
    return {s: lax.ppermute(blocks[s], "tile", routes[s]) for s in slots}


def shards(queries, keys, values, grad_output, out_weight, rotations):
    tile_count = lax.axis_size("tile")
    token_count, features = queries.shape
    model = out_weight.shape[0]
    pairs = features // PAIR
    far = tile_count // NEAR
    chunk = model // tile_count
    heads = lax.axis_size("head")
    columns = tile_count // 4
    queries, keys, values, out_weight, rotations = (
        in_hbm(a) for a in (queries, keys, values, out_weight, rotations)
    )

    def bf16(*shape):
        return jax.ShapeDtypeStruct(shape, jnp.bfloat16)

    def f32(*shape):
        return jax.ShapeDtypeStruct(shape, jnp.float32)

    strip_types = [bf16(2, STRIP, features)] * 4
    picked = call(
        functools.partial(pick_kernel, columns),
        "pick_strips",
        strip_types,
        (rotations, keys, values),
        scratch=[
            pltpu.VMEM((2, CELLS, features), jnp.bfloat16),
            pltpu.VMEM((4 * STRIP, CELLS), jnp.bfloat16),
            pltpu.SemaphoreType.DMA((2,)),
        ],
        smem=1,
        unused=2,
    )
    grad_output, *picked = lax.optimization_barrier((grad_output, *picked))
    strips = with_partners(picked, (3, 2, 1, 0))
    strips = [strips[s] for s in range(4)]

    cotangents = [
        lax.ppermute(grad_output, "head", [((h + k) % heads, h) for h in range(heads)]) for k in range(1, heads)
    ]
    dout, dout_turned, turned, turned_sent = call(
        functools.partial(cotangent_kernel, heads),
        "cotangent",
        [bf16(CELLS, features), bf16(features, CELLS)] + [bf16(2, far, chunk, CELLS)] * 2,
        (in_hbm(grad_output), *cotangents, out_weight),
        gflop=1.0,
    )
    turned_arrived = across(turned_sent, (1, 2))
    part_types = [f32(pairs, 2, 2 * CELLS), f32(pairs, HEAD_DIM, 2 * CELLS)]
    raw_centre, stats_centre, sums_centre, product_centre, queries, keys = call(
        centre_kernel,
        "centre",
        [f32(pairs, CELLS, 2 * CELLS)] + part_types + [f32(pairs, CELLS, 2 * CELLS)] + [bf16(CELLS, features)] * 2,
        (queries, keys, values, dout),
        scratch=[pltpu.VMEM((CELLS, CELLS), jnp.float32)],
        gflop=3.0,
    )
    strip_scratch = [pltpu.VMEM((STRIP, CELLS), jnp.float32)]
    raw_columns, stats_columns, sums_columns, product_columns, row_bias, rim_chosen, chosen = call(
        functools.partial(column_kernel, columns),
        "columns",
        [f32(pairs, STRIP, 2 * CELLS)]
        + part_types
        + [f32(pairs, STRIP, 2 * CELLS), f32(STRIP, CELLS), bf16(4, LANES, CELLS), bf16(CELLS, 4 * LANES)],
        (rotations, strips[2], strips[3], queries, dout),
        scratch=strip_scratch,
        smem=1,
        gflop=2.0,
    )
    raw_rows, attention, rows, factors = call(
        row_kernel,
        "rows",
        [f32(pairs, STRIP, 2 * CELLS), bf16(CELLS, features)] + [f32(k, 2 * pairs, CELLS) for k in (3, 2)],
        (strips[0], strips[1], queries, dout_turned, stats_centre, sums_centre, stats_columns, sums_columns, row_bias),
    )
    attention_arrived = across(attention, (1, 2))
    rims = call(
        rim_kernel,
        "rims",
        [bf16(2 * STRIP + 16, features)] * 4,
        (queries, dout, rows, rim_chosen, turned_arrived),
        unused=1,
    )
    rims_arrived = with_partners(rims, (3, 2))
    kept, sent = call(
        partial_kernel,
        "partial",
        [f32(far, chunk, features), bf16(far, chunk, features)],
        (attention, attention_arrived, turned, turned_arrived, rims[0]),
        unused=1,
    )
    terms = [kept, across(sent, (2, 1))]
    rims = lax.optimization_barrier((*rims, sent))[:4]
    rims_arrived |= with_partners(rims, (1, 0))
    grad_queries, centre = call(
        backward_kernel,
        "backward",
        [bf16(CELLS, features), f32(2, CELLS, features)],
        (
            *strips[::-1], queries, keys, dout, raw_centre, raw_columns, raw_rows, product_centre, product_columns,
            rows, factors, sent,
        ),
        unused=1,
        gflop=3.0,
    )
    stride = NEAR
    while stride < tile_count:
        ways = min(NEAR, tile_count // stride)
        sums = call(
            functools.partial(sum_kernel, len(terms)),
            "plane_sum",
            [bf16(tile_count // stride // ways, chunk, features)] * ways,
            (*terms, centre, rims_arrived[3], rims_arrived[2]),
            unused=3,
        )
        terms = exchanged(sums, stride)
        stride *= ways

    grad_keys, grad_values = call(
        side_kernel,
        "sides",
        [bf16(CELLS, features)] * 2,
        (centre, chosen, *(picked[s] for s in SIDE_ORDER), *(rims_arrived[s] for s in SIDE_ORDER)),
        scratch=[pltpu.VMEM((STRIP, LANES), jnp.float32)]
        + [pltpu.VMEM((CELLS, features), jnp.bfloat16)] * 2
        + [pltpu.SemaphoreType.DMA((2 * pairs,))],
        gflop=3.0,
        out_space=pl.ANY,
    )
    grad_out_weight = call(
        functools.partial(weight_kernel, 1.0 / math.sqrt(token_count * tile_count)),
        "weight_sum",
        f32(chunk, features),
        terms,
    )
    return (grad_queries, grad_keys, grad_values, grad_out_weight)


def solution(mesh):
    placed = (
        P("tile", "head"),
        P("tile", "head"),
        P("tile", "head"),
        P("tile", "head"),
        P(None, "head"),
        P("tile", None),
    )
    return jax.shard_map(
        shards,
        mesh=mesh,
        in_specs=placed,
        out_specs=(P("tile", "head"), P("tile", "head"), P("tile", "head"), P("tile", "head")),
        check_vma=False,
    )
```

```python
import functools
import math

import jax
import jax.numpy as jnp
from jax import lax
from jax.experimental import pallas as pl
from jax.experimental.pallas import tpu as pltpu
from jax.sharding import PartitionSpec as P

HEAD_DIM = 64
RADIUS = 6
SIDE = 16
CELLS = SIDE * SIDE
STRIP = RADIUS * SIDE
NEAR = 4
LANES = 128
PAIR = 2 * HEAD_DIM
VMEM_LIMIT = 32 * 1024 * 1024
NT = (((1,), (1,)), ((), ()))


def mm(a, b):
    return jnp.dot(a, b, preferred_element_type=jnp.float32)


def mm_nt(a, b):
    return lax.dot_general(a, b, NT, preferred_element_type=jnp.float32)


def strip_token(side_index, rotation, cell):
    turn = lax.rem(side_index + 6 - rotation, 4)
    depth = cell >> 4
    along = cell & (SIDE - 1)
    far = SIDE - 1 - along
    near_rim = RADIUS - 1 - depth
    far_rim = SIDE - RADIUS + depth
    row = jnp.where(turn == 0, far_rim, jnp.where(turn == 1, along, jnp.where(turn == 2, near_rim, far)))
    col = jnp.where(turn == 0, along, jnp.where(turn == 1, near_rim, jnp.where(turn == 2, far, far_rim)))
    return row * SIDE + col


def slot_side(slot, columns):
    tile = lax.axis_index("tile")
    if slot < 2:
        return jnp.where((tile + slot) & 1 == 0, 1, 3)
    return jnp.where((lax.div(tile, columns) + slot) & 1 == 0, 2, 0)


def partner(tile, tile_count, slot):
    columns = tile_count // 4
    if slot < 2:
        return (tile + (1 if (tile + slot) % 2 == 0 else -1)) % tile_count
    return (tile + (columns if (tile // columns + slot) % 2 == 0 else -columns)) % tile_count


def pick_kernel(columns, rotations_ref, keys_ref, values_ref, *out_refs):
    cell = lax.broadcasted_iota(jnp.int32, (STRIP, CELLS), 0)
    token = lax.broadcasted_iota(jnp.int32, (STRIP, CELLS), 1)
    for slot, out_ref in enumerate(out_refs):
        side = slot_side(slot, columns)
        wanted = strip_token(side, rotations_ref[0, side], cell)
        chosen = jnp.where(token == wanted, 1.0, 0.0).astype(jnp.bfloat16)
        out_ref[0] = mm(chosen, keys_ref[...]).astype(jnp.bfloat16)
        out_ref[1] = mm(chosen, values_ref[...]).astype(jnp.bfloat16)


def weight_kernel(scale, *refs):
    total = refs[0][0].astype(jnp.float32)
    for ref in refs[1:-1]:
        total += ref[0].astype(jnp.float32)
    refs[-1][...] = total * scale


def partial_kernel(attention_ref, arrived_ref, turned_ref, turned_arrived_ref, unused_ref, kept_ref, sent_ref):
    for index, out_ref in enumerate((kept_ref, sent_ref)):
        total = None
        for turned_part, attention_part in ((turned_ref, attention_ref), (turned_arrived_ref, arrived_ref)):
            turned = turned_part[index]
            turned = turned.reshape(turned.shape[0] * turned.shape[1], turned.shape[2])
            term = mm(turned, attention_part[...])
            total = term if total is None else total + term
        out_ref[...] = total.astype(out_ref.dtype).reshape(out_ref.shape)


def sum_kernel(count, *refs):
    terms, outs = refs[:count], refs[count + 3 :]
    for q in range(terms[0].shape[0]):
        total = terms[0][q].astype(jnp.float32)
        for ref in terms[1:]:
            total += ref[q].astype(jnp.float32)
        outs[q % len(outs)][q // len(outs)] = total.astype(jnp.bfloat16)


def rim_token(side_index, place):
    depth = place >> 4
    along = place & (SIDE - 1)
    last = SIDE - 1
    north, east, south = side_index == 0, side_index == 1, side_index == 2
    row = jnp.where(north, depth, jnp.where(east, along, jnp.where(south, last - depth, last - along)))
    col = jnp.where(north, along, jnp.where(east, last - depth, jnp.where(south, last - along, depth)))
    return row * SIDE + col


def cotangent_kernel(heads, *refs):
    blocks, out_weight_ref, outs = refs[:heads], refs[heads], refs[heads + 1 :]
    dout_ref, dout_turned_ref, turned_ref, turned_sent_ref = outs
    head = lax.axis_index("head")
    axis = head & 1
    tile = lax.axis_index("tile")
    chunk = turned_ref.shape[2]
    width = blocks[0].shape[1]
    total = None
    for distance, block_ref in enumerate(blocks):
        owner = lax.rem(head + distance, heads)
        start = pl.multiple_of(owner * width, width)
        block = block_ref[...]
        term = mm(block, out_weight_ref[pl.ds(start, width), :])
        total = term if total is None else total + term
        turned = block.T
        first = owner * (width // chunk)
        for index in range(width // chunk):
            target = (first + index) ^ tile
            rows = turned[index * chunk : (index + 1) * chunk]
            for parity, out_ref in enumerate((turned_ref, turned_sent_ref)):

                @pl.when((target >> axis) & 1 == parity)
                def _():
                    out_ref[(target >> (1 - axis)) & 1, target >> 2] = rows

    dout = total.astype(jnp.bfloat16)
    dout_ref[...] = dout
    dout_turned_ref[...] = dout.T


def split(exact, count):
    parts = []
    for _ in range(count):
        part = exact.astype(jnp.bfloat16).astype(jnp.float32)
        parts.append(part)
        exact = exact - part
    return parts


PARTS = (3, 2, 2)
SIDE_ORDER = (3, 2, 1, 0)


def rim_kernel(query_ref, dout_ref, rows_ref, chosen_ref, unused_ref, *rim_refs):
    parts = [part for kind, count in enumerate(PARTS) for part in split(rows_ref[kind], count)]
    pairs = rows_ref.shape[1] // 2
    filler = jnp.zeros((16 - 2 * len(parts), CELLS), jnp.float32)
    rows = [
        jnp.concatenate([part[2 * pair : 2 * pair + 2] for part in parts] + [filler], axis=0) for pair in range(pairs)
    ]
    rows = jnp.concatenate(rows, axis=0).astype(jnp.bfloat16)
    for slot, rim_ref in enumerate(rim_refs):
        chosen = chosen_ref[slot]
        rim_ref[:STRIP] = mm(chosen[:STRIP], query_ref[...]).astype(jnp.bfloat16)
        rim_ref[STRIP : 2 * STRIP] = mm(chosen[:STRIP], dout_ref[...]).astype(jnp.bfloat16)
        spread = mm_nt(rows, chosen).astype(jnp.bfloat16)
        for pair in range(pairs):
            rim_ref[2 * STRIP :, pair * PAIR : (pair + 1) * PAIR] = spread[16 * pair : 16 * pair + 16]


def window(cell_row, cell_col, query):
    query_row = (query >> 4) + RADIUS
    query_col = (query & (SIDE - 1)) + RADIUS
    near = (jnp.abs(cell_row - query_row) <= RADIUS) & (jnp.abs(cell_col - query_col) <= RADIUS)
    return jnp.where(near, 0.0, -1e30)


def centre_bias(bias_ref):
    query = lax.broadcasted_iota(jnp.int32, (CELLS, CELLS), 1)
    cell = lax.broadcasted_iota(jnp.int32, (CELLS, CELLS), 0)
    bias_ref[...] = window((cell >> 4) + RADIUS, (cell & (SIDE - 1)) + RADIUS, query)


def strip_bias(kind, bias_ref):
    query = lax.broadcasted_iota(jnp.int32, (STRIP, CELLS), 1)
    cell = lax.broadcasted_iota(jnp.int32, (STRIP, CELLS), 0)
    depth = cell >> 4
    along = cell & (SIDE - 1)
    last = SIDE + 2 * RADIUS - 1
    if kind:
        first, second = (last - RADIUS - along, depth), (RADIUS + along, last - depth)
    else:
        first, second = (depth, RADIUS + along), (last - depth, last - RADIUS - along)
    in_first = first_half(query, kind)
    row = jnp.where(in_first, first[0], second[0])
    col = jnp.where(in_first, first[1], second[1])
    bias_ref[...] = window(row, col, query)


def first_half(query, kind):
    return (query & (SIDE - 1)) < SIDE // 2 if kind else query < CELLS // 2


def one_head(block, head):
    lane = lax.broadcasted_iota(jnp.int32, block.shape, 1)
    kept = (lane >= HEAD_DIM) if head else (lane < HEAD_DIM)
    return jnp.where(kept, block, jnp.zeros_like(block))


def halves(block, kind):
    kept = first_half(lax.broadcasted_iota(jnp.int32, block.shape, 0), kind)
    zero = jnp.zeros_like(block)
    return jnp.concatenate([jnp.where(kept, block, zero), jnp.where(kept, zero, block)], axis=1)


def by_half(stacked, kind):
    rows = stacked.shape[0] // 2
    kept = first_half(lax.broadcasted_iota(jnp.int32, (rows, CELLS), 1), kind)
    return jnp.where(kept, stacked[:rows], stacked[rows:])


def side_blocks(strips, part, kind, cols):
    tile = lax.axis_index("tile")
    second, first = strips
    straight = (tile if kind else lax.div(tile, lax.axis_size("tile") // 4)) & 1 == 0
    first, second = first[part, :, cols], second[part, :, cols]
    return jnp.where(straight, first, second), jnp.where(straight, second, first)


def side_cells(strips, part, kind, cols):
    return jnp.concatenate(side_blocks(strips, part, kind, cols), axis=1)


def halves(block, kind):
    kept = first_half(lax.broadcasted_iota(jnp.int32, block.shape, 0), kind)
    zero = jnp.zeros_like(block)
    return jnp.concatenate([jnp.where(kept, block, zero), jnp.where(kept, zero, block)], axis=1)


def by_half(stacked, kind):
    rows = stacked.shape[0] // 2
    kept = first_half(lax.broadcasted_iota(jnp.int32, (rows, CELLS), 1), kind)
    return jnp.where(kept, stacked[:rows], stacked[rows:])


def side_blocks(strips, part, kind, cols):
    tile = lax.axis_index("tile")
    second, first = strips
    straight = (tile if kind else lax.div(tile, lax.axis_size("tile") // 4)) & 1 == 0
    first, second = first[part, :, cols], second[part, :, cols]
    return jnp.where(straight, first, second), jnp.where(straight, second, first)


def side_cells(strips, part, kind, cols):
    return jnp.concatenate(side_blocks(strips, part, kind, cols), axis=1)


def side_products(cells, rows_head):
    return [mm_nt(cells[kind], halves(rows_head, kind)) for kind in range(2)]


def turned_sides(strips, part, kind, cols):
    return [block.T for block in side_blocks(strips, part, kind, cols)]


def pair_cols(pair):
    return pl.ds(pl.multiple_of(pair * PAIR, PAIR), PAIR)


def head_rows(turned, head):
    return turned[head * HEAD_DIM : (head + 1) * HEAD_DIM]


def over_side(turned, head, kind, sides):
    return by_half(mm(jnp.concatenate([head_rows(t, head) for t in turned], axis=0), sides), kind)


SCORE_SCALE = HEAD_DIM ** (-0.5)
LOG_SCALE = SCORE_SCALE * math.log2(math.e)


def lanes_of(head):
    return slice(head * CELLS, (head + 1) * CELLS)


def centre_kernel(
    query_ref, key_ref, value_ref, dout_ref,
    raw_ref, stats_ref, sums_ref, product_ref, query_out, key_out, bias_ref,
):
    centre_bias(bias_ref)

    def step(pair, carry):
        cols = pair_cols(pair)
        query, key, value, dout = (ref[:, cols] for ref in (query_ref, key_ref, value_ref, dout_ref))
        turned = value.T
        for head in range(2):
            lanes = lanes_of(head)
            scores = mm_nt(key, one_head(query, head)) + bias_ref[...]
            top = jnp.max(scores, axis=0, keepdims=True)
            raw = jnp.exp2((scores - top) * LOG_SCALE)
            raw_ref[pair, :, lanes] = raw
            stats_ref[pair, 0:1, lanes] = top
            stats_ref[pair, 1:2, lanes] = jnp.sum(raw, axis=0, keepdims=True)
            sums_ref[pair, :, lanes] = mm(head_rows(turned, head), raw.astype(jnp.bfloat16))
            product_ref[pair, :, lanes] = mm_nt(value, one_head(dout, head))
        query_out[:, cols] = query
        key_out[:, cols] = key
        return carry

    lax.fori_loop(0, raw_ref.shape[0], step, 0)


def column_kernel(
    columns, rotations_ref, first_ref, second_ref, query_ref, dout_ref,
    raw_ref, stats_ref, sums_ref, product_ref, row_bias_ref, rim_chosen_ref, chosen_ref, bias_ref,
):
    strips = (first_ref, second_ref)
    strip_bias(0, bias_ref)
    strip_bias(1, row_bias_ref)
    place = lax.broadcasted_iota(jnp.int32, (LANES, CELLS), 0)
    token = lax.broadcasted_iota(jnp.int32, (LANES, CELLS), 1)
    for slot in range(4):
        wanted = rim_token(slot_side(slot, columns), place)
        chosen = jnp.where((token == wanted) & (place < STRIP), 1.0, 0.0).astype(jnp.bfloat16)
        rim_chosen_ref[slot] = chosen
    place = lax.broadcasted_iota(jnp.int32, (CELLS, LANES), 1)
    token = lax.broadcasted_iota(jnp.int32, (CELLS, LANES), 0)
    for index, slot in enumerate(SIDE_ORDER):
        side = slot_side(slot, columns)
        wanted = jnp.where(place < STRIP, strip_token(side, rotations_ref[0, side], place), -1)
        chosen = jnp.where(token == wanted, 1.0, 0.0).astype(jnp.bfloat16)
        chosen_ref[:, index * LANES : (index + 1) * LANES] = chosen

    def step(pair, carry):
        cols = pair_cols(pair)
        keys = side_cells(strips, 0, 0, cols)
        values = side_cells(strips, 1, 0, cols)
        turned = turned_sides(strips, 1, 0, cols)
        for head in range(2):
            lanes = lanes_of(head)
            scores = mm_nt(keys, halves(one_head(query_ref[:, cols], head), 0)) + bias_ref[...]
            top = jnp.max(scores, axis=0, keepdims=True)
            raw = jnp.exp2((scores - top) * LOG_SCALE)
            raw_ref[pair, :, lanes] = raw
            stats_ref[pair, 0:1, lanes] = top
            stats_ref[pair, 1:2, lanes] = jnp.sum(raw, axis=0, keepdims=True)
            sums_ref[pair, :, lanes] = over_side(turned, head, 0, raw.astype(jnp.bfloat16))
            product_ref[pair, :, lanes] = mm_nt(values, halves(one_head(dout_ref[:, cols], head), 0))
        return carry

    lax.fori_loop(0, raw_ref.shape[0], step, 0)


def row_kernel(
    first_ref, second_ref, query_ref, dout_turned_ref, centre_stats_ref, centre_sums_ref, stats_ref, sums_ref, bias_ref,
    raw_ref, attention_ref, rows_ref, factors_ref,
):
    strips = (first_ref, second_ref)

    def step(pair, carry):
        cols = pair_cols(pair)
        keys = side_cells(strips, 0, 1, cols)
        turned = turned_sides(strips, 1, 1, cols)
        parts = []
        for head in range(2):
            lanes = lanes_of(head)
            scores = mm_nt(keys, halves(one_head(query_ref[:, cols], head), 1)) + bias_ref[...]
            tops = [ref[pair, 0:1, lanes] for ref in (centre_stats_ref, stats_ref)]
            top = jnp.maximum(jnp.max(scores, axis=0, keepdims=True), jnp.maximum(*tops))
            raw = jnp.exp2((scores - top) * LOG_SCALE)
            raw_ref[pair, :, lanes] = raw
            lifted = [jnp.exp2((t - top) * LOG_SCALE) for t in tops]
            total = jnp.sum(raw, axis=0, keepdims=True)
            total += lifted[0] * centre_stats_ref[pair, 1:2, lanes] + lifted[1] * stats_ref[pair, 1:2, lanes]
            inverse = 1.0 / total
            factors = [l * inverse for l in lifted]
            part = over_side(turned, head, 1, raw.astype(jnp.bfloat16)) * inverse
            part += factors[0] * centre_sums_ref[pair, :, lanes] + factors[1] * sums_ref[pair, :, lanes]
            parts.append(part)
            place = pl.ds(2 * pair + head, 1)
            features = pl.ds(pl.multiple_of((2 * pair + head) * HEAD_DIM, HEAD_DIM), HEAD_DIM)
            product = dout_turned_ref[features, :].astype(jnp.float32) * part
            rows_ref[0, place, :] = top
            rows_ref[1, place, :] = inverse
            rows_ref[2, place, :] = jnp.sum(product, axis=0, keepdims=True)
            factors_ref[0, place, :] = factors[0]
            factors_ref[1, place, :] = factors[1]
        attention_ref[:, cols] = jnp.concatenate(parts, axis=0).T.astype(jnp.bfloat16)
        return carry

    lax.fori_loop(0, raw_ref.shape[0], step, 0, unroll=True)


def backward_kernel(
    fourth_ref, third_ref, second_ref, first_ref, query_ref, key_ref, dout_ref, centre_raw_ref, column_raw_ref,
    row_raw_ref, centre_product_ref, column_product_ref, rows_ref, factors_ref, unused_ref,
    grad_query_ref, centre_ref,
):
    columns, rows = (third_ref, fourth_ref), (first_ref, second_ref)

    def step(pair, carry):
        cols = pair_cols(pair)
        query = query_ref[:, cols]
        dout = dout_ref[:, cols]
        turned_centre = key_ref[:, cols].T
        turned_columns = turned_sides(columns, 0, 0, cols)
        turned_rows = turned_sides(rows, 0, 1, cols)
        row_values = side_cells(rows, 1, 1, cols)
        parts = []
        centre_scores = []
        centre_weights = []
        for head in range(2):
            lanes = lanes_of(head)
            place = pl.ds(2 * pair + head, 1)
            delta = rows_ref[2, place, :]
            row_product = mm_nt(row_values, halves(one_head(dout, head), 1))

            def dscore(weights, product):
                return (weights * (product - delta)).astype(jnp.bfloat16)

            weights = centre_raw_ref[pair, :, lanes] * factors_ref[0, place, :]
            centre_weights.append(weights.astype(jnp.bfloat16))
            centre_scores.append(dscore(weights, centre_product_ref[pair, :, lanes]))
            column_weights = column_raw_ref[pair, :, lanes] * factors_ref[1, place, :]
            column_score = dscore(column_weights, column_product_ref[pair, :, lanes])
            row_score = dscore(row_raw_ref[pair, :, lanes] * rows_ref[1, place, :], row_product)
            part = mm(head_rows(turned_centre, head), centre_scores[-1])
            part += over_side(turned_columns, head, 0, column_score) + over_side(turned_rows, head, 1, row_score)
            parts.append(part)
        grad_query = jnp.concatenate(parts, axis=0).T * SCORE_SCALE
        grad_query_ref[:, cols] = grad_query.astype(jnp.bfloat16)
        grad_key, grad_value = joint_mm(
            jnp.concatenate(centre_scores, axis=1),
            jnp.concatenate(centre_weights, axis=1),
            both_heads(query),
            both_heads(dout),
        )
        centre_ref[0, :, cols] = grad_key * SCORE_SCALE
        centre_ref[1, :, cols] = grad_value
        return carry

    lax.fori_loop(0, centre_raw_ref.shape[0], step, 0)


def joint_mm(first, second, first_rows, second_rows):
    rows = first.shape[0]
    product = mm(jnp.concatenate([first, second], axis=0), jnp.concatenate([first_rows, second_rows], axis=1))
    return product[:rows, :PAIR], product[rows:, PAIR:]


def both_heads(block):
    return jnp.concatenate([one_head(block, head) for head in range(2)], axis=0)


def padded(block):
    return jnp.concatenate([block, jnp.zeros((LANES - block.shape[0], block.shape[1]), block.dtype)], axis=0)


def statistics(rows):
    first = 0
    for count in PARTS:
        heads = []
        for head in range(2):
            parts = [rows[2 * index + head : 2 * index + head + 1] for index in range(first, first + count)]
            heads.append(functools.reduce(jnp.add, parts))
        first += count
        yield jnp.concatenate(heads, axis=1)


def side_kernel(centre_ref, chosen_ref, *refs):
    picked, rims = refs[:4], refs[4:8]
    keys_ref, values_ref, bias_ref, keys_done, values_done, sems = refs[8:]
    cell = lax.broadcasted_iota(jnp.int32, (STRIP, LANES), 0)
    query = lax.broadcasted_iota(jnp.int32, (STRIP, LANES), 1)
    near = jnp.abs((cell & (SIDE - 1)) - (query & (SIDE - 1))) <= RADIUS
    near = near & ((cell >> 4) >= (query >> 4)) & (query < STRIP)
    bias_ref[...] = jnp.where(near, 0.0, -1e30)
    copies = []
    for pair in range(keys_ref.shape[1] // PAIR):
        cols = slice(pair * PAIR, (pair + 1) * PAIR)
        grads = []
        bias = jnp.concatenate([bias_ref[...]] * 2, axis=1)
        for picked_ref, rim_ref in zip(picked, rims):
            query = both_heads(padded(rim_ref[:STRIP, cols]))
            dout = both_heads(padded(rim_ref[STRIP : 2 * STRIP, cols]))
            top, inverse, delta = statistics(rim_ref[2 * STRIP :, cols].astype(jnp.float32))
            scores = mm_nt(picked_ref[0, :, cols], query) + bias
            weights = jnp.exp2((scores - top) * LOG_SCALE) * inverse
            product = mm_nt(picked_ref[1, :, cols], dout)
            dscore = (weights * (product - delta)).astype(jnp.bfloat16)
            grad = jnp.concatenate([mm(dscore, query) * SCORE_SCALE, mm(weights.astype(jnp.bfloat16), dout)], axis=1)
            grads.append(padded(grad.astype(jnp.bfloat16)))
        total = mm(chosen_ref[...], jnp.concatenate(grads, axis=0))
        keys_done[:, cols] = (centre_ref[0, :, cols] + total[:, :PAIR]).astype(jnp.bfloat16)
        values_done[:, cols] = (centre_ref[1, :, cols] + total[:, PAIR:]).astype(jnp.bfloat16)
        for index, (done, out_ref) in enumerate(((keys_done, keys_ref), (values_done, values_ref))):
            copy = pltpu.make_async_copy(done.at[:, cols], out_ref.at[:, cols], sems.at[2 * pair + index])
            copy.start()
            copies.append(copy)
    for copy in copies:
        copy.wait()


def call(kernel, name, out_shape, operands, scratch=(), smem=0, unused=0, gflop=0.1, out_space=pltpu.VMEM):
    specs = [pl.BlockSpec(memory_space=pltpu.SMEM)] * smem
    specs += [pl.BlockSpec(memory_space=pltpu.VMEM)] * (len(operands) - smem - unused)
    specs += [pl.BlockSpec(memory_space=pl.ANY)] * unused
    single = not isinstance(out_shape, list)
    outs = pl.BlockSpec(memory_space=out_space)
    return pl.pallas_call(
        kernel,
        out_shape=out_shape,
        in_specs=specs,
        out_specs=outs if single else [outs] * len(out_shape),
        scratch_shapes=list(scratch),
        compiler_params=pltpu.CompilerParams(vmem_limit_bytes=VMEM_LIMIT),
        cost_estimate=pl.CostEstimate(flops=int(gflop * 1e9), bytes_accessed=1 << 20, transcendentals=0),
        name=name,
    )(*operands)


def in_hbm(array):
    return pltpu.with_memory_space_constraint(array, pltpu.HBM)


def across(block, distances):
    heads = lax.axis_size("head")
    devices = [(tile, head) for tile in range(lax.axis_size("tile")) for head in range(heads)]
    route = [(tile * heads + head, (tile ^ distances[head % 2]) * heads + head) for tile, head in devices]
    return lax.ppermute(block, ("tile", "head"), route)


def exchanged(blocks, stride):
    terms = list(blocks[:1])
    for distance in range(1, len(blocks)):
        route = [(tile, tile ^ (distance * stride)) for tile in range(lax.axis_size("tile"))]
        terms.append(lax.ppermute(blocks[distance], "tile", route))
    return terms


def with_partners(blocks, slots):
    tile_count = lax.axis_size("tile")
    routes = {s: [(tile, partner(tile, tile_count, s)) for tile in range(tile_count)] for s in slots}
    return {s: lax.ppermute(blocks[s], "tile", routes[s]) for s in slots}


def shards(queries, keys, values, grad_output, out_weight, rotations):
    tile_count = lax.axis_size("tile")
    token_count, features = queries.shape
    model = out_weight.shape[0]
    pairs = features // PAIR
    far = tile_count // NEAR
    chunk = model // tile_count
    heads = lax.axis_size("head")
    columns = tile_count // 4
    queries, keys, values, out_weight, rotations = (
        in_hbm(a) for a in (queries, keys, values, out_weight, rotations)
    )

    def bf16(*shape):
        return jax.ShapeDtypeStruct(shape, jnp.bfloat16)

    def f32(*shape):
        return jax.ShapeDtypeStruct(shape, jnp.float32)

    strip_types = [bf16(2, STRIP, features)] * 4
    picked = call(
        functools.partial(pick_kernel, columns), "pick_strips", strip_types, (rotations, keys, values), smem=1
    )
    grad_output, *picked = lax.optimization_barrier((grad_output, *picked))
    strips = with_partners(picked, (3, 2, 1, 0))
    strips = [strips[s] for s in range(4)]

    cotangents = [
        lax.ppermute(grad_output, "head", [((h + k) % heads, h) for h in range(heads)]) for k in range(1, heads)
    ]
    dout, dout_turned, turned, turned_sent = call(
        functools.partial(cotangent_kernel, heads),
        "cotangent",
        [bf16(CELLS, features), bf16(features, CELLS)] + [bf16(2, far, chunk, CELLS)] * 2,
        (in_hbm(grad_output), *cotangents, out_weight),
        gflop=1.0,
    )
    turned_arrived = across(turned_sent, (1, 2))
    part_types = [f32(pairs, 2, 2 * CELLS), f32(pairs, HEAD_DIM, 2 * CELLS)]
    raw_centre, stats_centre, sums_centre, product_centre, queries, keys = call(
        centre_kernel,
        "centre",
        [f32(pairs, CELLS, 2 * CELLS)] + part_types + [f32(pairs, CELLS, 2 * CELLS)] + [bf16(CELLS, features)] * 2,
        (queries, keys, values, dout),
        scratch=[pltpu.VMEM((CELLS, CELLS), jnp.float32)],
        gflop=3.0,
    )
    strip_scratch = [pltpu.VMEM((STRIP, CELLS), jnp.float32)]
    raw_columns, stats_columns, sums_columns, product_columns, row_bias, rim_chosen, chosen = call(
        functools.partial(column_kernel, columns),
        "columns",
        [f32(pairs, STRIP, 2 * CELLS)]
        + part_types
        + [f32(pairs, STRIP, 2 * CELLS), f32(STRIP, CELLS), bf16(4, LANES, CELLS), bf16(CELLS, 4 * LANES)],
        (rotations, strips[2], strips[3], queries, dout),
        scratch=strip_scratch,
        smem=1,
        gflop=2.0,
    )
    raw_rows, attention, rows, factors = call(
        row_kernel,
        "rows",
        [f32(pairs, STRIP, 2 * CELLS), bf16(CELLS, features)] + [f32(k, 2 * pairs, CELLS) for k in (3, 2)],
        (strips[0], strips[1], queries, dout_turned, stats_centre, sums_centre, stats_columns, sums_columns, row_bias),
    )
    attention_arrived = across(attention, (1, 2))
    rims = call(
        rim_kernel,
        "rims",
        [bf16(2 * STRIP + 16, features)] * 4,
        (queries, dout, rows, rim_chosen, turned_arrived),
        unused=1,
    )
    rims_arrived = with_partners(rims, (3, 2))
    kept, sent = call(
        partial_kernel,
        "partial",
        [f32(far, chunk, features), bf16(far, chunk, features)],
        (attention, attention_arrived, turned, turned_arrived, rims[0]),
        unused=1,
    )
    terms = [kept, across(sent, (2, 1))]
    rims = lax.optimization_barrier((*rims, sent))[:4]
    rims_arrived |= with_partners(rims, (1, 0))
    grad_queries, centre = call(
        backward_kernel,
        "backward",
        [bf16(CELLS, features), f32(2, CELLS, features)],
        (
            *strips[::-1], queries, keys, dout, raw_centre, raw_columns, raw_rows, product_centre, product_columns,
            rows, factors, sent,
        ),
        unused=1,
        gflop=3.0,
    )
    stride = NEAR
    while stride < tile_count:
        ways = min(NEAR, tile_count // stride)
        sums = call(
            functools.partial(sum_kernel, len(terms)),
            "plane_sum",
            [bf16(tile_count // stride // ways, chunk, features)] * ways,
            (*terms, centre, rims_arrived[3], rims_arrived[2]),
            unused=3,
        )
        terms = exchanged(sums, stride)
        stride *= ways

    grad_keys, grad_values = call(
        side_kernel,
        "sides",
        [bf16(CELLS, features)] * 2,
        (centre, chosen, *(picked[s] for s in SIDE_ORDER), *(rims_arrived[s] for s in SIDE_ORDER)),
        scratch=[pltpu.VMEM((STRIP, LANES), jnp.float32)]
        + [pltpu.VMEM((CELLS, features), jnp.bfloat16)] * 2
        + [pltpu.SemaphoreType.DMA((2 * pairs,))],
        gflop=3.0,
        out_space=pl.ANY,
    )
    grad_out_weight = call(
        functools.partial(weight_kernel, 1.0 / math.sqrt(token_count * tile_count)),
        "weight_sum",
        f32(chunk, features),
        terms,
    )
    return (grad_queries, grad_keys, grad_values, grad_out_weight)


def solution(mesh):
    placed = (
        P("tile", "head"),
        P("tile", "head"),
        P("tile", "head"),
        P("tile", "head"),
        P(None, "head"),
        P("tile", None),
    )
    return jax.shard_map(
        shards,
        mesh=mesh,
        in_specs=placed,
        out_specs=(P("tile", "head"), P("tile", "head"), P("tile", "head"), P("tile", "head")),
        check_vma=False,
    )
```

```python
import functools
import math

import jax
import jax.numpy as jnp
from jax import lax
from jax.experimental import pallas as pl
from jax.experimental.pallas import tpu as pltpu
from jax.sharding import PartitionSpec as P

HEAD_DIM = 64
RADIUS = 6
SIDE = 16
CELLS = SIDE * SIDE
STRIP = RADIUS * SIDE
NEAR = 4
LANES = 128
PAIR = 2 * HEAD_DIM
VMEM_LIMIT = 32 * 1024 * 1024
NT = (((1,), (1,)), ((), ()))


def mm(a, b):
    return jnp.dot(a, b, preferred_element_type=jnp.float32)


def mm_nt(a, b):
    return lax.dot_general(a, b, NT, preferred_element_type=jnp.float32)


def strip_token(side_index, rotation, cell):
    turn = lax.rem(side_index + 6 - rotation, 4)
    depth = cell >> 4
    along = cell & (SIDE - 1)
    far = SIDE - 1 - along
    near_rim = RADIUS - 1 - depth
    far_rim = SIDE - RADIUS + depth
    row = jnp.where(turn == 0, far_rim, jnp.where(turn == 1, along, jnp.where(turn == 2, near_rim, far)))
    col = jnp.where(turn == 0, along, jnp.where(turn == 1, near_rim, jnp.where(turn == 2, far, far_rim)))
    return row * SIDE + col


def slot_side(slot, columns):
    tile = lax.axis_index("tile")
    if slot < 2:
        return jnp.where((tile + slot) & 1 == 0, 1, 3)
    return jnp.where((lax.div(tile, columns) + slot) & 1 == 0, 2, 0)


def partner(tile, tile_count, slot):
    columns = tile_count // 4
    if slot < 2:
        return (tile + (1 if (tile + slot) % 2 == 0 else -1)) % tile_count
    return (tile + (columns if (tile // columns + slot) % 2 == 0 else -columns)) % tile_count


def pick_kernel(columns, rotations_ref, keys_ref, values_ref, *out_refs):
    cell = lax.broadcasted_iota(jnp.int32, (STRIP, CELLS), 0)
    token = lax.broadcasted_iota(jnp.int32, (STRIP, CELLS), 1)
    for slot, out_ref in enumerate(out_refs):
        side = slot_side(slot, columns)
        wanted = strip_token(side, rotations_ref[0, side], cell)
        chosen = jnp.where(token == wanted, 1.0, 0.0).astype(jnp.bfloat16)
        out_ref[0] = mm(chosen, keys_ref[...]).astype(jnp.bfloat16)
        out_ref[1] = mm(chosen, values_ref[...]).astype(jnp.bfloat16)


def weight_kernel(scale, *refs):
    total = refs[0][0].astype(jnp.float32)
    for ref in refs[1:-1]:
        total += ref[0].astype(jnp.float32)
    refs[-1][...] = total * scale


def partial_kernel(attention_ref, arrived_ref, turned_ref, turned_arrived_ref, unused_ref, kept_ref, sent_ref):
    for index, out_ref in enumerate((kept_ref, sent_ref)):
        total = None
        for turned_part, attention_part in ((turned_ref, attention_ref), (turned_arrived_ref, arrived_ref)):
            turned = turned_part[index]
            turned = turned.reshape(turned.shape[0] * turned.shape[1], turned.shape[2])
            term = mm(turned, attention_part[...])
            total = term if total is None else total + term
        out_ref[...] = total.astype(out_ref.dtype).reshape(out_ref.shape)


def sum_kernel(count, *refs):
    terms, outs = refs[:count], refs[count + 3 :]
    for q in range(terms[0].shape[0]):
        total = terms[0][q].astype(jnp.float32)
        for ref in terms[1:]:
            total += ref[q].astype(jnp.float32)
        outs[q % len(outs)][q // len(outs)] = total.astype(jnp.bfloat16)


def rim_token(side_index, place):
    depth = place >> 4
    along = place & (SIDE - 1)
    last = SIDE - 1
    north, east, south = side_index == 0, side_index == 1, side_index == 2
    row = jnp.where(north, depth, jnp.where(east, along, jnp.where(south, last - depth, last - along)))
    col = jnp.where(north, along, jnp.where(east, last - depth, jnp.where(south, last - along, depth)))
    return row * SIDE + col


def cotangent_kernel(heads, *refs):
    blocks, out_weight_ref, outs = refs[:heads], refs[heads], refs[heads + 1 :]
    dout_ref, dout_turned_ref, turned_ref, turned_sent_ref = outs
    head = lax.axis_index("head")
    axis = head & 1
    tile = lax.axis_index("tile")
    chunk = turned_ref.shape[2]
    width = blocks[0].shape[1]
    total = None
    for distance, block_ref in enumerate(blocks):
        owner = lax.rem(head + distance, heads)
        start = pl.multiple_of(owner * width, width)
        block = block_ref[...]
        term = mm(block, out_weight_ref[pl.ds(start, width), :])
        total = term if total is None else total + term
        turned = block.T
        first = owner * (width // chunk)
        for index in range(width // chunk):
            target = (first + index) ^ tile
            rows = turned[index * chunk : (index + 1) * chunk]
            for parity, out_ref in enumerate((turned_ref, turned_sent_ref)):

                @pl.when((target >> axis) & 1 == parity)
                def _():
                    out_ref[(target >> (1 - axis)) & 1, target >> 2] = rows

    dout = total.astype(jnp.bfloat16)
    dout_ref[...] = dout
    dout_turned_ref[...] = dout.T


def split(exact, count):
    parts = []
    for _ in range(count):
        part = exact.astype(jnp.bfloat16).astype(jnp.float32)
        parts.append(part)
        exact = exact - part
    return parts


PARTS = (3, 2, 2)
SIDE_ORDER = (3, 2, 1, 0)


def rim_kernel(query_ref, dout_ref, rows_ref, chosen_ref, unused_ref, *rim_refs):
    parts = [part for kind, count in enumerate(PARTS) for part in split(rows_ref[kind], count)]
    pairs = rows_ref.shape[1] // 2
    filler = jnp.zeros((16 - 2 * len(parts), CELLS), jnp.float32)
    rows = [
        jnp.concatenate([part[2 * pair : 2 * pair + 2] for part in parts] + [filler], axis=0) for pair in range(pairs)
    ]
    rows = jnp.concatenate(rows, axis=0).astype(jnp.bfloat16)
    for slot, rim_ref in enumerate(rim_refs):
        chosen = chosen_ref[slot]
        rim_ref[:STRIP] = mm(chosen[:STRIP], query_ref[...]).astype(jnp.bfloat16)
        rim_ref[STRIP : 2 * STRIP] = mm(chosen[:STRIP], dout_ref[...]).astype(jnp.bfloat16)
        spread = mm_nt(rows, chosen).astype(jnp.bfloat16)
        for pair in range(pairs):
            rim_ref[2 * STRIP :, pair * PAIR : (pair + 1) * PAIR] = spread[16 * pair : 16 * pair + 16]


def window(cell_row, cell_col, query):
    query_row = (query >> 4) + RADIUS
    query_col = (query & (SIDE - 1)) + RADIUS
    near = (jnp.abs(cell_row - query_row) <= RADIUS) & (jnp.abs(cell_col - query_col) <= RADIUS)
    return jnp.where(near, 0.0, -1e30)


def centre_bias(bias_ref):
    query = lax.broadcasted_iota(jnp.int32, (CELLS, CELLS), 1)
    cell = lax.broadcasted_iota(jnp.int32, (CELLS, CELLS), 0)
    bias_ref[...] = window((cell >> 4) + RADIUS, (cell & (SIDE - 1)) + RADIUS, query)


def strip_bias(kind, bias_ref):
    query = lax.broadcasted_iota(jnp.int32, (STRIP, CELLS), 1)
    cell = lax.broadcasted_iota(jnp.int32, (STRIP, CELLS), 0)
    depth = cell >> 4
    along = cell & (SIDE - 1)
    last = SIDE + 2 * RADIUS - 1
    if kind:
        first, second = (last - RADIUS - along, depth), (RADIUS + along, last - depth)
    else:
        first, second = (depth, RADIUS + along), (last - depth, last - RADIUS - along)
    in_first = first_half(query, kind)
    row = jnp.where(in_first, first[0], second[0])
    col = jnp.where(in_first, first[1], second[1])
    bias_ref[...] = window(row, col, query)


def first_half(query, kind):
    return (query & (SIDE - 1)) < SIDE // 2 if kind else query < CELLS // 2


def one_head(block, head):
    lane = lax.broadcasted_iota(jnp.int32, block.shape, 1)
    kept = (lane >= HEAD_DIM) if head else (lane < HEAD_DIM)
    return jnp.where(kept, block, jnp.zeros_like(block))


def halves(block, kind):
    kept = first_half(lax.broadcasted_iota(jnp.int32, block.shape, 0), kind)
    zero = jnp.zeros_like(block)
    return jnp.concatenate([jnp.where(kept, block, zero), jnp.where(kept, zero, block)], axis=1)


def by_half(stacked, kind):
    rows = stacked.shape[0] // 2
    kept = first_half(lax.broadcasted_iota(jnp.int32, (rows, CELLS), 1), kind)
    return jnp.where(kept, stacked[:rows], stacked[rows:])


def side_blocks(strips, part, kind, cols):
    tile = lax.axis_index("tile")
    second, first = strips
    straight = (tile if kind else lax.div(tile, lax.axis_size("tile") // 4)) & 1 == 0
    first, second = first[part, :, cols], second[part, :, cols]
    return jnp.where(straight, first, second), jnp.where(straight, second, first)


def side_cells(strips, part, kind, cols):
    return jnp.concatenate(side_blocks(strips, part, kind, cols), axis=1)


def halves(block, kind):
    kept = first_half(lax.broadcasted_iota(jnp.int32, block.shape, 0), kind)
    zero = jnp.zeros_like(block)
    return jnp.concatenate([jnp.where(kept, block, zero), jnp.where(kept, zero, block)], axis=1)


def by_half(stacked, kind):
    rows = stacked.shape[0] // 2
    kept = first_half(lax.broadcasted_iota(jnp.int32, (rows, CELLS), 1), kind)
    return jnp.where(kept, stacked[:rows], stacked[rows:])


def side_blocks(strips, part, kind, cols):
    tile = lax.axis_index("tile")
    second, first = strips
    straight = (tile if kind else lax.div(tile, lax.axis_size("tile") // 4)) & 1 == 0
    first, second = first[part, :, cols], second[part, :, cols]
    return jnp.where(straight, first, second), jnp.where(straight, second, first)


def side_cells(strips, part, kind, cols):
    return jnp.concatenate(side_blocks(strips, part, kind, cols), axis=1)


def side_products(cells, rows_head):
    return [mm_nt(cells[kind], halves(rows_head, kind)) for kind in range(2)]


def turned_sides(strips, part, kind, cols):
    return [block.T for block in side_blocks(strips, part, kind, cols)]


def pair_cols(pair):
    return pl.ds(pl.multiple_of(pair * PAIR, PAIR), PAIR)


def head_rows(turned, head):
    return turned[head * HEAD_DIM : (head + 1) * HEAD_DIM]


def over_side(turned, head, kind, sides):
    return by_half(mm(jnp.concatenate([head_rows(t, head) for t in turned], axis=0), sides), kind)


SCORE_SCALE = HEAD_DIM ** (-0.5)
LOG_SCALE = SCORE_SCALE * math.log2(math.e)


def lanes_of(head):
    return slice(head * CELLS, (head + 1) * CELLS)


def centre_kernel(
    query_ref, key_ref, value_ref, dout_ref,
    raw_ref, stats_ref, sums_ref, product_ref, query_out, key_out, bias_ref,
):
    centre_bias(bias_ref)

    def step(pair, carry):
        cols = pair_cols(pair)
        query, key, value, dout = (ref[:, cols] for ref in (query_ref, key_ref, value_ref, dout_ref))
        turned = value.T
        for head in range(2):
            lanes = lanes_of(head)
            scores = mm_nt(key, one_head(query, head)) + bias_ref[...]
            top = jnp.max(scores, axis=0, keepdims=True)
            raw = jnp.exp2((scores - top) * LOG_SCALE)
            raw_ref[pair, :, lanes] = raw
            stats_ref[pair, 0:1, lanes] = top
            stats_ref[pair, 1:2, lanes] = jnp.sum(raw, axis=0, keepdims=True)
            sums_ref[pair, :, lanes] = mm(head_rows(turned, head), raw.astype(jnp.bfloat16))
            product_ref[pair, :, lanes] = mm_nt(value, one_head(dout, head))
        query_out[:, cols] = query
        key_out[:, cols] = key
        return carry

    lax.fori_loop(0, raw_ref.shape[0], step, 0)


def column_kernel(
    columns, rotations_ref, first_ref, second_ref, query_ref, dout_ref,
    raw_ref, stats_ref, sums_ref, product_ref, row_bias_ref, rim_chosen_ref, chosen_ref, bias_ref,
):
    strips = (first_ref, second_ref)
    strip_bias(0, bias_ref)
    strip_bias(1, row_bias_ref)
    place = lax.broadcasted_iota(jnp.int32, (LANES, CELLS), 0)
    token = lax.broadcasted_iota(jnp.int32, (LANES, CELLS), 1)
    for slot in range(4):
        wanted = rim_token(slot_side(slot, columns), place)
        chosen = jnp.where((token == wanted) & (place < STRIP), 1.0, 0.0).astype(jnp.bfloat16)
        rim_chosen_ref[slot] = chosen
    place = lax.broadcasted_iota(jnp.int32, (CELLS, LANES), 1)
    token = lax.broadcasted_iota(jnp.int32, (CELLS, LANES), 0)
    for index, slot in enumerate(SIDE_ORDER):
        side = slot_side(slot, columns)
        wanted = jnp.where(place < STRIP, strip_token(side, rotations_ref[0, side], place), -1)
        chosen = jnp.where(token == wanted, 1.0, 0.0).astype(jnp.bfloat16)
        chosen_ref[:, index * LANES : (index + 1) * LANES] = chosen

    def step(pair, carry):
        cols = pair_cols(pair)
        keys = side_cells(strips, 0, 0, cols)
        values = side_cells(strips, 1, 0, cols)
        turned = turned_sides(strips, 1, 0, cols)
        for head in range(2):
            lanes = lanes_of(head)
            scores = mm_nt(keys, halves(one_head(query_ref[:, cols], head), 0)) + bias_ref[...]
            top = jnp.max(scores, axis=0, keepdims=True)
            raw = jnp.exp2((scores - top) * LOG_SCALE)
            raw_ref[pair, :, lanes] = raw
            stats_ref[pair, 0:1, lanes] = top
            stats_ref[pair, 1:2, lanes] = jnp.sum(raw, axis=0, keepdims=True)
            sums_ref[pair, :, lanes] = over_side(turned, head, 0, raw.astype(jnp.bfloat16))
            product_ref[pair, :, lanes] = mm_nt(values, halves(one_head(dout_ref[:, cols], head), 0))
        return carry

    lax.fori_loop(0, raw_ref.shape[0], step, 0)


def row_kernel(
    first_ref, second_ref, query_ref, dout_turned_ref, centre_stats_ref, centre_sums_ref, stats_ref, sums_ref, bias_ref,
    raw_ref, attention_ref, rows_ref, factors_ref,
):
    strips = (first_ref, second_ref)

    def step(pair, carry):
        cols = pair_cols(pair)
        keys = side_cells(strips, 0, 1, cols)
        turned = turned_sides(strips, 1, 1, cols)
        parts = []
        for head in range(2):
            lanes = lanes_of(head)
            scores = mm_nt(keys, halves(one_head(query_ref[:, cols], head), 1)) + bias_ref[...]
            tops = [ref[pair, 0:1, lanes] for ref in (centre_stats_ref, stats_ref)]
            top = jnp.maximum(jnp.max(scores, axis=0, keepdims=True), jnp.maximum(*tops))
            raw = jnp.exp2((scores - top) * LOG_SCALE)
            raw_ref[pair, :, lanes] = raw
            lifted = [jnp.exp2((t - top) * LOG_SCALE) for t in tops]
            total = jnp.sum(raw, axis=0, keepdims=True)
            total += lifted[0] * centre_stats_ref[pair, 1:2, lanes] + lifted[1] * stats_ref[pair, 1:2, lanes]
            inverse = 1.0 / total
            factors = [l * inverse for l in lifted]
            part = over_side(turned, head, 1, raw.astype(jnp.bfloat16)) * inverse
            part += factors[0] * centre_sums_ref[pair, :, lanes] + factors[1] * sums_ref[pair, :, lanes]
            parts.append(part)
            place = pl.ds(2 * pair + head, 1)
            features = pl.ds(pl.multiple_of((2 * pair + head) * HEAD_DIM, HEAD_DIM), HEAD_DIM)
            product = dout_turned_ref[features, :].astype(jnp.float32) * part
            rows_ref[0, place, :] = top
            rows_ref[1, place, :] = inverse
            rows_ref[2, place, :] = jnp.sum(product, axis=0, keepdims=True)
            factors_ref[0, place, :] = factors[0]
            factors_ref[1, place, :] = factors[1]
        attention_ref[:, cols] = jnp.concatenate(parts, axis=0).T.astype(jnp.bfloat16)
        return carry

    lax.fori_loop(0, raw_ref.shape[0], step, 0, unroll=True)


def backward_kernel(
    fourth_ref, third_ref, second_ref, first_ref, query_ref, key_ref, dout_ref, centre_raw_ref, column_raw_ref,
    row_raw_ref, centre_product_ref, column_product_ref, rows_ref, factors_ref, unused_ref,
    grad_query_ref, centre_ref,
):
    columns, rows = (third_ref, fourth_ref), (first_ref, second_ref)

    def step(pair, carry):
        cols = pair_cols(pair)
        query = query_ref[:, cols]
        dout = dout_ref[:, cols]
        turned_centre = key_ref[:, cols].T
        turned_columns = turned_sides(columns, 0, 0, cols)
        turned_rows = turned_sides(rows, 0, 1, cols)
        row_values = side_cells(rows, 1, 1, cols)
        parts = []
        centre_scores = []
        centre_weights = []
        for head in range(2):
            lanes = lanes_of(head)
            place = pl.ds(2 * pair + head, 1)
            delta = rows_ref[2, place, :]
            row_product = mm_nt(row_values, halves(one_head(dout, head), 1))

            def dscore(weights, product):
                return (weights * (product - delta)).astype(jnp.bfloat16)

            weights = centre_raw_ref[pair, :, lanes] * factors_ref[0, place, :]
            centre_weights.append(weights.astype(jnp.bfloat16))
            centre_scores.append(dscore(weights, centre_product_ref[pair, :, lanes]))
            column_weights = column_raw_ref[pair, :, lanes] * factors_ref[1, place, :]
            column_score = dscore(column_weights, column_product_ref[pair, :, lanes])
            row_score = dscore(row_raw_ref[pair, :, lanes] * rows_ref[1, place, :], row_product)
            part = mm(head_rows(turned_centre, head), centre_scores[-1])
            part += over_side(turned_columns, head, 0, column_score) + over_side(turned_rows, head, 1, row_score)
            parts.append(part)
        grad_query = jnp.concatenate(parts, axis=0).T * SCORE_SCALE
        grad_query_ref[:, cols] = grad_query.astype(jnp.bfloat16)
        grad_key, grad_value = joint_mm(
            jnp.concatenate(centre_scores, axis=1),
            jnp.concatenate(centre_weights, axis=1),
            both_heads(query),
            both_heads(dout),
        )
        centre_ref[0, :, cols] = grad_key * SCORE_SCALE
        centre_ref[1, :, cols] = grad_value
        return carry

    lax.fori_loop(0, centre_raw_ref.shape[0], step, 0)


def joint_mm(first, second, first_rows, second_rows):
    rows = first.shape[0]
    product = mm(jnp.concatenate([first, second], axis=0), jnp.concatenate([first_rows, second_rows], axis=1))
    return product[:rows, :PAIR], product[rows:, PAIR:]


def both_heads(block):
    return jnp.concatenate([one_head(block, head) for head in range(2)], axis=0)


def padded(block):
    return jnp.concatenate([block, jnp.zeros((LANES - block.shape[0], block.shape[1]), block.dtype)], axis=0)


def statistics(rows):
    first = 0
    for count in PARTS:
        heads = []
        for head in range(2):
            parts = [rows[2 * index + head : 2 * index + head + 1] for index in range(first, first + count)]
            heads.append(functools.reduce(jnp.add, parts))
        first += count
        yield jnp.concatenate(heads, axis=1)


def side_kernel(centre_ref, chosen_ref, *refs):
    picked, rims = refs[:4], refs[4:8]
    keys_ref, values_ref, bias_ref, keys_done, values_done, sems = refs[8:]
    cell = lax.broadcasted_iota(jnp.int32, (STRIP, LANES), 0)
    query = lax.broadcasted_iota(jnp.int32, (STRIP, LANES), 1)
    near = jnp.abs((cell & (SIDE - 1)) - (query & (SIDE - 1))) <= RADIUS
    near = near & ((cell >> 4) >= (query >> 4)) & (query < STRIP)
    bias_ref[...] = jnp.where(near, 0.0, -1e30)
    copies = []
    for pair in range(keys_ref.shape[1] // PAIR):
        cols = slice(pair * PAIR, (pair + 1) * PAIR)
        grads = []
        bias = jnp.concatenate([bias_ref[...]] * 2, axis=1)
        for picked_ref, rim_ref in zip(picked, rims):
            query = both_heads(padded(rim_ref[:STRIP, cols]))
            dout = both_heads(padded(rim_ref[STRIP : 2 * STRIP, cols]))
            top, inverse, delta = statistics(rim_ref[2 * STRIP :, cols].astype(jnp.float32))
            scores = mm_nt(picked_ref[0, :, cols], query) + bias
            weights = jnp.exp2((scores - top) * LOG_SCALE) * inverse
            product = mm_nt(picked_ref[1, :, cols], dout)
            dscore = (weights * (product - delta)).astype(jnp.bfloat16)
            grad = jnp.concatenate([mm(dscore, query) * SCORE_SCALE, mm(weights.astype(jnp.bfloat16), dout)], axis=1)
            grads.append(padded(grad.astype(jnp.bfloat16)))
        total = mm(chosen_ref[...], jnp.concatenate(grads, axis=0))
        keys_done[:, cols] = (centre_ref[0, :, cols] + total[:, :PAIR]).astype(jnp.bfloat16)
        values_done[:, cols] = (centre_ref[1, :, cols] + total[:, PAIR:]).astype(jnp.bfloat16)
        for index, (done, out_ref) in enumerate(((keys_done, keys_ref), (values_done, values_ref))):
            copy = pltpu.make_async_copy(done.at[:, cols], out_ref.at[:, cols], sems.at[2 * pair + index])
            copy.start()
            copies.append(copy)
    for copy in copies:
        copy.wait()


def call(kernel, name, out_shape, operands, scratch=(), smem=0, unused=0, gflop=0.1, out_space=pltpu.VMEM):
    specs = [pl.BlockSpec(memory_space=pltpu.SMEM)] * smem
    specs += [pl.BlockSpec(memory_space=pltpu.VMEM)] * (len(operands) - smem - unused)
    specs += [pl.BlockSpec(memory_space=pl.ANY)] * unused
    single = not isinstance(out_shape, list)
    outs = pl.BlockSpec(memory_space=out_space)
    return pl.pallas_call(
        kernel,
        out_shape=out_shape,
        in_specs=specs,
        out_specs=outs if single else [outs] * len(out_shape),
        scratch_shapes=list(scratch),
        compiler_params=pltpu.CompilerParams(vmem_limit_bytes=VMEM_LIMIT),
        cost_estimate=pl.CostEstimate(flops=int(gflop * 1e9), bytes_accessed=1 << 20, transcendentals=0),
        name=name,
    )(*operands)


def in_hbm(array):
    return pltpu.with_memory_space_constraint(array, pltpu.HBM)


def across(block, distances):
    heads = lax.axis_size("head")
    devices = [(tile, head) for tile in range(lax.axis_size("tile")) for head in range(heads)]
    route = [(tile * heads + head, (tile ^ distances[head % 2]) * heads + head) for tile, head in devices]
    return lax.ppermute(block, ("tile", "head"), route)


def exchanged(blocks, stride):
    terms = list(blocks[:1])
    for distance in (2, 3, 1) if len(blocks) == 4 else (1,):
        route = [(tile, tile ^ (distance * stride)) for tile in range(lax.axis_size("tile"))]
        terms.append(lax.ppermute(blocks[distance], "tile", route))
    return terms


def with_partners(blocks, slots):
    tile_count = lax.axis_size("tile")
    routes = {s: [(tile, partner(tile, tile_count, s)) for tile in range(tile_count)] for s in slots}
    return {s: lax.ppermute(blocks[s], "tile", routes[s]) for s in slots}


def shards(queries, keys, values, grad_output, out_weight, rotations):
    tile_count = lax.axis_size("tile")
    token_count, features = queries.shape
    model = out_weight.shape[0]
    pairs = features // PAIR
    far = tile_count // NEAR
    chunk = model // tile_count
    heads = lax.axis_size("head")
    columns = tile_count // 4
    queries, keys, values, out_weight, rotations = (
        in_hbm(a) for a in (queries, keys, values, out_weight, rotations)
    )

    def bf16(*shape):
        return jax.ShapeDtypeStruct(shape, jnp.bfloat16)

    def f32(*shape):
        return jax.ShapeDtypeStruct(shape, jnp.float32)

    strip_types = [bf16(2, STRIP, features)] * 4
    picked = call(
        functools.partial(pick_kernel, columns), "pick_strips", strip_types, (rotations, keys, values), smem=1
    )
    grad_output, *picked = lax.optimization_barrier((grad_output, *picked))
    strips = with_partners(picked, (3, 2, 1, 0))
    strips = [strips[s] for s in range(4)]

    cotangents = [
        lax.ppermute(grad_output, "head", [((h + k) % heads, h) for h in range(heads)]) for k in range(1, heads)
    ]
    dout, dout_turned, turned, turned_sent = call(
        functools.partial(cotangent_kernel, heads),
        "cotangent",
        [bf16(CELLS, features), bf16(features, CELLS)] + [bf16(2, far, chunk, CELLS)] * 2,
        (in_hbm(grad_output), *cotangents, out_weight),
        gflop=1.0,
    )
    turned_arrived = across(turned_sent, (1, 2))
    part_types = [f32(pairs, 2, 2 * CELLS), f32(pairs, HEAD_DIM, 2 * CELLS)]
    raw_centre, stats_centre, sums_centre, product_centre, queries, keys = call(
        centre_kernel,
        "centre",
        [f32(pairs, CELLS, 2 * CELLS)] + part_types + [f32(pairs, CELLS, 2 * CELLS)] + [bf16(CELLS, features)] * 2,
        (queries, keys, values, dout),
        scratch=[pltpu.VMEM((CELLS, CELLS), jnp.float32)],
        gflop=3.0,
    )
    strip_scratch = [pltpu.VMEM((STRIP, CELLS), jnp.float32)]
    raw_columns, stats_columns, sums_columns, product_columns, row_bias, rim_chosen, chosen = call(
        functools.partial(column_kernel, columns),
        "columns",
        [f32(pairs, STRIP, 2 * CELLS)]
        + part_types
        + [f32(pairs, STRIP, 2 * CELLS), f32(STRIP, CELLS), bf16(4, LANES, CELLS), bf16(CELLS, 4 * LANES)],
        (rotations, strips[2], strips[3], queries, dout),
        scratch=strip_scratch,
        smem=1,
        gflop=2.0,
    )
    raw_rows, attention, rows, factors = call(
        row_kernel,
        "rows",
        [f32(pairs, STRIP, 2 * CELLS), bf16(CELLS, features)] + [f32(k, 2 * pairs, CELLS) for k in (3, 2)],
        (strips[0], strips[1], queries, dout_turned, stats_centre, sums_centre, stats_columns, sums_columns, row_bias),
    )
    attention_arrived = across(attention, (1, 2))
    rims = call(
        rim_kernel,
        "rims",
        [bf16(2 * STRIP + 16, features)] * 4,
        (queries, dout, rows, rim_chosen, turned_arrived),
        unused=1,
    )
    rims_arrived = with_partners(rims, (3, 2))
    kept, sent = call(
        partial_kernel,
        "partial",
        [f32(far, chunk, features), bf16(far, chunk, features)],
        (attention, attention_arrived, turned, turned_arrived, rims[0]),
        unused=1,
    )
    terms = [kept, across(sent, (2, 1))]
    rims = lax.optimization_barrier((*rims, sent))[:4]
    rims_arrived |= with_partners(rims, (1, 0))
    grad_queries, centre = call(
        backward_kernel,
        "backward",
        [bf16(CELLS, features), f32(2, CELLS, features)],
        (
            *strips[::-1], queries, keys, dout, raw_centre, raw_columns, raw_rows, product_centre, product_columns,
            rows, factors, sent,
        ),
        unused=1,
        gflop=3.0,
    )
    stride = NEAR
    while stride < tile_count:
        ways = min(NEAR, tile_count // stride)
        sums = call(
            functools.partial(sum_kernel, len(terms)),
            "plane_sum",
            [bf16(tile_count // stride // ways, chunk, features)] * ways,
            (*terms, centre, rims_arrived[3], rims_arrived[2]),
            unused=3,
        )
        terms = exchanged(sums, stride)
        stride *= ways

    grad_keys, grad_values = call(
        side_kernel,
        "sides",
        [bf16(CELLS, features)] * 2,
        (centre, chosen, *(picked[s] for s in SIDE_ORDER), *(rims_arrived[s] for s in SIDE_ORDER)),
        scratch=[pltpu.VMEM((STRIP, LANES), jnp.float32)]
        + [pltpu.VMEM((CELLS, features), jnp.bfloat16)] * 2
        + [pltpu.SemaphoreType.DMA((2 * pairs,))],
        gflop=3.0,
        out_space=pl.ANY,
    )
    grad_out_weight = call(
        functools.partial(weight_kernel, 1.0 / math.sqrt(token_count * tile_count)),
        "weight_sum",
        f32(chunk, features),
        terms,
    )
    return (grad_queries, grad_keys, grad_values, grad_out_weight)


def solution(mesh):
    placed = (
        P("tile", "head"),
        P("tile", "head"),
        P("tile", "head"),
        P("tile", "head"),
        P(None, "head"),
        P("tile", None),
    )
    return jax.shard_map(
        shards,
        mesh=mesh,
        in_specs=placed,
        out_specs=(P("tile", "head"), P("tile", "head"), P("tile", "head"), P("tile", "head")),
        check_vma=False,
    )
```

```python
import functools
import math

import jax
import jax.numpy as jnp
from jax import lax
from jax.experimental import pallas as pl
from jax.experimental.pallas import tpu as pltpu
from jax.sharding import PartitionSpec as P

HEAD_DIM = 64
RADIUS = 6
SIDE = 16
CELLS = SIDE * SIDE
STRIP = RADIUS * SIDE
NEAR = 4
LANES = 128
PAIR = 2 * HEAD_DIM
VMEM_LIMIT = 32 * 1024 * 1024
NT = (((1,), (1,)), ((), ()))


def mm(a, b):
    return jnp.dot(a, b, preferred_element_type=jnp.float32)


def mm_nt(a, b):
    return lax.dot_general(a, b, NT, preferred_element_type=jnp.float32)


def strip_token(side_index, rotation, cell):
    turn = lax.rem(side_index + 6 - rotation, 4)
    depth = cell >> 4
    along = cell & (SIDE - 1)
    far = SIDE - 1 - along
    near_rim = RADIUS - 1 - depth
    far_rim = SIDE - RADIUS + depth
    row = jnp.where(turn == 0, far_rim, jnp.where(turn == 1, along, jnp.where(turn == 2, near_rim, far)))
    col = jnp.where(turn == 0, along, jnp.where(turn == 1, near_rim, jnp.where(turn == 2, far, far_rim)))
    return row * SIDE + col


def slot_side(slot, columns):
    tile = lax.axis_index("tile")
    if slot < 2:
        return jnp.where((tile + slot) & 1 == 0, 1, 3)
    return jnp.where((lax.div(tile, columns) + slot) & 1 == 0, 2, 0)


def partner(tile, tile_count, slot):
    columns = tile_count // 4
    if slot < 2:
        return (tile + (1 if (tile + slot) % 2 == 0 else -1)) % tile_count
    return (tile + (columns if (tile // columns + slot) % 2 == 0 else -columns)) % tile_count


def pick_kernel(columns, rotations_ref, keys_ref, values_ref, *out_refs):
    cell = lax.broadcasted_iota(jnp.int32, (STRIP, CELLS), 0)
    token = lax.broadcasted_iota(jnp.int32, (STRIP, CELLS), 1)
    for slot, out_ref in enumerate(out_refs):
        side = slot_side(slot, columns)
        wanted = strip_token(side, rotations_ref[0, side], cell)
        chosen = jnp.where(token == wanted, 1.0, 0.0).astype(jnp.bfloat16)
        out_ref[0] = mm(chosen, keys_ref[...]).astype(jnp.bfloat16)
        out_ref[1] = mm(chosen, values_ref[...]).astype(jnp.bfloat16)


def weight_kernel(scale, *refs):
    total = refs[0][0].astype(jnp.float32)
    for ref in refs[1:-1]:
        total += ref[0].astype(jnp.float32)
    refs[-1][...] = total * scale


def partial_kernel(attention_ref, arrived_ref, turned_ref, turned_arrived_ref, unused_ref, kept_ref, sent_ref):
    for index, out_ref in enumerate((kept_ref, sent_ref)):
        total = None
        for turned_part, attention_part in ((turned_ref, attention_ref), (turned_arrived_ref, arrived_ref)):
            turned = turned_part[index]
            turned = turned.reshape(turned.shape[0] * turned.shape[1], turned.shape[2])
            term = mm(turned, attention_part[...])
            total = term if total is None else total + term
        out_ref[...] = total.astype(out_ref.dtype).reshape(out_ref.shape)


def sum_kernel(count, *refs):
    terms, outs = refs[:count], refs[count + 3 :]
    for q in range(terms[0].shape[0]):
        total = terms[0][q].astype(jnp.float32)
        for ref in terms[1:]:
            total += ref[q].astype(jnp.float32)
        outs[q % len(outs)][q // len(outs)] = total.astype(jnp.bfloat16)


def rim_token(side_index, place):
    depth = place >> 4
    along = place & (SIDE - 1)
    last = SIDE - 1
    north, east, south = side_index == 0, side_index == 1, side_index == 2
    row = jnp.where(north, depth, jnp.where(east, along, jnp.where(south, last - depth, last - along)))
    col = jnp.where(north, along, jnp.where(east, last - depth, jnp.where(south, last - along, depth)))
    return row * SIDE + col


def cotangent_kernel(heads, *refs):
    blocks, out_weight_ref, outs = refs[:heads], refs[heads], refs[heads + 1 :]
    dout_ref, dout_turned_ref, turned_ref, turned_sent_ref = outs
    head = lax.axis_index("head")
    axis = head & 1
    tile = lax.axis_index("tile")
    chunk = turned_ref.shape[2]
    width = blocks[0].shape[1]
    total = None
    for distance, block_ref in enumerate(blocks):
        owner = lax.rem(head + distance, heads)
        start = pl.multiple_of(owner * width, width)
        block = block_ref[...]
        term = mm(block, out_weight_ref[pl.ds(start, width), :])
        total = term if total is None else total + term
        turned = block.T
        first = owner * (width // chunk)
        for index in range(width // chunk):
            target = (first + index) ^ tile
            rows = turned[index * chunk : (index + 1) * chunk]
            for parity, out_ref in enumerate((turned_ref, turned_sent_ref)):

                @pl.when((target >> axis) & 1 == parity)
                def _():
                    out_ref[(target >> (1 - axis)) & 1, target >> 2] = rows

    dout = total.astype(jnp.bfloat16)
    dout_ref[...] = dout
    dout_turned_ref[...] = dout.T


def split(exact, count):
    parts = []
    for _ in range(count):
        part = exact.astype(jnp.bfloat16).astype(jnp.float32)
        parts.append(part)
        exact = exact - part
    return parts


PARTS = (3, 2, 2)
SIDE_ORDER = (3, 2, 1, 0)


def rim_kernel(query_ref, dout_ref, rows_ref, chosen_ref, unused_ref, *rim_refs):
    parts = [part for kind, count in enumerate(PARTS) for part in split(rows_ref[kind], count)]
    pairs = rows_ref.shape[1] // 2
    filler = jnp.zeros((16 - 2 * len(parts), CELLS), jnp.float32)
    rows = [
        jnp.concatenate([part[2 * pair : 2 * pair + 2] for part in parts] + [filler], axis=0) for pair in range(pairs)
    ]
    rows = jnp.concatenate(rows, axis=0).astype(jnp.bfloat16)
    for slot, rim_ref in enumerate(rim_refs):
        chosen = chosen_ref[slot]
        rim_ref[:STRIP] = mm(chosen[:STRIP], query_ref[...]).astype(jnp.bfloat16)
        rim_ref[STRIP : 2 * STRIP] = mm(chosen[:STRIP], dout_ref[...]).astype(jnp.bfloat16)
        spread = mm_nt(rows, chosen).astype(jnp.bfloat16)
        for pair in range(pairs):
            rim_ref[2 * STRIP :, pair * PAIR : (pair + 1) * PAIR] = spread[16 * pair : 16 * pair + 16]


def window(cell_row, cell_col, query):
    query_row = (query >> 4) + RADIUS
    query_col = (query & (SIDE - 1)) + RADIUS
    near = (jnp.abs(cell_row - query_row) <= RADIUS) & (jnp.abs(cell_col - query_col) <= RADIUS)
    return jnp.where(near, 0.0, -1e30)


def centre_bias(bias_ref):
    query = lax.broadcasted_iota(jnp.int32, (CELLS, CELLS), 1)
    cell = lax.broadcasted_iota(jnp.int32, (CELLS, CELLS), 0)
    bias_ref[...] = window((cell >> 4) + RADIUS, (cell & (SIDE - 1)) + RADIUS, query)


def strip_bias(kind, bias_ref):
    query = lax.broadcasted_iota(jnp.int32, (STRIP, CELLS), 1)
    cell = lax.broadcasted_iota(jnp.int32, (STRIP, CELLS), 0)
    depth = cell >> 4
    along = cell & (SIDE - 1)
    last = SIDE + 2 * RADIUS - 1
    if kind:
        first, second = (last - RADIUS - along, depth), (RADIUS + along, last - depth)
    else:
        first, second = (depth, RADIUS + along), (last - depth, last - RADIUS - along)
    in_first = first_half(query, kind)
    row = jnp.where(in_first, first[0], second[0])
    col = jnp.where(in_first, first[1], second[1])
    bias_ref[...] = window(row, col, query)


def first_half(query, kind):
    return (query & (SIDE - 1)) < SIDE // 2 if kind else query < CELLS // 2


def one_head(block, head):
    lane = lax.broadcasted_iota(jnp.int32, block.shape, 1)
    kept = (lane >= HEAD_DIM) if head else (lane < HEAD_DIM)
    return jnp.where(kept, block, jnp.zeros_like(block))


def halves(block, kind):
    kept = first_half(lax.broadcasted_iota(jnp.int32, block.shape, 0), kind)
    zero = jnp.zeros_like(block)
    return jnp.concatenate([jnp.where(kept, block, zero), jnp.where(kept, zero, block)], axis=1)


def by_half(stacked, kind):
    rows = stacked.shape[0] // 2
    kept = first_half(lax.broadcasted_iota(jnp.int32, (rows, CELLS), 1), kind)
    return jnp.where(kept, stacked[:rows], stacked[rows:])


def side_blocks(strips, part, kind, cols):
    tile = lax.axis_index("tile")
    second, first = strips
    straight = (tile if kind else lax.div(tile, lax.axis_size("tile") // 4)) & 1 == 0
    first, second = first[part, :, cols], second[part, :, cols]
    return jnp.where(straight, first, second), jnp.where(straight, second, first)


def side_cells(strips, part, kind, cols):
    return jnp.concatenate(side_blocks(strips, part, kind, cols), axis=1)


def halves(block, kind):
    kept = first_half(lax.broadcasted_iota(jnp.int32, block.shape, 0), kind)
    zero = jnp.zeros_like(block)
    return jnp.concatenate([jnp.where(kept, block, zero), jnp.where(kept, zero, block)], axis=1)


def by_half(stacked, kind):
    rows = stacked.shape[0] // 2
    kept = first_half(lax.broadcasted_iota(jnp.int32, (rows, CELLS), 1), kind)
    return jnp.where(kept, stacked[:rows], stacked[rows:])


def side_blocks(strips, part, kind, cols):
    tile = lax.axis_index("tile")
    second, first = strips
    straight = (tile if kind else lax.div(tile, lax.axis_size("tile") // 4)) & 1 == 0
    first, second = first[part, :, cols], second[part, :, cols]
    return jnp.where(straight, first, second), jnp.where(straight, second, first)


def side_cells(strips, part, kind, cols):
    return jnp.concatenate(side_blocks(strips, part, kind, cols), axis=1)


def side_products(cells, rows_head):
    return [mm_nt(cells[kind], halves(rows_head, kind)) for kind in range(2)]


def turned_sides(strips, part, kind, cols):
    return [block.T for block in side_blocks(strips, part, kind, cols)]


def pair_cols(pair):
    return pl.ds(pl.multiple_of(pair * PAIR, PAIR), PAIR)


def head_rows(turned, head):
    return turned[head * HEAD_DIM : (head + 1) * HEAD_DIM]


def over_side(turned, head, kind, sides):
    return by_half(mm(jnp.concatenate([head_rows(t, head) for t in turned], axis=0), sides), kind)


SCORE_SCALE = HEAD_DIM ** (-0.5)
LOG_SCALE = SCORE_SCALE * math.log2(math.e)


def lanes_of(head):
    return slice(head * CELLS, (head + 1) * CELLS)


def centre_kernel(
    query_ref, key_ref, value_ref, dout_ref,
    raw_ref, stats_ref, sums_ref, product_ref, query_out, key_out, bias_ref,
):
    centre_bias(bias_ref)

    def step(pair, carry):
        cols = pair_cols(pair)
        query, key, value, dout = (ref[:, cols] for ref in (query_ref, key_ref, value_ref, dout_ref))
        turned = value.T
        for head in range(2):
            lanes = lanes_of(head)
            scores = mm_nt(key, one_head(query, head)) + bias_ref[...]
            top = jnp.max(scores, axis=0, keepdims=True)
            raw = jnp.exp2((scores - top) * LOG_SCALE)
            raw_ref[pair, :, lanes] = raw
            stats_ref[pair, 0:1, lanes] = top
            stats_ref[pair, 1:2, lanes] = jnp.sum(raw, axis=0, keepdims=True)
            sums_ref[pair, :, lanes] = mm(head_rows(turned, head), raw.astype(jnp.bfloat16))
            product_ref[pair, :, lanes] = mm_nt(value, one_head(dout, head))
        query_out[:, cols] = query
        key_out[:, cols] = key
        return carry

    lax.fori_loop(0, raw_ref.shape[0], step, 0)


def column_kernel(
    columns, rotations_ref, first_ref, second_ref, query_ref, dout_ref,
    raw_ref, stats_ref, sums_ref, product_ref, row_bias_ref, rim_chosen_ref, chosen_ref, bias_ref,
):
    strips = (first_ref, second_ref)
    strip_bias(0, bias_ref)
    strip_bias(1, row_bias_ref)
    place = lax.broadcasted_iota(jnp.int32, (LANES, CELLS), 0)
    token = lax.broadcasted_iota(jnp.int32, (LANES, CELLS), 1)
    for slot in range(4):
        wanted = rim_token(slot_side(slot, columns), place)
        chosen = jnp.where((token == wanted) & (place < STRIP), 1.0, 0.0).astype(jnp.bfloat16)
        rim_chosen_ref[slot] = chosen
    place = lax.broadcasted_iota(jnp.int32, (CELLS, LANES), 1)
    token = lax.broadcasted_iota(jnp.int32, (CELLS, LANES), 0)
    for index, slot in enumerate(SIDE_ORDER):
        side = slot_side(slot, columns)
        wanted = jnp.where(place < STRIP, strip_token(side, rotations_ref[0, side], place), -1)
        chosen = jnp.where(token == wanted, 1.0, 0.0).astype(jnp.bfloat16)
        chosen_ref[:, index * LANES : (index + 1) * LANES] = chosen

    def step(pair, carry):
        cols = pair_cols(pair)
        keys = side_cells(strips, 0, 0, cols)
        values = side_cells(strips, 1, 0, cols)
        turned = turned_sides(strips, 1, 0, cols)
        for head in range(2):
            lanes = lanes_of(head)
            scores = mm_nt(keys, halves(one_head(query_ref[:, cols], head), 0)) + bias_ref[...]
            top = jnp.max(scores, axis=0, keepdims=True)
            raw = jnp.exp2((scores - top) * LOG_SCALE)
            raw_ref[pair, :, lanes] = raw
            stats_ref[pair, 0:1, lanes] = top
            stats_ref[pair, 1:2, lanes] = jnp.sum(raw, axis=0, keepdims=True)
            sums_ref[pair, :, lanes] = over_side(turned, head, 0, raw.astype(jnp.bfloat16))
            product_ref[pair, :, lanes] = mm_nt(values, halves(one_head(dout_ref[:, cols], head), 0))
        return carry

    lax.fori_loop(0, raw_ref.shape[0], step, 0)


def row_kernel(
    first_ref, second_ref, query_ref, dout_turned_ref, centre_stats_ref, centre_sums_ref, stats_ref, sums_ref, bias_ref,
    raw_ref, attention_ref, rows_ref, factors_ref,
):
    strips = (first_ref, second_ref)

    def step(pair, carry):
        cols = pair_cols(pair)
        keys = side_cells(strips, 0, 1, cols)
        turned = turned_sides(strips, 1, 1, cols)
        parts = []
        for head in range(2):
            lanes = lanes_of(head)
            scores = mm_nt(keys, halves(one_head(query_ref[:, cols], head), 1)) + bias_ref[...]
            tops = [ref[pair, 0:1, lanes] for ref in (centre_stats_ref, stats_ref)]
            top = jnp.maximum(jnp.max(scores, axis=0, keepdims=True), jnp.maximum(*tops))
            raw = jnp.exp2((scores - top) * LOG_SCALE)
            raw_ref[pair, :, lanes] = raw
            lifted = [jnp.exp2((t - top) * LOG_SCALE) for t in tops]
            total = jnp.sum(raw, axis=0, keepdims=True)
            total += lifted[0] * centre_stats_ref[pair, 1:2, lanes] + lifted[1] * stats_ref[pair, 1:2, lanes]
            inverse = 1.0 / total
            factors = [l * inverse for l in lifted]
            part = over_side(turned, head, 1, raw.astype(jnp.bfloat16)) * inverse
            part += factors[0] * centre_sums_ref[pair, :, lanes] + factors[1] * sums_ref[pair, :, lanes]
            parts.append(part)
            place = pl.ds(2 * pair + head, 1)
            features = pl.ds(pl.multiple_of((2 * pair + head) * HEAD_DIM, HEAD_DIM), HEAD_DIM)
            product = dout_turned_ref[features, :].astype(jnp.float32) * part
            rows_ref[0, place, :] = top
            rows_ref[1, place, :] = inverse
            rows_ref[2, place, :] = jnp.sum(product, axis=0, keepdims=True)
            factors_ref[0, place, :] = factors[0]
            factors_ref[1, place, :] = factors[1]
        attention_ref[:, cols] = jnp.concatenate(parts, axis=0).T.astype(jnp.bfloat16)
        return carry

    lax.fori_loop(0, raw_ref.shape[0], step, 0, unroll=True)


def backward_kernel(
    third_ref, fourth_ref, second_ref, first_ref, query_ref, key_ref, dout_ref, centre_raw_ref, column_raw_ref,
    row_raw_ref, centre_product_ref, column_product_ref, rows_ref, factors_ref, unused_ref,
    grad_query_ref, centre_ref,
):
    columns, rows = (third_ref, fourth_ref), (first_ref, second_ref)

    def step(pair, carry):
        cols = pair_cols(pair)
        query = query_ref[:, cols]
        dout = dout_ref[:, cols]
        turned_centre = key_ref[:, cols].T
        turned_columns = turned_sides(columns, 0, 0, cols)
        turned_rows = turned_sides(rows, 0, 1, cols)
        row_values = side_cells(rows, 1, 1, cols)
        parts = []
        centre_scores = []
        centre_weights = []
        for head in range(2):
            lanes = lanes_of(head)
            place = pl.ds(2 * pair + head, 1)
            delta = rows_ref[2, place, :]
            row_product = mm_nt(row_values, halves(one_head(dout, head), 1))

            def dscore(weights, product):
                return (weights * (product - delta)).astype(jnp.bfloat16)

            weights = centre_raw_ref[pair, :, lanes] * factors_ref[0, place, :]
            centre_weights.append(weights.astype(jnp.bfloat16))
            centre_scores.append(dscore(weights, centre_product_ref[pair, :, lanes]))
            column_weights = column_raw_ref[pair, :, lanes] * factors_ref[1, place, :]
            column_score = dscore(column_weights, column_product_ref[pair, :, lanes])
            row_score = dscore(row_raw_ref[pair, :, lanes] * rows_ref[1, place, :], row_product)
            part = mm(head_rows(turned_centre, head), centre_scores[-1])
            part += over_side(turned_columns, head, 0, column_score) + over_side(turned_rows, head, 1, row_score)
            parts.append(part)
        grad_query = jnp.concatenate(parts, axis=0).T * SCORE_SCALE
        grad_query_ref[:, cols] = grad_query.astype(jnp.bfloat16)
        grad_key, grad_value = joint_mm(
            jnp.concatenate(centre_scores, axis=1),
            jnp.concatenate(centre_weights, axis=1),
            both_heads(query),
            both_heads(dout),
        )
        centre_ref[0, :, cols] = grad_key * SCORE_SCALE
        centre_ref[1, :, cols] = grad_value
        return carry

    lax.fori_loop(0, centre_raw_ref.shape[0], step, 0)


def joint_mm(first, second, first_rows, second_rows):
    rows = first.shape[0]
    product = mm(jnp.concatenate([first, second], axis=0), jnp.concatenate([first_rows, second_rows], axis=1))
    return product[:rows, :PAIR], product[rows:, PAIR:]


def both_heads(block):
    return jnp.concatenate([one_head(block, head) for head in range(2)], axis=0)


def padded(block):
    return jnp.concatenate([block, jnp.zeros((LANES - block.shape[0], block.shape[1]), block.dtype)], axis=0)


def statistics(rows):
    first = 0
    for count in PARTS:
        heads = []
        for head in range(2):
            parts = [rows[2 * index + head : 2 * index + head + 1] for index in range(first, first + count)]
            heads.append(functools.reduce(jnp.add, parts))
        first += count
        yield jnp.concatenate(heads, axis=1)


def side_kernel(centre_ref, chosen_ref, *refs):
    picked, rims = refs[:4], refs[4:8]
    keys_ref, values_ref, bias_ref, keys_done, values_done, sems = refs[8:]
    cell = lax.broadcasted_iota(jnp.int32, (STRIP, LANES), 0)
    query = lax.broadcasted_iota(jnp.int32, (STRIP, LANES), 1)
    near = jnp.abs((cell & (SIDE - 1)) - (query & (SIDE - 1))) <= RADIUS
    near = near & ((cell >> 4) >= (query >> 4)) & (query < STRIP)
    bias_ref[...] = jnp.where(near, 0.0, -1e30)
    copies = []
    for pair in range(keys_ref.shape[1] // PAIR):
        cols = slice(pair * PAIR, (pair + 1) * PAIR)
        grads = []
        bias = jnp.concatenate([bias_ref[...]] * 2, axis=1)
        for picked_ref, rim_ref in zip(picked, rims):
            query = both_heads(padded(rim_ref[:STRIP, cols]))
            dout = both_heads(padded(rim_ref[STRIP : 2 * STRIP, cols]))
            top, inverse, delta = statistics(rim_ref[2 * STRIP :, cols].astype(jnp.float32))
            scores = mm_nt(picked_ref[0, :, cols], query) + bias
            weights = jnp.exp2((scores - top) * LOG_SCALE) * inverse
            product = mm_nt(picked_ref[1, :, cols], dout)
            dscore = (weights * (product - delta)).astype(jnp.bfloat16)
            grad = jnp.concatenate([mm(dscore, query) * SCORE_SCALE, mm(weights.astype(jnp.bfloat16), dout)], axis=1)
            grads.append(padded(grad.astype(jnp.bfloat16)))
        total = mm(chosen_ref[...], jnp.concatenate(grads, axis=0))
        keys_done[:, cols] = (centre_ref[0, :, cols] + total[:, :PAIR]).astype(jnp.bfloat16)
        values_done[:, cols] = (centre_ref[1, :, cols] + total[:, PAIR:]).astype(jnp.bfloat16)
        for index, (done, out_ref) in enumerate(((keys_done, keys_ref), (values_done, values_ref))):
            copy = pltpu.make_async_copy(done.at[:, cols], out_ref.at[:, cols], sems.at[2 * pair + index])
            copy.start()
            copies.append(copy)
    for copy in copies:
        copy.wait()


def call(kernel, name, out_shape, operands, scratch=(), smem=0, unused=0, gflop=0.1, out_space=pltpu.VMEM):
    specs = [pl.BlockSpec(memory_space=pltpu.SMEM)] * smem
    specs += [pl.BlockSpec(memory_space=pltpu.VMEM)] * (len(operands) - smem - unused)
    specs += [pl.BlockSpec(memory_space=pl.ANY)] * unused
    single = not isinstance(out_shape, list)
    outs = pl.BlockSpec(memory_space=out_space)
    return pl.pallas_call(
        kernel,
        out_shape=out_shape,
        in_specs=specs,
        out_specs=outs if single else [outs] * len(out_shape),
        scratch_shapes=list(scratch),
        compiler_params=pltpu.CompilerParams(vmem_limit_bytes=VMEM_LIMIT),
        cost_estimate=pl.CostEstimate(flops=int(gflop * 1e9), bytes_accessed=1 << 20, transcendentals=0),
        name=name,
    )(*operands)


def in_hbm(array):
    return pltpu.with_memory_space_constraint(array, pltpu.HBM)


def across(block, distances):
    heads = lax.axis_size("head")
    devices = [(tile, head) for tile in range(lax.axis_size("tile")) for head in range(heads)]
    route = [(tile * heads + head, (tile ^ distances[head % 2]) * heads + head) for tile, head in devices]
    return lax.ppermute(block, ("tile", "head"), route)


def exchanged(blocks, stride):
    terms = list(blocks[:1])
    for distance in (2, 3, 1) if len(blocks) == 4 else (1,):
        route = [(tile, tile ^ (distance * stride)) for tile in range(lax.axis_size("tile"))]
        terms.append(lax.ppermute(blocks[distance], "tile", route))
    return terms


def with_partners(blocks, slots):
    tile_count = lax.axis_size("tile")
    routes = {s: [(tile, partner(tile, tile_count, s)) for tile in range(tile_count)] for s in slots}
    return {s: lax.ppermute(blocks[s], "tile", routes[s]) for s in slots}


def shards(queries, keys, values, grad_output, out_weight, rotations):
    tile_count = lax.axis_size("tile")
    token_count, features = queries.shape
    model = out_weight.shape[0]
    pairs = features // PAIR
    far = tile_count // NEAR
    chunk = model // tile_count
    heads = lax.axis_size("head")
    columns = tile_count // 4
    queries, keys, values, out_weight, rotations = (
        in_hbm(a) for a in (queries, keys, values, out_weight, rotations)
    )

    def bf16(*shape):
        return jax.ShapeDtypeStruct(shape, jnp.bfloat16)

    def f32(*shape):
        return jax.ShapeDtypeStruct(shape, jnp.float32)

    strip_types = [bf16(2, STRIP, features)] * 4
    picked = call(
        functools.partial(pick_kernel, columns), "pick_strips", strip_types, (rotations, keys, values), smem=1
    )
    grad_output, *picked = lax.optimization_barrier((grad_output, *picked))
    strips = with_partners(picked, (2, 3, 1, 0))
    strips = [strips[s] for s in range(4)]

    cotangents = [
        lax.ppermute(grad_output, "head", [((h + k) % heads, h) for h in range(heads)]) for k in range(1, heads)
    ]
    dout, dout_turned, turned, turned_sent = call(
        functools.partial(cotangent_kernel, heads),
        "cotangent",
        [bf16(CELLS, features), bf16(features, CELLS)] + [bf16(2, far, chunk, CELLS)] * 2,
        (in_hbm(grad_output), *cotangents, out_weight),
        gflop=1.0,
    )
    turned_arrived = across(turned_sent, (1, 2))
    part_types = [f32(pairs, 2, 2 * CELLS), f32(pairs, HEAD_DIM, 2 * CELLS)]
    raw_centre, stats_centre, sums_centre, product_centre, queries, keys = call(
        centre_kernel,
        "centre",
        [f32(pairs, CELLS, 2 * CELLS)] + part_types + [f32(pairs, CELLS, 2 * CELLS)] + [bf16(CELLS, features)] * 2,
        (queries, keys, values, dout),
        scratch=[pltpu.VMEM((CELLS, CELLS), jnp.float32)],
        gflop=3.0,
    )
    strip_scratch = [pltpu.VMEM((STRIP, CELLS), jnp.float32)]
    raw_columns, stats_columns, sums_columns, product_columns, row_bias, rim_chosen, chosen = call(
        functools.partial(column_kernel, columns),
        "columns",
        [f32(pairs, STRIP, 2 * CELLS)]
        + part_types
        + [f32(pairs, STRIP, 2 * CELLS), f32(STRIP, CELLS), bf16(4, LANES, CELLS), bf16(CELLS, 4 * LANES)],
        (rotations, strips[2], strips[3], queries, dout),
        scratch=strip_scratch,
        smem=1,
        gflop=2.0,
    )
    raw_rows, attention, rows, factors = call(
        row_kernel,
        "rows",
        [f32(pairs, STRIP, 2 * CELLS), bf16(CELLS, features)] + [f32(k, 2 * pairs, CELLS) for k in (3, 2)],
        (strips[0], strips[1], queries, dout_turned, stats_centre, sums_centre, stats_columns, sums_columns, row_bias),
    )
    attention_arrived = across(attention, (1, 2))
    rims = call(
        rim_kernel,
        "rims",
        [bf16(2 * STRIP + 16, features)] * 4,
        (queries, dout, rows, rim_chosen, turned_arrived),
        unused=1,
    )
    rims_arrived = with_partners(rims, (3, 2))
    kept, sent = call(
        partial_kernel,
        "partial",
        [f32(far, chunk, features), bf16(far, chunk, features)],
        (attention, attention_arrived, turned, turned_arrived, rims[0]),
        unused=1,
    )
    terms = [kept, across(sent, (2, 1))]
    rims = lax.optimization_barrier((*rims, sent))[:4]
    rims_arrived |= with_partners(rims, (1, 0))
    grad_queries, centre = call(
        backward_kernel,
        "backward",
        [bf16(CELLS, features), f32(2, CELLS, features)],
        (
            strips[2], strips[3], strips[1], strips[0], queries, keys, dout, raw_centre, raw_columns, raw_rows, product_centre, product_columns,
            rows, factors, sent,
        ),
        unused=1,
        gflop=3.0,
    )
    stride = NEAR
    while stride < tile_count:
        ways = min(NEAR, tile_count // stride)
        sums = call(
            functools.partial(sum_kernel, len(terms)),
            "plane_sum",
            [bf16(tile_count // stride // ways, chunk, features)] * ways,
            (*terms, centre, rims_arrived[3], rims_arrived[2]),
            unused=3,
        )
        terms = exchanged(sums, stride)
        stride *= ways

    grad_keys, grad_values = call(
        side_kernel,
        "sides",
        [bf16(CELLS, features)] * 2,
        (centre, chosen, *(picked[s] for s in SIDE_ORDER), *(rims_arrived[s] for s in SIDE_ORDER)),
        scratch=[pltpu.VMEM((STRIP, LANES), jnp.float32)]
        + [pltpu.VMEM((CELLS, features), jnp.bfloat16)] * 2
        + [pltpu.SemaphoreType.DMA((2 * pairs,))],
        gflop=3.0,
        out_space=pl.ANY,
    )
    grad_out_weight = call(
        functools.partial(weight_kernel, 1.0 / math.sqrt(token_count * tile_count)),
        "weight_sum",
        f32(chunk, features),
        terms,
    )
    return (grad_queries, grad_keys, grad_values, grad_out_weight)


def solution(mesh):
    placed = (
        P("tile", "head"),
        P("tile", "head"),
        P("tile", "head"),
        P("tile", "head"),
        P(None, "head"),
        P("tile", None),
    )
    return jax.shard_map(
        shards,
        mesh=mesh,
        in_specs=placed,
        out_specs=(P("tile", "head"), P("tile", "head"), P("tile", "head"), P("tile", "head")),
        check_vma=False,
    )
```

```python
import functools
import math

import jax
import jax.numpy as jnp
from jax import lax
from jax.experimental import pallas as pl
from jax.experimental.pallas import tpu as pltpu
from jax.sharding import PartitionSpec as P

HEAD_DIM = 64
RADIUS = 6
SIDE = 16
CELLS = SIDE * SIDE
STRIP = RADIUS * SIDE
NEAR = 4
LANES = 128
PAIR = 2 * HEAD_DIM
VMEM_LIMIT = 32 * 1024 * 1024
NT = (((1,), (1,)), ((), ()))


def mm(a, b):
    return jnp.dot(a, b, preferred_element_type=jnp.float32)


def mm_nt(a, b):
    return lax.dot_general(a, b, NT, preferred_element_type=jnp.float32)


def strip_token(side_index, rotation, cell):
    turn = lax.rem(side_index + 6 - rotation, 4)
    depth = cell >> 4
    along = cell & (SIDE - 1)
    far = SIDE - 1 - along
    near_rim = RADIUS - 1 - depth
    far_rim = SIDE - RADIUS + depth
    row = jnp.where(turn == 0, far_rim, jnp.where(turn == 1, along, jnp.where(turn == 2, near_rim, far)))
    col = jnp.where(turn == 0, along, jnp.where(turn == 1, near_rim, jnp.where(turn == 2, far, far_rim)))
    return row * SIDE + col


def slot_side(slot, columns):
    tile = lax.axis_index("tile")
    if slot < 2:
        return jnp.where((tile + slot) & 1 == 0, 1, 3)
    return jnp.where((lax.div(tile, columns) + slot) & 1 == 0, 2, 0)


def partner(tile, tile_count, slot):
    columns = tile_count // 4
    if slot < 2:
        return (tile + (1 if (tile + slot) % 2 == 0 else -1)) % tile_count
    return (tile + (columns if (tile // columns + slot) % 2 == 0 else -columns)) % tile_count


def pick_kernel(columns, rotations_ref, keys_ref, values_ref, *out_refs):
    cell = lax.broadcasted_iota(jnp.int32, (STRIP, CELLS), 0)
    token = lax.broadcasted_iota(jnp.int32, (STRIP, CELLS), 1)
    for slot, out_ref in enumerate(out_refs):
        side = slot_side(slot, columns)
        wanted = strip_token(side, rotations_ref[0, side], cell)
        chosen = jnp.where(token == wanted, 1.0, 0.0).astype(jnp.bfloat16)
        out_ref[0] = mm(chosen, keys_ref[...]).astype(jnp.bfloat16)
        out_ref[1] = mm(chosen, values_ref[...]).astype(jnp.bfloat16)


def weight_kernel(scale, *refs):
    total = refs[0][0].astype(jnp.float32)
    for ref in refs[1:-1]:
        total += ref[0].astype(jnp.float32)
    refs[-1][...] = total * scale


def partial_kernel(attention_ref, arrived_ref, turned_ref, turned_arrived_ref, unused_ref, kept_ref, sent_ref):
    for index, out_ref in enumerate((kept_ref, sent_ref)):
        total = None
        for turned_part, attention_part in ((turned_ref, attention_ref), (turned_arrived_ref, arrived_ref)):
            turned = turned_part[index]
            turned = turned.reshape(turned.shape[0] * turned.shape[1], turned.shape[2])
            term = mm(turned, attention_part[...])
            total = term if total is None else total + term
        out_ref[...] = total.astype(out_ref.dtype).reshape(out_ref.shape)


def sum_kernel(count, *refs):
    terms, outs = refs[:count], refs[count + 3 :]
    for q in range(terms[0].shape[0]):
        total = terms[0][q].astype(jnp.float32)
        for ref in terms[1:]:
            total += ref[q].astype(jnp.float32)
        outs[q % len(outs)][q // len(outs)] = total.astype(jnp.bfloat16)


def rim_token(side_index, place):
    depth = place >> 4
    along = place & (SIDE - 1)
    last = SIDE - 1
    north, east, south = side_index == 0, side_index == 1, side_index == 2
    row = jnp.where(north, depth, jnp.where(east, along, jnp.where(south, last - depth, last - along)))
    col = jnp.where(north, along, jnp.where(east, last - depth, jnp.where(south, last - along, depth)))
    return row * SIDE + col


def cotangent_kernel(heads, *refs):
    blocks, out_weight_ref, outs = refs[:heads], refs[heads], refs[heads + 1 :]
    dout_ref, dout_turned_ref, turned_ref, turned_sent_ref = outs
    head = lax.axis_index("head")
    axis = head & 1
    tile = lax.axis_index("tile")
    chunk = turned_ref.shape[2]
    width = blocks[0].shape[1]
    total = None
    for distance, block_ref in enumerate(blocks):
        owner = lax.rem(head + distance, heads)
        start = pl.multiple_of(owner * width, width)
        block = block_ref[...]
        term = mm(block, out_weight_ref[pl.ds(start, width), :])
        total = term if total is None else total + term
        turned = block.T
        first = owner * (width // chunk)
        for index in range(width // chunk):
            target = (first + index) ^ tile
            rows = turned[index * chunk : (index + 1) * chunk]
            for parity, out_ref in enumerate((turned_ref, turned_sent_ref)):

                @pl.when((target >> axis) & 1 == parity)
                def _():
                    out_ref[(target >> (1 - axis)) & 1, target >> 2] = rows

    dout = total.astype(jnp.bfloat16)
    dout_ref[...] = dout
    dout_turned_ref[...] = dout.T


def split(exact, count):
    parts = []
    for _ in range(count):
        part = exact.astype(jnp.bfloat16).astype(jnp.float32)
        parts.append(part)
        exact = exact - part
    return parts


PARTS = (3, 2, 2)
SIDE_ORDER = (3, 2, 1, 0)


def rim_kernel(query_ref, dout_ref, rows_ref, chosen_ref, unused_ref, *rim_refs):
    parts = [part for kind, count in enumerate(PARTS) for part in split(rows_ref[kind], count)]
    pairs = rows_ref.shape[1] // 2
    filler = jnp.zeros((16 - 2 * len(parts), CELLS), jnp.float32)
    rows = [
        jnp.concatenate([part[2 * pair : 2 * pair + 2] for part in parts] + [filler], axis=0) for pair in range(pairs)
    ]
    rows = jnp.concatenate(rows, axis=0).astype(jnp.bfloat16)
    for slot, rim_ref in enumerate(rim_refs):
        chosen = chosen_ref[slot]
        rim_ref[:STRIP] = mm(chosen[:STRIP], query_ref[...]).astype(jnp.bfloat16)
        rim_ref[STRIP : 2 * STRIP] = mm(chosen[:STRIP], dout_ref[...]).astype(jnp.bfloat16)
        spread = mm_nt(rows, chosen).astype(jnp.bfloat16)
        for pair in range(pairs):
            rim_ref[2 * STRIP :, pair * PAIR : (pair + 1) * PAIR] = spread[16 * pair : 16 * pair + 16]


def window(cell_row, cell_col, query):
    query_row = (query >> 4) + RADIUS
    query_col = (query & (SIDE - 1)) + RADIUS
    near = (jnp.abs(cell_row - query_row) <= RADIUS) & (jnp.abs(cell_col - query_col) <= RADIUS)
    return jnp.where(near, 0.0, -1e30)


def centre_bias(bias_ref):
    query = lax.broadcasted_iota(jnp.int32, (CELLS, CELLS), 1)
    cell = lax.broadcasted_iota(jnp.int32, (CELLS, CELLS), 0)
    bias_ref[...] = window((cell >> 4) + RADIUS, (cell & (SIDE - 1)) + RADIUS, query)


def strip_bias(kind, bias_ref):
    query = lax.broadcasted_iota(jnp.int32, (STRIP, CELLS), 1)
    cell = lax.broadcasted_iota(jnp.int32, (STRIP, CELLS), 0)
    depth = cell >> 4
    along = cell & (SIDE - 1)
    last = SIDE + 2 * RADIUS - 1
    if kind:
        first, second = (last - RADIUS - along, depth), (RADIUS + along, last - depth)
    else:
        first, second = (depth, RADIUS + along), (last - depth, last - RADIUS - along)
    in_first = first_half(query, kind)
    row = jnp.where(in_first, first[0], second[0])
    col = jnp.where(in_first, first[1], second[1])
    bias_ref[...] = window(row, col, query)


def first_half(query, kind):
    return (query & (SIDE - 1)) < SIDE // 2 if kind else query < CELLS // 2


def one_head(block, head):
    lane = lax.broadcasted_iota(jnp.int32, block.shape, 1)
    kept = (lane >= HEAD_DIM) if head else (lane < HEAD_DIM)
    return jnp.where(kept, block, jnp.zeros_like(block))


def halves(block, kind):
    kept = first_half(lax.broadcasted_iota(jnp.int32, block.shape, 0), kind)
    zero = jnp.zeros_like(block)
    return jnp.concatenate([jnp.where(kept, block, zero), jnp.where(kept, zero, block)], axis=1)


def by_half(stacked, kind):
    rows = stacked.shape[0] // 2
    kept = first_half(lax.broadcasted_iota(jnp.int32, (rows, CELLS), 1), kind)
    return jnp.where(kept, stacked[:rows], stacked[rows:])


def side_blocks(strips, part, kind, cols):
    tile = lax.axis_index("tile")
    second, first = strips
    straight = (tile if kind else lax.div(tile, lax.axis_size("tile") // 4)) & 1 == 0
    first, second = first[part, :, cols], second[part, :, cols]
    return jnp.where(straight, first, second), jnp.where(straight, second, first)


def side_cells(strips, part, kind, cols):
    return jnp.concatenate(side_blocks(strips, part, kind, cols), axis=1)


def halves(block, kind):
    kept = first_half(lax.broadcasted_iota(jnp.int32, block.shape, 0), kind)
    zero = jnp.zeros_like(block)
    return jnp.concatenate([jnp.where(kept, block, zero), jnp.where(kept, zero, block)], axis=1)


def by_half(stacked, kind):
    rows = stacked.shape[0] // 2
    kept = first_half(lax.broadcasted_iota(jnp.int32, (rows, CELLS), 1), kind)
    return jnp.where(kept, stacked[:rows], stacked[rows:])


def side_blocks(strips, part, kind, cols):
    tile = lax.axis_index("tile")
    second, first = strips
    straight = (tile if kind else lax.div(tile, lax.axis_size("tile") // 4)) & 1 == 0
    first, second = first[part, :, cols], second[part, :, cols]
    return jnp.where(straight, first, second), jnp.where(straight, second, first)


def side_cells(strips, part, kind, cols):
    return jnp.concatenate(side_blocks(strips, part, kind, cols), axis=1)


def side_products(cells, rows_head):
    return [mm_nt(cells[kind], halves(rows_head, kind)) for kind in range(2)]


def turned_sides(strips, part, kind, cols):
    return [block.T for block in side_blocks(strips, part, kind, cols)]


def pair_cols(pair):
    return pl.ds(pl.multiple_of(pair * PAIR, PAIR), PAIR)


def head_rows(turned, head):
    return turned[head * HEAD_DIM : (head + 1) * HEAD_DIM]


def over_side(turned, head, kind, sides):
    return by_half(mm(jnp.concatenate([head_rows(t, head) for t in turned], axis=0), sides), kind)


SCORE_SCALE = HEAD_DIM ** (-0.5)
LOG_SCALE = SCORE_SCALE * math.log2(math.e)


def lanes_of(head):
    return slice(head * CELLS, (head + 1) * CELLS)


def centre_kernel(
    query_ref, key_ref, value_ref, dout_ref,
    raw_ref, stats_ref, sums_ref, product_ref, query_out, key_out, bias_ref,
):
    centre_bias(bias_ref)

    def step(pair, carry):
        cols = pair_cols(pair)
        query, key, value, dout = (ref[:, cols] for ref in (query_ref, key_ref, value_ref, dout_ref))
        turned = value.T
        for head in range(2):
            lanes = lanes_of(head)
            scores = mm_nt(key, one_head(query, head)) + bias_ref[...]
            top = jnp.max(scores, axis=0, keepdims=True)
            raw = jnp.exp2((scores - top) * LOG_SCALE)
            raw_ref[pair, :, lanes] = raw
            stats_ref[pair, 0:1, lanes] = top
            stats_ref[pair, 1:2, lanes] = jnp.sum(raw, axis=0, keepdims=True)
            sums_ref[pair, :, lanes] = mm(head_rows(turned, head), raw.astype(jnp.bfloat16))
            product_ref[pair, :, lanes] = mm_nt(value, one_head(dout, head))
        query_out[:, cols] = query
        key_out[:, cols] = key
        return carry

    lax.fori_loop(0, raw_ref.shape[0], step, 0)


def column_kernel(
    columns, rotations_ref, first_ref, second_ref, query_ref, dout_ref,
    raw_ref, stats_ref, sums_ref, product_ref, row_bias_ref, rim_chosen_ref, chosen_ref, bias_ref,
):
    strips = (first_ref, second_ref)
    strip_bias(0, bias_ref)
    strip_bias(1, row_bias_ref)
    place = lax.broadcasted_iota(jnp.int32, (LANES, CELLS), 0)
    token = lax.broadcasted_iota(jnp.int32, (LANES, CELLS), 1)
    for slot in range(4):
        wanted = rim_token(slot_side(slot, columns), place)
        chosen = jnp.where((token == wanted) & (place < STRIP), 1.0, 0.0).astype(jnp.bfloat16)
        rim_chosen_ref[slot] = chosen
    place = lax.broadcasted_iota(jnp.int32, (CELLS, LANES), 1)
    token = lax.broadcasted_iota(jnp.int32, (CELLS, LANES), 0)
    for index, slot in enumerate(SIDE_ORDER):
        side = slot_side(slot, columns)
        wanted = jnp.where(place < STRIP, strip_token(side, rotations_ref[0, side], place), -1)
        chosen = jnp.where(token == wanted, 1.0, 0.0).astype(jnp.bfloat16)
        chosen_ref[:, index * LANES : (index + 1) * LANES] = chosen

    def step(pair, carry):
        cols = pair_cols(pair)
        keys = side_cells(strips, 0, 0, cols)
        values = side_cells(strips, 1, 0, cols)
        turned = turned_sides(strips, 1, 0, cols)
        for head in range(2):
            lanes = lanes_of(head)
            scores = mm_nt(keys, halves(one_head(query_ref[:, cols], head), 0)) + bias_ref[...]
            top = jnp.max(scores, axis=0, keepdims=True)
            raw = jnp.exp2((scores - top) * LOG_SCALE)
            raw_ref[pair, :, lanes] = raw
            stats_ref[pair, 0:1, lanes] = top
            stats_ref[pair, 1:2, lanes] = jnp.sum(raw, axis=0, keepdims=True)
            sums_ref[pair, :, lanes] = over_side(turned, head, 0, raw.astype(jnp.bfloat16))
            product_ref[pair, :, lanes] = mm_nt(values, halves(one_head(dout_ref[:, cols], head), 0))
        return carry

    lax.fori_loop(0, raw_ref.shape[0], step, 0)


def row_kernel(
    first_ref, second_ref, query_ref, dout_turned_ref, centre_stats_ref, centre_sums_ref, stats_ref, sums_ref, bias_ref,
    raw_ref, attention_ref, rows_ref, factors_ref,
):
    strips = (first_ref, second_ref)

    def step(pair, carry):
        cols = pair_cols(pair)
        keys = side_cells(strips, 0, 1, cols)
        turned = turned_sides(strips, 1, 1, cols)
        parts = []
        for head in range(2):
            lanes = lanes_of(head)
            scores = mm_nt(keys, halves(one_head(query_ref[:, cols], head), 1)) + bias_ref[...]
            tops = [ref[pair, 0:1, lanes] for ref in (centre_stats_ref, stats_ref)]
            top = jnp.maximum(jnp.max(scores, axis=0, keepdims=True), jnp.maximum(*tops))
            raw = jnp.exp2((scores - top) * LOG_SCALE)
            raw_ref[pair, :, lanes] = raw
            lifted = [jnp.exp2((t - top) * LOG_SCALE) for t in tops]
            total = jnp.sum(raw, axis=0, keepdims=True)
            total += lifted[0] * centre_stats_ref[pair, 1:2, lanes] + lifted[1] * stats_ref[pair, 1:2, lanes]
            inverse = 1.0 / total
            factors = [l * inverse for l in lifted]
            part = over_side(turned, head, 1, raw.astype(jnp.bfloat16)) * inverse
            part += factors[0] * centre_sums_ref[pair, :, lanes] + factors[1] * sums_ref[pair, :, lanes]
            parts.append(part)
            place = pl.ds(2 * pair + head, 1)
            features = pl.ds(pl.multiple_of((2 * pair + head) * HEAD_DIM, HEAD_DIM), HEAD_DIM)
            product = dout_turned_ref[features, :].astype(jnp.float32) * part
            rows_ref[0, place, :] = top
            rows_ref[1, place, :] = inverse
            rows_ref[2, place, :] = jnp.sum(product, axis=0, keepdims=True)
            factors_ref[0, place, :] = factors[0]
            factors_ref[1, place, :] = factors[1]
        attention_ref[:, cols] = jnp.concatenate(parts, axis=0).T.astype(jnp.bfloat16)
        return carry

    lax.fori_loop(0, raw_ref.shape[0], step, 0, unroll=True)


def backward_kernel(
    fourth_ref, third_ref, second_ref, first_ref, query_ref, key_ref, dout_ref, centre_raw_ref, column_raw_ref,
    row_raw_ref, centre_product_ref, column_product_ref, rows_ref, factors_ref, unused_ref,
    grad_query_ref, centre_ref,
):
    columns, rows = (third_ref, fourth_ref), (first_ref, second_ref)

    def step(pair, carry):
        cols = pair_cols(pair)
        query = query_ref[:, cols]
        dout = dout_ref[:, cols]
        turned_centre = key_ref[:, cols].T
        turned_columns = turned_sides(columns, 0, 0, cols)
        turned_rows = turned_sides(rows, 0, 1, cols)
        row_values = side_cells(rows, 1, 1, cols)
        parts = []
        centre_scores = []
        centre_weights = []
        for head in range(2):
            lanes = lanes_of(head)
            place = pl.ds(2 * pair + head, 1)
            delta = rows_ref[2, place, :]
            row_product = mm_nt(row_values, halves(one_head(dout, head), 1))

            def dscore(weights, product):
                return (weights * (product - delta)).astype(jnp.bfloat16)

            weights = centre_raw_ref[pair, :, lanes] * factors_ref[0, place, :]
            centre_weights.append(weights.astype(jnp.bfloat16))
            centre_scores.append(dscore(weights, centre_product_ref[pair, :, lanes]))
            column_weights = column_raw_ref[pair, :, lanes] * factors_ref[1, place, :]
            column_score = dscore(column_weights, column_product_ref[pair, :, lanes])
            row_score = dscore(row_raw_ref[pair, :, lanes] * rows_ref[1, place, :], row_product)
            part = mm(head_rows(turned_centre, head), centre_scores[-1])
            part += over_side(turned_columns, head, 0, column_score) + over_side(turned_rows, head, 1, row_score)
            parts.append(part)
        grad_query = jnp.concatenate(parts, axis=0).T * SCORE_SCALE
        grad_query_ref[:, cols] = grad_query.astype(jnp.bfloat16)
        grad_key, grad_value = joint_mm(
            jnp.concatenate(centre_scores, axis=1),
            jnp.concatenate(centre_weights, axis=1),
            both_heads(query),
            both_heads(dout),
        )
        centre_ref[0, :, cols] = grad_key * SCORE_SCALE
        centre_ref[1, :, cols] = grad_value
        return carry

    lax.fori_loop(0, centre_raw_ref.shape[0], step, 0)


def joint_mm(first, second, first_rows, second_rows):
    rows = first.shape[0]
    product = mm(jnp.concatenate([first, second], axis=0), jnp.concatenate([first_rows, second_rows], axis=1))
    return product[:rows, :PAIR], product[rows:, PAIR:]


def both_heads(block):
    return jnp.concatenate([one_head(block, head) for head in range(2)], axis=0)


def padded(block):
    return jnp.concatenate([block, jnp.zeros((LANES - block.shape[0], block.shape[1]), block.dtype)], axis=0)


def statistics(rows):
    first = 0
    for count in PARTS:
        heads = []
        for head in range(2):
            parts = [rows[2 * index + head : 2 * index + head + 1] for index in range(first, first + count)]
            heads.append(functools.reduce(jnp.add, parts))
        first += count
        yield jnp.concatenate(heads, axis=1)


def side_kernel(centre_ref, chosen_ref, *refs):
    picked, rims = refs[:4], refs[4:8]
    keys_ref, values_ref, bias_ref, keys_done, values_done, sems = refs[8:]
    cell = lax.broadcasted_iota(jnp.int32, (STRIP, LANES), 0)
    query = lax.broadcasted_iota(jnp.int32, (STRIP, LANES), 1)
    near = jnp.abs((cell & (SIDE - 1)) - (query & (SIDE - 1))) <= RADIUS
    near = near & ((cell >> 4) >= (query >> 4)) & (query < STRIP)
    bias_ref[...] = jnp.where(near, 0.0, -1e30)
    copies = []
    for pair in range(keys_ref.shape[1] // PAIR):
        cols = slice(pair * PAIR, (pair + 1) * PAIR)
        grads = []
        bias = jnp.concatenate([bias_ref[...]] * 2, axis=1)
        for picked_ref, rim_ref in zip(picked, rims):
            query = both_heads(padded(rim_ref[:STRIP, cols]))
            dout = both_heads(padded(rim_ref[STRIP : 2 * STRIP, cols]))
            top, inverse, delta = statistics(rim_ref[2 * STRIP :, cols].astype(jnp.float32))
            scores = mm_nt(picked_ref[0, :, cols], query) + bias
            weights = jnp.exp2((scores - top) * LOG_SCALE) * inverse
            product = mm_nt(picked_ref[1, :, cols], dout)
            dscore = (weights * (product - delta)).astype(jnp.bfloat16)
            grad = jnp.concatenate([mm(dscore, query) * SCORE_SCALE, mm(weights.astype(jnp.bfloat16), dout)], axis=1)
            grads.append(padded(grad.astype(jnp.bfloat16)))
        total = mm(chosen_ref[...], jnp.concatenate(grads, axis=0))
        keys_done[:, cols] = (centre_ref[0, :, cols] + total[:, :PAIR]).astype(jnp.bfloat16)
        values_done[:, cols] = (centre_ref[1, :, cols] + total[:, PAIR:]).astype(jnp.bfloat16)
        for index, (done, out_ref) in enumerate(((keys_done, keys_ref), (values_done, values_ref))):
            copy = pltpu.make_async_copy(done.at[:, cols], out_ref.at[:, cols], sems.at[2 * pair + index])
            copy.start()
            copies.append(copy)
    for copy in copies:
        copy.wait()


def call(kernel, name, out_shape, operands, scratch=(), smem=0, unused=0, gflop=0.1, out_space=pltpu.VMEM):
    specs = [pl.BlockSpec(memory_space=pltpu.SMEM)] * smem
    specs += [pl.BlockSpec(memory_space=pltpu.VMEM)] * (len(operands) - smem - unused)
    specs += [pl.BlockSpec(memory_space=pl.ANY)] * unused
    single = not isinstance(out_shape, list)
    outs = pl.BlockSpec(memory_space=out_space)
    return pl.pallas_call(
        kernel,
        out_shape=out_shape,
        in_specs=specs,
        out_specs=outs if single else [outs] * len(out_shape),
        scratch_shapes=list(scratch),
        compiler_params=pltpu.CompilerParams(vmem_limit_bytes=VMEM_LIMIT),
        cost_estimate=pl.CostEstimate(flops=int(gflop * 1e9), bytes_accessed=1 << 20, transcendentals=0),
        name=name,
    )(*operands)


def in_hbm(array):
    return pltpu.with_memory_space_constraint(array, pltpu.HBM)


def across(block, distances):
    heads = lax.axis_size("head")
    devices = [(tile, head) for tile in range(lax.axis_size("tile")) for head in range(heads)]
    route = [(tile * heads + head, (tile ^ distances[head % 2]) * heads + head) for tile, head in devices]
    return lax.ppermute(block, ("tile", "head"), route)


def exchanged(blocks, stride):
    terms = list(blocks[:1])
    for distance in (3, 2, 1) if len(blocks) == 4 else (1,):
        route = [(tile, tile ^ (distance * stride)) for tile in range(lax.axis_size("tile"))]
        terms.append(lax.ppermute(blocks[distance], "tile", route))
    return terms


def with_partners(blocks, slots):
    tile_count = lax.axis_size("tile")
    routes = {s: [(tile, partner(tile, tile_count, s)) for tile in range(tile_count)] for s in slots}
    return {s: lax.ppermute(blocks[s], "tile", routes[s]) for s in slots}


def shards(queries, keys, values, grad_output, out_weight, rotations):
    tile_count = lax.axis_size("tile")
    token_count, features = queries.shape
    model = out_weight.shape[0]
    pairs = features // PAIR
    far = tile_count // NEAR
    chunk = model // tile_count
    heads = lax.axis_size("head")
    columns = tile_count // 4
    queries, keys, values, out_weight, rotations = (
        in_hbm(a) for a in (queries, keys, values, out_weight, rotations)
    )

    def bf16(*shape):
        return jax.ShapeDtypeStruct(shape, jnp.bfloat16)

    def f32(*shape):
        return jax.ShapeDtypeStruct(shape, jnp.float32)

    strip_types = [bf16(2, STRIP, features)] * 4
    picked = call(
        functools.partial(pick_kernel, columns), "pick_strips", strip_types, (rotations, keys, values), smem=1
    )
    grad_output, *picked = lax.optimization_barrier((grad_output, *picked))
    strips = with_partners(picked, (3, 2, 1, 0))
    strips = [strips[s] for s in range(4)]

    cotangents = [
        lax.ppermute(grad_output, "head", [((h + k) % heads, h) for h in range(heads)]) for k in range(1, heads)
    ]
    dout, dout_turned, turned, turned_sent = call(
        functools.partial(cotangent_kernel, heads),
        "cotangent",
        [bf16(CELLS, features), bf16(features, CELLS)] + [bf16(2, far, chunk, CELLS)] * 2,
        (in_hbm(grad_output), *cotangents, out_weight),
        gflop=1.0,
    )
    turned_arrived = across(turned_sent, (1, 2))
    part_types = [f32(pairs, 2, 2 * CELLS), f32(pairs, HEAD_DIM, 2 * CELLS)]
    raw_centre, stats_centre, sums_centre, product_centre, queries, keys = call(
        centre_kernel,
        "centre",
        [f32(pairs, CELLS, 2 * CELLS)] + part_types + [f32(pairs, CELLS, 2 * CELLS)] + [bf16(CELLS, features)] * 2,
        (queries, keys, values, dout),
        scratch=[pltpu.VMEM((CELLS, CELLS), jnp.float32)],
        gflop=3.0,
    )
    strip_scratch = [pltpu.VMEM((STRIP, CELLS), jnp.float32)]
    raw_columns, stats_columns, sums_columns, product_columns, row_bias, rim_chosen, chosen = call(
        functools.partial(column_kernel, columns),
        "columns",
        [f32(pairs, STRIP, 2 * CELLS)]
        + part_types
        + [f32(pairs, STRIP, 2 * CELLS), f32(STRIP, CELLS), bf16(4, LANES, CELLS), bf16(CELLS, 4 * LANES)],
        (rotations, strips[2], strips[3], queries, dout),
        scratch=strip_scratch,
        smem=1,
        gflop=2.0,
    )
    raw_rows, attention, rows, factors = call(
        row_kernel,
        "rows",
        [f32(pairs, STRIP, 2 * CELLS), bf16(CELLS, features)] + [f32(k, 2 * pairs, CELLS) for k in (3, 2)],
        (strips[0], strips[1], queries, dout_turned, stats_centre, sums_centre, stats_columns, sums_columns, row_bias),
    )
    attention_arrived = across(attention, (1, 2))
    rims = call(
        rim_kernel,
        "rims",
        [bf16(2 * STRIP + 16, features)] * 4,
        (queries, dout, rows, rim_chosen, turned_arrived),
        unused=1,
    )
    rims_arrived = with_partners(rims, (3, 2))
    kept, sent = call(
        partial_kernel,
        "partial",
        [f32(far, chunk, features), bf16(far, chunk, features)],
        (attention, attention_arrived, turned, turned_arrived, rims[0]),
        unused=1,
    )
    terms = [kept, across(sent, (2, 1))]
    rims = lax.optimization_barrier((*rims, sent))[:4]
    rims_arrived |= with_partners(rims, (1, 0))
    grad_queries, centre = call(
        backward_kernel,
        "backward",
        [bf16(CELLS, features), f32(2, CELLS, features)],
        (
            *strips[::-1], queries, keys, dout, raw_centre, raw_columns, raw_rows, product_centre, product_columns,
            rows, factors, sent,
        ),
        unused=1,
        gflop=3.0,
    )
    stride = NEAR
    while stride < tile_count:
        ways = min(NEAR, tile_count // stride)
        sums = call(
            functools.partial(sum_kernel, len(terms)),
            "plane_sum",
            [bf16(tile_count // stride // ways, chunk, features)] * ways,
            (*terms, centre, rims_arrived[3], rims_arrived[2]),
            unused=3,
        )
        terms = exchanged(sums, stride)
        stride *= ways

    grad_keys, grad_values = call(
        side_kernel,
        "sides",
        [bf16(CELLS, features)] * 2,
        (centre, chosen, *(picked[s] for s in SIDE_ORDER), *(rims_arrived[s] for s in SIDE_ORDER)),
        scratch=[pltpu.VMEM((STRIP, LANES), jnp.float32)]
        + [pltpu.VMEM((CELLS, features), jnp.bfloat16)] * 2
        + [pltpu.SemaphoreType.DMA((2 * pairs,))],
        gflop=3.0,
        out_space=pl.ANY,
    )
    grad_out_weight = call(
        functools.partial(weight_kernel, 1.0 / math.sqrt(token_count * tile_count)),
        "weight_sum",
        f32(chunk, features),
        terms,
    )
    return (grad_queries, grad_keys, grad_values, grad_out_weight)


def solution(mesh):
    placed = (
        P("tile", "head"),
        P("tile", "head"),
        P("tile", "head"),
        P("tile", "head"),
        P(None, "head"),
        P("tile", None),
    )
    return jax.shard_map(
        shards,
        mesh=mesh,
        in_specs=placed,
        out_specs=(P("tile", "head"), P("tile", "head"), P("tile", "head"), P("tile", "head")),
        check_vma=False,
    )
```

```python
import functools
import math

import jax
import jax.numpy as jnp
from jax import lax
from jax.experimental import pallas as pl
from jax.experimental.pallas import tpu as pltpu
from jax.sharding import PartitionSpec as P

HEAD_DIM = 64
RADIUS = 6
SIDE = 16
CELLS = SIDE * SIDE
STRIP = RADIUS * SIDE
NEAR = 4
LANES = 128
PAIR = 2 * HEAD_DIM
VMEM_LIMIT = 32 * 1024 * 1024
NT = (((1,), (1,)), ((), ()))


def mm(a, b):
    return jnp.dot(a, b, preferred_element_type=jnp.float32)


def mm_nt(a, b):
    return lax.dot_general(a, b, NT, preferred_element_type=jnp.float32)


def strip_token(side_index, rotation, cell):
    turn = lax.rem(side_index + 6 - rotation, 4)
    depth = cell >> 4
    along = cell & (SIDE - 1)
    far = SIDE - 1 - along
    near_rim = RADIUS - 1 - depth
    far_rim = SIDE - RADIUS + depth
    row = jnp.where(turn == 0, far_rim, jnp.where(turn == 1, along, jnp.where(turn == 2, near_rim, far)))
    col = jnp.where(turn == 0, along, jnp.where(turn == 1, near_rim, jnp.where(turn == 2, far, far_rim)))
    return row * SIDE + col


def slot_side(slot, columns):
    tile = lax.axis_index("tile")
    if slot < 2:
        return jnp.where((tile + slot) & 1 == 0, 1, 3)
    return jnp.where((lax.div(tile, columns) + slot) & 1 == 0, 2, 0)


def partner(tile, tile_count, slot):
    columns = tile_count // 4
    if slot < 2:
        return (tile + (1 if (tile + slot) % 2 == 0 else -1)) % tile_count
    return (tile + (columns if (tile // columns + slot) % 2 == 0 else -columns)) % tile_count


def pick_kernel(columns, rotations_ref, keys_ref, values_ref, *out_refs):
    cell = lax.broadcasted_iota(jnp.int32, (STRIP, CELLS), 0)
    token = lax.broadcasted_iota(jnp.int32, (STRIP, CELLS), 1)
    for slot, out_ref in enumerate(out_refs):
        side = slot_side(slot, columns)
        wanted = strip_token(side, rotations_ref[0, side], cell)
        chosen = jnp.where(token == wanted, 1.0, 0.0).astype(jnp.bfloat16)
        out_ref[0] = mm(chosen, keys_ref[...]).astype(jnp.bfloat16)
        out_ref[1] = mm(chosen, values_ref[...]).astype(jnp.bfloat16)


def weight_kernel(scale, *refs):
    total = refs[0][0].astype(jnp.float32)
    for ref in refs[1:-1]:
        total += ref[0].astype(jnp.float32)
    refs[-1][...] = total * scale


def partial_kernel(attention_ref, arrived_ref, turned_ref, turned_arrived_ref, unused_ref, kept_ref, sent_ref):
    for index, out_ref in enumerate((kept_ref, sent_ref)):
        total = None
        for turned_part, attention_part in ((turned_ref, attention_ref), (turned_arrived_ref, arrived_ref)):
            turned = turned_part[index]
            turned = turned.reshape(turned.shape[0] * turned.shape[1], turned.shape[2])
            term = mm(turned, attention_part[...])
            total = term if total is None else total + term
        out_ref[...] = total.astype(out_ref.dtype).reshape(out_ref.shape)


def sum_kernel(count, *refs):
    terms, outs = refs[:count], refs[count + 3 :]
    for q in range(terms[0].shape[0]):
        total = terms[0][q].astype(jnp.float32)
        for ref in terms[1:]:
            total += ref[q].astype(jnp.float32)
        outs[q % len(outs)][q // len(outs)] = total.astype(jnp.bfloat16)


def rim_token(side_index, place):
    depth = place >> 4
    along = place & (SIDE - 1)
    last = SIDE - 1
    north, east, south = side_index == 0, side_index == 1, side_index == 2
    row = jnp.where(north, depth, jnp.where(east, along, jnp.where(south, last - depth, last - along)))
    col = jnp.where(north, along, jnp.where(east, last - depth, jnp.where(south, last - along, depth)))
    return row * SIDE + col


def cotangent_kernel(heads, *refs):
    blocks, out_weight_ref, outs = refs[:heads], refs[heads], refs[heads + 1 :]
    dout_ref, dout_turned_ref, turned_ref, turned_sent_ref = outs
    head = lax.axis_index("head")
    axis = head & 1
    tile = lax.axis_index("tile")
    chunk = turned_ref.shape[2]
    width = blocks[0].shape[1]
    total = None
    for distance, block_ref in enumerate(blocks):
        owner = lax.rem(head + distance, heads)
        start = pl.multiple_of(owner * width, width)
        block = block_ref[...]
        term = mm(block, out_weight_ref[pl.ds(start, width), :])
        total = term if total is None else total + term
        turned = block.T
        first = owner * (width // chunk)
        for index in range(width // chunk):
            target = (first + index) ^ tile
            rows = turned[index * chunk : (index + 1) * chunk]
            for parity, out_ref in enumerate((turned_ref, turned_sent_ref)):

                @pl.when((target >> axis) & 1 == parity)
                def _():
                    out_ref[(target >> (1 - axis)) & 1, target >> 2] = rows

    dout = total.astype(jnp.bfloat16)
    dout_ref[...] = dout
    dout_turned_ref[...] = dout.T


def split(exact, count):
    parts = []
    for _ in range(count):
        part = exact.astype(jnp.bfloat16).astype(jnp.float32)
        parts.append(part)
        exact = exact - part
    return parts


PARTS = (3, 2, 2)
SIDE_ORDER = (3, 2, 1, 0)


def rim_kernel(rim_rows_ref, rows_ref, chosen_ref, unused_ref, *rim_refs):
    parts = [part for kind, count in enumerate(PARTS) for part in split(rows_ref[kind], count)]
    pairs = rows_ref.shape[1] // 2
    filler = jnp.zeros((16 - 2 * len(parts), CELLS), jnp.float32)
    rows = [
        jnp.concatenate([part[2 * pair : 2 * pair + 2] for part in parts] + [filler], axis=0) for pair in range(pairs)
    ]
    rows = jnp.concatenate(rows, axis=0).astype(jnp.bfloat16)
    for slot, rim_ref in enumerate(rim_refs):
        chosen = chosen_ref[slot]
        rim_ref[: 2 * STRIP] = rim_rows_ref[slot]
        spread = mm_nt(rows, chosen).astype(jnp.bfloat16)
        for pair in range(pairs):
            rim_ref[2 * STRIP :, pair * PAIR : (pair + 1) * PAIR] = spread[16 * pair : 16 * pair + 16]


def window(cell_row, cell_col, query):
    query_row = (query >> 4) + RADIUS
    query_col = (query & (SIDE - 1)) + RADIUS
    near = (jnp.abs(cell_row - query_row) <= RADIUS) & (jnp.abs(cell_col - query_col) <= RADIUS)
    return jnp.where(near, 0.0, -1e30)


def centre_bias(bias_ref):
    query = lax.broadcasted_iota(jnp.int32, (CELLS, CELLS), 1)
    cell = lax.broadcasted_iota(jnp.int32, (CELLS, CELLS), 0)
    bias_ref[...] = window((cell >> 4) + RADIUS, (cell & (SIDE - 1)) + RADIUS, query)


def strip_bias(kind, bias_ref):
    query = lax.broadcasted_iota(jnp.int32, (STRIP, CELLS), 1)
    cell = lax.broadcasted_iota(jnp.int32, (STRIP, CELLS), 0)
    depth = cell >> 4
    along = cell & (SIDE - 1)
    last = SIDE + 2 * RADIUS - 1
    if kind:
        first, second = (last - RADIUS - along, depth), (RADIUS + along, last - depth)
    else:
        first, second = (depth, RADIUS + along), (last - depth, last - RADIUS - along)
    in_first = first_half(query, kind)
    row = jnp.where(in_first, first[0], second[0])
    col = jnp.where(in_first, first[1], second[1])
    bias_ref[...] = window(row, col, query)


def first_half(query, kind):
    return (query & (SIDE - 1)) < SIDE // 2 if kind else query < CELLS // 2


def one_head(block, head):
    lane = lax.broadcasted_iota(jnp.int32, block.shape, 1)
    kept = (lane >= HEAD_DIM) if head else (lane < HEAD_DIM)
    return jnp.where(kept, block, jnp.zeros_like(block))


def halves(block, kind):
    kept = first_half(lax.broadcasted_iota(jnp.int32, block.shape, 0), kind)
    zero = jnp.zeros_like(block)
    return jnp.concatenate([jnp.where(kept, block, zero), jnp.where(kept, zero, block)], axis=1)


def by_half(stacked, kind):
    rows = stacked.shape[0] // 2
    kept = first_half(lax.broadcasted_iota(jnp.int32, (rows, CELLS), 1), kind)
    return jnp.where(kept, stacked[:rows], stacked[rows:])


def side_blocks(strips, part, kind, cols):
    tile = lax.axis_index("tile")
    second, first = strips
    straight = (tile if kind else lax.div(tile, lax.axis_size("tile") // 4)) & 1 == 0
    first, second = first[part, :, cols], second[part, :, cols]
    return jnp.where(straight, first, second), jnp.where(straight, second, first)


def side_cells(strips, part, kind, cols):
    return jnp.concatenate(side_blocks(strips, part, kind, cols), axis=1)


def halves(block, kind):
    kept = first_half(lax.broadcasted_iota(jnp.int32, block.shape, 0), kind)
    zero = jnp.zeros_like(block)
    return jnp.concatenate([jnp.where(kept, block, zero), jnp.where(kept, zero, block)], axis=1)


def by_half(stacked, kind):
    rows = stacked.shape[0] // 2
    kept = first_half(lax.broadcasted_iota(jnp.int32, (rows, CELLS), 1), kind)
    return jnp.where(kept, stacked[:rows], stacked[rows:])


def side_blocks(strips, part, kind, cols):
    tile = lax.axis_index("tile")
    second, first = strips
    straight = (tile if kind else lax.div(tile, lax.axis_size("tile") // 4)) & 1 == 0
    first, second = first[part, :, cols], second[part, :, cols]
    return jnp.where(straight, first, second), jnp.where(straight, second, first)


def side_cells(strips, part, kind, cols):
    return jnp.concatenate(side_blocks(strips, part, kind, cols), axis=1)


def side_products(cells, rows_head):
    return [mm_nt(cells[kind], halves(rows_head, kind)) for kind in range(2)]


def turned_sides(strips, part, kind, cols):
    return [block.T for block in side_blocks(strips, part, kind, cols)]


def pair_cols(pair):
    return pl.ds(pl.multiple_of(pair * PAIR, PAIR), PAIR)


def head_rows(turned, head):
    return turned[head * HEAD_DIM : (head + 1) * HEAD_DIM]


def over_side(turned, head, kind, sides):
    return by_half(mm(jnp.concatenate([head_rows(t, head) for t in turned], axis=0), sides), kind)


SCORE_SCALE = HEAD_DIM ** (-0.5)
LOG_SCALE = SCORE_SCALE * math.log2(math.e)


def lanes_of(head):
    return slice(head * CELLS, (head + 1) * CELLS)


def centre_kernel(
    query_ref, key_ref, value_ref, dout_ref,
    raw_ref, stats_ref, sums_ref, product_ref, query_out, key_out, bias_ref,
):
    centre_bias(bias_ref)

    def step(pair, carry):
        cols = pair_cols(pair)
        query, key, value, dout = (ref[:, cols] for ref in (query_ref, key_ref, value_ref, dout_ref))
        turned = value.T
        for head in range(2):
            lanes = lanes_of(head)
            scores = mm_nt(key, one_head(query, head)) + bias_ref[...]
            top = jnp.max(scores, axis=0, keepdims=True)
            raw = jnp.exp2((scores - top) * LOG_SCALE)
            raw_ref[pair, :, lanes] = raw
            stats_ref[pair, 0:1, lanes] = top
            stats_ref[pair, 1:2, lanes] = jnp.sum(raw, axis=0, keepdims=True)
            sums_ref[pair, :, lanes] = mm(head_rows(turned, head), raw.astype(jnp.bfloat16))
            product_ref[pair, :, lanes] = mm_nt(value, one_head(dout, head))
        query_out[:, cols] = query
        key_out[:, cols] = key
        return carry

    lax.fori_loop(0, raw_ref.shape[0], step, 0)


def column_kernel(
    columns, rotations_ref, first_ref, second_ref, query_ref, dout_ref,
    raw_ref, stats_ref, sums_ref, product_ref, row_bias_ref, rim_chosen_ref, chosen_ref, rim_rows_ref, bias_ref,
):
    strips = (first_ref, second_ref)
    strip_bias(0, bias_ref)
    strip_bias(1, row_bias_ref)
    place = lax.broadcasted_iota(jnp.int32, (LANES, CELLS), 0)
    token = lax.broadcasted_iota(jnp.int32, (LANES, CELLS), 1)
    for slot in range(4):
        wanted = rim_token(slot_side(slot, columns), place)
        chosen = jnp.where((token == wanted) & (place < STRIP), 1.0, 0.0).astype(jnp.bfloat16)
        rim_chosen_ref[slot] = chosen
        rim_rows_ref[slot, :STRIP] = mm(chosen[:STRIP], query_ref[...]).astype(jnp.bfloat16)
        rim_rows_ref[slot, STRIP:] = mm(chosen[:STRIP], dout_ref[...]).astype(jnp.bfloat16)
    place = lax.broadcasted_iota(jnp.int32, (CELLS, LANES), 1)
    token = lax.broadcasted_iota(jnp.int32, (CELLS, LANES), 0)
    for index, slot in enumerate(SIDE_ORDER):
        side = slot_side(slot, columns)
        wanted = jnp.where(place < STRIP, strip_token(side, rotations_ref[0, side], place), -1)
        chosen = jnp.where(token == wanted, 1.0, 0.0).astype(jnp.bfloat16)
        chosen_ref[:, index * LANES : (index + 1) * LANES] = chosen

    def step(pair, carry):
        cols = pair_cols(pair)
        keys = side_cells(strips, 0, 0, cols)
        values = side_cells(strips, 1, 0, cols)
        turned = turned_sides(strips, 1, 0, cols)
        for head in range(2):
            lanes = lanes_of(head)
            scores = mm_nt(keys, halves(one_head(query_ref[:, cols], head), 0)) + bias_ref[...]
            top = jnp.max(scores, axis=0, keepdims=True)
            raw = jnp.exp2((scores - top) * LOG_SCALE)
            raw_ref[pair, :, lanes] = raw
            stats_ref[pair, 0:1, lanes] = top
            stats_ref[pair, 1:2, lanes] = jnp.sum(raw, axis=0, keepdims=True)
            sums_ref[pair, :, lanes] = over_side(turned, head, 0, raw.astype(jnp.bfloat16))
            product_ref[pair, :, lanes] = mm_nt(values, halves(one_head(dout_ref[:, cols], head), 0))
        return carry

    lax.fori_loop(0, raw_ref.shape[0], step, 0)


def row_kernel(
    first_ref, second_ref, query_ref, dout_turned_ref, centre_stats_ref, centre_sums_ref, stats_ref, sums_ref, bias_ref,
    raw_ref, attention_ref, rows_ref, factors_ref,
):
    strips = (first_ref, second_ref)

    def step(pair, carry):
        cols = pair_cols(pair)
        keys = side_cells(strips, 0, 1, cols)
        turned = turned_sides(strips, 1, 1, cols)
        parts = []
        for head in range(2):
            lanes = lanes_of(head)
            scores = mm_nt(keys, halves(one_head(query_ref[:, cols], head), 1)) + bias_ref[...]
            tops = [ref[pair, 0:1, lanes] for ref in (centre_stats_ref, stats_ref)]
            top = jnp.maximum(jnp.max(scores, axis=0, keepdims=True), jnp.maximum(*tops))
            raw = jnp.exp2((scores - top) * LOG_SCALE)
            raw_ref[pair, :, lanes] = raw
            lifted = [jnp.exp2((t - top) * LOG_SCALE) for t in tops]
            total = jnp.sum(raw, axis=0, keepdims=True)
            total += lifted[0] * centre_stats_ref[pair, 1:2, lanes] + lifted[1] * stats_ref[pair, 1:2, lanes]
            inverse = 1.0 / total
            factors = [l * inverse for l in lifted]
            part = over_side(turned, head, 1, raw.astype(jnp.bfloat16)) * inverse
            part += factors[0] * centre_sums_ref[pair, :, lanes] + factors[1] * sums_ref[pair, :, lanes]
            parts.append(part)
            place = pl.ds(2 * pair + head, 1)
            features = pl.ds(pl.multiple_of((2 * pair + head) * HEAD_DIM, HEAD_DIM), HEAD_DIM)
            product = dout_turned_ref[features, :].astype(jnp.float32) * part
            rows_ref[0, place, :] = top
            rows_ref[1, place, :] = inverse
            rows_ref[2, place, :] = jnp.sum(product, axis=0, keepdims=True)
            factors_ref[0, place, :] = factors[0]
            factors_ref[1, place, :] = factors[1]
        attention_ref[:, cols] = jnp.concatenate(parts, axis=0).T.astype(jnp.bfloat16)
        return carry

    lax.fori_loop(0, raw_ref.shape[0], step, 0, unroll=True)


def backward_kernel(
    fourth_ref, third_ref, second_ref, first_ref, query_ref, key_ref, dout_ref, centre_raw_ref, column_raw_ref,
    row_raw_ref, centre_product_ref, column_product_ref, rows_ref, factors_ref, unused_ref,
    grad_query_ref, centre_ref,
):
    columns, rows = (third_ref, fourth_ref), (first_ref, second_ref)

    def step(pair, carry):
        cols = pair_cols(pair)
        query = query_ref[:, cols]
        dout = dout_ref[:, cols]
        turned_centre = key_ref[:, cols].T
        turned_columns = turned_sides(columns, 0, 0, cols)
        turned_rows = turned_sides(rows, 0, 1, cols)
        row_values = side_cells(rows, 1, 1, cols)
        parts = []
        centre_scores = []
        centre_weights = []
        for head in range(2):
            lanes = lanes_of(head)
            place = pl.ds(2 * pair + head, 1)
            delta = rows_ref[2, place, :]
            row_product = mm_nt(row_values, halves(one_head(dout, head), 1))

            def dscore(weights, product):
                return (weights * (product - delta)).astype(jnp.bfloat16)

            weights = centre_raw_ref[pair, :, lanes] * factors_ref[0, place, :]
            centre_weights.append(weights.astype(jnp.bfloat16))
            centre_scores.append(dscore(weights, centre_product_ref[pair, :, lanes]))
            column_weights = column_raw_ref[pair, :, lanes] * factors_ref[1, place, :]
            column_score = dscore(column_weights, column_product_ref[pair, :, lanes])
            row_score = dscore(row_raw_ref[pair, :, lanes] * rows_ref[1, place, :], row_product)
            part = mm(head_rows(turned_centre, head), centre_scores[-1])
            part += over_side(turned_columns, head, 0, column_score) + over_side(turned_rows, head, 1, row_score)
            parts.append(part)
        grad_query = jnp.concatenate(parts, axis=0).T * SCORE_SCALE
        grad_query_ref[:, cols] = grad_query.astype(jnp.bfloat16)
        grad_key, grad_value = joint_mm(
            jnp.concatenate(centre_scores, axis=1),
            jnp.concatenate(centre_weights, axis=1),
            both_heads(query),
            both_heads(dout),
        )
        centre_ref[0, :, cols] = grad_key * SCORE_SCALE
        centre_ref[1, :, cols] = grad_value
        return carry

    lax.fori_loop(0, centre_raw_ref.shape[0], step, 0)


def joint_mm(first, second, first_rows, second_rows):
    rows = first.shape[0]
    product = mm(jnp.concatenate([first, second], axis=0), jnp.concatenate([first_rows, second_rows], axis=1))
    return product[:rows, :PAIR], product[rows:, PAIR:]


def both_heads(block):
    return jnp.concatenate([one_head(block, head) for head in range(2)], axis=0)


def padded(block):
    return jnp.concatenate([block, jnp.zeros((LANES - block.shape[0], block.shape[1]), block.dtype)], axis=0)


def statistics(rows):
    first = 0
    for count in PARTS:
        heads = []
        for head in range(2):
            parts = [rows[2 * index + head : 2 * index + head + 1] for index in range(first, first + count)]
            heads.append(functools.reduce(jnp.add, parts))
        first += count
        yield jnp.concatenate(heads, axis=1)


def side_kernel(centre_ref, chosen_ref, *refs):
    picked, rims = refs[:4], refs[4:8]
    keys_ref, values_ref, bias_ref, keys_done, values_done, sems = refs[8:]
    cell = lax.broadcasted_iota(jnp.int32, (STRIP, LANES), 0)
    query = lax.broadcasted_iota(jnp.int32, (STRIP, LANES), 1)
    near = jnp.abs((cell & (SIDE - 1)) - (query & (SIDE - 1))) <= RADIUS
    near = near & ((cell >> 4) >= (query >> 4)) & (query < STRIP)
    bias_ref[...] = jnp.where(near, 0.0, -1e30)
    copies = []
    for pair in range(keys_ref.shape[1] // PAIR):
        cols = slice(pair * PAIR, (pair + 1) * PAIR)
        grads = []
        bias = jnp.concatenate([bias_ref[...]] * 2, axis=1)
        for picked_ref, rim_ref in zip(picked, rims):
            query = both_heads(padded(rim_ref[:STRIP, cols]))
            dout = both_heads(padded(rim_ref[STRIP : 2 * STRIP, cols]))
            top, inverse, delta = statistics(rim_ref[2 * STRIP :, cols].astype(jnp.float32))
            scores = mm_nt(picked_ref[0, :, cols], query) + bias
            weights = jnp.exp2((scores - top) * LOG_SCALE) * inverse
            product = mm_nt(picked_ref[1, :, cols], dout)
            dscore = (weights * (product - delta)).astype(jnp.bfloat16)
            grad = jnp.concatenate([mm(dscore, query) * SCORE_SCALE, mm(weights.astype(jnp.bfloat16), dout)], axis=1)
            grads.append(padded(grad.astype(jnp.bfloat16)))
        total = mm(chosen_ref[...], jnp.concatenate(grads, axis=0))
        keys_done[:, cols] = (centre_ref[0, :, cols] + total[:, :PAIR]).astype(jnp.bfloat16)
        values_done[:, cols] = (centre_ref[1, :, cols] + total[:, PAIR:]).astype(jnp.bfloat16)
        for index, (done, out_ref) in enumerate(((keys_done, keys_ref), (values_done, values_ref))):
            copy = pltpu.make_async_copy(done.at[:, cols], out_ref.at[:, cols], sems.at[2 * pair + index])
            copy.start()
            copies.append(copy)
    for copy in copies:
        copy.wait()


def call(kernel, name, out_shape, operands, scratch=(), smem=0, unused=0, gflop=0.1, out_space=pltpu.VMEM):
    specs = [pl.BlockSpec(memory_space=pltpu.SMEM)] * smem
    specs += [pl.BlockSpec(memory_space=pltpu.VMEM)] * (len(operands) - smem - unused)
    specs += [pl.BlockSpec(memory_space=pl.ANY)] * unused
    single = not isinstance(out_shape, list)
    outs = pl.BlockSpec(memory_space=out_space)
    return pl.pallas_call(
        kernel,
        out_shape=out_shape,
        in_specs=specs,
        out_specs=outs if single else [outs] * len(out_shape),
        scratch_shapes=list(scratch),
        compiler_params=pltpu.CompilerParams(vmem_limit_bytes=VMEM_LIMIT),
        cost_estimate=pl.CostEstimate(flops=int(gflop * 1e9), bytes_accessed=1 << 20, transcendentals=0),
        name=name,
    )(*operands)


def in_hbm(array):
    return pltpu.with_memory_space_constraint(array, pltpu.HBM)


def across(block, distances):
    heads = lax.axis_size("head")
    devices = [(tile, head) for tile in range(lax.axis_size("tile")) for head in range(heads)]
    route = [(tile * heads + head, (tile ^ distances[head % 2]) * heads + head) for tile, head in devices]
    return lax.ppermute(block, ("tile", "head"), route)


def exchanged(blocks, stride):
    terms = list(blocks[:1])
    for distance in (2, 3, 1) if len(blocks) == 4 else (1,):
        route = [(tile, tile ^ (distance * stride)) for tile in range(lax.axis_size("tile"))]
        terms.append(lax.ppermute(blocks[distance], "tile", route))
    return terms


def with_partners(blocks, slots):
    tile_count = lax.axis_size("tile")
    routes = {s: [(tile, partner(tile, tile_count, s)) for tile in range(tile_count)] for s in slots}
    return {s: lax.ppermute(blocks[s], "tile", routes[s]) for s in slots}


def shards(queries, keys, values, grad_output, out_weight, rotations):
    tile_count = lax.axis_size("tile")
    token_count, features = queries.shape
    model = out_weight.shape[0]
    pairs = features // PAIR
    far = tile_count // NEAR
    chunk = model // tile_count
    heads = lax.axis_size("head")
    columns = tile_count // 4
    queries, keys, values, out_weight, rotations = (
        in_hbm(a) for a in (queries, keys, values, out_weight, rotations)
    )

    def bf16(*shape):
        return jax.ShapeDtypeStruct(shape, jnp.bfloat16)

    def f32(*shape):
        return jax.ShapeDtypeStruct(shape, jnp.float32)

    strip_types = [bf16(2, STRIP, features)] * 4
    picked = call(
        functools.partial(pick_kernel, columns), "pick_strips", strip_types, (rotations, keys, values), smem=1
    )
    grad_output, *picked = lax.optimization_barrier((grad_output, *picked))
    strips = with_partners(picked, (3, 2, 1, 0))
    strips = [strips[s] for s in range(4)]

    cotangents = [
        lax.ppermute(grad_output, "head", [((h + k) % heads, h) for h in range(heads)]) for k in range(1, heads)
    ]
    dout, dout_turned, turned, turned_sent = call(
        functools.partial(cotangent_kernel, heads),
        "cotangent",
        [bf16(CELLS, features), bf16(features, CELLS)] + [bf16(2, far, chunk, CELLS)] * 2,
        (in_hbm(grad_output), *cotangents, out_weight),
        gflop=1.0,
    )
    turned_arrived = across(turned_sent, (1, 2))
    part_types = [f32(pairs, 2, 2 * CELLS), f32(pairs, HEAD_DIM, 2 * CELLS)]
    raw_centre, stats_centre, sums_centre, product_centre, queries, keys = call(
        centre_kernel,
        "centre",
        [f32(pairs, CELLS, 2 * CELLS)] + part_types + [f32(pairs, CELLS, 2 * CELLS)] + [bf16(CELLS, features)] * 2,
        (queries, keys, values, dout),
        scratch=[pltpu.VMEM((CELLS, CELLS), jnp.float32)],
        gflop=3.0,
    )
    strip_scratch = [pltpu.VMEM((STRIP, CELLS), jnp.float32)]
    raw_columns, stats_columns, sums_columns, product_columns, row_bias, rim_chosen, chosen, rim_rows = call(
        functools.partial(column_kernel, columns),
        "columns",
        [f32(pairs, STRIP, 2 * CELLS)]
        + part_types
        + [f32(pairs, STRIP, 2 * CELLS), f32(STRIP, CELLS), bf16(4, LANES, CELLS), bf16(CELLS, 4 * LANES)]
        + [bf16(4, 2 * STRIP, features)],
        (rotations, strips[2], strips[3], queries, dout),
        scratch=strip_scratch,
        smem=1,
        gflop=2.0,
    )
    raw_rows, attention, rows, factors = call(
        row_kernel,
        "rows",
        [f32(pairs, STRIP, 2 * CELLS), bf16(CELLS, features)] + [f32(k, 2 * pairs, CELLS) for k in (3, 2)],
        (strips[0], strips[1], queries, dout_turned, stats_centre, sums_centre, stats_columns, sums_columns, row_bias),
    )
    attention_arrived = across(attention, (1, 2))
    rims = call(
        rim_kernel,
        "rims",
        [bf16(2 * STRIP + 16, features)] * 4,
        (rim_rows, rows, rim_chosen, turned_arrived),
        unused=1,
    )
    rims_arrived = with_partners(rims, (3, 2))
    kept, sent = call(
        partial_kernel,
        "partial",
        [f32(far, chunk, features), bf16(far, chunk, features)],
        (attention, attention_arrived, turned, turned_arrived, rims[0]),
        unused=1,
    )
    terms = [kept, across(sent, (2, 1))]
    rims = lax.optimization_barrier((*rims, sent))[:4]
    rims_arrived |= with_partners(rims, (1, 0))
    grad_queries, centre = call(
        backward_kernel,
        "backward",
        [bf16(CELLS, features), f32(2, CELLS, features)],
        (
            *strips[::-1], queries, keys, dout, raw_centre, raw_columns, raw_rows, product_centre, product_columns,
            rows, factors, sent,
        ),
        unused=1,
        gflop=3.0,
    )
    stride = NEAR
    while stride < tile_count:
        ways = min(NEAR, tile_count // stride)
        sums = call(
            functools.partial(sum_kernel, len(terms)),
            "plane_sum",
            [bf16(tile_count // stride // ways, chunk, features)] * ways,
            (*terms, centre, rims_arrived[3], rims_arrived[2]),
            unused=3,
        )
        terms = exchanged(sums, stride)
        stride *= ways

    grad_keys, grad_values = call(
        side_kernel,
        "sides",
        [bf16(CELLS, features)] * 2,
        (centre, chosen, *(picked[s] for s in SIDE_ORDER), *(rims_arrived[s] for s in SIDE_ORDER)),
        scratch=[pltpu.VMEM((STRIP, LANES), jnp.float32)]
        + [pltpu.VMEM((CELLS, features), jnp.bfloat16)] * 2
        + [pltpu.SemaphoreType.DMA((2 * pairs,))],
        gflop=3.0,
        out_space=pl.ANY,
    )
    grad_out_weight = call(
        functools.partial(weight_kernel, 1.0 / math.sqrt(token_count * tile_count)),
        "weight_sum",
        f32(chunk, features),
        terms,
    )
    return (grad_queries, grad_keys, grad_values, grad_out_weight)


def solution(mesh):
    placed = (
        P("tile", "head"),
        P("tile", "head"),
        P("tile", "head"),
        P("tile", "head"),
        P(None, "head"),
        P("tile", None),
    )
    return jax.shard_map(
        shards,
        mesh=mesh,
        in_specs=placed,
        out_specs=(P("tile", "head"), P("tile", "head"), P("tile", "head"), P("tile", "head")),
        check_vma=False,
    )
```
